32 devices in a mesh: seq: 8 (over z, y), tp: 4 (over x, core).
Axes of the slice: x: 2, y: 2, z: 4, core: 2. Of those that a mesh axis runs over, the one named last changes fastest.
Arguments:
- stream_in: bfloat16 [4, 2048, 1024], P(None, 'seq'), may hold values from -6 to 6
- norm_gain: bfloat16 [2, 1024], replicated, may hold values from 0.099609375 to 1.8984375
- in_proj: bfloat16 [2, 1024, 3, 1024], P(None, None, None, 'tp'), may hold values from -0.1875 to 0.1875
- conv_taps: bfloat16 [2, 3, 1024], P(None, None, 'tp'), may hold values from -3.5 to 3.5
- out_proj: bfloat16 [2, 1024, 1024], P(None, 'tp'), may hold values from -0.1875 to 0.1875
- ffn_gain: bfloat16 [2, 1024], replicated, may hold values from 0.099609375 to 1.8984375
- gate_proj: bfloat16 [2, 1024, 4608], P(None, None, 'tp'), may hold values from -0.1875 to 0.1875
- up_proj: bfloat16 [2, 1024, 4608], P(None, None, 'tp'), may hold values from -0.1875 to 0.1875
- down_proj: bfloat16 [2, 4608, 1024], P(None, 'tp'), may hold values from -0.09375 to 0.09375
- out_grad: bfloat16 [4, 2048, 1024], P(None, 'seq'), may hold values from -6 to 6
Outputs:
- stream_out: bfloat16 [4, 2048, 1024], P(None, 'seq')
- stream_grad: float32 [4, 2048, 1024], P(None, 'seq')
- norm_gain_grad: float32 [2, 1024], P(None, 'tp')
- in_proj_grad: float32 [2, 1024, 3, 1024], P(None, 'seq', None, 'tp')
- conv_grad: float32 [2, 3, 1024], P(None, None, 'tp')
- out_proj_grad: float32 [2, 1024, 1024], P(None, 'tp', 'seq')
- ffn_gain_grad: float32 [2, 1024], P(None, 'tp')
- gate_grad: float32 [2, 1024, 4608], P(None, 'seq', 'tp')
- up_grad: float32 [2, 1024, 4608], P(None, 'seq', 'tp')
- down_grad: float32 [2, 4608, 1024], P(None, 'tp', 'seq')
The draws below stay inside these ranges and needn't reach their ends.
All inputs are finite; a program needn't handle non-finite values.
Results may differ from the reference program's by a relative error of at most 0.022.
Values may be sent and summed in bfloat16 or wider, within the bound.
A program may use at most 256 MiB of HBM per device.

```python
import jax
import jax.numpy as jnp
from jax import lax

D = 1024
FF = 4608
LAYERS = 2
MICRO = 4
LENGTH = 2048


def with_spikes(values, own_key, source, target, parts, factor):
    owner, partner = [(jnp.arange(values.shape[position]) // (values.shape[position] // parts)).reshape([-1 if axis == position else 1 for axis in range(values.ndim)]) for position in (source, target)]
    chosen = jax.random.permutation(own_key, parts)[partner]
    strong = (owner == chosen) | (owner == (partner + parts // 2) % parts)
    return jnp.where(strong, factor * values, values)


def block_levels(own_key, dims, split, low, high):
    level = 1.0
    for position, parts in split:
        steps = jax.random.uniform(jax.random.fold_in(jax.random.fold_in(own_key, 6), position), (parts,), jnp.float32, low / len(split), high / len(split))
        level = level * jnp.repeat(jnp.exp(steps), dims[position] // parts).reshape((-1,) + (1,) * (len(dims) - 1 - position))
    return level


def gaussian(rng, extent, width, most, shards=(), dtype=jnp.bfloat16):
    drawn = jax.random.normal(rng, extent, jnp.float32) * width
    if len(shards) > 0:
        drawn = block_levels(rng, extent, shards, -0.22, 0.18) * drawn
    return jnp.clip(drawn, min=-most, max=most).astype(dtype)


def bell_draw_with(key, extent, spread, reach, pieces, heavy, kind=jnp.bfloat16):
    array = spread * jax.random.normal(key, extent, jnp.float32)
    if pieces:
        array = array * block_levels(key, extent, pieces, -0.22, 0.18)
    return jnp.clip(with_spikes(array, jax.random.fold_in(key, 3), *heavy), -reach, reach).astype(kind)


def setup_inputs(seed: int = 0) -> dict:
    key_of = jax.random.split(jax.random.key(seed), 11)
    return {
        "stream_in": gaussian(key_of[0], (MICRO, LENGTH, D), 1.0, 6.0, ((1, 8),)),
        "norm_gain": jnp.clip(1.0 + 0.18 * jax.random.normal(key_of[1], (LAYERS, D), jnp.float32), 0.099609375, 1.8984375).astype(jnp.bfloat16),
        "in_proj": gaussian(key_of[2], (LAYERS, D, 3, D), D ** -0.5, 0.1875, ((3, 4),)),
        "conv_taps": gaussian(key_of[3], (LAYERS, 3, D), 3 ** -0.5, 3.5, ((2, 4),)),
        "out_proj": gaussian(key_of[4], (LAYERS, D, D), D ** -0.5, 0.1875, ((1, 4),)),
        "ffn_gain": jnp.clip(1.0 + 0.18 * jax.random.normal(key_of[5], (LAYERS, D), jnp.float32), 0.099609375, 1.8984375).astype(jnp.bfloat16),
        "gate_proj": gaussian(key_of[6], (LAYERS, D, FF), D ** -0.5, 0.1875, ((2, 4),)),
        "up_proj": gaussian(key_of[7], (LAYERS, D, FF), D ** -0.5, 0.1875, ((2, 4),)),
        "down_proj": gaussian(key_of[8], (LAYERS, FF, D), FF ** -0.5, 0.09375, ((1, 4),)),
        "out_grad": bell_draw_with(key_of[9], (MICRO, LENGTH, D), 1.0, 6.0, ((1, 8),), (1, 2, 8, 2.0)),
    }


EPS = 1e-05
HIGH = lax.Precision.HIGHEST

@jax.custom_vjp
def low(v):
    return lax.optimization_barrier(v.astype(jnp.bfloat16)).astype(jnp.float32)

@jax.custom_vjp
def low_back(v):
    return v

def low_keep(v):
    return (low(v), None)

def low_pass(kept, grad):
    return (grad,)

def back_keep(v):
    return (v, None)

def back_low(kept, grad):
    return (low(grad),)
low.defvjp(low_keep, low_pass)
low_back.defvjp(back_keep, back_low)

def normed(h, gain):
    return h * lax.rsqrt(lax.optimization_barrier(jnp.mean(h * h, axis=-1, keepdims=True)) + EPS) * gain

def forward(hidden, norm_gain, in_proj, conv_taps, out_proj, ffn_gain, gate_proj, up_proj, down_proj):
    for layer in range(LAYERS):
        first = low(normed(hidden, norm_gain[layer]))
        proj = low_back(jnp.einsum('td,dkc->tkc', first, in_proj[layer], precision=HIGH))
        bgate = proj[:, 0]
        cgate = proj[:, 1]
        xinput = proj[:, 2]
        mixed = low(bgate * xinput)
        padded = jnp.concatenate([jnp.zeros((2, mixed.shape[1]), jnp.float32), mixed], axis=0)
        taps = conv_taps[layer]
        conved = taps[0] * padded[:-2] + taps[1] * padded[1:-1] + taps[2] * padded[2:]
        gated = low(cgate * conved)
        branch = low_back(jnp.dot(gated, out_proj[layer], precision=HIGH))
        middle = hidden + branch
        second = low(normed(middle, ffn_gain[layer]))
        gate_val = low_back(jnp.dot(second, gate_proj[layer], precision=HIGH))
        up_val = low_back(jnp.dot(second, up_proj[layer], precision=HIGH))
        act = low(jax.nn.silu(gate_val) * up_val)
        ffn_out = low_back(jnp.dot(act, down_proj[layer], precision=HIGH))
        hidden = middle + ffn_out
    return hidden

def reference(stream_in, norm_gain, in_proj, conv_taps, out_proj, ffn_gain, gate_proj, up_proj, down_proj, out_grad):
    weights = tuple((w.astype(jnp.float32) for w in (norm_gain, in_proj, conv_taps, out_proj, ffn_gain, gate_proj, up_proj, down_proj)))
    sequences = stream_in.astype(jnp.float32)
    cotangents = out_grad.astype(jnp.float32)

    def step(totals, pair):
        seq_val, cot_val = pair
        result, pull = jax.vjp(forward, seq_val, *weights)
        grads = pull(cot_val)
        totals = tuple((t + g for t, g in zip(totals, grads[1:])))
        return (totals, (result, grads[0]))
    start = tuple((jnp.zeros_like(w) for w in weights))
    totals, (results, in_grads) = lax.scan(step, start, (sequences, cotangents))
    return (results.astype(jnp.bfloat16), in_grads, totals[0], totals[1], totals[2], totals[3], totals[4], totals[5], totals[6], totals[7])
```

```python
import functools

import jax
import jax.numpy as jnp
from jax import lax
from jax.experimental import pallas as pl
from jax.experimental.pallas import tpu as pltpu
from jax.sharding import PartitionSpec as P

LAYERS = 2


EPS = 1e-05


def passed_along(block, axis, distance):
    devices = range(lax.axis_size(axis))
    route = [(i - distance, i) for i in devices if i - distance in devices]
    return lax.ppermute(block, axis, route)


def norm_rate(hidden):
    return lax.rsqrt(jnp.mean(hidden * hidden, axis=-1, keepdims=True) + EPS)


def norm_back(grad_in, gain, normed_val, rate):
    scaled = grad_in * gain
    return rate * (scaled - normed_val * jnp.mean(scaled * normed_val, axis=-1, keepdims=True))


def reduce_weights(grads):
    return (
        lax.psum_scatter(
            grads[0].astype(jnp.bfloat16), "seq", scatter_dimension=1, tiled=True
        ).astype(jnp.float32),
        lax.psum_scatter(
            grads[1].astype(jnp.bfloat16), "seq", scatter_dimension=2, tiled=True
        ).astype(jnp.float32),
        lax.psum_scatter(
            grads[2].astype(jnp.bfloat16), "seq", scatter_dimension=1, tiled=True
        ).astype(jnp.float32),
        lax.psum_scatter(
            grads[3].astype(jnp.bfloat16), "seq", scatter_dimension=1, tiled=True
        ).astype(jnp.float32),
        lax.psum_scatter(
            grads[4].astype(jnp.bfloat16), "seq", scatter_dimension=2, tiled=True
        ).astype(jnp.float32),
    )


def reduce_small(grads):
    return lax.psum((grads[0], grads[1], grads[2]), "seq")


def body(
    stream_in,
    norm_gain,
    in_proj,
    conv_taps,
    out_proj,
    ffn_gain,
    gate_proj,
    up_proj,
    down_proj,
    out_grad,
):
    f32 = jnp.float32
    bf16 = jnp.bfloat16
    width = in_proj.shape[-1]
    offset = lax.axis_index("tp") * width
    hidden = stream_in.astype(f32)
    kept = []
    for layer in range(LAYERS):
        gain_one = norm_gain[layer].astype(f32)
        gain_two = ffn_gain[layer].astype(f32)
        taps = conv_taps[layer].astype(f32)
        rate_one = norm_rate(hidden)
        normed_one = hidden * rate_one
        first = (normed_one * gain_one).astype(bf16)
        proj = jnp.einsum("msd,dkc->mskc", first, in_proj[layer], preferred_element_type=f32)
        bgate = proj[:, :, 0]
        cgate = proj[:, :, 1]
        xinput = proj[:, :, 2]
        mixed = (bgate * xinput).astype(bf16)
        prior = passed_along(mixed[:, -2:], "seq", 1)
        extended = jnp.concatenate([prior, mixed], axis=1).astype(f32)
        conved = (
            taps[0] * extended[:, :-2] + taps[1] * extended[:, 1:-1] + taps[2] * extended[:, 2:]
        )
        gated = (cgate * conved).astype(bf16)
        partial_out = jnp.einsum("msc,cd->msd", gated, out_proj[layer], preferred_element_type=f32)
        middle = hidden + lax.psum(partial_out, "tp")
        rate_two = norm_rate(middle)
        normed_two = middle * rate_two
        second = (normed_two * gain_two).astype(bf16)
        gate_val = jnp.einsum("msd,df->msf", second, gate_proj[layer], preferred_element_type=f32)
        up_val = jnp.einsum("msd,df->msf", second, up_proj[layer], preferred_element_type=f32)
        sigma = jax.nn.sigmoid(gate_val)
        silu_val = gate_val * sigma
        act = (silu_val * up_val).astype(bf16)
        partial_ffn = jnp.einsum("msf,fd->msd", act, down_proj[layer], preferred_element_type=f32)
        kept.append(
            (
                rate_one,
                normed_one,
                first,
                bgate,
                cgate,
                xinput,
                extended,
                conved,
                gated,
                rate_two,
                normed_two,
                second,
                gate_val,
                up_val,
                sigma,
                silu_val,
                act,
            )
        )
        hidden = middle + lax.psum(partial_ffn, "tp")
    grad_h = out_grad.astype(f32)
    collected = [None] * LAYERS
    for layer in reversed(range(LAYERS)):
        (
            rate_one,
            normed_one,
            first,
            bgate,
            cgate,
            xinput,
            extended,
            conved,
            gated,
            rate_two,
            normed_two,
            second,
            gate_val,
            up_val,
            sigma,
            silu_val,
            act,
        ) = kept[layer]
        gain_one = norm_gain[layer].astype(f32)
        gain_two = ffn_gain[layer].astype(f32)
        taps = conv_taps[layer].astype(f32)
        grad_f = grad_h.astype(bf16)
        grad_act = jnp.einsum("msd,fd->msf", grad_f, down_proj[layer], preferred_element_type=f32)
        down_g = jnp.einsum("msf,msd->fd", act, grad_f, preferred_element_type=f32)
        grad_gate = (grad_act * up_val * sigma * (1.0 + gate_val * (1.0 - sigma))).astype(bf16)
        grad_up = (grad_act * silu_val).astype(bf16)
        part_two = jnp.einsum(
            "msf,df->msd", grad_gate, gate_proj[layer], preferred_element_type=f32
        )
        part_two = part_two + jnp.einsum(
            "msf,df->msd", grad_up, up_proj[layer], preferred_element_type=f32
        )
        gate_g = jnp.einsum("msd,msf->df", second, grad_gate, preferred_element_type=f32)
        up_g = jnp.einsum("msd,msf->df", second, grad_up, preferred_element_type=f32)
        grad_two = lax.psum(part_two.astype(jnp.bfloat16), "tp").astype(jnp.float32)
        ffn_gain_g = jnp.sum(grad_two * normed_two, axis=(0, 1))
        grad_mid = grad_h + norm_back(grad_two, gain_two, normed_two, rate_two)
        grad_o = grad_mid.astype(bf16)
        grad_gated = jnp.einsum("msd,cd->msc", grad_o, out_proj[layer], preferred_element_type=f32)
        out_g = jnp.einsum("msc,msd->cd", gated, grad_o, preferred_element_type=f32)
        grad_conv = grad_gated * cgate
        grad_cgate = grad_gated * conved
        after = passed_along(grad_conv[:, :2], "seq", -1)
        grad_ext = jnp.concatenate([grad_conv, after], axis=1)
        grad_mixed = (
            taps[2] * grad_ext[:, :-2] + taps[1] * grad_ext[:, 1:-1] + taps[0] * grad_ext[:, 2:]
        )
        count = grad_conv.shape[1]
        conv_g = jnp.stack(
            [jnp.sum(grad_conv * extended[:, k : k + count], axis=(0, 1)) for k in range(3)], axis=0
        )
        grad_proj = jnp.stack([grad_mixed * xinput, grad_cgate, grad_mixed * bgate], axis=2).astype(
            bf16
        )
        part_one = jnp.einsum(
            "mskc,dkc->msd", grad_proj, in_proj[layer], preferred_element_type=f32
        )
        in_g = jnp.einsum("msd,mskc->dkc", first, grad_proj, preferred_element_type=f32)
        grad_one = lax.psum(part_one.astype(jnp.bfloat16), "tp").astype(jnp.float32)
        norm_gain_g = jnp.sum(grad_one * normed_one, axis=(0, 1))
        grad_h = grad_mid + norm_back(grad_one, gain_one, normed_one, rate_one)
        norm_piece = lax.dynamic_slice_in_dim(norm_gain_g, offset, width)
        ffn_piece = lax.dynamic_slice_in_dim(ffn_gain_g, offset, width)
        small = (norm_piece, conv_g, ffn_piece)
        large = (in_g, out_g, gate_g, up_g, down_g)
        collected[layer] = (small, large)
    norm_stack = jnp.stack([c[0][0] for c in collected], axis=0)
    conv_stack = jnp.stack([c[0][1] for c in collected], axis=0)
    ffn_stack = jnp.stack([c[0][2] for c in collected], axis=0)
    large_stack = tuple((jnp.stack([c[1][i] for c in collected], axis=0) for i in range(5)))
    large_stack = reduce_weights(large_stack)
    norm_stack, conv_stack, ffn_stack = reduce_small((norm_stack, conv_stack, ffn_stack))
    stream_out = hidden.astype(bf16)
    in_grad, out_grad_w, gate_grad, up_grad, down_grad = large_stack
    return (
        stream_out,
        grad_h,
        norm_stack,
        in_grad,
        conv_stack,
        out_grad_w,
        ffn_stack,
        gate_grad,
        up_grad,
        down_grad,
    )


VMEM_BYTES = 62 * 2**20
MESH = pl.DeviceIdType.MESH
f32 = jnp.float32
bf16 = jnp.bfloat16
NN = (((1,), (0,)), ((), ()))
NT = (((1,), (1,)), ((), ()))
ORDERS = ((0, 1, 2), (1, 2, 0))
SLOTS = 4
N1, N2, DF, DO = range(4)


def mm(lhs, rhs, dims=NN):
    return lax.dot_general(lhs, rhs, dims, preferred_element_type=f32)


def fused(
    dims,
    stream_in, norm_gain, win, taps, wout, ffn_gain, wgate, wup, wdown, out_grad,
    out_stream, out_sgrad, out_units, out_small,
    L, R, WIN, WOUT, WG, WU, WD, H, RATE, PB, PR, XR,
    GA, GB, RA0, RA1, RA2, RB0, RB1, RB2, RT, FO,
    EXT, DYE, CF, HALO, DHALO, GAIN, TAPS, GACC, CACC, SMR,
    load_sem, ps, pr, xs, xr, ags, agr, hs, hr, rss, rsr, fos, oss, sms, smr,
):
    M, TOK, D, C, F, U = dims
    half = TOK // 2
    CS, CA, CB, CP, CZ = 0, F, 2 * F, 3 * F, 3 * F + 3 * C
    UNITS = 2 * (-(-(CZ + C) // U))
    PER = UNITS // 2
    rows_of = (GA.shape[2], GB.shape[2])
    seq = lax.axis_index("seq")
    tp = lax.axis_index("tp")
    n = lax.axis_size("seq")
    core = lax.rem(tp, 2)
    xi = lax.div(tp, 2)
    sib = {"seq": seq, "tp": tp + 1 - 2 * core}
    xpart = {"seq": seq, "tp": tp + 2 - 4 * xi}
    bits = [lax.rem(lax.div(seq, 1 << k), 2) for k in range(3)]
    parts = [{"seq": seq + (1 << k) - 2 * (1 << k) * bits[k], "tp": tp} for k in range(3)]
    nxt = {"seq": lax.rem(seq + 1, n), "tp": tp}
    prv = {"seq": lax.rem(seq + n - 1, n), "tp": tp}
    mine = pl.ds(pl.multiple_of(core * half, half), half)
    theirs = pl.ds(pl.multiple_of((1 - core) * half, half), half)

    def remote(src, dst, ssem, rsem, dev):
        return pltpu.make_async_remote_copy(
            src_ref=src, dst_ref=dst, send_sem=ssem, recv_sem=rsem, device_id=dev, device_id_type=MESH
        )

    def load_stream(m):
        return pltpu.make_async_copy(stream_in.at[m], L.at[0, N1, m], load_sem.at[m])

    def load_conv(l):
        b = 4 + 4 * l
        return [
            pltpu.make_async_copy(win.at[l, k], WIN.at[l, :, pl.ds(k * C, C)], load_sem.at[b + k])
            for k in range(3)
        ] + [pltpu.make_async_copy(wout.at[l], WOUT.at[l], load_sem.at[b + 3])]

    def load_ffn(l):
        return [
            pltpu.make_async_copy(s.at[l], d, load_sem.at[12 + i])
            for i, (s, d) in enumerate(((wgate, WG), (wup, WU), (wdown, WD)))
        ]

    load_og = pltpu.make_async_copy(out_grad, L.at[1, DF], load_sem.at[15])
    for m in range(M):
        load_stream(m).start()
    for cp in load_conv(0) + load_ffn(0) + load_conv(1) + [load_og]:
        cp.start()

    barrier = pltpu.get_barrier_semaphore()
    others = [sib, xpart, nxt, prv] + parts
    for dev in others:
        pl.semaphore_signal(barrier, inc=1, device_id=dev, device_id_type=MESH)

    GAIN[0] = norm_gain[...].astype(f32)
    GAIN[1] = ffn_gain[...].astype(f32)
    GAIN[2] = 1.0 / norm_gain[...].astype(f32)
    GAIN[3] = 1.0 / ffn_gain[...].astype(f32)
    TAPS[...] = taps[...].astype(f32)
    GACC[...] = jnp.zeros_like(GACC)
    CACC[...] = jnp.zeros_like(CACC)

    pl.semaphore_wait(barrier, len(others))

    def pcopy(m):
        return remote(PB.at[m, theirs], PR.at[m], ps.at[m], pr.at[m], sib)

    def xcopy(m):
        return remote(PB.at[m, mine], XR.at[m], xs.at[m], xr.at[m], xpart)

    def mid(m):
        pcopy(m).wait()

        def chunk(i, _):
            off = pl.multiple_of(i * 32, 32)
            rows = pl.ds(pl.multiple_of(core * half + off, 32), 32)
            got = PR[m, pl.ds(off, 32)].astype(f32) + PB[m, rows].astype(f32)
            PB[m, rows] = got.astype(bf16)
            return 0

        lax.fori_loop(0, half // 32, chunk, 0)
        xcopy(m).start()

    def agcopy(l, kind, m):
        ref = L.at[l, kind, m, mine]
        return remote(ref, ref, ags.at[m], agr.at[m], sib)

    def rows_loop(m, body):
        def chunk(i, _):
            off = pl.multiple_of(i * 32, 32)
            rows = pl.ds(pl.multiple_of(core * half + off, 32), 32)
            total = PB[m, rows].astype(f32) + XR[m, pl.ds(off, 32)].astype(f32)
            body(pl.ds(off, 32), rows, total)
            return 0

        lax.fori_loop(0, half // 32, chunk, 0)

    def rate_of(val):
        return lax.rsqrt(jnp.mean(val * val, axis=-1, keepdims=True) + EPS)

    def finish_norm(l, which, kind, m):
        xcopy(m).wait()
        gain = GAIN[which, l : l + 1, :]

        def body(loc, rows, total):
            hid = H[m, loc] + total
            H[m, loc] = hid
            rate = rate_of(hid)
            RATE[l, which, m, loc] = rate
            L[l, kind, m, rows] = (hid * rate * gain).astype(bf16)

        rows_loop(m, body)
        agcopy(l, kind, m).start()

    def stream_copies(m):
        ref = PB.at[m, mine]
        return (
            pltpu.make_async_copy(ref, out_stream.at[m, mine], oss.at[m]),
            remote(ref, out_stream.at[m, mine], ags.at[m], agr.at[m], sib),
        )

    def finish_stream(m):
        xcopy(m).wait()

        def body(loc, rows, total):
            PB[m, rows] = (H[m, loc] + total).astype(bf16)

        rows_loop(m, body)
        for cp in stream_copies(m):
            cp.start()

    def norm_back(l, which, kind, m, emit):
        xcopy(m).wait()
        gain = GAIN[which, l : l + 1, :]
        inv = GAIN[2 + which, l : l + 1, :]

        def body(loc, rows, total):
            nrm = L[l, kind, m, rows].astype(f32) * inv
            prod = total * nrm
            GACC[2 * which + l] += prod[0:8] + prod[8:16] + prod[16:24] + prod[24:32]
            mean = jnp.mean(prod * gain, axis=-1, keepdims=True)
            emit(loc, rows, RATE[l, which, m, loc] * (total * gain - nrm * mean))

        rows_loop(m, body)

    def finish_dn2(l, m):
        def emit(loc, rows, delta):
            prev = L[1, DF, m, rows].astype(f32) if l == 1 else H[m, loc]
            new = prev + delta
            H[m, loc] = new
            L[l, DO, m, rows] = new.astype(bf16)

        norm_back(l, 1, N2, m, emit)
        agcopy(l, DO, m).start()

    def finish_dn1(l, m):
        def emit(loc, rows, delta):
            new = H[m, loc] + delta
            H[m, loc] = new
            if l == 1:
                L[0, DF, m, rows] = new.astype(bf16)

        norm_back(l, 0, N1, m, emit)
        if l == 1:
            agcopy(0, DF, m).start()
        else:
            for cp in grad_copies(m):
                cp.start()

    def grad_copies(m):
        return (
            pltpu.make_async_copy(H.at[m], out_sgrad.at[m, mine], oss.at[m]),
            remote(H.at[m], out_sgrad.at[m, mine], ags.at[m], agr.at[m], sib),
        )

    def put_partial(m, tile):
        def step(j, _):
            cols = pl.ds(pl.multiple_of(j * 256, 256), 256)
            PB[m, :, cols] = tile(cols).astype(bf16)
            return 0

        lax.fori_loop(0, D // 256, step, 0)
        pcopy(m).start()

    def hcopy(l, m):
        return remote(EXT.at[pl.ds(TOK, 8)], HALO.at[l, m], hs, hr.at[0, l, m], nxt)

    def dhcopy(l, m):
        return remote(DYE.at[pl.ds(0, 8)], DHALO.at[l, m], hs, hr.at[1, l, m], prv)

    def tap(l, k):
        return TAPS[k, l : l + 1, :]

    def conv_now(l, m):
        EXT[0:8] = jnp.where(seq == 0, 0.0, HALO[l, m])
        return (
            tap(l, 0) * EXT[6 : 6 + TOK] + tap(l, 1) * EXT[7 : 7 + TOK] + tap(l, 2) * EXT[8 : 8 + TOK]
        )

    def conv_fwd_a(l, m):
        if l == 0:
            load_stream(m).wait()
            gain = GAIN[0, 0:1, :]
            hid = L[0, N1, m, mine].astype(f32)
            H[m] = hid
            RATE[0, 0, m] = rate_of(hid)

            def chunk(i, _):
                rows = pl.ds(pl.multiple_of(i * 32, 32), 32)
                val = L[0, N1, m, rows].astype(f32)
                L[0, N1, m, rows] = (val * rate_of(val) * gain).astype(bf16)
                return 0

            lax.fori_loop(0, TOK // 32, chunk, 0)
        else:
            agcopy(1, N1, m).wait()
        first = L[l, N1, m]
        bgate = mm(first, WIN[l, :, 0:C])
        R[l, m, :, CP : CP + C] = bgate.astype(bf16)
        xin = mm(first, WIN[l, :, 2 * C : 3 * C])
        R[l, m, :, CP + 2 * C : CP + 3 * C] = xin.astype(bf16)
        EXT[8 : 8 + TOK] = (bgate * xin).astype(bf16).astype(f32)
        hcopy(l, m).start()
        cgate = mm(first, WIN[l, :, C : 2 * C])
        R[l, m, :, CP + C : CP + 2 * C] = cgate.astype(bf16)
        CF[...] = cgate

    def conv_fwd_b(l, m):
        hcopy(l, m).wait()
        R[l, m, :, CZ : CZ + C] = (CF[...] * conv_now(l, m)).astype(bf16)
        gated = R[l, m, :, CZ : CZ + C]
        put_partial(m, lambda cols: mm(gated, WOUT[l, :, cols]))

    def ffn_tiles(body):
        def step(t, _):
            body(pl.multiple_of(t * U, 128))
            return 0

        lax.fori_loop(0, F // U, step, 0)

    def ffn_fwd(l, m):
        agcopy(l, N2, m).wait()
        second = L[l, N2, m]

        def body(off):
            cols = pl.ds(off, U)
            a = mm(second, WG[:, cols])
            b = mm(second, WU[:, cols])
            sig = jax.nn.sigmoid(a)
            silu = a * sig
            R[l, m, :, pl.ds(CS + off, U)] = (silu * b).astype(bf16)
            if l == 0:
                R[l, m, :, pl.ds(CA + off, U)] = a.astype(bf16)
                R[l, m, :, pl.ds(CB + off, U)] = b.astype(bf16)
            else:
                ds = mm(L[l, DF, m], WD[pl.ds(off, U), :], NT)
                R[l, m, :, pl.ds(CA + off, U)] = (ds * b * sig * (1.0 + a * (1.0 - sig))).astype(bf16)
                R[l, m, :, pl.ds(CB + off, U)] = (ds * silu).astype(bf16)

        ffn_tiles(body)
        act = R[l, m, :, CS : CS + F]
        put_partial(m, lambda cols: mm(act, WD[:, cols]))

    def ffn_bwd(l, m):
        if l == 0:
            agcopy(0, DF, m).wait()

            def body(off):
                a = R[l, m, :, pl.ds(CA + off, U)].astype(f32)
                b = R[l, m, :, pl.ds(CB + off, U)].astype(f32)
                sig = jax.nn.sigmoid(a)
                ds = mm(L[l, DF, m], WD[pl.ds(off, U), :], NT)
                R[l, m, :, pl.ds(CA + off, U)] = (ds * b * sig * (1.0 + a * (1.0 - sig))).astype(bf16)
                R[l, m, :, pl.ds(CB + off, U)] = (ds * a * sig).astype(bf16)

            ffn_tiles(body)
        else:
            for cp in stream_copies(m):
                cp.wait()
        da = R[l, m, :, CA : CA + F]
        db = R[l, m, :, CB : CB + F]
        put_partial(m, lambda cols: mm(da, WG[cols, :], NT) + mm(db, WU[cols, :], NT))

    def conv_bwd_a(l, m):
        agcopy(l, DO, m).wait()
        dz = mm(L[l, DO, m], WOUT[l], NT)
        bgate = R[l, m, :, CP : CP + C].astype(f32)
        xin = R[l, m, :, CP + 2 * C : CP + 3 * C].astype(f32)
        EXT[8 : 8 + TOK] = (bgate * xin).astype(bf16).astype(f32)
        dy = dz * R[l, m, :, CP + C : CP + 2 * C].astype(f32)
        DYE[0:TOK] = dy
        dhcopy(l, m).start()
        R[l, m, :, CP + C : CP + 2 * C] = (dz * conv_now(l, m)).astype(bf16)
        for k in range(3):
            prod = dy * EXT[6 + k : 6 + k + TOK]
            CACC[l, k] += jnp.sum(prod.reshape(TOK // 8, 8, C), axis=0)

    def conv_bwd_b(l, m):
        dhcopy(l, m).wait()
        DYE[TOK : TOK + 8] = jnp.where(seq == n - 1, 0.0, DHALO[l, m])
        dbx = tap(l, 2) * DYE[0:TOK] + tap(l, 1) * DYE[1 : 1 + TOK] + tap(l, 0) * DYE[2 : 2 + TOK]
        bgate = R[l, m, :, CP : CP + C].astype(f32)
        xin = R[l, m, :, CP + 2 * C : CP + 3 * C].astype(f32)
        R[l, m, :, CP : CP + C] = (dbx * xin).astype(bf16)
        R[l, m, :, CP + 2 * C : CP + 3 * C] = (dbx * bgate).astype(bf16)
        dp = R[l, m, :, CP : CP + 3 * C]
        put_partial(m, lambda cols: mm(dp, WIN[l, cols, :], NT))

    lanes = ((GA, (RA0, RA1, RA2)), (GB, (RB0, RB1, RB2)))

    def keep(lane, step):
        b = [bits[o] for o in ORDERS[lane]]
        return [b[0] * 4, b[0] * 4 + b[1] * 2, b[0] * 4 + b[1] * 2 + b[2]][step]

    def rs_copy(lane, step, t):
        G, recv = lanes[lane]
        slot = lax.rem(t, SLOTS)
        size = 4 >> step
        o = ORDERS[lane][step]
        off = keep(lane, step) + size - 2 * size * bits[o]
        return remote(
            G.at[slot, pl.ds(off, size)], recv[step].at[slot],
            rss.at[lane, step, slot], rsr.at[lane, step, slot], parts[o],
        )

    def rs_gen(t):
        l = 1 - lax.div(t, PER)
        v = lax.rem(t, PER)
        fu = F // U
        kind = jnp.where(v < fu, DF, jnp.where(v < 3 * fu, N2, jnp.where(v < PER - 1, N1, DO)))
        slot = lax.rem(t, SLOTS)
        cols = pl.ds(pl.multiple_of(v * U, 128), U)
        for m in range(M):
            RT[:, m * TOK : (m + 1) * TOK] = R[l, m, :, cols].T

        def step(j, _):
            src = L[l, kind, :, :, pl.ds(pl.multiple_of(j * 256, 256), 256)].reshape(M * TOK, 256)
            res = mm(RT[...], src).astype(bf16)
            hi, lo = lax.div(j, 2), lax.rem(j, 2)
            cut = rows_of[0]
            for y in range(2):
                block = res[:, y * 128 : (y + 1) * 128]
                GA[slot, y * 4 + lo * 2 + hi] = block[:cut]
                GB[slot, lo * 4 + hi * 2 + y] = block[cut:]
            return 0

        lax.fori_loop(0, D // 256, step, 0)
        for lane in range(2):
            rs_copy(lane, 0, t).start()

    def rs_add(step, t):
        slot = lax.rem(t, SLOTS)
        for lane in range(2):
            G, recv = lanes[lane]
            rs_copy(lane, step, t).wait()
            base = keep(lane, step)

            def add(i, _):
                G[slot, base + i] = (
                    G[slot, base + i].astype(f32) + recv[step][slot, i].astype(f32)
                ).astype(bf16)
                return 0

            lax.fori_loop(0, 4 >> step, add, 0)
            rs_copy(lane, step + 1, t).start()

    def unit_copy(t):
        l = 1 - lax.div(t, PER)
        v = lax.rem(t, PER)
        s = lax.rem(t, 2)
        return pltpu.make_async_copy(
            FO.at[s], out_units.at[l, pl.ds(pl.multiple_of(v * U, 128), U)], fos.at[s]
        )

    def rs_last(t):
        slot = lax.rem(t, SLOTS)
        s = lax.rem(t, 2)
        for lane in range(2):
            rs_copy(lane, 2, t).wait()

        @pl.when(t >= 2)
        def _():
            unit_copy(t - 2).wait()

        cut = rows_of[0]
        FO[s, 0:cut] = GA[slot, keep(0, 2)].astype(f32) + RA2[slot, 0].astype(f32)
        FO[s, cut:U] = GB[slot, keep(1, 2)].astype(f32) + RB2[slot, 0].astype(f32)
        unit_copy(t).start()

    def tick(t):
        static = isinstance(t, int)

        def at(cond, fn, arg):
            if static:
                if cond(t):
                    fn(jnp.int32(arg))
            else:
                pl.when(cond(t))(lambda: fn(arg))

        at(lambda q: q < UNITS, rs_gen, t)
        at(lambda q: (q >= 1) & (q < UNITS + 1), functools.partial(rs_add, 0), t - 1)
        at(lambda q: (q >= 2) & (q < UNITS + 2), functools.partial(rs_add, 1), t - 2)
        at(lambda q: (q >= 3) & (q < UNITS + 3), rs_last, t - 3)

    finishers = [
        lambda m: finish_norm(0, 1, N2, m),
        lambda m: finish_norm(1, 0, N1, m),
        lambda m: finish_norm(1, 1, N2, m),
        finish_stream,
        lambda m: finish_dn2(1, m),
        lambda m: finish_dn1(1, m),
        lambda m: finish_dn2(0, m),
        lambda m: finish_dn1(0, m),
    ]

    def behind(p, m):
        @pl.when((m > 0) | (p > 0))
        def _():
            mid(lax.rem(m + M - 1, M))

        if p > 0:
            @pl.when(m < 2)
            def _():
                finishers[p - 1](m + M - 2)

        @pl.when(m >= 2)
        def _():
            finishers[p](m - 2)

    def phase(p, first, second, tick_base=None):
        def step(m, _):
            first(m)
            if second is None:
                behind(p, m)
                if tick_base is not None:
                    tick(tick_base + m)
            else:
                if tick_base is not None:
                    tick(tick_base + m)
                behind(p, m)
                second(m)
            return 0

        lax.fori_loop(0, M, step, 0)

    def arrived(copies):
        for cp in copies:
            cp.wait()

    arrived(load_conv(0))
    phase(0, lambda m: conv_fwd_a(0, m), lambda m: conv_fwd_b(0, m))
    arrived(load_ffn(0))
    phase(1, lambda m: ffn_fwd(0, m), None)
    for cp in load_ffn(1):
        cp.start()
    arrived(load_conv(1))
    phase(2, lambda m: conv_fwd_a(1, m), lambda m: conv_fwd_b(1, m))
    arrived(load_ffn(1) + [load_og])
    phase(3, lambda m: ffn_fwd(1, m), None)
    phase(4, lambda m: ffn_bwd(1, m), None, 0)
    for cp in load_ffn(0):
        cp.start()
    phase(5, lambda m: conv_bwd_a(1, m), lambda m: conv_bwd_b(1, m), M)
    arrived(load_ffn(0))
    phase(6, lambda m: ffn_bwd(0, m), None, 2 * M)
    phase(7, lambda m: conv_bwd_a(0, m), lambda m: conv_bwd_b(0, m), 3 * M)
    mid(M - 1)
    finishers[7](M - 2)
    tick(4 * M)
    finishers[7](M - 1)

    for i in range(4):
        out_small[i : i + 1] = jnp.sum(GACC[i], axis=0, keepdims=True)
    out_small[4:8] = jnp.zeros((4, D), f32)
    for l in range(2):
        for k in range(3):
            out_small[4 + l : 5 + l, k * C : (k + 1) * C] = jnp.sum(CACC[l, k], axis=0, keepdims=True)

    def small(i):
        return remote(out_small, SMR.at[i], sms.at[i], smr.at[i], [sib, *parts][i])

    small(0).start()
    t = 4 * M + 1
    for i in range(4):
        tick(t)
        t += 1
        small(i).wait()
        if i == 0:
            out_small[0:4] += SMR[0, 0:4]
        else:
            out_small[...] += SMR[i]
        if i < 3:
            small(i + 1).start()
    while t < UNITS + 3:
        tick(t)
        t += 1
    for q in (UNITS - 2, UNITS - 1):
        unit_copy(jnp.int32(q)).wait()
    for m in range(M):
        for cp in grad_copies(m):
            cp.wait()


def fused_call(stream_in, norm_gain, win, taps, wout, ffn_gain, wgate, wup, wdown, out_grad):
    M, TOK, D = stream_in.shape
    C, F = wout.shape[1], wgate.shape[2]
    U = 384
    per = -(-(3 * F + 4 * C) // U)
    rb = U // 6
    ra = U - rb
    half = TOK // 2
    vm = pltpu.VMEM
    dma = pltpu.SemaphoreType.DMA
    S = SLOTS
    anys = pl.BlockSpec(memory_space=pl.ANY)
    vmem = pl.BlockSpec(memory_space=pltpu.VMEM)
    return pl.pallas_call(
        functools.partial(fused, (M, TOK, D, C, F, U)),
        out_shape=[
            jax.ShapeDtypeStruct((M, TOK, D), bf16),
            jax.ShapeDtypeStruct((M, TOK, D), f32),
            jax.ShapeDtypeStruct((LAYERS, per * U, 128), f32),
            jax.ShapeDtypeStruct((8, D), f32),
        ],
        in_specs=[anys, vmem, anys, vmem, anys, vmem, anys, anys, anys, anys],
        out_specs=[anys, anys, anys, vmem],
        scratch_shapes=[
            vm((LAYERS, 4, M, TOK, D), bf16),
            vm((LAYERS, M, TOK, per * U), bf16),
            vm((LAYERS, D, 3 * C), bf16),
            vm((LAYERS, C, D), bf16),
            vm((D, F), bf16),
            vm((D, F), bf16),
            vm((F, D), bf16),
            vm((M, half, D), f32),
            vm((LAYERS, 2, M, half, 1), f32),
            vm((M, TOK, D), bf16),
            vm((M, half, D), bf16),
            vm((M, half, D), bf16),
            vm((S, 8, ra, 128), bf16),
            vm((S, 8, rb, 128), bf16),
            vm((S, 4, ra, 128), bf16),
            vm((S, 2, ra, 128), bf16),
            vm((S, 1, ra, 128), bf16),
            vm((S, 4, rb, 128), bf16),
            vm((S, 2, rb, 128), bf16),
            vm((S, 1, rb, 128), bf16),
            vm((U, M * TOK), bf16),
            vm((2, U, 128), f32),
            vm((TOK + 8, C), f32),
            vm((TOK + 8, C), f32),
            vm((TOK, C), f32),
            vm((LAYERS, M, 8, C), f32),
            vm((LAYERS, M, 8, C), f32),
            vm((4, LAYERS, D), f32),
            vm((3, LAYERS, C), f32),
            vm((4, 8, D), f32),
            vm((LAYERS, 3, 8, C), f32),
            vm((4, 8, D), f32),
            dma((16,)),
            dma((M,)), dma((M,)), dma((M,)), dma((M,)), dma((M,)), dma((M,)),
            dma, dma((2, LAYERS, M)),
            dma((2, 3, S)), dma((2, 3, S)),
            dma((2,)), dma((M,)), dma((4,)), dma((4,)),
        ],
        name="fused",
        compiler_params=pltpu.CompilerParams(
            collective_id=0, has_side_effects=True, vmem_limit_bytes=VMEM_BYTES
        ),
    )(stream_in, norm_gain, win, taps, wout, ffn_gain, wgate, wup, wdown, out_grad)


def body_fused(
    stream_in, norm_gain, in_proj, conv_taps, out_proj, ffn_gain, gate_proj, up_proj, down_proj, out_grad
):
    C, F = out_proj.shape[1], gate_proj.shape[2]
    D = stream_in.shape[2]
    out_stream, out_sgrad, units, small = fused_call(
        stream_in, norm_gain, jnp.transpose(in_proj, (0, 2, 1, 3)), jnp.transpose(conv_taps, (1, 0, 2)),
        out_proj, ffn_gain, gate_proj, up_proj, down_proj, out_grad,
    )
    offset = lax.axis_index("tp") * C
    norm_g = lax.dynamic_slice_in_dim(small[0:2], offset, C, axis=1)
    ffn_g = lax.dynamic_slice_in_dim(small[2:4], offset, C, axis=1)
    conv_g = small[4:6, : 3 * C].reshape(LAYERS, 3, C)
    down_g = units[:, :F]
    gate_g = jnp.swapaxes(units[:, F : 2 * F], 1, 2)
    up_g = jnp.swapaxes(units[:, 2 * F : 3 * F], 1, 2)
    in_g = units[:, 3 * F : 3 * F + 3 * C].reshape(LAYERS, 3, C, 128).transpose(0, 3, 1, 2)
    out_g = units[:, 3 * F + 3 * C : 3 * F + 4 * C]
    return (out_stream, out_sgrad, norm_g, in_g, conv_g, out_g, ffn_g, gate_g, up_g, down_g)


def solution(mesh):
    in_specs = (
        P(None, "seq", None),
        P(),
        P(None, None, None, "tp"),
        P(None, None, "tp"),
        P(None, "tp", None),
        P(),
        P(None, None, "tp"),
        P(None, None, "tp"),
        P(None, "tp", None),
        P(None, "seq", None),
    )
    out_specs = (
        P(None, "seq", None),
        P(None, "seq", None),
        P(None, "tp"),
        P(None, "seq", None, "tp"),
        P(None, None, "tp"),
        P(None, "tp", "seq"),
        P(None, "tp"),
        P(None, "seq", "tp"),
        P(None, "seq", "tp"),
        P(None, "tp", "seq"),
    )
    chosen = body_fused if (mesh.shape["seq"], mesh.shape["tp"]) == (8, 4) else body
    return jax.shard_map(chosen, mesh=mesh, in_specs=in_specs, out_specs=out_specs, check_vma=False)
```

```python
import functools

import jax
import jax.numpy as jnp
from jax import lax
from jax.experimental import pallas as pl
from jax.experimental.pallas import tpu as pltpu
from jax.sharding import PartitionSpec as P

LAYERS = 2


EPS = 1e-05


def passed_along(block, axis, distance):
    devices = range(lax.axis_size(axis))
    route = [(i - distance, i) for i in devices if i - distance in devices]
    return lax.ppermute(block, axis, route)


def norm_rate(hidden):
    return lax.rsqrt(jnp.mean(hidden * hidden, axis=-1, keepdims=True) + EPS)


def norm_back(grad_in, gain, normed_val, rate):
    scaled = grad_in * gain
    return rate * (scaled - normed_val * jnp.mean(scaled * normed_val, axis=-1, keepdims=True))


def reduce_weights(grads):
    return (
        lax.psum_scatter(
            grads[0].astype(jnp.bfloat16), "seq", scatter_dimension=1, tiled=True
        ).astype(jnp.float32),
        lax.psum_scatter(
            grads[1].astype(jnp.bfloat16), "seq", scatter_dimension=2, tiled=True
        ).astype(jnp.float32),
        lax.psum_scatter(
            grads[2].astype(jnp.bfloat16), "seq", scatter_dimension=1, tiled=True
        ).astype(jnp.float32),
        lax.psum_scatter(
            grads[3].astype(jnp.bfloat16), "seq", scatter_dimension=1, tiled=True
        ).astype(jnp.float32),
        lax.psum_scatter(
            grads[4].astype(jnp.bfloat16), "seq", scatter_dimension=2, tiled=True
        ).astype(jnp.float32),
    )


def reduce_small(grads):
    return lax.psum((grads[0], grads[1], grads[2]), "seq")


def body(
    stream_in,
    norm_gain,
    in_proj,
    conv_taps,
    out_proj,
    ffn_gain,
    gate_proj,
    up_proj,
    down_proj,
    out_grad,
):
    f32 = jnp.float32
    bf16 = jnp.bfloat16
    width = in_proj.shape[-1]
    offset = lax.axis_index("tp") * width
    hidden = stream_in.astype(f32)
    kept = []
    for layer in range(LAYERS):
        gain_one = norm_gain[layer].astype(f32)
        gain_two = ffn_gain[layer].astype(f32)
        taps = conv_taps[layer].astype(f32)
        rate_one = norm_rate(hidden)
        normed_one = hidden * rate_one
        first = (normed_one * gain_one).astype(bf16)
        proj = jnp.einsum("msd,dkc->mskc", first, in_proj[layer], preferred_element_type=f32)
        bgate = proj[:, :, 0]
        cgate = proj[:, :, 1]
        xinput = proj[:, :, 2]
        mixed = (bgate * xinput).astype(bf16)
        prior = passed_along(mixed[:, -2:], "seq", 1)
        extended = jnp.concatenate([prior, mixed], axis=1).astype(f32)
        conved = (
            taps[0] * extended[:, :-2] + taps[1] * extended[:, 1:-1] + taps[2] * extended[:, 2:]
        )
        gated = (cgate * conved).astype(bf16)
        partial_out = jnp.einsum("msc,cd->msd", gated, out_proj[layer], preferred_element_type=f32)
        middle = hidden + lax.psum(partial_out, "tp")
        rate_two = norm_rate(middle)
        normed_two = middle * rate_two
        second = (normed_two * gain_two).astype(bf16)
        gate_val = jnp.einsum("msd,df->msf", second, gate_proj[layer], preferred_element_type=f32)
        up_val = jnp.einsum("msd,df->msf", second, up_proj[layer], preferred_element_type=f32)
        sigma = jax.nn.sigmoid(gate_val)
        silu_val = gate_val * sigma
        act = (silu_val * up_val).astype(bf16)
        partial_ffn = jnp.einsum("msf,fd->msd", act, down_proj[layer], preferred_element_type=f32)
        kept.append(
            (
                rate_one,
                normed_one,
                first,
                bgate,
                cgate,
                xinput,
                extended,
                conved,
                gated,
                rate_two,
                normed_two,
                second,
                gate_val,
                up_val,
                sigma,
                silu_val,
                act,
            )
        )
        hidden = middle + lax.psum(partial_ffn, "tp")
    grad_h = out_grad.astype(f32)
    collected = [None] * LAYERS
    for layer in reversed(range(LAYERS)):
        (
            rate_one,
            normed_one,
            first,
            bgate,
            cgate,
            xinput,
            extended,
            conved,
            gated,
            rate_two,
            normed_two,
            second,
            gate_val,
            up_val,
            sigma,
            silu_val,
            act,
        ) = kept[layer]
        gain_one = norm_gain[layer].astype(f32)
        gain_two = ffn_gain[layer].astype(f32)
        taps = conv_taps[layer].astype(f32)
        grad_f = grad_h.astype(bf16)
        grad_act = jnp.einsum("msd,fd->msf", grad_f, down_proj[layer], preferred_element_type=f32)
        down_g = jnp.einsum("msf,msd->fd", act, grad_f, preferred_element_type=f32)
        grad_gate = (grad_act * up_val * sigma * (1.0 + gate_val * (1.0 - sigma))).astype(bf16)
        grad_up = (grad_act * silu_val).astype(bf16)
        part_two = jnp.einsum(
            "msf,df->msd", grad_gate, gate_proj[layer], preferred_element_type=f32
        )
        part_two = part_two + jnp.einsum(
            "msf,df->msd", grad_up, up_proj[layer], preferred_element_type=f32
        )
        gate_g = jnp.einsum("msd,msf->df", second, grad_gate, preferred_element_type=f32)
        up_g = jnp.einsum("msd,msf->df", second, grad_up, preferred_element_type=f32)
        grad_two = lax.psum(part_two.astype(jnp.bfloat16), "tp").astype(jnp.float32)
        ffn_gain_g = jnp.sum(grad_two * normed_two, axis=(0, 1))
        grad_mid = grad_h + norm_back(grad_two, gain_two, normed_two, rate_two)
        grad_o = grad_mid.astype(bf16)
        grad_gated = jnp.einsum("msd,cd->msc", grad_o, out_proj[layer], preferred_element_type=f32)
        out_g = jnp.einsum("msc,msd->cd", gated, grad_o, preferred_element_type=f32)
        grad_conv = grad_gated * cgate
        grad_cgate = grad_gated * conved
        after = passed_along(grad_conv[:, :2], "seq", -1)
        grad_ext = jnp.concatenate([grad_conv, after], axis=1)
        grad_mixed = (
            taps[2] * grad_ext[:, :-2] + taps[1] * grad_ext[:, 1:-1] + taps[0] * grad_ext[:, 2:]
        )
        count = grad_conv.shape[1]
        conv_g = jnp.stack(
            [jnp.sum(grad_conv * extended[:, k : k + count], axis=(0, 1)) for k in range(3)], axis=0
        )
        grad_proj = jnp.stack([grad_mixed * xinput, grad_cgate, grad_mixed * bgate], axis=2).astype(
            bf16
        )
        part_one = jnp.einsum(
            "mskc,dkc->msd", grad_proj, in_proj[layer], preferred_element_type=f32
        )
        in_g = jnp.einsum("msd,mskc->dkc", first, grad_proj, preferred_element_type=f32)
        grad_one = lax.psum(part_one.astype(jnp.bfloat16), "tp").astype(jnp.float32)
        norm_gain_g = jnp.sum(grad_one * normed_one, axis=(0, 1))
        grad_h = grad_mid + norm_back(grad_one, gain_one, normed_one, rate_one)
        norm_piece = lax.dynamic_slice_in_dim(norm_gain_g, offset, width)
        ffn_piece = lax.dynamic_slice_in_dim(ffn_gain_g, offset, width)
        small = (norm_piece, conv_g, ffn_piece)
        large = (in_g, out_g, gate_g, up_g, down_g)
        collected[layer] = (small, large)
    norm_stack = jnp.stack([c[0][0] for c in collected], axis=0)
    conv_stack = jnp.stack([c[0][1] for c in collected], axis=0)
    ffn_stack = jnp.stack([c[0][2] for c in collected], axis=0)
    large_stack = tuple((jnp.stack([c[1][i] for c in collected], axis=0) for i in range(5)))
    large_stack = reduce_weights(large_stack)
    norm_stack, conv_stack, ffn_stack = reduce_small((norm_stack, conv_stack, ffn_stack))
    stream_out = hidden.astype(bf16)
    in_grad, out_grad_w, gate_grad, up_grad, down_grad = large_stack
    return (
        stream_out,
        grad_h,
        norm_stack,
        in_grad,
        conv_stack,
        out_grad_w,
        ffn_stack,
        gate_grad,
        up_grad,
        down_grad,
    )


VMEM_BYTES = 64 * 2**20
MESH = pl.DeviceIdType.MESH
f32 = jnp.float32
bf16 = jnp.bfloat16
NN = (((1,), (0,)), ((), ()))
NT = (((1,), (1,)), ((), ()))
ORDERS = ((0, 1, 2), (1, 2, 0))
SLOTS = 4
N1, N2, DF, DO = range(4)


def rem(a, b):
    return a % b if isinstance(a, int) else lax.rem(a, b)


def div(a, b):
    return a // b if isinstance(a, int) else lax.div(a, b)


def cases(value, branches):
    for low, high, fn in branches:
        if isinstance(value, int):
            if low <= value < high:
                fn()
        else:
            pl.when((value >= low) & (value < high))(fn)


def mm(lhs, rhs, dims=NN):
    return lax.dot_general(lhs, rhs, dims, preferred_element_type=f32)


def fused(
    dims,
    stream_in, norm_gain, win, taps, wout, ffn_gain, wgate, wup, wdown, out_grad,
    out_stream, out_sgrad, out_norm, out_in, out_conv, out_out, out_ffn, out_gate, out_up, out_down,
    L, R, WIN, WOUT, WG, WU, WD, H, DH, RATE, PB, PR, XR,
    GA, GB, RA0, RA1, RA2, RB0, RB1, RB2, RT, FO, FT, SM,
    EXT, DYE, HALO, DHALO, GAIN, TAPS, GACC, CACC, SMR,
    load_sem, ps, pr, xs, xr, ags, agr, hs, dhs, hr, rss, rsr, fos, oss, sts, str_, sms, smr,
):
    M, TOK, D, C, F, U = dims
    half = TOK // 2
    CS, CA, CB, CP, CZ = 0, F, 2 * F, 3 * F, 3 * F + 3 * C
    UNITS = 2 * (-(-(CZ + C) // U))
    PER = UNITS // 2
    full = (U, GA.shape[2], GB.shape[2])
    width = CZ + C - (PER - 1) * U
    tail_b = width // 6 // 16 * 16 + 16 * (width % 96 > 0)
    short = (width, width - tail_b, tail_b)
    seq = lax.axis_index("seq")
    tp = lax.axis_index("tp")
    n = lax.axis_size("seq")
    core = lax.rem(tp, 2)
    xi = lax.div(tp, 2)
    sib = {"seq": seq, "tp": tp + 1 - 2 * core}
    xpart = {"seq": seq, "tp": tp + 2 - 4 * xi}
    bits = [lax.rem(lax.div(seq, 1 << k), 2) for k in range(3)]
    parts = [{"seq": seq + (1 << k) - 2 * (1 << k) * bits[k], "tp": tp} for k in range(3)]
    nxt = {"seq": lax.rem(seq + 1, n), "tp": tp}
    prv = {"seq": lax.rem(seq + n - 1, n), "tp": tp}
    mine = pl.ds(pl.multiple_of(core * half, half), half)
    theirs = pl.ds(pl.multiple_of((1 - core) * half, half), half)

    def remote(src, dst, ssem, rsem, dev):
        return pltpu.make_async_remote_copy(
            src_ref=src, dst_ref=dst, send_sem=ssem, recv_sem=rsem, device_id=dev, device_id_type=MESH
        )

    def load_stream(m):
        return pltpu.make_async_copy(stream_in.at[m], L.at[0, N1, m], load_sem.at[m])

    def load_conv(l):
        b = 4 + 4 * l
        return [
            pltpu.make_async_copy(win.at[l, k], WIN.at[l, :, pl.ds(k * C, C)], load_sem.at[b + k])
            for k in range(3)
        ] + [pltpu.make_async_copy(wout.at[l], WOUT.at[l], load_sem.at[b + 3])]

    def load_ffn(l):
        return [
            pltpu.make_async_copy(s.at[l], d, load_sem.at[12 + i])
            for i, (s, d) in enumerate(((wgate, WG), (wup, WU), (wdown, WD)))
        ]

    load_og = pltpu.make_async_copy(out_grad, L.at[1, DF], load_sem.at[15])
    for m in range(M):
        load_stream(m).start()
    for cp in load_conv(0) + load_ffn(0) + load_conv(1) + [load_og]:
        cp.start()

    barrier = pltpu.get_barrier_semaphore()
    others = [sib, xpart, nxt, prv] + parts
    for dev in others:
        pl.semaphore_signal(barrier, inc=1, device_id=dev, device_id_type=MESH)

    GAIN[0] = norm_gain[...].astype(f32)
    GAIN[1] = ffn_gain[...].astype(f32)
    GAIN[2] = 1.0 / norm_gain[...].astype(f32)
    GAIN[3] = 1.0 / ffn_gain[...].astype(f32)
    TAPS[...] = taps[...].astype(f32)
    GACC[...] = jnp.zeros_like(GACC)
    CACC[...] = jnp.zeros_like(CACC)

    pl.semaphore_wait(barrier, len(others))

    def pcopy(m):
        return remote(PB.at[m, theirs], PR.at[m], ps.at[m], pr.at[m], sib)

    def xcopy(m):
        return remote(PB.at[m, mine], XR.at[m], xs.at[m], xr.at[m], xpart)

    def mid(m):
        pcopy(m).wait()

        def chunk(i, _):
            off = pl.multiple_of(i * 32, 32)
            rows = pl.ds(pl.multiple_of(core * half + off, 32), 32)
            got = PR[m, pl.ds(off, 32)].astype(f32) + PB[m, rows].astype(f32)
            PB[m, rows] = got.astype(bf16)
            return 0

        lax.fori_loop(0, half // 32, chunk, 0)
        xcopy(m).start()

    def agcopy(l, kind, m):
        ref = L.at[l, kind, m, mine]
        return remote(ref, ref, ags.at[m], agr.at[m], sib)

    def rows_loop(m, body):
        def chunk(i, _):
            off = pl.multiple_of(i * 32, 32)
            rows = pl.ds(pl.multiple_of(core * half + off, 32), 32)
            total = PB[m, rows].astype(f32) + XR[m, pl.ds(off, 32)].astype(f32)
            body(pl.ds(off, 32), rows, total)
            return 0

        lax.fori_loop(0, half // 32, chunk, 0)

    def rate_of(val):
        return lax.rsqrt(jnp.mean(val * val, axis=-1, keepdims=True) + EPS)

    def finish_norm(l, which, kind, m):
        xcopy(m).wait()
        gain = GAIN[which, l : l + 1, :]

        def body(loc, rows, total):
            hid = H[m, loc] + total
            H[m, loc] = hid
            rate = rate_of(hid)
            RATE[m, loc, 2 * l + which : 2 * l + which + 1] = rate
            L[l, kind, m, rows] = (hid * rate * gain).astype(bf16)

        rows_loop(m, body)
        agcopy(l, kind, m).start()

    def stream_copies(m):
        ref = PB.at[m, mine]
        return (
            pltpu.make_async_copy(ref, out_stream.at[m, mine], oss.at[m]),
            remote(ref, out_stream.at[m, mine], sts.at[m], str_.at[m], sib),
        )

    def finish_stream(m):
        xcopy(m).wait()

        def body(loc, rows, total):
            PB[m, rows] = (H[m, loc] + total).astype(bf16)

        rows_loop(m, body)
        for cp in stream_copies(m):
            cp.start()

    def norm_back(l, which, kind, m, emit):
        xcopy(m).wait()
        gain = GAIN[which, l : l + 1, :]
        inv = GAIN[2 + which, l : l + 1, :]

        def body(loc, rows, total):
            nrm = L[l, kind, m, rows].astype(f32) * inv
            prod = total * nrm
            GACC[2 * which + l] += prod[0:8] + prod[8:16] + prod[16:24] + prod[24:32]
            mean = jnp.mean(prod * gain, axis=-1, keepdims=True)
            emit(loc, rows, RATE[m, loc, 2 * l + which : 2 * l + which + 1] * (total * gain - nrm * mean))

        rows_loop(m, body)

    def finish_dn2(l, m):
        def emit(loc, rows, delta):
            prev = L[1, DF, m, rows].astype(f32) if l == 1 else DH[m, loc]
            new = prev + delta
            DH[m, loc] = new
            L[l, DO, m, rows] = new.astype(bf16)

        norm_back(l, 1, N2, m, emit)
        agcopy(l, DO, m).start()

    def finish_dn1(l, m):
        def emit(loc, rows, delta):
            new = DH[m, loc] + delta
            DH[m, loc] = new
            if l == 1:
                L[0, DF, m, rows] = new.astype(bf16)

        norm_back(l, 0, N1, m, emit)
        if l == 1:
            agcopy(0, DF, m).start()
        else:
            for cp in grad_copies(m):
                cp.start()

    def grad_copies(m):
        return (
            pltpu.make_async_copy(DH.at[m], out_sgrad.at[m, mine], oss.at[m]),
            remote(DH.at[m], out_sgrad.at[m, mine], ags.at[m], agr.at[m], sib),
        )

    def put_partial(m, tile):
        def step(j, _):
            cols = pl.ds(pl.multiple_of(j * 256, 256), 256)
            PB[m, :, cols] = tile(cols).astype(bf16)
            return 0

        lax.fori_loop(0, D // 256, step, 0)
        pcopy(m).start()

    def hcopy(l, m):
        return remote(EXT.at[pl.ds(TOK, 8)], HALO.at[l, m], hs, hr.at[0, l, m], nxt)

    def dhcopy(l, m):
        return remote(DYE.at[rem(m, 2), pl.ds(0, 8)], DHALO.at[l, m], dhs.at[rem(m, 2)], hr.at[1, l, m], prv)

    def tap(l, k):
        return TAPS[k, l : l + 1, :]

    def conv_now(l, m):
        EXT[0:8] = jnp.where(seq == 0, 0.0, HALO[l, m])
        return (
            tap(l, 0) * EXT[6 : 6 + TOK] + tap(l, 1) * EXT[7 : 7 + TOK] + tap(l, 2) * EXT[8 : 8 + TOK]
        )

    def conv_fwd_a(l, m):
        if l == 0:
            load_stream(m).wait()
            gain = GAIN[0, 0:1, :]
            hid = L[0, N1, m, mine].astype(f32)
            H[m] = hid
            RATE[m, :, 0:1] = rate_of(hid)

            def chunk(i, _):
                rows = pl.ds(pl.multiple_of(i * 32, 32), 32)
                val = L[0, N1, m, rows].astype(f32)
                L[0, N1, m, rows] = (val * rate_of(val) * gain).astype(bf16)
                return 0

            lax.fori_loop(0, TOK // 32, chunk, 0)
        else:
            agcopy(1, N1, m).wait()
        first = L[l, N1, m]
        bgate = mm(first, WIN[l, :, 0:C])
        R[l, m, :, CP : CP + C] = bgate.astype(bf16)
        xin = mm(first, WIN[l, :, 2 * C : 3 * C])
        R[l, m, :, CP + 2 * C : CP + 3 * C] = xin.astype(bf16)
        EXT[8 : 8 + TOK] = (bgate * xin).astype(bf16).astype(f32)
        hcopy(l, m).start()
        cgate = mm(first, WIN[l, :, C : 2 * C])
        R[l, m, :, CP + C : CP + 2 * C] = cgate.astype(bf16)
        DYE[0, 0:TOK] = cgate

    def conv_fwd_b(l, m):
        hcopy(l, m).wait()
        R[l, m, :, CZ : CZ + C] = (DYE[0, 0:TOK] * conv_now(l, m)).astype(bf16)
        gated = R[l, m, :, CZ : CZ + C]
        put_partial(m, lambda cols: mm(gated, WOUT[l, :, cols]))

    def ffn_tiles(body, low=0, high=None):
        def step(t, _):
            body(pl.multiple_of(t * U, 128))
            return 0

        lax.fori_loop(low, F // U if high is None else high, step, 0)

    def ffn_fwd(l, m, low=0, high=None):
        def body(off):
            cols = pl.ds(off, U)
            second = L[l, N2, m]
            a = mm(second, WG[:, cols])
            b = mm(second, WU[:, cols])
            sig = jax.nn.sigmoid(a)
            silu = a * sig
            R[l, m, :, pl.ds(CS + off, U)] = (silu * b).astype(bf16)
            if l == 0:
                R[l, m, :, pl.ds(CA + off, U)] = a.astype(bf16)
                R[l, m, :, pl.ds(CB + off, U)] = b.astype(bf16)
            else:
                ds = mm(L[l, DF, m], WD[pl.ds(off, U), :], NT)
                R[l, m, :, pl.ds(CA + off, U)] = (ds * b * sig * (1.0 + a * (1.0 - sig))).astype(bf16)
                R[l, m, :, pl.ds(CB + off, U)] = (ds * silu).astype(bf16)

        ffn_tiles(body, low, high)

    def ffn_down(l, m):
        act = R[l, m, :, CS : CS + F]
        put_partial(m, lambda cols: mm(act, WD[:, cols]))

    def ffn_bwd(l, m):
        if l == 0:
            def body(off):
                a = R[l, m, :, pl.ds(CA + off, U)].astype(f32)
                b = R[l, m, :, pl.ds(CB + off, U)].astype(f32)
                sig = jax.nn.sigmoid(a)
                ds = mm(L[l, DF, m], WD[pl.ds(off, U), :], NT)
                R[l, m, :, pl.ds(CA + off, U)] = (ds * b * sig * (1.0 + a * (1.0 - sig))).astype(bf16)
                R[l, m, :, pl.ds(CB + off, U)] = (ds * a * sig).astype(bf16)

            ffn_tiles(body)
        da = R[l, m, :, CA : CA + F]
        db = R[l, m, :, CB : CB + F]
        put_partial(m, lambda cols: mm(da, WG[cols, :], NT) + mm(db, WU[cols, :], NT))

    def conv_bwd_a(l, m):
        dz = mm(L[l, DO, m], WOUT[l], NT)
        bgate = R[l, m, :, CP : CP + C].astype(f32)
        xin = R[l, m, :, CP + 2 * C : CP + 3 * C].astype(f32)
        EXT[8 : 8 + TOK] = (bgate * xin).astype(bf16).astype(f32)
        dy = dz * R[l, m, :, CP + C : CP + 2 * C].astype(f32)
        DYE[rem(m, 2), 0:TOK] = dy
        dhcopy(l, m).start()
        R[l, m, :, CP + C : CP + 2 * C] = (dz * conv_now(l, m)).astype(bf16)
        for k in range(3):
            prod = dy * EXT[6 + k : 6 + k + TOK]
            CACC[l, k] += jnp.sum(prod.reshape(TOK // 8, 8, C), axis=0)

    def conv_bwd_b(l, m):
        dhcopy(l, m).wait()
        s = rem(m, 2)
        DYE[s, TOK : TOK + 8] = jnp.where(seq == n - 1, 0.0, DHALO[l, m])
        dbx = (
            tap(l, 2) * DYE[s, 0:TOK] + tap(l, 1) * DYE[s, 1 : 1 + TOK] + tap(l, 0) * DYE[s, 2 : 2 + TOK]
        )
        bgate = R[l, m, :, CP : CP + C].astype(f32)
        xin = R[l, m, :, CP + 2 * C : CP + 3 * C].astype(f32)
        R[l, m, :, CP : CP + C] = (dbx * xin).astype(bf16)
        R[l, m, :, CP + 2 * C : CP + 3 * C] = (dbx * bgate).astype(bf16)
        dp = R[l, m, :, CP : CP + 3 * C]
        put_partial(m, lambda cols: mm(dp, WIN[l, cols, :], NT))

    lanes = ((GA, (RA0, RA1, RA2)), (GB, (RB0, RB1, RB2)))

    def keep(lane, step):
        b = [bits[o] for o in ORDERS[lane]]
        return [b[0] * 4, b[0] * 4 + b[1] * 2, b[0] * 4 + b[1] * 2 + b[2]][step]

    def sized(t, fn):
        cases(rem(t, PER), [(0, PER - 1, lambda: fn(full)), (PER - 1, PER, lambda: fn(short))])

    def rs_copy(lane, step, t, rows):
        G, recv = lanes[lane]
        slot = rem(t, SLOTS)
        size = 4 >> step
        o = ORDERS[lane][step]
        off = keep(lane, step) + size - 2 * size * bits[o]
        cut = pl.ds(0, rows[1 + lane])
        return remote(
            G.at[slot, pl.ds(off, size), cut], recv[step].at[slot, :, cut],
            rss.at[lane, step, slot], rsr.at[lane, step, slot], parts[o],
        )

    def rs_gen(t):
        l = 1 - div(t, PER)
        v = rem(t, PER)
        fu = F // U
        kind = jnp.where(v < fu, DF, jnp.where(v < 3 * fu, N2, jnp.where(v < PER - 1, N1, DO)))
        slot = rem(t, SLOTS)

        def make(rows):
            wide, cut, _ = rows
            start = v * U if isinstance(v, int) else pl.multiple_of(v * U, 128)
            for m in range(M):
                RT[0:wide, m * TOK : (m + 1) * TOK] = R[l, m, :, pl.ds(start, wide)].T

            def step(j, _):
                src = L[l, kind, :, :, pl.ds(pl.multiple_of(j * 256, 256), 256)].reshape(M * TOK, 256)
                res = mm(RT[0:wide], src).astype(bf16)
                hi, lo = lax.div(j, 2), lax.rem(j, 2)
                for y in range(2):
                    block = res[:, y * 128 : (y + 1) * 128]
                    GA[slot, y * 4 + lo * 2 + hi, 0:cut] = block[:cut]
                    GB[slot, lo * 4 + hi * 2 + y, 0 : wide - cut] = block[cut:]
                return 0

            lax.fori_loop(0, D // 256, step, 0)
            for lane in range(2):
                rs_copy(lane, 0, t, rows).start()

        sized(t, make)

    def rs_add(step, t):
        slot = rem(t, SLOTS)

        def go(rows):
            for lane in range(2):
                G, recv = lanes[lane]
                rs_copy(lane, step, t, rows).wait()
                base = keep(lane, step)
                cut = rows[1 + lane]

                def add(i, _):
                    G[slot, base + i, 0:cut] = (
                        G[slot, base + i, 0:cut].astype(f32) + recv[step][slot, i, 0:cut].astype(f32)
                    ).astype(bf16)
                    return 0

                lax.fori_loop(0, 4 >> step, add, 0)
                rs_copy(lane, step + 1, t, rows).start()

        sized(t, go)

    def unit_copies(t, which):
        l = 1 - div(t, PER)
        v = rem(t, PER)
        fu = F // U

        def at(first):
            return pl.ds((v - first) * U if isinstance(v, int) else pl.multiple_of((v - first) * U, 128), U)

        if which == 0:
            pairs = [(FO, out_down.at[l, at(0)])]
        elif which == 1:
            pairs = [(FT, out_gate.at[l, :, at(fu)])]
        elif which == 2:
            pairs = [(FT, out_up.at[l, :, at(2 * fu)])]
        elif which == 3:
            pairs = [(FT.at[:, pl.ds(0, C)], out_in.at[l, 0]),
                     (FT.at[:, pl.ds(C, U - C)], out_in.at[l, 1, :, pl.ds(0, U - C)])]
        elif which == 4:
            pairs = [(FT.at[:, pl.ds(0, 2 * C - U)], out_in.at[l, 1, :, pl.ds(U - C, 2 * C - U)]),
                     (FT.at[:, pl.ds(2 * C - U, C)], out_in.at[l, 2])]
        else:
            pairs = [(FO.at[pl.ds(0, width)], out_out.at[l])]
        return [pltpu.make_async_copy(a, b, fos.at[i]) for i, (a, b) in enumerate(pairs)]

    def by_target(t, fn):
        fu = F // U
        edges = (0, fu, 2 * fu, 3 * fu, 3 * fu + 1, 3 * fu + 2, PER)
        cases(rem(t, PER), [(edges[i], edges[i + 1], functools.partial(fn, i)) for i in range(6)])

    def unit_wait(t):
        def go(which):
            for cp in unit_copies(t, which):
                cp.wait()

        by_target(t, go)

    def rs_last(t):
        slot = rem(t, SLOTS)
        if isinstance(t, int):
            if t >= 1:
                unit_wait(t - 1)
        else:
            pl.when(t >= 1)(lambda: unit_wait(t - 1))

        def go(rows):
            wide, cut, _ = rows
            for lane in range(2):
                rs_copy(lane, 2, t, rows).wait()
            FO[0:cut] = GA[slot, keep(0, 2), 0:cut].astype(f32) + RA2[slot, 0, 0:cut].astype(f32)
            FO[cut:wide] = (
                GB[slot, keep(1, 2), 0 : wide - cut].astype(f32) + RB2[slot, 0, 0 : wide - cut].astype(f32)
            )

        sized(t, go)

        def send(which):
            if which in (1, 2, 3, 4):
                FT[...] = FO[...].T
            for cp in unit_copies(t, which):
                cp.start()

        by_target(t, send)

    def tick_gen(t):
        if not isinstance(t, int) or t < UNITS:
            rs_gen(t)

    def tick_rest(t):
        steps = (functools.partial(rs_add, 0), functools.partial(rs_add, 1), rs_last)
        for lag, fn in enumerate(steps, 1):
            if isinstance(t, int):
                if 0 <= t - lag < UNITS:
                    fn(t - lag)
            else:
                pl.when(t >= lag)(functools.partial(fn, t - lag))

    def behind(prev, cur, m):
        if prev is None:
            pl.when(m > 0)(lambda: mid(m - 1))
        else:
            mid(lax.rem(m + M - 1, M))
            pl.when(m < 2)(lambda: prev(m + M - 2))
        pl.when(m >= 2)(lambda: cur(m - 2))

    def phase(prev, cur, first, second=None, tick=None, ahead=None):
        def step(m, _):
            if ahead is not None:
                ahead(m)
            if tick is not None:
                tick_gen(tick + m)
            if first is not None:
                first(m)
            behind(prev, cur, m)
            if second is not None:
                second(m)
            if tick is not None:
                tick_rest(tick + m)
            return 0

        lax.fori_loop(0, M, step, 0)

    def arrived(copies):
        for cp in copies:
            cp.wait()

    end_o0 = functools.partial(finish_norm, 0, 1, N2)
    end_f0 = functools.partial(finish_norm, 1, 0, N1)
    end_o1 = functools.partial(finish_norm, 1, 1, N2)
    end_n1 = functools.partial(finish_dn2, 1)
    end_c1 = functools.partial(finish_dn1, 1)
    end_n0 = functools.partial(finish_dn2, 0)
    end_c0 = functools.partial(finish_dn1, 0)

    arrived(load_conv(0))
    phase(None, end_o0, lambda m: conv_fwd_a(0, m), lambda m: conv_fwd_b(0, m))
    arrived(load_ffn(0))

    def f0(m):
        agcopy(0, N2, m).wait()
        ffn_fwd(0, m)
        ffn_down(0, m)

    phase(end_o0, end_f0, f0)
    for cp in load_ffn(1):
        cp.start()
    arrived(load_conv(1))
    phase(end_f0, end_o1, lambda m: conv_fwd_a(1, m), lambda m: conv_fwd_b(1, m))
    arrived(load_ffn(1) + [load_og])

    agcopy(1, N2, 0).wait()
    ffn_fwd(1, 0)
    mid(M - 1)
    end_o1(M - 2)
    agcopy(1, N2, 1).wait()
    ffn_fwd(1, 1)
    agcopy(1, N2, 2).wait()
    ffn_fwd(1, 2, 0, 2)
    end_o1(M - 1)
    ffn_fwd(1, 2, 2)
    agcopy(1, N2, 3).wait()
    ffn_fwd(1, 3)
    tick_gen(0)

    def start_c1(m):
        agcopy(1, DO, m).wait()
        conv_bwd_a(1, m)

    def last_only(fn):
        return lambda m: pl.when(m == M - 1)(lambda: fn(0))

    def next_one(fn):
        return lambda m: pl.when(m < M - 1)(lambda: fn(m + 1))

    phase(None, end_n1, lambda m: ffn_bwd(1, m), tick=1, ahead=last_only(start_c1))
    for cp in load_ffn(0):
        cp.start()
    phase(end_n1, end_c1, None, lambda m: conv_bwd_b(1, m), tick=1 + M, ahead=next_one(start_c1))
    arrived(load_ffn(0))

    def n0(m):
        ffn_bwd(0, m)

    def n0_tick(m, _):
        pl.when(m == 0)(lambda: agcopy(0, DF, 0).wait())
        pl.when(m == 1)(lambda: agcopy(0, DF, 1).wait())

        @pl.when(m == 2)
        def _():
            agcopy(0, DF, 2).wait()
            agcopy(0, DF, 3).wait()

        tick_gen(1 + 2 * M + m)
        n0(m)
        behind(end_c1, end_n0, m)
        tick_rest(1 + 2 * M + m)
        return 0

    lax.fori_loop(0, M, n0_tick, 0)
    load_ffn(1)[2].start()
    load_ffn(1)[2].wait()

    def f1(m):
        agcopy(0, DO, m).wait()
        ffn_down(1, m)

    def start_c0(m):
        conv_bwd_a(0, m)

    phase(end_n0, finish_stream, f1, tick=1 + 3 * M, ahead=last_only(start_c0))

    def c0(m):
        for cp in stream_copies(m):
            cp.wait()
        conv_bwd_b(0, m)

    phase(finish_stream, end_c0, None, c0, tick=1 + 4 * M, ahead=next_one(start_c0))
    t = 1 + 5 * M
    tick_gen(t)
    mid(M - 1)
    end_c0(M - 2)
    tick_rest(t)
    tick_gen(t + 1)
    end_c0(M - 1)

    for i in range(4):
        SM[i : i + 1] = jnp.sum(GACC[i], axis=0, keepdims=True)
    SM[4:8] = jnp.zeros((4, D), f32)
    for l in range(2):
        for k in range(3):
            SM[4 + l : 5 + l, k * C : (k + 1) * C] = jnp.sum(CACC[l, k], axis=0, keepdims=True)

    def small(i):
        return remote(SM, SMR.at[i], sms.at[i], smr.at[i], [sib, *parts][i])

    small(0).start()
    tick_rest(t + 1)
    t += 2
    for i in range(4):
        tick_gen(t)
        small(i).wait()
        if i == 0:
            SM[0:4] += SMR[0, 0:4]
        else:
            SM[...] += SMR[i]
        if i < 3:
            small(i + 1).start()
        tick_rest(t)
        t += 1
    while t < UNITS + 3:
        tick_gen(t)
        tick_rest(t)
        t += 1
    own = pl.ds(pl.multiple_of(tp * C, 128), C)
    out_norm[...] = SM[0:2, own]
    out_ffn[...] = SM[2:4, own]
    for l in range(2):
        for k in range(3):
            out_conv[k, l : l + 1, :] = SM[4 + l : 5 + l, k * C : (k + 1) * C]
    unit_wait(UNITS - 1)
    for m in range(M):
        for cp in grad_copies(m):
            cp.wait()


def fused_call(stream_in, norm_gain, win, taps, wout, ffn_gain, wgate, wup, wdown, out_grad):
    M, TOK, D = stream_in.shape
    C, F = wout.shape[1], wgate.shape[2]
    U = 384
    rb = U // 6
    ra = U - rb
    half = TOK // 2
    vm = pltpu.VMEM
    dma = pltpu.SemaphoreType.DMA
    S = SLOTS
    anys = pl.BlockSpec(memory_space=pl.ANY)
    vmem = pl.BlockSpec(memory_space=pltpu.VMEM)
    return pl.pallas_call(
        functools.partial(fused, (M, TOK, D, C, F, U)),
        out_shape=[
            jax.ShapeDtypeStruct((M, TOK, D), bf16),
            jax.ShapeDtypeStruct((M, TOK, D), f32),
            jax.ShapeDtypeStruct((LAYERS, C), f32),
            jax.ShapeDtypeStruct((LAYERS, 3, 128, C), f32),
            jax.ShapeDtypeStruct((3, LAYERS, C), f32),
            jax.ShapeDtypeStruct((LAYERS, C, 128), f32),
            jax.ShapeDtypeStruct((LAYERS, C), f32),
            jax.ShapeDtypeStruct((LAYERS, 128, F), f32),
            jax.ShapeDtypeStruct((LAYERS, 128, F), f32),
            jax.ShapeDtypeStruct((LAYERS, F, 128), f32),
        ],
        in_specs=[anys, vmem, anys, vmem, anys, vmem, anys, anys, anys, anys],
        out_specs=[anys, anys, vmem, anys, vmem, anys, vmem, anys, anys, anys],
        scratch_shapes=[
            vm((LAYERS, 4, M, TOK, D), bf16),
            vm((LAYERS, M, TOK, 3 * F + 4 * C), bf16),
            vm((LAYERS, D, 3 * C), bf16),
            vm((LAYERS, C, D), bf16),
            vm((D, F), bf16),
            vm((D, F), bf16),
            vm((F, D), bf16),
            vm((M, half, D), f32),
            vm((M, half, D), f32),
            vm((M, half, 2 * LAYERS), f32),
            vm((M, TOK, D), bf16),
            vm((M, half, D), bf16),
            vm((M, half, D), bf16),
            vm((S, 8, ra, 128), bf16),
            vm((S, 8, rb, 128), bf16),
            vm((S, 4, ra, 128), bf16),
            vm((S, 2, ra, 128), bf16),
            vm((S, 1, ra, 128), bf16),
            vm((S, 4, rb, 128), bf16),
            vm((S, 2, rb, 128), bf16),
            vm((S, 1, rb, 128), bf16),
            vm((U, M * TOK), bf16),
            vm((U, 128), f32),
            vm((128, U), f32),
            vm((8, D), f32),
            vm((TOK + 8, C), f32),
            vm((2, TOK + 8, C), f32),
            vm((LAYERS, M, 8, C), f32),
            vm((LAYERS, M, 8, C), f32),
            vm((4, LAYERS, D), f32),
            vm((3, LAYERS, C), f32),
            vm((4, 8, D), f32),
            vm((LAYERS, 3, 8, C), f32),
            vm((4, 8, D), f32),
            dma((16,)),
            dma((M,)), dma((M,)), dma((M,)), dma((M,)), dma((M,)), dma((M,)),
            dma, dma((2,)), dma((2, LAYERS, M)),
            dma((2, 3, S)), dma((2, 3, S)),
            dma((2,)), dma((M,)), dma((M,)), dma((M,)), dma((4,)), dma((4,)),
        ],
        name="fused",
        compiler_params=pltpu.CompilerParams(
            collective_id=0, has_side_effects=True, vmem_limit_bytes=VMEM_BYTES
        ),
    )(stream_in, norm_gain, win, taps, wout, ffn_gain, wgate, wup, wdown, out_grad)


def body_fused(
    stream_in, norm_gain, in_proj, conv_taps, out_proj, ffn_gain, gate_proj, up_proj, down_proj, out_grad
):
    (out_stream, out_sgrad, norm_g, in_g, conv_g, out_g, ffn_g, gate_g, up_g, down_g) = fused_call(
        stream_in, norm_gain, jnp.transpose(in_proj, (0, 2, 1, 3)), jnp.transpose(conv_taps, (1, 0, 2)),
        out_proj, ffn_gain, gate_proj, up_proj, down_proj, out_grad,
    )
    in_g = jnp.transpose(in_g, (0, 2, 1, 3))
    conv_g = jnp.transpose(conv_g, (1, 0, 2))
    return (out_stream, out_sgrad, norm_g, in_g, conv_g, out_g, ffn_g, gate_g, up_g, down_g)


def solution(mesh):
    in_specs = (
        P(None, "seq", None),
        P(),
        P(None, None, None, "tp"),
        P(None, None, "tp"),
        P(None, "tp", None),
        P(),
        P(None, None, "tp"),
        P(None, None, "tp"),
        P(None, "tp", None),
        P(None, "seq", None),
    )
    out_specs = (
        P(None, "seq", None),
        P(None, "seq", None),
        P(None, "tp"),
        P(None, "seq", None, "tp"),
        P(None, None, "tp"),
        P(None, "tp", "seq"),
        P(None, "tp"),
        P(None, "seq", "tp"),
        P(None, "seq", "tp"),
        P(None, "tp", "seq"),
    )
    chosen = body_fused if (mesh.shape["seq"], mesh.shape["tp"]) == (8, 4) else body
    return jax.shard_map(chosen, mesh=mesh, in_specs=in_specs, out_specs=out_specs, check_vma=False)
```

```python
import functools

import jax
import jax.numpy as jnp
from jax import lax
from jax.experimental import pallas as pl
from jax.experimental.pallas import tpu as pltpu
from jax.sharding import PartitionSpec as P

LAYERS = 2


EPS = 1e-05


def passed_along(block, axis, distance):
    devices = range(lax.axis_size(axis))
    route = [(i - distance, i) for i in devices if i - distance in devices]
    return lax.ppermute(block, axis, route)


def norm_rate(hidden):
    return lax.rsqrt(jnp.mean(hidden * hidden, axis=-1, keepdims=True) + EPS)


def norm_back(grad_in, gain, normed_val, rate):
    scaled = grad_in * gain
    return rate * (scaled - normed_val * jnp.mean(scaled * normed_val, axis=-1, keepdims=True))


def reduce_weights(grads):
    return (
        lax.psum_scatter(
            grads[0].astype(jnp.bfloat16), "seq", scatter_dimension=1, tiled=True
        ).astype(jnp.float32),
        lax.psum_scatter(
            grads[1].astype(jnp.bfloat16), "seq", scatter_dimension=2, tiled=True
        ).astype(jnp.float32),
        lax.psum_scatter(
            grads[2].astype(jnp.bfloat16), "seq", scatter_dimension=1, tiled=True
        ).astype(jnp.float32),
        lax.psum_scatter(
            grads[3].astype(jnp.bfloat16), "seq", scatter_dimension=1, tiled=True
        ).astype(jnp.float32),
        lax.psum_scatter(
            grads[4].astype(jnp.bfloat16), "seq", scatter_dimension=2, tiled=True
        ).astype(jnp.float32),
    )


def reduce_small(grads):
    return lax.psum((grads[0], grads[1], grads[2]), "seq")


def body(
    stream_in,
    norm_gain,
    in_proj,
    conv_taps,
    out_proj,
    ffn_gain,
    gate_proj,
    up_proj,
    down_proj,
    out_grad,
):
    f32 = jnp.float32
    bf16 = jnp.bfloat16
    width = in_proj.shape[-1]
    offset = lax.axis_index("tp") * width
    hidden = stream_in.astype(f32)
    kept = []
    for layer in range(LAYERS):
        gain_one = norm_gain[layer].astype(f32)
        gain_two = ffn_gain[layer].astype(f32)
        taps = conv_taps[layer].astype(f32)
        rate_one = norm_rate(hidden)
        normed_one = hidden * rate_one
        first = (normed_one * gain_one).astype(bf16)
        proj = jnp.einsum("msd,dkc->mskc", first, in_proj[layer], preferred_element_type=f32)
        bgate = proj[:, :, 0]
        cgate = proj[:, :, 1]
        xinput = proj[:, :, 2]
        mixed = (bgate * xinput).astype(bf16)
        prior = passed_along(mixed[:, -2:], "seq", 1)
        extended = jnp.concatenate([prior, mixed], axis=1).astype(f32)
        conved = (
            taps[0] * extended[:, :-2] + taps[1] * extended[:, 1:-1] + taps[2] * extended[:, 2:]
        )
        gated = (cgate * conved).astype(bf16)
        partial_out = jnp.einsum("msc,cd->msd", gated, out_proj[layer], preferred_element_type=f32)
        middle = hidden + lax.psum(partial_out, "tp")
        rate_two = norm_rate(middle)
        normed_two = middle * rate_two
        second = (normed_two * gain_two).astype(bf16)
        gate_val = jnp.einsum("msd,df->msf", second, gate_proj[layer], preferred_element_type=f32)
        up_val = jnp.einsum("msd,df->msf", second, up_proj[layer], preferred_element_type=f32)
        sigma = jax.nn.sigmoid(gate_val)
        silu_val = gate_val * sigma
        act = (silu_val * up_val).astype(bf16)
        partial_ffn = jnp.einsum("msf,fd->msd", act, down_proj[layer], preferred_element_type=f32)
        kept.append(
            (
                rate_one,
                normed_one,
                first,
                bgate,
                cgate,
                xinput,
                extended,
                conved,
                gated,
                rate_two,
                normed_two,
                second,
                gate_val,
                up_val,
                sigma,
                silu_val,
                act,
            )
        )
        hidden = middle + lax.psum(partial_ffn, "tp")
    grad_h = out_grad.astype(f32)
    collected = [None] * LAYERS
    for layer in reversed(range(LAYERS)):
        (
            rate_one,
            normed_one,
            first,
            bgate,
            cgate,
            xinput,
            extended,
            conved,
            gated,
            rate_two,
            normed_two,
            second,
            gate_val,
            up_val,
            sigma,
            silu_val,
            act,
        ) = kept[layer]
        gain_one = norm_gain[layer].astype(f32)
        gain_two = ffn_gain[layer].astype(f32)
        taps = conv_taps[layer].astype(f32)
        grad_f = grad_h.astype(bf16)
        grad_act = jnp.einsum("msd,fd->msf", grad_f, down_proj[layer], preferred_element_type=f32)
        down_g = jnp.einsum("msf,msd->fd", act, grad_f, preferred_element_type=f32)
        grad_gate = (grad_act * up_val * sigma * (1.0 + gate_val * (1.0 - sigma))).astype(bf16)
        grad_up = (grad_act * silu_val).astype(bf16)
        part_two = jnp.einsum(
            "msf,df->msd", grad_gate, gate_proj[layer], preferred_element_type=f32
        )
        part_two = part_two + jnp.einsum(
            "msf,df->msd", grad_up, up_proj[layer], preferred_element_type=f32
        )
        gate_g = jnp.einsum("msd,msf->df", second, grad_gate, preferred_element_type=f32)
        up_g = jnp.einsum("msd,msf->df", second, grad_up, preferred_element_type=f32)
        grad_two = lax.psum(part_two.astype(jnp.bfloat16), "tp").astype(jnp.float32)
        ffn_gain_g = jnp.sum(grad_two * normed_two, axis=(0, 1))
        grad_mid = grad_h + norm_back(grad_two, gain_two, normed_two, rate_two)
        grad_o = grad_mid.astype(bf16)
        grad_gated = jnp.einsum("msd,cd->msc", grad_o, out_proj[layer], preferred_element_type=f32)
        out_g = jnp.einsum("msc,msd->cd", gated, grad_o, preferred_element_type=f32)
        grad_conv = grad_gated * cgate
        grad_cgate = grad_gated * conved
        after = passed_along(grad_conv[:, :2], "seq", -1)
        grad_ext = jnp.concatenate([grad_conv, after], axis=1)
        grad_mixed = (
            taps[2] * grad_ext[:, :-2] + taps[1] * grad_ext[:, 1:-1] + taps[0] * grad_ext[:, 2:]
        )
        count = grad_conv.shape[1]
        conv_g = jnp.stack(
            [jnp.sum(grad_conv * extended[:, k : k + count], axis=(0, 1)) for k in range(3)], axis=0
        )
        grad_proj = jnp.stack([grad_mixed * xinput, grad_cgate, grad_mixed * bgate], axis=2).astype(
            bf16
        )
        part_one = jnp.einsum(
            "mskc,dkc->msd", grad_proj, in_proj[layer], preferred_element_type=f32
        )
        in_g = jnp.einsum("msd,mskc->dkc", first, grad_proj, preferred_element_type=f32)
        grad_one = lax.psum(part_one.astype(jnp.bfloat16), "tp").astype(jnp.float32)
        norm_gain_g = jnp.sum(grad_one * normed_one, axis=(0, 1))
        grad_h = grad_mid + norm_back(grad_one, gain_one, normed_one, rate_one)
        norm_piece = lax.dynamic_slice_in_dim(norm_gain_g, offset, width)
        ffn_piece = lax.dynamic_slice_in_dim(ffn_gain_g, offset, width)
        small = (norm_piece, conv_g, ffn_piece)
        large = (in_g, out_g, gate_g, up_g, down_g)
        collected[layer] = (small, large)
    norm_stack = jnp.stack([c[0][0] for c in collected], axis=0)
    conv_stack = jnp.stack([c[0][1] for c in collected], axis=0)
    ffn_stack = jnp.stack([c[0][2] for c in collected], axis=0)
    large_stack = tuple((jnp.stack([c[1][i] for c in collected], axis=0) for i in range(5)))
    large_stack = reduce_weights(large_stack)
    norm_stack, conv_stack, ffn_stack = reduce_small((norm_stack, conv_stack, ffn_stack))
    stream_out = hidden.astype(bf16)
    in_grad, out_grad_w, gate_grad, up_grad, down_grad = large_stack
    return (
        stream_out,
        grad_h,
        norm_stack,
        in_grad,
        conv_stack,
        out_grad_w,
        ffn_stack,
        gate_grad,
        up_grad,
        down_grad,
    )


VMEM_BYTES = 64 * 2**20
MESH = pl.DeviceIdType.MESH
f32 = jnp.float32
bf16 = jnp.bfloat16
NN = (((1,), (0,)), ((), ()))
NT = (((1,), (1,)), ((), ()))
ORDERS = ((0, 1, 2), (1, 2, 0))
SLOTS = 4
WIDE = 512
N1, N2, DF, DO = range(4)


def rem(a, b):
    return a % b if isinstance(a, int) else lax.rem(a, b)


def div(a, b):
    return a // b if isinstance(a, int) else lax.div(a, b)


def cases(value, branches):
    for low, high, fn in branches:
        if isinstance(value, int):
            if low <= value < high:
                fn()
        else:
            pl.when((value >= low) & (value < high))(fn)


def mm(lhs, rhs, dims=NN):
    return lax.dot_general(lhs, rhs, dims, preferred_element_type=f32)


def fused(
    dims,
    stream_in, norm_gain, win, taps, wout, ffn_gain, wgate, wup, wdown, out_grad,
    out_stream, out_sgrad, out_norm, out_in, out_conv, out_out, out_ffn, out_gate, out_up, out_down,
    L, R, WIN, WOUT, WGU, WD, H, DH, RATE, PB, PR, XR,
    GA, GB, RA0, RA1, RA2, RB0, RB1, RB2, RT, FO, FT, SM,
    EXT, DYE, CF, HALO, HALO2, DHALO, GAIN, TAPS, TAPS2, GACC, CACC, SMR,
    load_sem, ps, pr, xs, xr, ags, agr, hs, dhs, hr, hs2, hr2, gs, gr, rss, rsr, fos, oss, sts, str_, sms, smr,
):
    M, TOK, D, C, F, U = dims
    half = TOK // 2
    CS, CA, CP, CZ = 0, F, 3 * F, 3 * F + 3 * C
    UNITS = 2 * (-(-(CZ + C) // U))
    PER = UNITS // 2
    full = (U, GA.shape[2], GB.shape[2])
    width = CZ + C - (PER - 1) * U
    tail_b = width // 6 // 16 * 16 + 16 * (width % 96 > 0)
    short = (width, width - tail_b, tail_b)
    seq = lax.axis_index("seq")
    tp = lax.axis_index("tp")
    n = lax.axis_size("seq")
    core = lax.rem(tp, 2)
    xi = lax.div(tp, 2)
    sib = {"seq": seq, "tp": tp + 1 - 2 * core}
    xpart = {"seq": seq, "tp": tp + 2 - 4 * xi}
    bits = [lax.rem(lax.div(seq, 1 << k), 2) for k in range(3)]
    parts = [{"seq": seq + (1 << k) - 2 * (1 << k) * bits[k], "tp": tp} for k in range(3)]
    nxt = {"seq": lax.rem(seq + 1, n), "tp": tp}
    prv = {"seq": lax.rem(seq + n - 1, n), "tp": tp}
    mine = pl.ds(pl.multiple_of(core * half, half), half)
    theirs = pl.ds(pl.multiple_of((1 - core) * half, half), half)

    def remote(src, dst, ssem, rsem, dev):
        return pltpu.make_async_remote_copy(
            src_ref=src, dst_ref=dst, send_sem=ssem, recv_sem=rsem, device_id=dev, device_id_type=MESH
        )

    def load_stream(m):
        return pltpu.make_async_copy(stream_in.at[m], L.at[0, N1, m], load_sem.at[m])

    def load_conv(l):
        return [
            pltpu.make_async_copy(win.at[l, k], WIN.at[:, pl.ds(k * C, C)], load_sem.at[4 + k])
            for k in range(3)
        ] + [pltpu.make_async_copy(wout.at[l], WOUT, load_sem.at[7])]

    def load_ffn(l):
        return [
            pltpu.make_async_copy(
                src.at[l, :, pl.ds(t * U, U)], WGU.at[:, pl.ds((2 * t + i) * U, U)], load_sem.at[10 + 2 * t + i]
            )
            for t in range(F // U)
            for i, src in enumerate((wgate, wup))
        ]

    def load_down(l):
        return pltpu.make_async_copy(wdown.at[l], WD, load_sem.at[9])

    load_og = pltpu.make_async_copy(out_grad, L.at[1, DF], load_sem.at[8])
    for cp in load_conv(0) + [load_stream(m) for m in range(M)]:
        cp.start()

    barrier = pltpu.get_barrier_semaphore()
    others = [sib, xpart, nxt, prv] + parts
    for dev in others:
        pl.semaphore_signal(barrier, inc=1, device_id=dev, device_id_type=MESH)

    GAIN[0] = norm_gain[...].astype(f32)
    GAIN[1] = ffn_gain[...].astype(f32)
    GAIN[2] = 1.0 / norm_gain[...].astype(f32)
    GAIN[3] = 1.0 / ffn_gain[...].astype(f32)
    TAPS[...] = taps[...].astype(f32)
    GACC[...] = jnp.zeros_like(GACC)
    CACC[...] = jnp.zeros_like(CACC)

    pl.semaphore_wait(barrier, len(others))

    zpos, ypos = lax.div(seq, 2), lax.rem(seq, 2)
    zfar, znear = lax.rem(zpos + 2, 4), zpos + 1 - 2 * lax.rem(zpos, 2)
    strip = D // 8

    def piece(s, z):
        rows = pl.ds(pl.multiple_of(ypos * strip, strip), strip)
        if s < 3:
            return L.at[0, DO, 1 + s, rows, pl.ds(pl.multiple_of(z * TOK, TOK), TOK)]
        return L.at[0, DO, 0, pl.ds(pl.multiple_of(ypos * strip + z * (C // 8), 16), C // 8)]

    def gathers(s, step):
        def send(i, src, dst, dev):
            return remote(src, dst, gs.at[s, i], gr.at[s, i], dev)

        if step == 0:
            if s < 3:
                src = win.at[1, s, pl.ds(pl.multiple_of(zpos * TOK + ypos * strip, strip), strip)]
            else:
                src = wout.at[1, pl.ds(pl.multiple_of(ypos * strip + zpos * (C // 8), 16), C // 8)]
            return [send(0, src, piece(s, zpos), xpart)]
        if step == 1:
            return [send(1, piece(s, zpos), piece(s, zpos), parts[2])]
        if step == 2:
            return [send(2 + i, piece(s, z), piece(s, z), parts[1]) for i, z in enumerate((zpos, zfar))]
        half_ref = L.at[0, DO, (1 + s) % 4, pl.ds(pl.multiple_of(ypos * strip, strip), strip)]
        return [send(4, half_ref, half_ref, parts[0])]

    def gather_at(j):
        for s in range(4):
            for step, when in enumerate((s, s + 2, s + 4, 7 + 2 * s)):
                if j == when:
                    for cp in gathers(s, step):
                        cp.wait()
                    if step < 3:
                        for cp in gathers(s, step + 1):
                            cp.start()

    def gather_dyn(base, m, late):
        for i in range(M):
            pl.when(m == i)(functools.partial(gather_at, base + 2 * i + late))

    for s in range(4):
        for cp in gathers(s, 0):
            cp.start()
    tap_copy = remote(TAPS, TAPS2, hs2.at[1], hr2.at[M], xpart)
    tap_copy.start()

    def pcopy(m):
        return remote(PB.at[m, theirs], PR.at[m], ps.at[m], pr.at[m], sib)

    def xcopy(m):
        return remote(PB.at[m, mine], XR.at[m], xs.at[m], xr.at[m], xpart)

    def mid(m):
        pcopy(m).wait()

        def chunk(i, _):
            off = pl.multiple_of(i * 32, 32)
            rows = pl.ds(pl.multiple_of(core * half + off, 32), 32)
            got = PR[m, pl.ds(off, 32)].astype(f32) + PB[m, rows].astype(f32)
            PB[m, rows] = got.astype(bf16)
            return 0

        lax.fori_loop(0, half // 32, chunk, 0)
        xcopy(m).start()

    def agcopy(l, kind, m):
        ref = L.at[l, kind, m, mine]
        return remote(ref, ref, ags.at[m], agr.at[m], sib)

    def rows_loop(m, body, received=XR):
        def chunk(i, _):
            off = pl.multiple_of(i * 32, 32)
            rows = pl.ds(pl.multiple_of(core * half + off, 32), 32)
            total = PB[m, rows].astype(f32) + received[m, pl.ds(off, 32)].astype(f32)
            body(pl.ds(off, 32), rows, total)
            return 0

        lax.fori_loop(0, half // 32, chunk, 0)

    def rate_of(val):
        return lax.rsqrt(jnp.mean(val * val, axis=-1, keepdims=True) + EPS)

    def finish_norm(l, which, kind, m, within=False):
        if within:
            pcopy(m).wait()
        else:
            xcopy(m).wait()
        gain = GAIN[which, l : l + 1, :]

        def body(loc, rows, total):
            hid = H[m, loc] + total
            H[m, loc] = hid
            rate = rate_of(hid)
            RATE[m, loc, 2 * l + which : 2 * l + which + 1] = rate
            L[l, kind, m, rows] = (hid * rate * gain).astype(bf16)

        rows_loop(m, body, PR if within else XR)
        agcopy(l, kind, m).start()

    def stream_copies(m):
        ref = PB.at[m, mine]
        return (
            pltpu.make_async_copy(ref, out_stream.at[m, mine], oss.at[m]),
            remote(ref, out_stream.at[m, mine], sts.at[m], str_.at[m], sib),
        )

    def finish_stream(m):
        xcopy(m).wait()

        def body(loc, rows, total):
            PB[m, rows] = (H[m, loc] + total).astype(bf16)

        rows_loop(m, body)
        for cp in stream_copies(m):
            cp.start()

    def norm_back(l, which, kind, m, emit):
        xcopy(m).wait()
        gain = GAIN[which, l : l + 1, :]
        inv = GAIN[2 + which, l : l + 1, :]

        def body(loc, rows, total):
            nrm = L[l, kind, m, rows].astype(f32) * inv
            prod = total * nrm
            GACC[2 * which + l] += prod[0:8] + prod[8:16] + prod[16:24] + prod[24:32]
            mean = jnp.mean(prod * gain, axis=-1, keepdims=True)
            emit(loc, rows, RATE[m, loc, 2 * l + which : 2 * l + which + 1] * (total * gain - nrm * mean))

        rows_loop(m, body)

    def finish_dn2(l, m):
        def emit(loc, rows, delta):
            prev = L[1, DF, m, rows].astype(f32) if l == 1 else DH[m, loc]
            new = prev + delta
            DH[m, loc] = new
            L[l, DO, m, rows] = new.astype(bf16)

        norm_back(l, 1, N2, m, emit)
        agcopy(l, DO, m).start()

    def finish_dn1(l, m):
        def emit(loc, rows, delta):
            new = DH[m, loc] + delta
            DH[m, loc] = new
            if l == 1:
                L[0, DF, m, rows] = new.astype(bf16)

        norm_back(l, 0, N1, m, emit)
        if l == 1:
            agcopy(0, DF, m).start()
        else:
            for cp in grad_copies(m):
                cp.start()

    def grad_copies(m):
        return (
            pltpu.make_async_copy(DH.at[m], out_sgrad.at[m, mine], oss.at[m]),
            remote(DH.at[m], out_sgrad.at[m, mine], ags.at[m], agr.at[m], sib),
        )

    def put_partial(m, tile):
        def step(j, _):
            cols = pl.ds(pl.multiple_of(j * WIDE, WIDE), WIDE)
            PB[m, :, cols] = tile(cols).astype(bf16)
            return 0

        lax.fori_loop(0, D // WIDE, step, 0)
        pcopy(m).start()

    def hcopy(l, m):
        return remote(EXT.at[pl.ds(TOK, 8)], HALO.at[l, m], hs, hr.at[0, l, m], nxt)

    def dhcopy(l, m):
        return remote(DYE.at[rem(m, 2), pl.ds(0, 8)], DHALO.at[l, m], dhs.at[rem(m, 2)], hr.at[1, l, m], prv)

    def hcopy2(m):
        return remote(DYE.at[1, pl.ds(TOK, 8)], HALO2.at[m], hs2.at[0], hr2.at[m], nxt)

    def tap(l, k):
        return TAPS[k, l : l + 1, :]

    def conv_of(ext, halo, taps_ref, l):
        ext[0:8] = jnp.where(seq == 0, 0.0, halo)
        t = [taps_ref[k, l : l + 1, :] for k in range(3)]
        return t[0] * ext[6 : 6 + TOK] + t[1] * ext[7 : 7 + TOK] + t[2] * ext[8 : 8 + TOK]

    def conv_now(l, m):
        return conv_of(EXT, HALO[l, m], TAPS, l)

    def other_in(k):
        blocks = [L[0, DO, 1 + k, :, r * TOK : (r + 1) * TOK] for r in range(D // TOK)]
        return jnp.concatenate(blocks, axis=0)

    def conv_fwd_a(l, m):
        if l == 0:
            load_stream(m).wait()
            gain = GAIN[0, 0:1, :]
            hid = L[0, N1, m, mine].astype(f32)
            H[m] = hid
            RATE[m, :, 0:1] = rate_of(hid)

            def chunk(i, _):
                rows = pl.ds(pl.multiple_of(i * 32, 32), 32)
                val = L[0, N1, m, rows].astype(f32)
                L[0, N1, m, rows] = (val * rate_of(val) * gain).astype(bf16)
                return 0

            lax.fori_loop(0, TOK // 32, chunk, 0)
        else:
            agcopy(1, N1, m).wait()
        first = L[l, N1, m]
        p = mm(first, WIN[...])
        bgate, cgate, xin = p[:, 0:C], p[:, C : 2 * C], p[:, 2 * C : 3 * C]
        R[l, m, :, CP : CP + 3 * C] = p.astype(bf16)
        EXT[8 : 8 + TOK] = (bgate * xin).astype(bf16).astype(f32)
        hcopy(l, m).start()
        DYE[0, 0:TOK] = cgate
        if l == 1:
            p = mm(first, jnp.concatenate([other_in(k) for k in range(3)], axis=1))
            DYE[1, 8 : 8 + TOK] = (p[:, 0:C] * p[:, 2 * C : 3 * C]).astype(bf16).astype(f32)
            hcopy2(m).start()
            CF[...] = p[:, C : 2 * C]

    def conv_fwd_b(l, m):
        hcopy(l, m).wait()
        gated = (DYE[0, 0:TOK] * conv_now(l, m)).astype(bf16)
        R[l, m, :, CZ : CZ + C] = gated
        if l == 0:
            put_partial(m, lambda cols: mm(R[l, m, :, CZ : CZ + C], WOUT[:, cols]))
        else:
            hcopy2(m).wait()
            L[0, DF, m, :, 0:C] = (CF[...] * conv_of(DYE.at[1], HALO2[m], TAPS2, l)).astype(bf16)
            put_partial(
                m,
                lambda cols: mm(R[l, m, :, CZ : CZ + C], WOUT[:, cols])
                + mm(L[0, DF, m, :, 0:C], L[0, DO, 0, :, cols]),
            )

    def down_back(m):
        ds = mm(L[1, DF, m], WD[...], NT).astype(bf16)
        for t in range(F // U):
            R[1, m, :, CA + (2 * t + 1) * U : CA + (2 * t + 2) * U] = ds[:, t * U : (t + 1) * U]

    def ffn_fwd(l, m):
        def step(t, _):
            off = pl.multiple_of(t * U, 128)
            off2 = pl.multiple_of(2 * t * U, 128)
            ab = mm(L[l, N2, m], WGU[:, pl.ds(off2, 2 * U)])
            a, b = ab[:, 0:U], ab[:, U : 2 * U]
            sig = jax.nn.sigmoid(a)
            silu = a * sig
            R[l, m, :, pl.ds(CS + off, U)] = (silu * b).astype(bf16)
            if l == 0:
                R[l, m, :, pl.ds(CA + off2, 2 * U)] = ab.astype(bf16)
            else:
                ds = R[l, m, :, pl.ds(CA + U + off2, U)].astype(f32)
                R[l, m, :, pl.ds(CA + off2, U)] = (ds * b * sig * (1.0 + a * (1.0 - sig))).astype(bf16)
                R[l, m, :, pl.ds(CA + U + off2, U)] = (ds * silu).astype(bf16)
            return 0

        lax.fori_loop(0, F // U, step, 0)

    def ffn_down(l, m):
        put_partial(m, lambda cols: mm(R[l, m, :, CS : CS + F], WD[:, cols]))

    def ffn_bwd(l, m):
        if l == 0:
            def step(t, _):
                off = pl.multiple_of(t * U, 128)
                off2 = pl.multiple_of(2 * t * U, 128)
                a = R[l, m, :, pl.ds(CA + off2, U)].astype(f32)
                b = R[l, m, :, pl.ds(CA + U + off2, U)].astype(f32)
                sig = jax.nn.sigmoid(a)
                ds = mm(L[l, DF, m], WD[pl.ds(off, U), :], NT)
                R[l, m, :, pl.ds(CA + off2, U)] = (ds * b * sig * (1.0 + a * (1.0 - sig))).astype(bf16)
                R[l, m, :, pl.ds(CA + U + off2, U)] = (ds * a * sig).astype(bf16)
                return 0

            lax.fori_loop(0, F // U, step, 0)
        put_partial(m, lambda cols: mm(R[l, m, :, CA : CA + 2 * F], WGU[cols, :], NT))

    def conv_bwd_a(l, m):
        dz = mm(L[l, DO, m], WOUT[...], NT)
        bgate = R[l, m, :, CP : CP + C].astype(f32)
        xin = R[l, m, :, CP + 2 * C : CP + 3 * C].astype(f32)
        EXT[8 : 8 + TOK] = (bgate * xin).astype(bf16).astype(f32)
        dy = dz * R[l, m, :, CP + C : CP + 2 * C].astype(f32)
        DYE[rem(m, 2), 0:TOK] = dy
        dhcopy(l, m).start()
        R[l, m, :, CP + C : CP + 2 * C] = (dz * conv_now(l, m)).astype(bf16)
        for k in range(3):
            prod = dy * EXT[6 + k : 6 + k + TOK]
            CACC[l, k] += jnp.sum(prod.reshape(TOK // 8, 8, C), axis=0)

    def conv_bwd_b(l, m):
        dhcopy(l, m).wait()
        s = rem(m, 2)
        DYE[s, TOK : TOK + 8] = jnp.where(seq == n - 1, 0.0, DHALO[l, m])
        dbx = (
            tap(l, 2) * DYE[s, 0:TOK] + tap(l, 1) * DYE[s, 1 : 1 + TOK] + tap(l, 0) * DYE[s, 2 : 2 + TOK]
        )
        bgate = R[l, m, :, CP : CP + C].astype(f32)
        xin = R[l, m, :, CP + 2 * C : CP + 3 * C].astype(f32)
        R[l, m, :, CP : CP + C] = (dbx * xin).astype(bf16)
        R[l, m, :, CP + 2 * C : CP + 3 * C] = (dbx * bgate).astype(bf16)
        put_partial(m, lambda cols: mm(R[l, m, :, CP : CP + 3 * C], WIN[cols, :], NT))

    lanes = ((GA, (RA0, RA1, RA2)), (GB, (RB0, RB1, RB2)))

    def keep(lane, step):
        b = [bits[o] for o in ORDERS[lane]]
        return [b[0] * 4, b[0] * 4 + b[1] * 2, b[0] * 4 + b[1] * 2 + b[2]][step]

    def sized(t, fn):
        cases(rem(t, PER), [(0, PER - 1, lambda: fn(full)), (PER - 1, PER, lambda: fn(short))])

    def rs_copy(lane, step, t, rows):
        G, recv = lanes[lane]
        slot = rem(t, SLOTS)
        size = 4 >> step
        o = ORDERS[lane][step]
        off = keep(lane, step) + size - 2 * size * bits[o]
        cut = pl.ds(0, rows[1 + lane])
        return remote(
            G.at[slot, pl.ds(off, size), cut], recv[step].at[slot, :, cut],
            rss.at[lane, step, slot], rsr.at[lane, step, slot], parts[o],
        )

    def rs_gen(t):
        l = 1 - div(t, PER)
        v = rem(t, PER)
        fu = F // U
        kind = jnp.where(v < fu, DF, jnp.where(v < 3 * fu, N2, jnp.where(v < PER - 1, N1, DO)))
        slot = rem(t, SLOTS)

        def make(rows):
            wide, cut, _ = rows
            start = v * U if isinstance(v, int) else pl.multiple_of(v * U, 128)
            for m in range(M):
                RT[0:wide, m * TOK : (m + 1) * TOK] = R[l, m, :, pl.ds(start, wide)].T

            def step(j, _):
                src = L[l, kind, :, :, pl.ds(pl.multiple_of(j * 512, 512), 512)].reshape(M * TOK, 512)
                res = mm(RT[0:wide], src).astype(bf16)
                for q in range(4):
                    lo, y = q // 2, q % 2
                    block = res[:, q * 128 : (q + 1) * 128]
                    GA[slot, y * 4 + lo * 2 + j, 0:cut] = block[:cut]
                    GB[slot, lo * 4 + j * 2 + y, 0 : wide - cut] = block[cut:]
                return 0

            lax.fori_loop(0, D // 512, step, 0)
            for lane in range(2):
                rs_copy(lane, 0, t, rows).start()

        sized(t, make)

    def rs_add(step, t):
        slot = rem(t, SLOTS)

        def go(rows):
            for lane in range(2):
                G, recv = lanes[lane]
                rs_copy(lane, step, t, rows).wait()
                base = keep(lane, step)
                cut = rows[1 + lane]

                def add(i, _):
                    G[slot, base + i, 0:cut] = (
                        G[slot, base + i, 0:cut].astype(f32) + recv[step][slot, i, 0:cut].astype(f32)
                    ).astype(bf16)
                    return 0

                lax.fori_loop(0, 4 >> step, add, 0)
                rs_copy(lane, step + 1, t, rows).start()

        sized(t, go)

    def unit_copies(t, which):
        l = 1 - div(t, PER)
        v = rem(t, PER)
        fu = F // U

        def at(first):
            return pl.ds((v - first) * U if isinstance(v, int) else pl.multiple_of((v - first) * U, 128), U)

        pair = div(v - fu, 2) * U
        tile = pl.ds(pair if isinstance(v, int) else pl.multiple_of(pair, 128), U)
        if which == 0:
            pairs = [(FO, out_down.at[l, at(0)])]
        elif which == 1:
            pairs = [(FT, out_gate.at[l, :, tile])]
        elif which == 2:
            pairs = [(FT, out_up.at[l, :, tile])]
        elif which == 3:
            pairs = [(FT.at[:, pl.ds(0, C)], out_in.at[l, 0]),
                     (FT.at[:, pl.ds(C, U - C)], out_in.at[l, 1, :, pl.ds(0, U - C)])]
        elif which == 4:
            pairs = [(FT.at[:, pl.ds(0, 2 * C - U)], out_in.at[l, 1, :, pl.ds(U - C, 2 * C - U)]),
                     (FT.at[:, pl.ds(2 * C - U, C)], out_in.at[l, 2])]
        else:
            pairs = [(FO.at[pl.ds(0, width)], out_out.at[l])]
        return [pltpu.make_async_copy(a, b, fos.at[i]) for i, (a, b) in enumerate(pairs)]

    def by_target(t, fn):
        v = rem(t, PER)
        fu = F // U
        if isinstance(v, int):
            fn(0 if v < fu else 1 + (v - fu) % 2 if v < 3 * fu else 3 + v - 3 * fu)
            return
        cases(v, [(0, fu, functools.partial(fn, 0))])
        for i in range(2):
            pl.when((v >= fu) & (v < 3 * fu) & (lax.rem(v + fu, 2) == i))(functools.partial(fn, 1 + i))
        cases(v, [(3 * fu + i, 3 * fu + i + 1, functools.partial(fn, 3 + i)) for i in range(3)])

    def unit_wait(t):
        def go(which):
            for cp in unit_copies(t, which):
                cp.wait()

        by_target(t, go)

    def rs_last(t):
        slot = rem(t, SLOTS)
        if isinstance(t, int):
            if t >= 1:
                unit_wait(t - 1)
        else:
            pl.when(t >= 1)(lambda: unit_wait(t - 1))

        def go(rows):
            wide, cut, _ = rows
            for lane in range(2):
                rs_copy(lane, 2, t, rows).wait()
            FO[0:cut] = GA[slot, keep(0, 2), 0:cut].astype(f32) + RA2[slot, 0, 0:cut].astype(f32)
            FO[cut:wide] = (
                GB[slot, keep(1, 2), 0 : wide - cut].astype(f32) + RB2[slot, 0, 0 : wide - cut].astype(f32)
            )

        sized(t, go)

        def send(which):
            if which in (1, 2, 3, 4):
                FT[...] = FO[...].T
            for cp in unit_copies(t, which):
                cp.start()

        by_target(t, send)

    def tick_gen(t):
        if not isinstance(t, int) or t < UNITS:
            rs_gen(t)

    def tick_rest(t):
        steps = (functools.partial(rs_add, 0), functools.partial(rs_add, 1), rs_last)
        for lag, fn in enumerate(steps, 1):
            if isinstance(t, int):
                if 0 <= t - lag < UNITS:
                    fn(t - lag)
            else:
                pl.when(t >= lag)(functools.partial(fn, t - lag))

    def behind(prev, cur, m):
        if prev is None:
            pl.when(m > 0)(lambda: mid(m - 1))
        else:
            mid(lax.rem(m + M - 1, M))
            pl.when(m < 2)(lambda: prev(m + M - 2))
        pl.when(m >= 2)(lambda: cur(m - 2))

    def phase(prev, cur, first, second=None, tick=None, ahead=None):
        def step(m, _):
            if ahead is not None:
                ahead(m)
            if tick is not None:
                tick_gen(tick + m)
            if first is not None:
                first(m)
            behind(prev, cur, m)
            if second is not None:
                second(m)
            if tick is not None:
                tick_rest(tick + m)
            return 0

        lax.fori_loop(0, M, step, 0)

    def arrived(copies):
        for cp in copies:
            cp.wait()

    end_o0 = functools.partial(finish_norm, 0, 1, N2)
    end_f0 = functools.partial(finish_norm, 1, 0, N1)
    end_o1 = functools.partial(finish_norm, 1, 1, N2, within=True)
    end_n1 = functools.partial(finish_dn2, 1)
    end_c1 = functools.partial(finish_dn1, 1)
    end_n0 = functools.partial(finish_dn2, 0)
    end_c0 = functools.partial(finish_dn1, 0)

    arrived(load_conv(0))
    for cp in [load_og, load_down(1)] + load_ffn(0):
        cp.start()

    conv_fwd_a(0, jnp.int32(0))

    def o0(m, _):
        conv_fwd_b(0, m)
        pl.when(m < M - 1)(lambda: conv_fwd_a(0, m + 1))
        behind(None, end_o0, m)
        gather_dyn(0, m, 0)

        @pl.when(m == 0)
        def _():
            arrived([load_og, load_down(1)])

        down_back(m)
        gather_dyn(0, m, 1)
        return 0

    lax.fori_loop(0, M, o0, 0)
    for cp in [load_down(0)] + load_conv(1):
        cp.start()
    arrived(load_ffn(0))

    def f0(m, _):
        agcopy(0, N2, m).wait()
        ffn_fwd(0, m)
        pl.when(m == 0)(lambda: load_down(0).wait())
        ffn_down(0, m)
        gather_dyn(2 * M, m, 0)
        behind(end_o0, end_f0, m)
        gather_dyn(2 * M, m, 1)

        @pl.when(m == M - 1)
        def _():
            arrived(load_conv(1) + [tap_copy])
            conv_fwd_a(1, 0)

        return 0

    lax.fori_loop(0, M, f0, 0)
    for cp in load_ffn(1):
        cp.start()

    def ffn_both(m):
        agcopy(1, N2, m).wait()
        ffn_fwd(1, m)

    def o1(m, _):
        pl.when(m == 0)(lambda: mid(M - 1))
        conv_fwd_b(1, m)
        pl.when(m < M - 1)(lambda: conv_fwd_a(1, m + 1))
        end_o1(m)
        pl.when(m == 1)(lambda: arrived(load_ffn(1)))
        pl.when(m >= 1)(lambda: ffn_both(m - 1))
        pl.when(m < 2)(lambda: end_f0(m + 2))
        return 0

    lax.fori_loop(0, M, o1, 0)
    ffn_both(M - 1)
    tick_gen(0)

    def start_c1(m):
        agcopy(1, DO, m).wait()
        conv_bwd_a(1, m)

    def last_only(fn):
        return lambda m: pl.when(m == M - 1)(lambda: fn(0))

    def next_one(fn):
        return lambda m: pl.when(m < M - 1)(lambda: fn(m + 1))

    phase(None, end_n1, lambda m: ffn_bwd(1, m), tick=1, ahead=last_only(start_c1))
    for cp in load_ffn(0):
        cp.start()
    phase(end_n1, end_c1, None, lambda m: conv_bwd_b(1, m), tick=1 + M, ahead=next_one(start_c1))
    for cp in load_conv(0):
        cp.start()
    arrived(load_ffn(0))

    def n0(m):
        ffn_bwd(0, m)

    def n0_tick(m, _):
        pl.when(m == 0)(lambda: agcopy(0, DF, 0).wait())
        pl.when(m == 1)(lambda: agcopy(0, DF, 1).wait())

        @pl.when(m == 2)
        def _():
            agcopy(0, DF, 2).wait()
            agcopy(0, DF, 3).wait()

        tick_gen(1 + 2 * M + m)
        n0(m)
        behind(end_c1, end_n0, m)
        tick_rest(1 + 2 * M + m)
        return 0

    lax.fori_loop(0, M, n0_tick, 0)
    load_down(1).start()
    load_down(1).wait()
    arrived(load_conv(0))

    def f1(m):
        agcopy(0, DO, m).wait()
        ffn_down(1, m)

    def start_c0(m):
        conv_bwd_a(0, m)

    phase(end_n0, finish_stream, f1, tick=1 + 3 * M, ahead=last_only(start_c0))

    def c0(m):
        for cp in stream_copies(m):
            cp.wait()
        conv_bwd_b(0, m)

    phase(finish_stream, end_c0, None, c0, tick=1 + 4 * M, ahead=next_one(start_c0))
    t = 1 + 5 * M
    tick_gen(t)
    mid(M - 1)
    end_c0(M - 2)
    tick_rest(t)
    tick_gen(t + 1)
    end_c0(M - 1)

    for i in range(4):
        SM[i : i + 1] = jnp.sum(GACC[i], axis=0, keepdims=True)
    SM[4:8] = jnp.zeros((4, D), f32)
    for l in range(2):
        for k in range(3):
            SM[4 + l : 5 + l, k * C : (k + 1) * C] = jnp.sum(CACC[l, k], axis=0, keepdims=True)

    def small(i):
        return remote(SM, SMR.at[i], sms.at[i], smr.at[i], [sib, *parts][i])

    small(0).start()
    tick_rest(t + 1)
    t += 2
    for i in range(4):
        tick_gen(t)
        small(i).wait()
        if i == 0:
            SM[0:4] += SMR[0, 0:4]
        else:
            SM[...] += SMR[i]
        if i < 3:
            small(i + 1).start()
        tick_rest(t)
        t += 1
    while t < UNITS + 3:
        tick_gen(t)
        tick_rest(t)
        t += 1
    own = pl.ds(pl.multiple_of(tp * C, 128), C)
    out_norm[...] = SM[0:2, own]
    out_ffn[...] = SM[2:4, own]
    for l in range(2):
        for k in range(3):
            out_conv[k, l : l + 1, :] = SM[4 + l : 5 + l, k * C : (k + 1) * C]
    unit_wait(UNITS - 1)
    for m in range(M):
        for cp in grad_copies(m):
            cp.wait()


def fused_call(stream_in, norm_gain, win, taps, wout, ffn_gain, wgate, wup, wdown, out_grad):
    M, TOK, D = stream_in.shape
    C, F = wout.shape[1], wgate.shape[2]
    U = 384
    rb = U // 6
    ra = U - rb
    half = TOK // 2
    vm = pltpu.VMEM
    dma = pltpu.SemaphoreType.DMA
    S = SLOTS
    anys = pl.BlockSpec(memory_space=pl.ANY)
    vmem = pl.BlockSpec(memory_space=pltpu.VMEM)
    return pl.pallas_call(
        functools.partial(fused, (M, TOK, D, C, F, U)),
        out_shape=[
            jax.ShapeDtypeStruct((M, TOK, D), bf16),
            jax.ShapeDtypeStruct((M, TOK, D), f32),
            jax.ShapeDtypeStruct((LAYERS, C), f32),
            jax.ShapeDtypeStruct((LAYERS, 3, 128, C), f32),
            jax.ShapeDtypeStruct((3, LAYERS, C), f32),
            jax.ShapeDtypeStruct((LAYERS, C, 128), f32),
            jax.ShapeDtypeStruct((LAYERS, C), f32),
            jax.ShapeDtypeStruct((LAYERS, 128, F), f32),
            jax.ShapeDtypeStruct((LAYERS, 128, F), f32),
            jax.ShapeDtypeStruct((LAYERS, F, 128), f32),
        ],
        in_specs=[anys, vmem, anys, vmem, anys, vmem, anys, anys, anys, anys],
        out_specs=[anys, anys, vmem, anys, vmem, anys, vmem, anys, anys, anys],
        scratch_shapes=[
            vm((LAYERS, 4, M, TOK, D), bf16),
            vm((LAYERS, M, TOK, 3 * F + 4 * C), bf16),
            vm((D, 3 * C), bf16),
            vm((C, D), bf16),
            vm((D, 2 * F), bf16),
            vm((F, D), bf16),
            vm((M, half, D), f32),
            vm((M, half, D), f32),
            vm((M, half, 2 * LAYERS), f32),
            vm((M, TOK, D), bf16),
            vm((M, half, D), bf16),
            vm((M, half, D), bf16),
            vm((S, 8, ra, 128), bf16),
            vm((S, 8, rb, 128), bf16),
            vm((S, 4, ra, 128), bf16),
            vm((S, 2, ra, 128), bf16),
            vm((S, 1, ra, 128), bf16),
            vm((S, 4, rb, 128), bf16),
            vm((S, 2, rb, 128), bf16),
            vm((S, 1, rb, 128), bf16),
            vm((U, M * TOK), bf16),
            vm((U, 128), f32),
            vm((128, U), f32),
            vm((8, D), f32),
            vm((TOK + 8, C), f32),
            vm((2, TOK + 8, C), f32),
            vm((TOK, C), f32),
            vm((LAYERS, M, 8, C), f32),
            vm((M, 8, C), f32),
            vm((LAYERS, M, 8, C), f32),
            vm((4, LAYERS, D), f32),
            vm((3, LAYERS, C), f32),
            vm((3, LAYERS, C), f32),
            vm((4, 8, D), f32),
            vm((LAYERS, 3, 8, C), f32),
            vm((4, 8, D), f32),
            dma((16,)),
            dma((M,)), dma((M,)), dma((M,)), dma((M,)), dma((M,)), dma((M,)),
            dma, dma((2,)), dma((2, LAYERS, M)), dma((2,)), dma((M + 1,)), dma((4, 5)), dma((4, 5)),
            dma((2, 3, S)), dma((2, 3, S)),
            dma((2,)), dma((M,)), dma((M,)), dma((M,)), dma((4,)), dma((4,)),
        ],
        name="fused",
        compiler_params=pltpu.CompilerParams(
            collective_id=0, has_side_effects=True, vmem_limit_bytes=VMEM_BYTES
        ),
    )(stream_in, norm_gain, win, taps, wout, ffn_gain, wgate, wup, wdown, out_grad)


def handed_on(*refs):
    count = (len(refs) - 2) // 3
    srcs, dsts, bufs = refs[:count], refs[count : 2 * count], refs[2 * count : 3 * count]
    sin, sout = refs[-2:]
    chunks = [(i, k) for i in range(count) for k in range(srcs[i].shape[0])]
    ins = [pltpu.make_async_copy(srcs[i].at[k], bufs[i].at[k], sin.at[i, k]) for i, k in chunks]
    outs = [pltpu.make_async_copy(bufs[i].at[k], dsts[i].at[k], sout.at[i, k]) for i, k in chunks]
    for cp in ins:
        cp.start()
    for first, second in zip(ins, outs):
        first.wait()
        second.start()
    for cp in outs:
        cp.wait()


def hand_on(arrays):
    anys = pl.BlockSpec(memory_space=pl.ANY)
    most = max(a.shape[0] for a in arrays)
    return pl.pallas_call(
        handed_on,
        out_shape=[jax.ShapeDtypeStruct(a.shape, a.dtype) for a in arrays],
        in_specs=[anys] * len(arrays),
        out_specs=[anys] * len(arrays),
        scratch_shapes=[pltpu.VMEM(a.shape, a.dtype) for a in arrays]
        + [pltpu.SemaphoreType.DMA((len(arrays), most))] * 2,
        name="hand_on",
        compiler_params=pltpu.CompilerParams(vmem_limit_bytes=VMEM_BYTES),
    )(*arrays)


def body_fused(
    stream_in, norm_gain, in_proj, conv_taps, out_proj, ffn_gain, gate_proj, up_proj, down_proj, out_grad
):
    results = fused_call(
        stream_in, norm_gain, jnp.transpose(in_proj, (0, 2, 1, 3)), jnp.transpose(conv_taps, (1, 0, 2)),
        out_proj, ffn_gain, gate_proj, up_proj, down_proj, out_grad,
    )
    (out_stream, out_sgrad, norm_g, in_g, conv_g, out_g, ffn_g, gate_g, up_g, down_g) = hand_on(results)
    in_g = jnp.transpose(in_g, (0, 2, 1, 3))
    conv_g = jnp.transpose(conv_g, (1, 0, 2))
    return (out_stream, out_sgrad, norm_g, in_g, conv_g, out_g, ffn_g, gate_g, up_g, down_g)


def solution(mesh):
    in_specs = (
        P(None, "seq", None),
        P(),
        P(None, None, None, "tp"),
        P(None, None, "tp"),
        P(None, "tp", None),
        P(),
        P(None, None, "tp"),
        P(None, None, "tp"),
        P(None, "tp", None),
        P(None, "seq", None),
    )
    out_specs = (
        P(None, "seq", None),
        P(None, "seq", None),
        P(None, "tp"),
        P(None, "seq", None, "tp"),
        P(None, None, "tp"),
        P(None, "tp", "seq"),
        P(None, "tp"),
        P(None, "seq", "tp"),
        P(None, "seq", "tp"),
        P(None, "tp", "seq"),
    )
    chosen = body_fused if (mesh.shape["seq"], mesh.shape["tp"]) == (8, 4) else body
    return jax.shard_map(chosen, mesh=mesh, in_specs=in_specs, out_specs=out_specs, check_vma=False)
```

```python
import functools

import jax
import jax.numpy as jnp
from jax import lax
from jax.experimental import pallas as pl
from jax.experimental.pallas import tpu as pltpu
from jax.sharding import PartitionSpec as P

LAYERS = 2


EPS = 1e-05


def passed_along(block, axis, distance):
    devices = range(lax.axis_size(axis))
    route = [(i - distance, i) for i in devices if i - distance in devices]
    return lax.ppermute(block, axis, route)


def norm_rate(hidden):
    return lax.rsqrt(jnp.mean(hidden * hidden, axis=-1, keepdims=True) + EPS)


def norm_back(grad_in, gain, normed_val, rate):
    scaled = grad_in * gain
    return rate * (scaled - normed_val * jnp.mean(scaled * normed_val, axis=-1, keepdims=True))


def reduce_weights(grads):
    return (
        lax.psum_scatter(
            grads[0].astype(jnp.bfloat16), "seq", scatter_dimension=1, tiled=True
        ).astype(jnp.float32),
        lax.psum_scatter(
            grads[1].astype(jnp.bfloat16), "seq", scatter_dimension=2, tiled=True
        ).astype(jnp.float32),
        lax.psum_scatter(
            grads[2].astype(jnp.bfloat16), "seq", scatter_dimension=1, tiled=True
        ).astype(jnp.float32),
        lax.psum_scatter(
            grads[3].astype(jnp.bfloat16), "seq", scatter_dimension=1, tiled=True
        ).astype(jnp.float32),
        lax.psum_scatter(
            grads[4].astype(jnp.bfloat16), "seq", scatter_dimension=2, tiled=True
        ).astype(jnp.float32),
    )


def reduce_small(grads):
    return lax.psum((grads[0], grads[1], grads[2]), "seq")


def body(
    stream_in,
    norm_gain,
    in_proj,
    conv_taps,
    out_proj,
    ffn_gain,
    gate_proj,
    up_proj,
    down_proj,
    out_grad,
):
    f32 = jnp.float32
    bf16 = jnp.bfloat16
    width = in_proj.shape[-1]
    offset = lax.axis_index("tp") * width
    hidden = stream_in.astype(f32)
    kept = []
    for layer in range(LAYERS):
        gain_one = norm_gain[layer].astype(f32)
        gain_two = ffn_gain[layer].astype(f32)
        taps = conv_taps[layer].astype(f32)
        rate_one = norm_rate(hidden)
        normed_one = hidden * rate_one
        first = (normed_one * gain_one).astype(bf16)
        proj = jnp.einsum("msd,dkc->mskc", first, in_proj[layer], preferred_element_type=f32)
        bgate = proj[:, :, 0]
        cgate = proj[:, :, 1]
        xinput = proj[:, :, 2]
        mixed = (bgate * xinput).astype(bf16)
        prior = passed_along(mixed[:, -2:], "seq", 1)
        extended = jnp.concatenate([prior, mixed], axis=1).astype(f32)
        conved = (
            taps[0] * extended[:, :-2] + taps[1] * extended[:, 1:-1] + taps[2] * extended[:, 2:]
        )
        gated = (cgate * conved).astype(bf16)
        partial_out = jnp.einsum("msc,cd->msd", gated, out_proj[layer], preferred_element_type=f32)
        middle = hidden + lax.psum(partial_out, "tp")
        rate_two = norm_rate(middle)
        normed_two = middle * rate_two
        second = (normed_two * gain_two).astype(bf16)
        gate_val = jnp.einsum("msd,df->msf", second, gate_proj[layer], preferred_element_type=f32)
        up_val = jnp.einsum("msd,df->msf", second, up_proj[layer], preferred_element_type=f32)
        sigma = jax.nn.sigmoid(gate_val)
        silu_val = gate_val * sigma
        act = (silu_val * up_val).astype(bf16)
        partial_ffn = jnp.einsum("msf,fd->msd", act, down_proj[layer], preferred_element_type=f32)
        kept.append(
            (
                rate_one,
                normed_one,
                first,
                bgate,
                cgate,
                xinput,
                extended,
                conved,
                gated,
                rate_two,
                normed_two,
                second,
                gate_val,
                up_val,
                sigma,
                silu_val,
                act,
            )
        )
        hidden = middle + lax.psum(partial_ffn, "tp")
    grad_h = out_grad.astype(f32)
    collected = [None] * LAYERS
    for layer in reversed(range(LAYERS)):
        (
            rate_one,
            normed_one,
            first,
            bgate,
            cgate,
            xinput,
            extended,
            conved,
            gated,
            rate_two,
            normed_two,
            second,
            gate_val,
            up_val,
            sigma,
            silu_val,
            act,
        ) = kept[layer]
        gain_one = norm_gain[layer].astype(f32)
        gain_two = ffn_gain[layer].astype(f32)
        taps = conv_taps[layer].astype(f32)
        grad_f = grad_h.astype(bf16)
        grad_act = jnp.einsum("msd,fd->msf", grad_f, down_proj[layer], preferred_element_type=f32)
        down_g = jnp.einsum("msf,msd->fd", act, grad_f, preferred_element_type=f32)
        grad_gate = (grad_act * up_val * sigma * (1.0 + gate_val * (1.0 - sigma))).astype(bf16)
        grad_up = (grad_act * silu_val).astype(bf16)
        part_two = jnp.einsum(
            "msf,df->msd", grad_gate, gate_proj[layer], preferred_element_type=f32
        )
        part_two = part_two + jnp.einsum(
            "msf,df->msd", grad_up, up_proj[layer], preferred_element_type=f32
        )
        gate_g = jnp.einsum("msd,msf->df", second, grad_gate, preferred_element_type=f32)
        up_g = jnp.einsum("msd,msf->df", second, grad_up, preferred_element_type=f32)
        grad_two = lax.psum(part_two.astype(jnp.bfloat16), "tp").astype(jnp.float32)
        ffn_gain_g = jnp.sum(grad_two * normed_two, axis=(0, 1))
        grad_mid = grad_h + norm_back(grad_two, gain_two, normed_two, rate_two)
        grad_o = grad_mid.astype(bf16)
        grad_gated = jnp.einsum("msd,cd->msc", grad_o, out_proj[layer], preferred_element_type=f32)
        out_g = jnp.einsum("msc,msd->cd", gated, grad_o, preferred_element_type=f32)
        grad_conv = grad_gated * cgate
        grad_cgate = grad_gated * conved
        after = passed_along(grad_conv[:, :2], "seq", -1)
        grad_ext = jnp.concatenate([grad_conv, after], axis=1)
        grad_mixed = (
            taps[2] * grad_ext[:, :-2] + taps[1] * grad_ext[:, 1:-1] + taps[0] * grad_ext[:, 2:]
        )
        count = grad_conv.shape[1]
        conv_g = jnp.stack(
            [jnp.sum(grad_conv * extended[:, k : k + count], axis=(0, 1)) for k in range(3)], axis=0
        )
        grad_proj = jnp.stack([grad_mixed * xinput, grad_cgate, grad_mixed * bgate], axis=2).astype(
            bf16
        )
        part_one = jnp.einsum(
            "mskc,dkc->msd", grad_proj, in_proj[layer], preferred_element_type=f32
        )
        in_g = jnp.einsum("msd,mskc->dkc", first, grad_proj, preferred_element_type=f32)
        grad_one = lax.psum(part_one.astype(jnp.bfloat16), "tp").astype(jnp.float32)
        norm_gain_g = jnp.sum(grad_one * normed_one, axis=(0, 1))
        grad_h = grad_mid + norm_back(grad_one, gain_one, normed_one, rate_one)
        norm_piece = lax.dynamic_slice_in_dim(norm_gain_g, offset, width)
        ffn_piece = lax.dynamic_slice_in_dim(ffn_gain_g, offset, width)
        small = (norm_piece, conv_g, ffn_piece)
        large = (in_g, out_g, gate_g, up_g, down_g)
        collected[layer] = (small, large)
    norm_stack = jnp.stack([c[0][0] for c in collected], axis=0)
    conv_stack = jnp.stack([c[0][1] for c in collected], axis=0)
    ffn_stack = jnp.stack([c[0][2] for c in collected], axis=0)
    large_stack = tuple((jnp.stack([c[1][i] for c in collected], axis=0) for i in range(5)))
    large_stack = reduce_weights(large_stack)
    norm_stack, conv_stack, ffn_stack = reduce_small((norm_stack, conv_stack, ffn_stack))
    stream_out = hidden.astype(bf16)
    in_grad, out_grad_w, gate_grad, up_grad, down_grad = large_stack
    return (
        stream_out,
        grad_h,
        norm_stack,
        in_grad,
        conv_stack,
        out_grad_w,
        ffn_stack,
        gate_grad,
        up_grad,
        down_grad,
    )


VMEM_BYTES = 64 * 2**20
MESH = pl.DeviceIdType.MESH
f32 = jnp.float32
bf16 = jnp.bfloat16
NN = (((1,), (0,)), ((), ()))
NT = (((1,), (1,)), ((), ()))
ORDERS = ((0, 1, 2), (1, 0, 2))
SLOTS = 4
WIDE = 512
N1, N2, DF, DO = range(4)


def rem(a, b):
    return a % b if isinstance(a, int) else lax.rem(a, b)


def div(a, b):
    return a // b if isinstance(a, int) else lax.div(a, b)


def cases(value, branches):
    for low, high, fn in branches:
        if isinstance(value, int):
            if low <= value < high:
                fn()
        else:
            pl.when((value >= low) & (value < high))(fn)


def mm(lhs, rhs, dims=NN):
    return lax.dot_general(lhs, rhs, dims, preferred_element_type=f32)


def fused(
    dims,
    stream_in, norm_gain, win, taps, wout, ffn_gain, wgate, wup, wdown, out_grad,
    out_stream, out_sgrad, out_norm, out_in, out_conv, out_out, out_ffn, out_gate, out_up, out_down,
    L, R, WIN, WOUT, WGU, WD, H, DH, RATE, PB, PR, XR,
    GA, GB, RA0, RA1, RA2, RB0, RB1, RB2, RT, FO, FT, SM,
    EXT, DYE, CF, HALO, HALO2, DHALO, GAIN, TAPS, TAPS2, GACC, CACC, SMR,
    GAIN_IN, FGAIN_IN, TAPS_IN, NORM_OUT, FFN_OUT, CONV_OUT,
    load_sem, ps, pr, xs, xr, ags, agr, hs, dhs, hr, hs2, hr2, gs, gr, rss, rsr, fos, oss, sts, str_, sms, smr,
):
    M, TOK, D, C, F, U = dims
    half = TOK // 2
    CS, CA, CP, CZ = 0, F, 3 * F, 3 * F + 3 * C
    PER = (CZ + C) // U
    first_units = [(1, 0, 128), (1, 128, U - 128)]
    TURN = PER + 2
    table = first_units + [(1, k * U, U) for k in range(1, PER)] + [(1, PER * U, CZ + C - PER * U)]
    table += [(0, k * U, U) for k in range(PER)]
    table += [(0, k, 128) for k in range(PER * U, CZ + C, 128)]
    UNITS = len(table)
    splits = {w: (w, w - w // 4, w // 4) for w in (128, 256, U)}
    seq = lax.axis_index("seq")
    tp = lax.axis_index("tp")
    n = lax.axis_size("seq")
    core = lax.rem(tp, 2)
    xi = lax.div(tp, 2)
    sib = {"seq": seq, "tp": tp + 1 - 2 * core}
    xpart = {"seq": seq, "tp": tp + 2 - 4 * xi}
    bits = [lax.rem(lax.div(seq, 1 << k), 2) for k in range(3)]
    parts = [{"seq": seq + (1 << k) - 2 * (1 << k) * bits[k], "tp": tp} for k in range(3)]
    nxt = {"seq": lax.rem(seq + 1, n), "tp": tp}
    prv = {"seq": lax.rem(seq + n - 1, n), "tp": tp}
    mine = pl.ds(pl.multiple_of(core * half, half), half)
    theirs = pl.ds(pl.multiple_of((1 - core) * half, half), half)

    def remote(src, dst, ssem, rsem, dev):
        return pltpu.make_async_remote_copy(
            src_ref=src, dst_ref=dst, send_sem=ssem, recv_sem=rsem, device_id=dev, device_id_type=MESH
        )

    def load_stream(m):
        return pltpu.make_async_copy(stream_in.at[m], L.at[0, N1, m], load_sem.at[m])

    def load_conv(l):
        return [
            pltpu.make_async_copy(win.at[l, k], WIN.at[:, pl.ds(k * C, C)], load_sem.at[4 + k])
            for k in range(3)
        ] + [pltpu.make_async_copy(wout.at[l], WOUT, load_sem.at[7])]

    def load_ffn(l):
        return [
            pltpu.make_async_copy(
                src.at[l, :, pl.ds(t * U, U)], WGU.at[:, pl.ds((2 * t + i) * U, U)], load_sem.at[10 + 2 * t + i]
            )
            for t in range(F // U)
            for i, src in enumerate((wgate, wup))
        ]

    def load_down(l):
        return pltpu.make_async_copy(wdown.at[l], WD, load_sem.at[9])

    load_og = pltpu.make_async_copy(out_grad, L.at[1, DF], load_sem.at[8])
    for cp in load_conv(0) + [load_stream(m) for m in range(M)]:
        cp.start()

    barrier = pltpu.get_barrier_semaphore()
    others = [sib, xpart, nxt, prv] + parts
    for dev in others:
        pl.semaphore_signal(barrier, inc=1, device_id=dev, device_id_type=MESH)

    small_in = [
        pltpu.make_async_copy(src, dst, load_sem.at[16 + i])
        for i, (src, dst) in enumerate(((norm_gain, GAIN_IN), (ffn_gain, FGAIN_IN), (taps, TAPS_IN)))
    ]
    for cp in small_in:
        cp.start()
    for cp in small_in:
        cp.wait()
    GAIN[0] = GAIN_IN[...].astype(f32)
    GAIN[1] = FGAIN_IN[...].astype(f32)
    GAIN[2] = 1.0 / GAIN_IN[...].astype(f32)
    GAIN[3] = 1.0 / FGAIN_IN[...].astype(f32)
    TAPS[...] = TAPS_IN[...].astype(f32)
    GACC[...] = jnp.zeros_like(GACC)
    CACC[...] = jnp.zeros_like(CACC)

    pl.semaphore_wait(barrier, len(others))

    zpos, ypos = lax.div(seq, 2), lax.rem(seq, 2)
    zfar, znear = lax.rem(zpos + 2, 4), zpos + 1 - 2 * lax.rem(zpos, 2)
    strip = D // 8

    def piece(s, z):
        rows = pl.ds(pl.multiple_of(ypos * strip, strip), strip)
        if s < 3:
            return L.at[0, DO, 1 + s, rows, pl.ds(pl.multiple_of(z * TOK, TOK), TOK)]
        return L.at[0, DO, 0, pl.ds(pl.multiple_of(ypos * strip + z * (C // 8), 16), C // 8)]

    def gathers(s, step):
        def send(i, src, dst, dev):
            return remote(src, dst, gs.at[s, i], gr.at[s, i], dev)

        if step == 0:
            if s < 3:
                src = win.at[1, s, pl.ds(pl.multiple_of(zpos * TOK + ypos * strip, strip), strip)]
            else:
                src = wout.at[1, pl.ds(pl.multiple_of(ypos * strip + zpos * (C // 8), 16), C // 8)]
            return [send(0, src, piece(s, zpos), xpart)]
        if step == 1:
            return [send(1, piece(s, zpos), piece(s, zpos), parts[2])]
        if step == 2:
            return [send(2 + i, piece(s, z), piece(s, z), parts[1]) for i, z in enumerate((zpos, zfar))]
        half_ref = L.at[0, DO, (1 + s) % 4, pl.ds(pl.multiple_of(ypos * strip, strip), strip)]
        return [send(4, half_ref, half_ref, parts[0])]

    def gather_at(j):
        for s in range(4):
            for step, when in enumerate((s, s + 2, s + 4, 7 + 2 * s)):
                if j == when:
                    for cp in gathers(s, step):
                        cp.wait()
                    if step < 3:
                        for cp in gathers(s, step + 1):
                            cp.start()

    def gather_dyn(base, m, late):
        for i in range(M):
            pl.when(m == i)(functools.partial(gather_at, base + 2 * i + late))

    for s in range(4):
        for cp in gathers(s, 0):
            cp.start()
    tap_copy = remote(TAPS, TAPS2, hs2.at[1], hr2.at[M], xpart)
    tap_copy.start()

    def pcopy(m):
        return remote(PB.at[m, theirs], PR.at[m], ps.at[m], pr.at[m], sib)

    def xcopy(m):
        return remote(PB.at[m, mine], XR.at[m], xs.at[m], xr.at[m], xpart)

    def mid(m):
        pcopy(m).wait()

        def chunk(i, _):
            off = pl.multiple_of(i * 32, 32)
            rows = pl.ds(pl.multiple_of(core * half + off, 32), 32)
            got = PR[m, pl.ds(off, 32)].astype(f32) + PB[m, rows].astype(f32)
            PB[m, rows] = got.astype(bf16)
            return 0

        lax.fori_loop(0, half // 32, chunk, 0)
        xcopy(m).start()

    def agcopy(l, kind, m):
        ref = L.at[l, kind, m, mine]
        return remote(ref, ref, ags.at[m], agr.at[m], sib)

    def rows_loop(m, body, received=XR):
        def chunk(i, _):
            off = pl.multiple_of(i * 32, 32)
            rows = pl.ds(pl.multiple_of(core * half + off, 32), 32)
            total = PB[m, rows].astype(f32) + received[m, pl.ds(off, 32)].astype(f32)
            body(pl.ds(off, 32), rows, total)
            return 0

        lax.fori_loop(0, half // 32, chunk, 0)

    def rate_of(val):
        return lax.rsqrt(jnp.mean(val * val, axis=-1, keepdims=True) + EPS)

    def finish_norm(l, which, kind, m, within=False):
        if within:
            pcopy(m).wait()
        else:
            xcopy(m).wait()
        gain = GAIN[which, l : l + 1, :]

        def body(loc, rows, total):
            hid = H[m, loc] + total
            H[m, loc] = hid
            rate = rate_of(hid)
            RATE[m, loc, 2 * l + which : 2 * l + which + 1] = rate
            L[l, kind, m, rows] = (hid * rate * gain).astype(bf16)

        rows_loop(m, body, PR if within else XR)
        agcopy(l, kind, m).start()

    def stream_copies(m):
        ref = PB.at[m, mine]
        return (
            pltpu.make_async_copy(ref, out_stream.at[m, mine], oss.at[m]),
            remote(ref, out_stream.at[m, mine], sts.at[m], str_.at[m], sib),
        )

    def finish_stream(m):
        xcopy(m).wait()

        def body(loc, rows, total):
            PB[m, rows] = (H[m, loc] + total).astype(bf16)

        rows_loop(m, body)
        for cp in stream_copies(m):
            cp.start()

    def norm_back(l, which, kind, m, emit):
        xcopy(m).wait()
        gain = GAIN[which, l : l + 1, :]
        inv = GAIN[2 + which, l : l + 1, :]

        def body(loc, rows, total):
            nrm = L[l, kind, m, rows].astype(f32) * inv
            prod = total * nrm
            GACC[2 * which + l] += prod[0:8] + prod[8:16] + prod[16:24] + prod[24:32]
            mean = jnp.mean(prod * gain, axis=-1, keepdims=True)
            emit(loc, rows, RATE[m, loc, 2 * l + which : 2 * l + which + 1] * (total * gain - nrm * mean))

        rows_loop(m, body)

    def finish_dn2(l, m):
        def emit(loc, rows, delta):
            prev = L[1, DF, m, rows].astype(f32) if l == 1 else DH[m, loc]
            new = prev + delta
            DH[m, loc] = new
            L[l, DO, m, rows] = new.astype(bf16)

        norm_back(l, 1, N2, m, emit)
        agcopy(l, DO, m).start()

    def finish_dn1(l, m):
        def emit(loc, rows, delta):
            new = DH[m, loc] + delta
            if l == 1:
                DH[m, loc] = new
                L[0, DF, m, rows] = new.astype(bf16)
            else:
                PB[m, rows] = new.astype(bf16)

        norm_back(l, 0, N1, m, emit)
        if l == 1:
            agcopy(0, DF, m).start()
        else:
            for cp in grad_copies(m):
                cp.start()

    def grad_copies(m):
        return (
            pltpu.make_async_copy(PB.at[m, mine], out_sgrad.at[m, mine], oss.at[m]),
            remote(PB.at[m, mine], out_sgrad.at[m, mine], ags.at[m], agr.at[m], sib),
        )

    def put_partial(m, tile):
        def step(j, _):
            cols = pl.ds(pl.multiple_of(j * WIDE, WIDE), WIDE)
            PB[m, :, cols] = tile(cols).astype(bf16)
            return 0

        lax.fori_loop(0, D // WIDE, step, 0)
        pcopy(m).start()

    def halo_rows(m):
        return pl.ds(m * 8 if isinstance(m, int) else pl.multiple_of(m * 8, 8), 8)

    def hcopy(l, m):
        return remote(EXT.at[pl.ds(TOK, 8)], HALO.at[l, halo_rows(m)], hs, hr.at[0, l, m], nxt)

    def dhcopy(l, m):
        return remote(DYE.at[rem(m, 2), pl.ds(0, 8)], DHALO.at[l, m], dhs.at[rem(m, 2)], hr.at[1, l, m], prv)

    def hcopy2(m):
        return remote(DYE.at[1, pl.ds(TOK, 8)], HALO2.at[m], hs2.at[0], hr2.at[m], nxt)

    def tap(l, k):
        return TAPS[k, l : l + 1, :]

    def conv_of(ext, halo, taps_ref, l):
        ext[0:8] = jnp.where(seq == 0, 0.0, halo)
        t = [taps_ref[k, l : l + 1, :] for k in range(3)]
        return t[0] * ext[6 : 6 + TOK] + t[1] * ext[7 : 7 + TOK] + t[2] * ext[8 : 8 + TOK]

    def conv_now(l, m):
        return conv_of(EXT, HALO[l, halo_rows(m)], TAPS, l)

    def other_in(k):
        blocks = [L[0, DO, 1 + k, :, r * TOK : (r + 1) * TOK] for r in range(D // TOK)]
        return jnp.concatenate(blocks, axis=0)

    first_halos = remote(DYE.at[1, pl.ds(0, 8 * M)], HALO.at[0], hs, hr.at[0, 0, 0], nxt)

    def send_first_halos():
        val = jnp.concatenate([L[0, N1, m, TOK - 16 : TOK] for m in range(M)], axis=0).astype(f32)
        p = mm((val * rate_of(val) * GAIN[0, 0:1, :]).astype(bf16), WIN[...])
        bx = (p[:, 0:C] * p[:, 2 * C : 3 * C]).astype(bf16).astype(f32)
        for m in range(M):
            DYE[1, 8 * m : 8 * m + 8] = bx[16 * m + 8 : 16 * m + 16]
        first_halos.start()

    def conv_fwd_a(l, m):
        if l == 0:
            gain = GAIN[0, 0:1, :]
            hid = L[0, N1, m, mine].astype(f32)
            H[m] = hid
            RATE[m, :, 0:1] = rate_of(hid)

            def chunk(i, _):
                rows = pl.ds(pl.multiple_of(i * 32, 32), 32)
                val = L[0, N1, m, rows].astype(f32)
                L[0, N1, m, rows] = (val * rate_of(val) * gain).astype(bf16)
                return 0

            lax.fori_loop(0, TOK // 32, chunk, 0)
        else:
            agcopy(1, N1, m).wait()
        first = L[l, N1, m]
        p = mm(first, WIN[...])
        bgate, cgate, xin = p[:, 0:C], p[:, C : 2 * C], p[:, 2 * C : 3 * C]
        R[l, m, :, CP : CP + 3 * C] = p.astype(bf16)
        EXT[8 : 8 + TOK] = (bgate * xin).astype(bf16).astype(f32)
        DYE[0, 0:TOK] = cgate
        if l == 1:
            hcopy(l, m).start()
            p = mm(first, jnp.concatenate([other_in(k) for k in range(3)], axis=1))
            DYE[1, 8 : 8 + TOK] = (p[:, 0:C] * p[:, 2 * C : 3 * C]).astype(bf16).astype(f32)
            hcopy2(m).start()
            CF[...] = p[:, C : 2 * C]

    def conv_fwd_b(l, m):
        if l == 0:
            pl.when(m == 0)(lambda: first_halos.wait())
        else:
            hcopy(l, m).wait()
        gated = (DYE[0, 0:TOK] * conv_now(l, m)).astype(bf16)
        R[l, m, :, CZ : CZ + C] = gated
        if l == 0:
            put_partial(m, lambda cols: mm(R[l, m, :, CZ : CZ + C], WOUT[:, cols]))
        else:
            hcopy2(m).wait()
            L[0, DF, m, :, 0:C] = (CF[...] * conv_of(DYE.at[1], HALO2[m], TAPS2, l)).astype(bf16)
            put_partial(
                m,
                lambda cols: mm(R[l, m, :, CZ : CZ + C], WOUT[:, cols])
                + mm(L[0, DF, m, :, 0:C], L[0, DO, 0, :, cols]),
            )

    def down_back(m):
        ds = mm(L[1, DF, m], WD[...], NT).astype(bf16)
        for t in range(F // U):
            R[1, m, :, CA + (2 * t + 1) * U : CA + (2 * t + 2) * U] = ds[:, t * U : (t + 1) * U]

    def ffn_fwd(l, m, low=0, high=F // U):
        def step(t, _):
            off = pl.multiple_of(t * U, 128)
            off2 = pl.multiple_of(2 * t * U, 128)
            ab = mm(L[l, N2, m], WGU[:, pl.ds(off2, 2 * U)])
            a, b = ab[:, 0:U], ab[:, U : 2 * U]
            sig = jax.nn.sigmoid(a)
            silu = a * sig
            R[l, m, :, pl.ds(CS + off, U)] = (silu * b).astype(bf16)
            if l == 0:
                R[l, m, :, pl.ds(CA + off2, 2 * U)] = ab.astype(bf16)
            else:
                ds = R[l, m, :, pl.ds(CA + U + off2, U)].astype(f32)
                R[l, m, :, pl.ds(CA + off2, U)] = (ds * b * sig * (1.0 + a * (1.0 - sig))).astype(bf16)
                R[l, m, :, pl.ds(CA + U + off2, U)] = (ds * silu).astype(bf16)
            return 0

        lax.fori_loop(low, high, step, 0)

    def ffn_down(l, m):
        put_partial(m, lambda cols: mm(R[l, m, :, CS : CS + F], WD[:, cols]))

    def ffn_bwd(l, m):
        if l == 0:
            def step(t, _):
                off = pl.multiple_of(t * U, 128)
                off2 = pl.multiple_of(2 * t * U, 128)
                a = R[l, m, :, pl.ds(CA + off2, U)].astype(f32)
                b = R[l, m, :, pl.ds(CA + U + off2, U)].astype(f32)
                sig = jax.nn.sigmoid(a)
                ds = mm(L[l, DF, m], WD[pl.ds(off, U), :], NT)
                R[l, m, :, pl.ds(CA + off2, U)] = (ds * b * sig * (1.0 + a * (1.0 - sig))).astype(bf16)
                R[l, m, :, pl.ds(CA + U + off2, U)] = (ds * a * sig).astype(bf16)
                return 0

            lax.fori_loop(0, F // U, step, 0)
        put_partial(m, lambda cols: mm(R[l, m, :, CA : CA + 2 * F], WGU[cols, :], NT))

    def conv_bwd_a(l, m):
        dz = mm(L[l, DO, m], WOUT[...], NT)
        bgate = R[l, m, :, CP : CP + C].astype(f32)
        xin = R[l, m, :, CP + 2 * C : CP + 3 * C].astype(f32)
        EXT[8 : 8 + TOK] = (bgate * xin).astype(bf16).astype(f32)
        dy = dz * R[l, m, :, CP + C : CP + 2 * C].astype(f32)
        DYE[rem(m, 2), 0:TOK] = dy
        dhcopy(l, m).start()
        R[l, m, :, CP + C : CP + 2 * C] = (dz * conv_now(l, m)).astype(bf16)
        for k in range(3):
            prod = dy * EXT[6 + k : 6 + k + TOK]
            CACC[l, k] += jnp.sum(prod.reshape(TOK // 8, 8, C), axis=0)

    def conv_bwd_b(l, m):
        dhcopy(l, m).wait()
        s = rem(m, 2)
        DYE[s, TOK : TOK + 8] = jnp.where(seq == n - 1, 0.0, DHALO[l, m])
        dbx = (
            tap(l, 2) * DYE[s, 0:TOK] + tap(l, 1) * DYE[s, 1 : 1 + TOK] + tap(l, 0) * DYE[s, 2 : 2 + TOK]
        )
        bgate = R[l, m, :, CP : CP + C].astype(f32)
        xin = R[l, m, :, CP + 2 * C : CP + 3 * C].astype(f32)
        R[l, m, :, CP : CP + C] = (dbx * xin).astype(bf16)
        R[l, m, :, CP + 2 * C : CP + 3 * C] = (dbx * bgate).astype(bf16)
        put_partial(m, lambda cols: mm(R[l, m, :, CP : CP + 3 * C], WIN[cols, :], NT))

    lanes = ((GA, (RA0, RA1, RA2)), (GB, (RB0, RB1, RB2)))

    def keep(lane, step):
        b = [bits[o] for o in ORDERS[lane]]
        return [b[0] * 4, b[0] * 4 + b[1] * 2, b[0] * 4 + b[1] * 2 + b[2]][step]

    def unit_at(t):
        if isinstance(t, int):
            return table[t][:2]
        k = jnp.where(t < TURN, t - 1, t - TURN)
        return jnp.where(t < TURN, 1, 0), jnp.where(t < 2, t * 128, k * U)

    def sized(t, fn):
        if isinstance(t, int):
            fn(splits[table[t][2]])
            return
        pl.when(t == 0)(lambda: fn(splits[128]))
        pl.when((t == 1) | (t == TURN - 1))(lambda: fn(splits[256]))
        pl.when((t > 1) & (t != TURN - 1))(lambda: fn(splits[U]))

    def rs_copy(lane, step, t, rows):
        G, recv = lanes[lane]
        slot = rem(t, SLOTS)
        size = 4 >> step
        o = ORDERS[lane][step]
        off = keep(lane, step) + size - 2 * size * bits[o]
        cut = pl.ds(0, rows[1 + lane])
        return remote(
            G.at[slot, pl.ds(off, size), cut], recv[step].at[slot, :, cut],
            rss.at[lane, step, slot], rsr.at[lane, step, slot], parts[o],
        )

    def rs_gen(t):
        l, start = unit_at(t)
        kind = jnp.where(start < CA, DF, jnp.where(start < CP, N2, jnp.where(start < CZ, N1, DO)))
        slot = rem(t, SLOTS)

        def make(rows):
            wide, cut, _ = rows
            cols = pl.ds(start if isinstance(start, int) else pl.multiple_of(start, 128), wide)
            for m in range(M):
                RT[0:wide, m * TOK : (m + 1) * TOK] = R[l, m, :, cols].T

            def step(j, _):
                src = L[l, kind, :, :, pl.ds(pl.multiple_of(j * 512, 512), 512)].reshape(M * TOK, 512)
                res = mm(RT[0:wide], src).astype(bf16)
                for q in range(4):
                    lo, y = q // 2, q % 2
                    block = res[:, q * 128 : (q + 1) * 128]
                    GA[slot, y * 4 + lo * 2 + j, 0:cut] = block[:cut]
                    GB[slot, lo * 4 + y * 2 + j, 0 : wide - cut] = block[cut:]
                return 0

            lax.fori_loop(0, D // 512, step, 0)
            for lane in range(2):
                rs_copy(lane, 0, t, rows).start()

        sized(t, make)

    def rs_add(step, t):
        slot = rem(t, SLOTS)

        def go(rows):
            for lane in range(2):
                G, recv = lanes[lane]
                rs_copy(lane, step, t, rows).wait()
                base = keep(lane, step)
                cut = rows[1 + lane]

                def add(i, _):
                    G[slot, base + i, 0:cut] = (
                        G[slot, base + i, 0:cut].astype(f32) + recv[step][slot, i, 0:cut].astype(f32)
                    ).astype(bf16)
                    return 0

                lax.fori_loop(0, 4 >> step, add, 0)
                rs_copy(lane, step + 1, t, rows).start()

        sized(t, go)

    def unit_copies(t, which, wide):
        l, start = unit_at(t)

        def at(off):
            return pl.ds(off if isinstance(off, int) else pl.multiple_of(off, 128), wide)

        tile = at(div(start - CA, 2 * U) * U)
        if which == 0:
            pairs = [(FO.at[pl.ds(0, wide)], out_down.at[l, at(start)])]
        elif which == 1:
            pairs = [(FT, out_gate.at[l, :, tile])]
        elif which == 2:
            pairs = [(FT, out_up.at[l, :, tile])]
        elif which == 3:
            pairs = [(FT.at[:, pl.ds(0, C)], out_in.at[l, 0]),
                     (FT.at[:, pl.ds(C, U - C)], out_in.at[l, 1, :, pl.ds(0, U - C)])]
        elif which == 4:
            pairs = [(FT.at[:, pl.ds(0, 2 * C - U)], out_in.at[l, 1, :, pl.ds(U - C, 2 * C - U)]),
                     (FT.at[:, pl.ds(2 * C - U, C)], out_in.at[l, 2])]
        else:
            pairs = [(FO.at[pl.ds(0, wide)], out_out.at[l, at(start - CZ)])]
        return [pltpu.make_async_copy(a, b, fos.at[i]) for i, (a, b) in enumerate(pairs)]

    def by_target(t, fn):
        if isinstance(t, int):
            _, start, wide = table[t]
            if start < CA:
                which = 0
            elif start < CP:
                which = 1 + (start - CA) // U % 2
            else:
                which = 5 if start >= CZ else 3 + (start - CP) // U
            fn(which, wide)
            return
        _, start = unit_at(t)
        pl.when(t == 0)(lambda: fn(0, 128))
        pl.when(t == 1)(lambda: fn(0, 256))
        pl.when((t > 1) & (start < CA))(lambda: fn(0, U))
        for i in range(2):
            odd = lax.rem(lax.div(start, U) + CA // U, 2) == i
            pl.when((start >= CA) & (start < CP) & odd)(functools.partial(fn, 1 + i, U))
            pl.when(start == CP + i * U)(functools.partial(fn, 3 + i, U))
        pl.when(start == CZ)(lambda: fn(5, 256))

    def unit_wait(t):
        def go(which, wide):
            for cp in unit_copies(t, which, wide):
                cp.wait()

        by_target(t, go)

    def rs_last(t):
        slot = rem(t, SLOTS)
        if isinstance(t, int):
            if t >= 1:
                unit_wait(t - 1)
        else:
            pl.when(t >= 1)(lambda: unit_wait(t - 1))

        def go(rows):
            wide, cut, _ = rows
            for lane in range(2):
                rs_copy(lane, 2, t, rows).wait()
            FO[0:cut] = (GA[slot, keep(0, 2), 0:cut].astype(f32) + RA2[slot, 0, 0:cut].astype(f32)).astype(bf16)
            FO[cut:wide] = (
                GB[slot, keep(1, 2), 0 : wide - cut].astype(f32) + RB2[slot, 0, 0 : wide - cut].astype(f32)
            ).astype(bf16)

        sized(t, go)

        def send(which, wide):
            if which in (1, 2, 3, 4):
                FT[...] = FO[...].T
            for cp in unit_copies(t, which, wide):
                cp.start()

        by_target(t, send)

    def tick_gen(t):
        if not isinstance(t, int) or t < UNITS:
            rs_gen(t)

    def tick_rest(t):
        steps = (functools.partial(rs_add, 0), functools.partial(rs_add, 1), rs_last)
        for lag, fn in enumerate(steps, 1):
            if isinstance(t, int):
                if 0 <= t - lag < UNITS:
                    fn(t - lag)
            else:
                pl.when(t >= lag)(functools.partial(fn, t - lag))

    def behind(prev, cur, m):
        if prev is None:
            pl.when(m > 0)(lambda: mid(m - 1))
        else:
            mid(lax.rem(m + M - 1, M))
            pl.when(m < 2)(lambda: prev(m + M - 2))
        pl.when(m >= 2)(lambda: cur(m - 2))

    def phase(prev, cur, first, second=None, tick=None, ahead=None):
        def step(m, _):
            if ahead is not None:
                ahead(m)
            if tick is not None:
                tick_gen(tick + m)
            if first is not None:
                first(m)
            behind(prev, cur, m)
            if second is not None:
                second(m)
            if tick is not None:
                tick_rest(tick + m)
            return 0

        lax.fori_loop(0, M, step, 0)

    def arrived(copies):
        for cp in copies:
            cp.wait()

    end_o0 = functools.partial(finish_norm, 0, 1, N2)
    end_f0 = functools.partial(finish_norm, 1, 0, N1)
    end_o1 = functools.partial(finish_norm, 1, 1, N2, within=True)
    end_n1 = functools.partial(finish_dn2, 1)
    end_c1 = functools.partial(finish_dn1, 1)
    end_n0 = functools.partial(finish_dn2, 0)
    end_c0 = functools.partial(finish_dn1, 0)

    arrived(load_conv(0) + [load_stream(m) for m in range(M)])
    send_first_halos()
    for cp in [load_og, load_down(1)] + load_ffn(0):
        cp.start()

    conv_fwd_a(0, jnp.int32(0))

    def o0(m, _):
        conv_fwd_b(0, m)
        pl.when(m < M - 1)(lambda: conv_fwd_a(0, m + 1))
        behind(None, end_o0, m)
        gather_dyn(0, m, 0)

        @pl.when(m == 0)
        def _():
            arrived([load_og, load_down(1)])

        down_back(m)
        gather_dyn(0, m, 1)
        return 0

    lax.fori_loop(0, M, o0, 0)
    for cp in [load_down(0)] + load_conv(1):
        cp.start()
    arrived(load_ffn(0))

    def f0(m, _):
        agcopy(0, N2, m).wait()
        ffn_fwd(0, m)
        pl.when(m == 0)(lambda: load_down(0).wait())
        ffn_down(0, m)
        gather_dyn(2 * M, m, 0)
        mid(lax.rem(m + M - 1, M))

        @pl.when(m == M - 1)
        def _():
            arrived(load_conv(1) + [tap_copy])
            conv_fwd_a(1, 0)

        pl.when(m < 2)(lambda: end_o0(m + M - 2))
        pl.when(m >= 2)(lambda: end_f0(m - 2))
        gather_dyn(2 * M, m, 1)
        return 0

    lax.fori_loop(0, M, f0, 0)
    for cp in load_ffn(1):
        cp.start()

    def ffn_both(m):
        agcopy(1, N2, m).wait()
        ffn_fwd(1, m)

    def o1(m, _):
        pl.when(m == 0)(lambda: mid(M - 1))
        conv_fwd_b(1, m)
        pl.when(m < M - 1)(lambda: conv_fwd_a(1, m + 1))
        end_o1(m)
        pl.when(m == 1)(lambda: arrived(load_ffn(1)))
        pl.when(m >= 1)(lambda: ffn_both(m - 1))
        pl.when(m < 2)(lambda: end_f0(m + 2))
        return 0

    lax.fori_loop(0, M, o1, 0)
    agcopy(1, N2, M - 1).wait()
    ffn_fwd(1, M - 1, 0, 1)
    tick_gen(0)
    ffn_fwd(1, M - 1, 1)

    def start_c1(m):
        agcopy(1, DO, m).wait()
        conv_bwd_a(1, m)

    def last_only(fn):
        return lambda m: pl.when(m == M - 1)(lambda: fn(0))

    def next_one(fn):
        return lambda m: pl.when(m < M - 1)(lambda: fn(m + 1))

    phase(None, end_n1, lambda m: ffn_bwd(1, m), tick=1, ahead=last_only(start_c1))
    for cp in load_ffn(0):
        cp.start()
    phase(end_n1, end_c1, None, lambda m: conv_bwd_b(1, m), tick=1 + M, ahead=next_one(start_c1))
    for cp in load_conv(0):
        cp.start()
    arrived(load_ffn(0))

    def n0(m):
        ffn_bwd(0, m)

    def n0_tick(m, _):
        pl.when(m == 0)(lambda: agcopy(0, DF, 0).wait())
        pl.when(m == 1)(lambda: agcopy(0, DF, 1).wait())

        @pl.when(m == 2)
        def _():
            agcopy(0, DF, 2).wait()
            agcopy(0, DF, 3).wait()

        tick_gen(1 + 2 * M + m)
        n0(m)
        behind(end_c1, end_n0, m)
        tick_rest(1 + 2 * M + m)
        return 0

    lax.fori_loop(0, M, n0_tick, 0)
    load_down(1).start()
    load_down(1).wait()
    arrived(load_conv(0))

    def f1(m):
        agcopy(0, DO, m).wait()
        ffn_down(1, m)

    def start_c0(m):
        conv_bwd_a(0, m)

    phase(end_n0, finish_stream, f1, tick=1 + 3 * M, ahead=last_only(start_c0))

    def c0(m):
        for cp in stream_copies(m):
            cp.wait()
        conv_bwd_b(0, m)

    phase(finish_stream, end_c0, None, c0, tick=1 + 4 * M, ahead=next_one(start_c0))
    t = 1 + 5 * M
    tick_gen(t)
    mid(M - 1)
    end_c0(M - 2)
    tick_rest(t)
    tick_gen(t + 1)
    end_c0(M - 1)

    for i in range(4):
        SM[i : i + 1] = jnp.sum(GACC[i], axis=0, keepdims=True)
    SM[4:8] = jnp.zeros((4, D), f32)
    for l in range(2):
        for k in range(3):
            SM[4 + l : 5 + l, k * C : (k + 1) * C] = jnp.sum(CACC[l, k], axis=0, keepdims=True)

    def small(i):
        return remote(SM, SMR.at[i], sms.at[i], smr.at[i], [sib, *parts][i])

    small(0).start()
    tick_rest(t + 1)
    t += 2
    for i in range(4):
        tick_gen(t)
        small(i).wait()
        if i == 0:
            SM[0:4] += SMR[0, 0:4]
        else:
            SM[...] += SMR[i]
        if i < 3:
            small(i + 1).start()
        tick_rest(t)
        t += 1
    own = pl.ds(pl.multiple_of(tp * C, 128), C)
    NORM_OUT[...] = SM[0:2, own]
    FFN_OUT[...] = SM[2:4, own]
    for l in range(2):
        for k in range(3):
            CONV_OUT[k, l : l + 1, :] = SM[4 + l : 5 + l, k * C : (k + 1) * C]
    small_out = [
        pltpu.make_async_copy(src, dst, load_sem.at[16 + i])
        for i, (src, dst) in enumerate(((NORM_OUT, out_norm), (FFN_OUT, out_ffn), (CONV_OUT, out_conv)))
    ]
    for cp in small_out:
        cp.start()
    while t < UNITS + 3:
        tick_gen(t)
        tick_rest(t)
        t += 1
    unit_wait(UNITS - 1)
    for cp in small_out:
        cp.wait()
    for m in range(M):
        for cp in grad_copies(m):
            cp.wait()


def fused_call(stream_in, norm_gain, win, taps, wout, ffn_gain, wgate, wup, wdown, out_grad):
    M, TOK, D = stream_in.shape
    C, F = wout.shape[1], wgate.shape[2]
    U = 384
    rb = U // 4
    ra = U - rb
    half = TOK // 2
    vm = pltpu.VMEM
    dma = pltpu.SemaphoreType.DMA
    S = SLOTS
    anys = pl.BlockSpec(memory_space=pl.ANY)
    return pl.pallas_call(
        functools.partial(fused, (M, TOK, D, C, F, U)),
        out_shape=[
            jax.ShapeDtypeStruct((M, TOK, D), bf16),
            jax.ShapeDtypeStruct((M, TOK, D), bf16),
            jax.ShapeDtypeStruct((LAYERS, C), f32),
            jax.ShapeDtypeStruct((LAYERS, 3, 128, C), bf16),
            jax.ShapeDtypeStruct((3, LAYERS, C), f32),
            jax.ShapeDtypeStruct((LAYERS, C, 128), bf16),
            jax.ShapeDtypeStruct((LAYERS, C), f32),
            jax.ShapeDtypeStruct((LAYERS, 128, F), bf16),
            jax.ShapeDtypeStruct((LAYERS, 128, F), bf16),
            jax.ShapeDtypeStruct((LAYERS, F, 128), bf16),
        ],
        in_specs=[anys] * 10,
        out_specs=[anys] * 10,
        scratch_shapes=[
            vm((LAYERS, 4, M, TOK, D), bf16),
            vm((LAYERS, M, TOK, 3 * F + 4 * C), bf16),
            vm((D, 3 * C), bf16),
            vm((C, D), bf16),
            vm((D, 2 * F), bf16),
            vm((F, D), bf16),
            vm((M, half, D), f32),
            vm((M, half, D), f32),
            vm((M, half, 2 * LAYERS), f32),
            vm((M, TOK, D), bf16),
            vm((M, half, D), bf16),
            vm((M, half, D), bf16),
            vm((S, 8, ra, 128), bf16),
            vm((S, 8, rb, 128), bf16),
            vm((S, 4, ra, 128), bf16),
            vm((S, 2, ra, 128), bf16),
            vm((S, 1, ra, 128), bf16),
            vm((S, 4, rb, 128), bf16),
            vm((S, 2, rb, 128), bf16),
            vm((S, 1, rb, 128), bf16),
            vm((U, M * TOK), bf16),
            vm((U, 128), bf16),
            vm((128, U), bf16),
            vm((8, D), f32),
            vm((TOK + 8, C), f32),
            vm((2, TOK + 8, C), f32),
            vm((TOK, C), f32),
            vm((LAYERS, M * 8, C), f32),
            vm((M, 8, C), f32),
            vm((LAYERS, M, 8, C), f32),
            vm((4, LAYERS, D), f32),
            vm((3, LAYERS, C), f32),
            vm((3, LAYERS, C), f32),
            vm((4, 8, D), f32),
            vm((LAYERS, 3, 8, C), f32),
            vm((4, 8, D), f32),
            vm((LAYERS, D), bf16),
            vm((LAYERS, D), bf16),
            vm((3, LAYERS, C), bf16),
            vm((LAYERS, C), f32),
            vm((LAYERS, C), f32),
            vm((3, LAYERS, C), f32),
            dma((19,)),
            dma((M,)), dma((M,)), dma((M,)), dma((M,)), dma((M,)), dma((M,)),
            dma, dma((2,)), dma((2, LAYERS, M)), dma((2,)), dma((M + 1,)), dma((4, 5)), dma((4, 5)),
            dma((2, 3, S)), dma((2, 3, S)),
            dma((2,)), dma((M,)), dma((M,)), dma((M,)), dma((4,)), dma((4,)),
        ],
        name="fused",
        compiler_params=pltpu.CompilerParams(
            collective_id=0, has_side_effects=True, vmem_limit_bytes=VMEM_BYTES
        ),
    )(stream_in, norm_gain, win, taps, wout, ffn_gain, wgate, wup, wdown, out_grad)


def handed_on(kinds, *refs):
    count = len(kinds)
    srcs, dsts, bufs, wides = (refs[k * count : (k + 1) * count] for k in range(4))
    sin, sout = refs[-2:]
    chunks = [(i, k) for i in range(count) for k in range(srcs[i].shape[0])]
    ins = [pltpu.make_async_copy(srcs[i].at[k], bufs[i].at[k], sin.at[i, k]) for i, k in chunks]
    outs = [
        pltpu.make_async_copy((wides if kinds[i] else bufs)[i].at[k], dsts[i].at[k], sout.at[i, k]) for i, k in chunks
    ]
    for cp in ins:
        cp.start()
    for (i, k), first, second in zip(chunks, ins, outs):
        first.wait()
        if kinds[i]:
            ref, wide = bufs[i].at[k], wides[i].at[k]
            rows = 64
            lead = ref.shape[:-2]

            def step(r, _):
                cut = pl.ds(pl.multiple_of(lax.rem(r, ref.shape[-2] // rows) * rows, rows), rows)
                at = (lax.div(r, ref.shape[-2] // rows), cut) if lead else (cut,)
                wide[at] = ref[at].astype(f32)
                return 0

            lax.fori_loop(0, (lead[0] if lead else 1) * ref.shape[-2] // rows, step, 0)
        second.start()
    for cp in outs:
        cp.wait()


def hand_on(arrays, types):
    anys = pl.BlockSpec(memory_space=pl.ANY)
    most = max(a.shape[0] for a in arrays)
    kinds = tuple(a.dtype != t for a, t in zip(arrays, types))
    return pl.pallas_call(
        functools.partial(handed_on, kinds),
        out_shape=[jax.ShapeDtypeStruct(a.shape, t) for a, t in zip(arrays, types)],
        in_specs=[anys] * len(arrays),
        out_specs=[anys] * len(arrays),
        scratch_shapes=[pltpu.VMEM(a.shape, a.dtype) for a in arrays]
        + [pltpu.VMEM(a.shape if k else (8, 128), f32) for a, k in zip(arrays, kinds)]
        + [pltpu.SemaphoreType.DMA((len(arrays), most))] * 2,
        name="hand_on",
        compiler_params=pltpu.CompilerParams(vmem_limit_bytes=VMEM_BYTES),
    )(*arrays)


def body_fused(
    stream_in, norm_gain, in_proj, conv_taps, out_proj, ffn_gain, gate_proj, up_proj, down_proj, out_grad
):
    results = fused_call(
        stream_in, norm_gain, jnp.transpose(in_proj, (0, 2, 1, 3)), jnp.transpose(conv_taps, (1, 0, 2)),
        out_proj, ffn_gain, gate_proj, up_proj, down_proj, out_grad,
    )
    (out_stream, out_sgrad, norm_g, in_g, conv_g, out_g, ffn_g, gate_g, up_g, down_g) = hand_on(
        results, [bf16] + [f32] * 9
    )
    in_g = jnp.transpose(in_g, (0, 2, 1, 3))
    conv_g = jnp.transpose(conv_g, (1, 0, 2))
    return (out_stream, out_sgrad, norm_g, in_g, conv_g, out_g, ffn_g, gate_g, up_g, down_g)


def solution(mesh):
    in_specs = (
        P(None, "seq", None),
        P(),
        P(None, None, None, "tp"),
        P(None, None, "tp"),
        P(None, "tp", None),
        P(),
        P(None, None, "tp"),
        P(None, None, "tp"),
        P(None, "tp", None),
        P(None, "seq", None),
    )
    out_specs = (
        P(None, "seq", None),
        P(None, "seq", None),
        P(None, "tp"),
        P(None, "seq", None, "tp"),
        P(None, None, "tp"),
        P(None, "tp", "seq"),
        P(None, "tp"),
        P(None, "seq", "tp"),
        P(None, "seq", "tp"),
        P(None, "tp", "seq"),
    )
    chosen = body_fused if (mesh.shape["seq"], mesh.shape["tp"]) == (8, 4) else body
    return jax.shard_map(chosen, mesh=mesh, in_specs=in_specs, out_specs=out_specs, check_vma=False)
```

```python
import functools

import jax
import jax.numpy as jnp
from jax import lax
from jax.experimental import pallas as pl
from jax.experimental.pallas import tpu as pltpu
from jax.sharding import PartitionSpec as P

LAYERS = 2


EPS = 1e-05


def passed_along(block, axis, distance):
    devices = range(lax.axis_size(axis))
    route = [(i - distance, i) for i in devices if i - distance in devices]
    return lax.ppermute(block, axis, route)


def norm_rate(hidden):
    return lax.rsqrt(jnp.mean(hidden * hidden, axis=-1, keepdims=True) + EPS)


def norm_back(grad_in, gain, normed_val, rate):
    scaled = grad_in * gain
    return rate * (scaled - normed_val * jnp.mean(scaled * normed_val, axis=-1, keepdims=True))


def reduce_weights(grads):
    return (
        lax.psum_scatter(
            grads[0].astype(jnp.bfloat16), "seq", scatter_dimension=1, tiled=True
        ).astype(jnp.float32),
        lax.psum_scatter(
            grads[1].astype(jnp.bfloat16), "seq", scatter_dimension=2, tiled=True
        ).astype(jnp.float32),
        lax.psum_scatter(
            grads[2].astype(jnp.bfloat16), "seq", scatter_dimension=1, tiled=True
        ).astype(jnp.float32),
        lax.psum_scatter(
            grads[3].astype(jnp.bfloat16), "seq", scatter_dimension=1, tiled=True
        ).astype(jnp.float32),
        lax.psum_scatter(
            grads[4].astype(jnp.bfloat16), "seq", scatter_dimension=2, tiled=True
        ).astype(jnp.float32),
    )


def reduce_small(grads):
    return lax.psum((grads[0], grads[1], grads[2]), "seq")


def body(
    stream_in,
    norm_gain,
    in_proj,
    conv_taps,
    out_proj,
    ffn_gain,
    gate_proj,
    up_proj,
    down_proj,
    out_grad,
):
    f32 = jnp.float32
    bf16 = jnp.bfloat16
    width = in_proj.shape[-1]
    offset = lax.axis_index("tp") * width
    hidden = stream_in.astype(f32)
    kept = []
    for layer in range(LAYERS):
        gain_one = norm_gain[layer].astype(f32)
        gain_two = ffn_gain[layer].astype(f32)
        taps = conv_taps[layer].astype(f32)
        rate_one = norm_rate(hidden)
        normed_one = hidden * rate_one
        first = (normed_one * gain_one).astype(bf16)
        proj = jnp.einsum("msd,dkc->mskc", first, in_proj[layer], preferred_element_type=f32)
        bgate = proj[:, :, 0]
        cgate = proj[:, :, 1]
        xinput = proj[:, :, 2]
        mixed = (bgate * xinput).astype(bf16)
        prior = passed_along(mixed[:, -2:], "seq", 1)
        extended = jnp.concatenate([prior, mixed], axis=1).astype(f32)
        conved = (
            taps[0] * extended[:, :-2] + taps[1] * extended[:, 1:-1] + taps[2] * extended[:, 2:]
        )
        gated = (cgate * conved).astype(bf16)
        partial_out = jnp.einsum("msc,cd->msd", gated, out_proj[layer], preferred_element_type=f32)
        middle = hidden + lax.psum(partial_out, "tp")
        rate_two = norm_rate(middle)
        normed_two = middle * rate_two
        second = (normed_two * gain_two).astype(bf16)
        gate_val = jnp.einsum("msd,df->msf", second, gate_proj[layer], preferred_element_type=f32)
        up_val = jnp.einsum("msd,df->msf", second, up_proj[layer], preferred_element_type=f32)
        sigma = jax.nn.sigmoid(gate_val)
        silu_val = gate_val * sigma
        act = (silu_val * up_val).astype(bf16)
        partial_ffn = jnp.einsum("msf,fd->msd", act, down_proj[layer], preferred_element_type=f32)
        kept.append(
            (
                rate_one,
                normed_one,
                first,
                bgate,
                cgate,
                xinput,
                extended,
                conved,
                gated,
                rate_two,
                normed_two,
                second,
                gate_val,
                up_val,
                sigma,
                silu_val,
                act,
            )
        )
        hidden = middle + lax.psum(partial_ffn, "tp")
    grad_h = out_grad.astype(f32)
    collected = [None] * LAYERS
    for layer in reversed(range(LAYERS)):
        (
            rate_one,
            normed_one,
            first,
            bgate,
            cgate,
            xinput,
            extended,
            conved,
            gated,
            rate_two,
            normed_two,
            second,
            gate_val,
            up_val,
            sigma,
            silu_val,
            act,
        ) = kept[layer]
        gain_one = norm_gain[layer].astype(f32)
        gain_two = ffn_gain[layer].astype(f32)
        taps = conv_taps[layer].astype(f32)
        grad_f = grad_h.astype(bf16)
        grad_act = jnp.einsum("msd,fd->msf", grad_f, down_proj[layer], preferred_element_type=f32)
        down_g = jnp.einsum("msf,msd->fd", act, grad_f, preferred_element_type=f32)
        grad_gate = (grad_act * up_val * sigma * (1.0 + gate_val * (1.0 - sigma))).astype(bf16)
        grad_up = (grad_act * silu_val).astype(bf16)
        part_two = jnp.einsum(
            "msf,df->msd", grad_gate, gate_proj[layer], preferred_element_type=f32
        )
        part_two = part_two + jnp.einsum(
            "msf,df->msd", grad_up, up_proj[layer], preferred_element_type=f32
        )
        gate_g = jnp.einsum("msd,msf->df", second, grad_gate, preferred_element_type=f32)
        up_g = jnp.einsum("msd,msf->df", second, grad_up, preferred_element_type=f32)
        grad_two = lax.psum(part_two.astype(jnp.bfloat16), "tp").astype(jnp.float32)
        ffn_gain_g = jnp.sum(grad_two * normed_two, axis=(0, 1))
        grad_mid = grad_h + norm_back(grad_two, gain_two, normed_two, rate_two)
        grad_o = grad_mid.astype(bf16)
        grad_gated = jnp.einsum("msd,cd->msc", grad_o, out_proj[layer], preferred_element_type=f32)
        out_g = jnp.einsum("msc,msd->cd", gated, grad_o, preferred_element_type=f32)
        grad_conv = grad_gated * cgate
        grad_cgate = grad_gated * conved
        after = passed_along(grad_conv[:, :2], "seq", -1)
        grad_ext = jnp.concatenate([grad_conv, after], axis=1)
        grad_mixed = (
            taps[2] * grad_ext[:, :-2] + taps[1] * grad_ext[:, 1:-1] + taps[0] * grad_ext[:, 2:]
        )
        count = grad_conv.shape[1]
        conv_g = jnp.stack(
            [jnp.sum(grad_conv * extended[:, k : k + count], axis=(0, 1)) for k in range(3)], axis=0
        )
        grad_proj = jnp.stack([grad_mixed * xinput, grad_cgate, grad_mixed * bgate], axis=2).astype(
            bf16
        )
        part_one = jnp.einsum(
            "mskc,dkc->msd", grad_proj, in_proj[layer], preferred_element_type=f32
        )
        in_g = jnp.einsum("msd,mskc->dkc", first, grad_proj, preferred_element_type=f32)
        grad_one = lax.psum(part_one.astype(jnp.bfloat16), "tp").astype(jnp.float32)
        norm_gain_g = jnp.sum(grad_one * normed_one, axis=(0, 1))
        grad_h = grad_mid + norm_back(grad_one, gain_one, normed_one, rate_one)
        norm_piece = lax.dynamic_slice_in_dim(norm_gain_g, offset, width)
        ffn_piece = lax.dynamic_slice_in_dim(ffn_gain_g, offset, width)
        small = (norm_piece, conv_g, ffn_piece)
        large = (in_g, out_g, gate_g, up_g, down_g)
        collected[layer] = (small, large)
    norm_stack = jnp.stack([c[0][0] for c in collected], axis=0)
    conv_stack = jnp.stack([c[0][1] for c in collected], axis=0)
    ffn_stack = jnp.stack([c[0][2] for c in collected], axis=0)
    large_stack = tuple((jnp.stack([c[1][i] for c in collected], axis=0) for i in range(5)))
    large_stack = reduce_weights(large_stack)
    norm_stack, conv_stack, ffn_stack = reduce_small((norm_stack, conv_stack, ffn_stack))
    stream_out = hidden.astype(bf16)
    in_grad, out_grad_w, gate_grad, up_grad, down_grad = large_stack
    return (
        stream_out,
        grad_h,
        norm_stack,
        in_grad,
        conv_stack,
        out_grad_w,
        ffn_stack,
        gate_grad,
        up_grad,
        down_grad,
    )


VMEM_BYTES = 64 * 2**20
MESH = pl.DeviceIdType.MESH
f32 = jnp.float32
bf16 = jnp.bfloat16
NN = (((1,), (0,)), ((), ()))
NT = (((1,), (1,)), ((), ()))
ORDERS = ((0, 1, 2), (1, 0, 2))
SLOTS = 4
WIDE = 1024
N1, N2, DF, DO = range(4)


def rem(a, b):
    return a % b if isinstance(a, int) else lax.rem(a, b)


def div(a, b):
    return a // b if isinstance(a, int) else lax.div(a, b)


def cases(value, branches):
    for low, high, fn in branches:
        if isinstance(value, int):
            if low <= value < high:
                fn()
        else:
            pl.when((value >= low) & (value < high))(fn)


def mm(lhs, rhs, dims=NN):
    return lax.dot_general(lhs, rhs, dims, preferred_element_type=f32)


def fused(
    dims,
    stream_in, norm_gain, win, taps, wout, ffn_gain, wgate, wup, wdown, out_grad,
    out_stream, out_sgrad, out_norm, out_in, out_conv, out_out, out_ffn, out_gate, out_up, out_down,
    L, R, WIN, WOUT, WGU, WD, H, DH, RATE, PB, PR, XR,
    GA, GB, RA0, RA1, RA2, RB0, RB1, RB2, RT, FO, FT, SM,
    EXT, DYE, CF, HALO, HALO2, DHALO, GAIN, TAPS, TAPS2, GACC, CACC, SMR,
    GAIN_IN, FGAIN_IN, TAPS_IN, NORM_OUT, FFN_OUT, CONV_OUT,
    load_sem, ps, pr, xs, xr, ags, agr, hs, dhs, hr, hs2, hr2, gs, gr, rss, rsr, fos, oss, sts, str_, sms, smr,
):
    M, TOK, D, C, F, U = dims
    half = TOK // 2
    CS, CA, CP, CZ = 0, F, 3 * F, 3 * F + 3 * C
    PER = (CZ + C) // U
    first_units = [(1, 0, 128), (1, 128, U - 128)]
    TURN = PER + 2
    table = first_units + [(1, k * U, U) for k in range(1, PER)] + [(1, PER * U, CZ + C - PER * U)]
    table += [(0, k * U, U) for k in range(PER)]
    table += [(0, k, 128) for k in range(PER * U, CZ + C, 128)]
    UNITS = len(table)
    splits = {w: (w, w - w // 4, w // 4) for w in (128, 256, U)}
    seq = lax.axis_index("seq")
    tp = lax.axis_index("tp")
    n = lax.axis_size("seq")
    core = lax.rem(tp, 2)
    xi = lax.div(tp, 2)
    sib = {"seq": seq, "tp": tp + 1 - 2 * core}
    xpart = {"seq": seq, "tp": tp + 2 - 4 * xi}
    bits = [lax.rem(lax.div(seq, 1 << k), 2) for k in range(3)]
    parts = [{"seq": seq + (1 << k) - 2 * (1 << k) * bits[k], "tp": tp} for k in range(3)]
    nxt = {"seq": lax.rem(seq + 1, n), "tp": tp}
    prv = {"seq": lax.rem(seq + n - 1, n), "tp": tp}
    mine = pl.ds(pl.multiple_of(core * half, half), half)
    theirs = pl.ds(pl.multiple_of((1 - core) * half, half), half)

    def remote(src, dst, ssem, rsem, dev):
        return pltpu.make_async_remote_copy(
            src_ref=src, dst_ref=dst, send_sem=ssem, recv_sem=rsem, device_id=dev, device_id_type=MESH
        )

    def load_stream(m):
        return pltpu.make_async_copy(stream_in.at[m], L.at[0, N1, m], load_sem.at[m])

    def load_conv(l):
        return [
            pltpu.make_async_copy(win.at[l, k], WIN.at[:, pl.ds(k * C, C)], load_sem.at[4 + k])
            for k in range(3)
        ] + [pltpu.make_async_copy(wout.at[l], WOUT, load_sem.at[7])]

    def load_ffn(l):
        return [
            pltpu.make_async_copy(
                src.at[l, :, pl.ds(t * U, U)], WGU.at[:, pl.ds((2 * t + i) * U, U)], load_sem.at[10 + 2 * t + i]
            )
            for t in range(F // U)
            for i, src in enumerate((wgate, wup))
        ]

    def load_down(l):
        return pltpu.make_async_copy(wdown.at[l], WD, load_sem.at[9])

    load_og = pltpu.make_async_copy(out_grad, L.at[1, DF], load_sem.at[8])
    for cp in load_conv(0) + [load_stream(m) for m in range(M)]:
        cp.start()

    barrier = pltpu.get_barrier_semaphore()
    others = [sib, xpart, nxt, prv] + parts
    for dev in others:
        pl.semaphore_signal(barrier, inc=1, device_id=dev, device_id_type=MESH)

    small_in = [
        pltpu.make_async_copy(src, dst, load_sem.at[16 + i])
        for i, (src, dst) in enumerate(((norm_gain, GAIN_IN), (ffn_gain, FGAIN_IN), (taps, TAPS_IN)))
    ]
    for cp in small_in:
        cp.start()
    for cp in small_in:
        cp.wait()
    GAIN[0] = GAIN_IN[...].astype(f32)
    GAIN[1] = FGAIN_IN[...].astype(f32)
    GAIN[2] = 1.0 / GAIN_IN[...].astype(f32)
    GAIN[3] = 1.0 / FGAIN_IN[...].astype(f32)
    TAPS[...] = TAPS_IN[...].astype(f32)
    GACC[...] = jnp.zeros_like(GACC)
    CACC[...] = jnp.zeros_like(CACC)

    pl.semaphore_wait(barrier, len(others))

    zpos, ypos = lax.div(seq, 2), lax.rem(seq, 2)
    zfar, znear = lax.rem(zpos + 2, 4), zpos + 1 - 2 * lax.rem(zpos, 2)
    strip = D // 8

    def piece(s, z):
        rows = pl.ds(pl.multiple_of(ypos * strip, strip), strip)
        if s < 3:
            return L.at[0, DO, 1 + s, rows, pl.ds(pl.multiple_of(z * TOK, TOK), TOK)]
        return L.at[0, DO, 0, pl.ds(pl.multiple_of(ypos * strip + z * (C // 8), 16), C // 8)]

    def gathers(s, step):
        def send(i, src, dst, dev):
            return remote(src, dst, gs.at[s, i], gr.at[s, i], dev)

        if step == 0:
            if s < 3:
                src = win.at[1, s, pl.ds(pl.multiple_of(zpos * TOK + ypos * strip, strip), strip)]
            else:
                src = wout.at[1, pl.ds(pl.multiple_of(ypos * strip + zpos * (C // 8), 16), C // 8)]
            return [send(0, src, piece(s, zpos), xpart)]
        if step == 1:
            return [send(1, piece(s, zpos), piece(s, zpos), parts[2])]
        if step == 2:
            return [send(2 + i, piece(s, z), piece(s, z), parts[1]) for i, z in enumerate((zpos, zfar))]
        half_ref = L.at[0, DO, (1 + s) % 4, pl.ds(pl.multiple_of(ypos * strip, strip), strip)]
        return [send(4, half_ref, half_ref, parts[0])]

    def gather_at(j):
        for s in range(4):
            for step, when in enumerate((s, s + 2, s + 4, 7 + 2 * s)):
                if j == when:
                    for cp in gathers(s, step):
                        cp.wait()
                    if step < 3:
                        for cp in gathers(s, step + 1):
                            cp.start()

    def gather_dyn(base, m, late):
        for i in range(M):
            pl.when(m == i)(functools.partial(gather_at, base + 2 * i + late))

    for s in range(4):
        for cp in gathers(s, 0):
            cp.start()
    tap_copy = remote(TAPS, TAPS2, hs2.at[1], hr2.at[M], xpart)
    tap_copy.start()

    def pcopy(m):
        return remote(PB.at[m, theirs], PR.at[m], ps.at[m], pr.at[m], sib)

    def xcopy(m):
        return remote(PB.at[m, mine], XR.at[m], xs.at[m], xr.at[m], xpart)

    def mid(m):
        pcopy(m).wait()

        def chunk(i, _):
            off = pl.multiple_of(i * 32, 32)
            rows = pl.ds(pl.multiple_of(core * half + off, 32), 32)
            got = PR[m, pl.ds(off, 32)].astype(f32) + PB[m, rows].astype(f32)
            PB[m, rows] = got.astype(bf16)
            return 0

        lax.fori_loop(0, half // 32, chunk, 0, unroll=True)
        xcopy(m).start()

    def agcopy(l, kind, m):
        ref = L.at[l, kind, m, mine]
        return remote(ref, ref, ags.at[m], agr.at[m], sib)

    def rows_loop(m, body, received=XR):
        def chunk(i, _):
            off = pl.multiple_of(i * 32, 32)
            rows = pl.ds(pl.multiple_of(core * half + off, 32), 32)
            total = PB[m, rows].astype(f32) + received[m, pl.ds(off, 32)].astype(f32)
            body(pl.ds(off, 32), rows, total)
            return 0

        lax.fori_loop(0, half // 32, chunk, 0, unroll=True)

    def rate_of(val):
        return lax.rsqrt(jnp.mean(val * val, axis=-1, keepdims=True) + EPS)

    def finish_norm(l, which, kind, m, within=False):
        if within:
            pcopy(m).wait()
        else:
            xcopy(m).wait()
        gain = GAIN[which, l : l + 1, :]

        def body(loc, rows, total):
            hid = H[m, loc] + total
            H[m, loc] = hid
            rate = rate_of(hid)
            RATE[m, loc, 2 * l + which : 2 * l + which + 1] = rate
            L[l, kind, m, rows] = (hid * rate * gain).astype(bf16)

        rows_loop(m, body, PR if within else XR)
        agcopy(l, kind, m).start()

    def stream_copies(m):
        ref = PB.at[m, mine]
        return (
            pltpu.make_async_copy(ref, out_stream.at[m, mine], oss.at[m]),
            remote(ref, out_stream.at[m, mine], sts.at[m], str_.at[m], sib),
        )

    def finish_stream(m):
        xcopy(m).wait()

        def body(loc, rows, total):
            PB[m, rows] = (H[m, loc] + total).astype(bf16)

        rows_loop(m, body)
        for cp in stream_copies(m):
            cp.start()

    def norm_back(l, which, kind, m, emit):
        xcopy(m).wait()
        gain = GAIN[which, l : l + 1, :]
        inv = GAIN[2 + which, l : l + 1, :]

        def body(loc, rows, total):
            nrm = L[l, kind, m, rows].astype(f32) * inv
            prod = total * nrm
            GACC[2 * which + l] += prod[0:8] + prod[8:16] + prod[16:24] + prod[24:32]
            mean = jnp.mean(prod * gain, axis=-1, keepdims=True)
            emit(loc, rows, RATE[m, loc, 2 * l + which : 2 * l + which + 1] * (total * gain - nrm * mean))

        rows_loop(m, body)

    def finish_dn2(l, m):
        def emit(loc, rows, delta):
            prev = L[1, DF, m, rows].astype(f32) if l == 1 else DH[m, loc]
            new = prev + delta
            DH[m, loc] = new
            L[l, DO, m, rows] = new.astype(bf16)

        norm_back(l, 1, N2, m, emit)
        agcopy(l, DO, m).start()

    def finish_dn1(l, m):
        def emit(loc, rows, delta):
            new = DH[m, loc] + delta
            if l == 1:
                DH[m, loc] = new
                L[0, DF, m, rows] = new.astype(bf16)
            else:
                PB[m, rows] = new.astype(bf16)

        norm_back(l, 0, N1, m, emit)
        if l == 1:
            agcopy(0, DF, m).start()
        else:
            for cp in grad_copies(m):
                cp.start()

    def grad_copies(m):
        return (
            pltpu.make_async_copy(PB.at[m, mine], out_sgrad.at[m, mine], oss.at[m]),
            remote(PB.at[m, mine], out_sgrad.at[m, mine], ags.at[m], agr.at[m], sib),
        )

    def put_partial(m, tile):
        def step(j, _):
            cols = pl.ds(pl.multiple_of(j * WIDE, WIDE), WIDE)
            PB[m, :, cols] = tile(cols).astype(bf16)
            return 0

        lax.fori_loop(0, D // WIDE, step, 0)
        pcopy(m).start()

    def halo_rows(m):
        return pl.ds(m * 8 if isinstance(m, int) else pl.multiple_of(m * 8, 8), 8)

    def hcopy(l, m):
        return remote(EXT.at[pl.ds(TOK, 8)], HALO.at[l, halo_rows(m)], hs, hr.at[0, l, m], nxt)

    def dhcopy(l, m):
        return remote(DYE.at[rem(m, 2), pl.ds(0, 8)], DHALO.at[l, m], dhs.at[rem(m, 2)], hr.at[1, l, m], prv)

    def hcopy2(m):
        return remote(DYE.at[1, pl.ds(TOK, 8)], HALO2.at[m], hs2.at[0], hr2.at[m], nxt)

    def tap(l, k):
        return TAPS[k, l : l + 1, :]

    def conv_of(ext, halo, taps_ref, l):
        ext[0:8] = jnp.where(seq == 0, 0.0, halo)
        t = [taps_ref[k, l : l + 1, :] for k in range(3)]
        return t[0] * ext[6 : 6 + TOK] + t[1] * ext[7 : 7 + TOK] + t[2] * ext[8 : 8 + TOK]

    def conv_now(l, m):
        return conv_of(EXT, HALO[l, halo_rows(m)], TAPS, l)

    def other_in(k):
        blocks = [L[0, DO, 1 + k, :, r * TOK : (r + 1) * TOK] for r in range(D // TOK)]
        return jnp.concatenate(blocks, axis=0)

    first_halos = remote(DYE.at[1, pl.ds(0, 8 * M)], HALO.at[0], hs, hr.at[0, 0, 0], nxt)

    def send_first_halos():
        val = jnp.concatenate([L[0, N1, m, TOK - 16 : TOK] for m in range(M)], axis=0).astype(f32)
        p = mm((val * rate_of(val) * GAIN[0, 0:1, :]).astype(bf16), WIN[...])
        bx = (p[:, 0:C] * p[:, 2 * C : 3 * C]).astype(bf16).astype(f32)
        for m in range(M):
            DYE[1, 8 * m : 8 * m + 8] = bx[16 * m + 8 : 16 * m + 16]
        first_halos.start()

    def conv_fwd_a(l, m):
        if l == 0:
            gain = GAIN[0, 0:1, :]
            hid = L[0, N1, m, mine].astype(f32)
            H[m] = hid
            RATE[m, :, 0:1] = rate_of(hid)

            def chunk(i, _):
                rows = pl.ds(pl.multiple_of(i * 32, 32), 32)
                val = L[0, N1, m, rows].astype(f32)
                L[0, N1, m, rows] = (val * rate_of(val) * gain).astype(bf16)
                return 0

            lax.fori_loop(0, TOK // 32, chunk, 0)
        else:
            agcopy(1, N1, m).wait()
        first = L[l, N1, m]
        p = mm(first, WIN[...])
        bgate, cgate, xin = p[:, 0:C], p[:, C : 2 * C], p[:, 2 * C : 3 * C]
        R[l, m, :, CP : CP + 3 * C] = p.astype(bf16)
        EXT[8 : 8 + TOK] = (bgate * xin).astype(bf16).astype(f32)
        DYE[0, 0:TOK] = cgate
        if l == 1:
            hcopy(l, m).start()
            p = mm(first, jnp.concatenate([other_in(k) for k in range(3)], axis=1))
            DYE[1, 8 : 8 + TOK] = (p[:, 0:C] * p[:, 2 * C : 3 * C]).astype(bf16).astype(f32)
            hcopy2(m).start()
            CF[...] = p[:, C : 2 * C]

    def conv_fwd_b(l, m):
        if l == 0:
            pl.when(m == 0)(lambda: first_halos.wait())
        else:
            hcopy(l, m).wait()
        gated = (DYE[0, 0:TOK] * conv_now(l, m)).astype(bf16)
        R[l, m, :, CZ : CZ + C] = gated
        if l == 0:
            put_partial(m, lambda cols: mm(R[l, m, :, CZ : CZ + C], WOUT[:, cols]))
        else:
            hcopy2(m).wait()
            L[0, DF, m, :, 0:C] = (CF[...] * conv_of(DYE.at[1], HALO2[m], TAPS2, l)).astype(bf16)
            put_partial(
                m,
                lambda cols: mm(R[l, m, :, CZ : CZ + C], WOUT[:, cols])
                + mm(L[0, DF, m, :, 0:C], L[0, DO, 0, :, cols]),
            )

    def down_back(m):
        ds = mm(L[1, DF, m], WD[...], NT).astype(bf16)
        for t in range(F // U):
            R[1, m, :, CA + (2 * t + 1) * U : CA + (2 * t + 2) * U] = ds[:, t * U : (t + 1) * U]

    def ffn_fwd(l, m, low=0, high=F // U):
        def step(t):
            off, off2 = t * U, 2 * t * U
            ab = mm(L[l, N2, m], WGU[:, pl.ds(off2, 2 * U)])
            a, b = ab[:, 0:U], ab[:, U : 2 * U]
            sig = jax.nn.sigmoid(a)
            silu = a * sig
            R[l, m, :, pl.ds(CS + off, U)] = (silu * b).astype(bf16)
            if l == 0:
                R[l, m, :, pl.ds(CA + off2, 2 * U)] = ab.astype(bf16)
            else:
                ds = R[l, m, :, pl.ds(CA + U + off2, U)].astype(f32)
                R[l, m, :, pl.ds(CA + off2, U)] = (ds * b * sig * (1.0 + a * (1.0 - sig))).astype(bf16)
                R[l, m, :, pl.ds(CA + U + off2, U)] = (ds * silu).astype(bf16)

        for t in range(low, high):
            step(t)

    def ffn_down(l, m):
        put_partial(m, lambda cols: mm(R[l, m, :, CS : CS + F], WD[:, cols]))

    def ffn_bwd(l, m):
        if l == 0:
            def step(t):
                off, off2 = t * U, 2 * t * U
                a = R[l, m, :, pl.ds(CA + off2, U)].astype(f32)
                b = R[l, m, :, pl.ds(CA + U + off2, U)].astype(f32)
                sig = jax.nn.sigmoid(a)
                ds = mm(L[l, DF, m], WD[pl.ds(off, U), :], NT)
                R[l, m, :, pl.ds(CA + off2, U)] = (ds * b * sig * (1.0 + a * (1.0 - sig))).astype(bf16)
                R[l, m, :, pl.ds(CA + U + off2, U)] = (ds * a * sig).astype(bf16)

            for t in range(F // U):
                step(t)
        put_partial(m, lambda cols: mm(R[l, m, :, CA : CA + 2 * F], WGU[cols, :], NT))

    def conv_bwd_a(l, m):
        dz = mm(L[l, DO, m], WOUT[...], NT)
        bgate = R[l, m, :, CP : CP + C].astype(f32)
        xin = R[l, m, :, CP + 2 * C : CP + 3 * C].astype(f32)
        EXT[8 : 8 + TOK] = (bgate * xin).astype(bf16).astype(f32)
        dy = dz * R[l, m, :, CP + C : CP + 2 * C].astype(f32)
        DYE[rem(m, 2), 0:TOK] = dy
        dhcopy(l, m).start()
        R[l, m, :, CP + C : CP + 2 * C] = (dz * conv_now(l, m)).astype(bf16)
        for k in range(3):
            prod = dy * EXT[6 + k : 6 + k + TOK]
            CACC[l, k] += jnp.sum(prod.reshape(TOK // 8, 8, C), axis=0)

    def conv_bwd_b(l, m):
        dhcopy(l, m).wait()
        s = rem(m, 2)
        DYE[s, TOK : TOK + 8] = jnp.where(seq == n - 1, 0.0, DHALO[l, m])
        dbx = (
            tap(l, 2) * DYE[s, 0:TOK] + tap(l, 1) * DYE[s, 1 : 1 + TOK] + tap(l, 0) * DYE[s, 2 : 2 + TOK]
        )
        bgate = R[l, m, :, CP : CP + C].astype(f32)
        xin = R[l, m, :, CP + 2 * C : CP + 3 * C].astype(f32)
        R[l, m, :, CP : CP + C] = (dbx * xin).astype(bf16)
        R[l, m, :, CP + 2 * C : CP + 3 * C] = (dbx * bgate).astype(bf16)
        put_partial(m, lambda cols: mm(R[l, m, :, CP : CP + 3 * C], WIN[cols, :], NT))

    lanes = ((GA, (RA0, RA1, RA2)), (GB, (RB0, RB1, RB2)))

    def keep(lane, step):
        b = [bits[o] for o in ORDERS[lane]]
        return [b[0] * 4, b[0] * 4 + b[1] * 2, b[0] * 4 + b[1] * 2 + b[2]][step]

    def unit_at(t):
        if isinstance(t, int):
            return table[t][:2]
        k = jnp.where(t < TURN, t - 1, t - TURN)
        return jnp.where(t < TURN, 1, 0), jnp.where(t < 2, t * 128, k * U)

    def sized(t, fn):
        if isinstance(t, int):
            fn(splits[table[t][2]])
            return
        pl.when(t == 0)(lambda: fn(splits[128]))
        pl.when((t == 1) | (t == TURN - 1))(lambda: fn(splits[256]))
        pl.when((t > 1) & (t != TURN - 1))(lambda: fn(splits[U]))

    def rs_copy(lane, step, t, rows):
        G, recv = lanes[lane]
        slot = rem(t, SLOTS)
        size = 4 >> step
        o = ORDERS[lane][step]
        off = keep(lane, step) + size - 2 * size * bits[o]
        cut = pl.ds(0, rows[1 + lane])
        return remote(
            G.at[slot, pl.ds(off, size), cut], recv[step].at[slot, :, cut],
            rss.at[lane, step, slot], rsr.at[lane, step, slot], parts[o],
        )

    def rs_gen(t):
        l, start = unit_at(t)
        kind = jnp.where(start < CA, DF, jnp.where(start < CP, N2, jnp.where(start < CZ, N1, DO)))
        slot = rem(t, SLOTS)

        def make(rows):
            wide, cut, _ = rows
            cols = pl.ds(start if isinstance(start, int) else pl.multiple_of(start, 128), wide)
            for m in range(M):
                RT[0:wide, m * TOK : (m + 1) * TOK] = R[l, m, :, cols].T

            def step(j, _):
                src = L[l, kind, :, :, pl.ds(pl.multiple_of(j * 512, 512), 512)].reshape(M * TOK, 512)
                res = mm(RT[0:wide], src).astype(bf16)
                for q in range(4):
                    lo, y = q // 2, q % 2
                    block = res[:, q * 128 : (q + 1) * 128]
                    GA[slot, y * 4 + lo * 2 + j, 0:cut] = block[:cut]
                    GB[slot, lo * 4 + y * 2 + j, 0 : wide - cut] = block[cut:]
                return 0

            lax.fori_loop(0, D // 512, step, 0)
            for lane in range(2):
                rs_copy(lane, 0, t, rows).start()

        sized(t, make)

    def rs_add(step, t):
        slot = rem(t, SLOTS)

        def go(rows):
            for lane in range(2):
                G, recv = lanes[lane]
                rs_copy(lane, step, t, rows).wait()
                base = keep(lane, step)
                cut = rows[1 + lane]

                def add(i, _):
                    G[slot, base + i, 0:cut] = (
                        G[slot, base + i, 0:cut].astype(f32) + recv[step][slot, i, 0:cut].astype(f32)
                    ).astype(bf16)
                    return 0

                lax.fori_loop(0, 4 >> step, add, 0)
                rs_copy(lane, step + 1, t, rows).start()

        sized(t, go)

    def unit_copies(t, which, wide):
        l, start = unit_at(t)

        def at(off):
            return pl.ds(off if isinstance(off, int) else pl.multiple_of(off, 128), wide)

        tile = at(div(start - CA, 2 * U) * U)
        if which == 0:
            pairs = [(FO.at[pl.ds(0, wide)], out_down.at[l, at(start)])]
        elif which == 1:
            pairs = [(FT, out_gate.at[l, :, tile])]
        elif which == 2:
            pairs = [(FT, out_up.at[l, :, tile])]
        elif which == 3:
            pairs = [(FT.at[:, pl.ds(0, C)], out_in.at[l, 0]),
                     (FT.at[:, pl.ds(C, U - C)], out_in.at[l, 1, :, pl.ds(0, U - C)])]
        elif which == 4:
            pairs = [(FT.at[:, pl.ds(0, 2 * C - U)], out_in.at[l, 1, :, pl.ds(U - C, 2 * C - U)]),
                     (FT.at[:, pl.ds(2 * C - U, C)], out_in.at[l, 2])]
        else:
            pairs = [(FO.at[pl.ds(0, wide)], out_out.at[l, at(start - CZ)])]
        return [pltpu.make_async_copy(a, b, fos.at[i]) for i, (a, b) in enumerate(pairs)]

    def by_target(t, fn):
        if isinstance(t, int):
            _, start, wide = table[t]
            if start < CA:
                which = 0
            elif start < CP:
                which = 1 + (start - CA) // U % 2
            else:
                which = 5 if start >= CZ else 3 + (start - CP) // U
            fn(which, wide)
            return
        _, start = unit_at(t)
        pl.when(t == 0)(lambda: fn(0, 128))
        pl.when(t == 1)(lambda: fn(0, 256))
        pl.when((t > 1) & (start < CA))(lambda: fn(0, U))
        for i in range(2):
            odd = lax.rem(lax.div(start, U) + CA // U, 2) == i
            pl.when((start >= CA) & (start < CP) & odd)(functools.partial(fn, 1 + i, U))
            pl.when(start == CP + i * U)(functools.partial(fn, 3 + i, U))
        pl.when(start == CZ)(lambda: fn(5, 256))

    def unit_wait(t):
        def go(which, wide):
            for cp in unit_copies(t, which, wide):
                cp.wait()

        by_target(t, go)

    def rs_last(t):
        slot = rem(t, SLOTS)
        if isinstance(t, int):
            if t >= 1:
                unit_wait(t - 1)
        else:
            pl.when(t >= 1)(lambda: unit_wait(t - 1))

        def go(rows):
            wide, cut, _ = rows
            for lane in range(2):
                rs_copy(lane, 2, t, rows).wait()
            FO[0:cut] = (GA[slot, keep(0, 2), 0:cut].astype(f32) + RA2[slot, 0, 0:cut].astype(f32)).astype(bf16)
            FO[cut:wide] = (
                GB[slot, keep(1, 2), 0 : wide - cut].astype(f32) + RB2[slot, 0, 0 : wide - cut].astype(f32)
            ).astype(bf16)

        sized(t, go)

        def send(which, wide):
            if which in (1, 2, 3, 4):
                FT[...] = FO[...].T
            for cp in unit_copies(t, which, wide):
                cp.start()

        by_target(t, send)

    def tick_gen(t):
        if not isinstance(t, int) or t < UNITS:
            rs_gen(t)

    def tick_rest(t):
        steps = (functools.partial(rs_add, 0), functools.partial(rs_add, 1), rs_last)
        for lag, fn in enumerate(steps, 1):
            if isinstance(t, int):
                if 0 <= t - lag < UNITS:
                    fn(t - lag)
            else:
                pl.when(t >= lag)(functools.partial(fn, t - lag))

    def behind(prev, cur, m):
        if prev is None:
            pl.when(m > 0)(lambda: mid(m - 1))
        else:
            mid(lax.rem(m + M - 1, M))
            pl.when(m < 2)(lambda: prev(m + M - 2))
        pl.when(m >= 2)(lambda: cur(m - 2))

    def phase(prev, cur, first, second=None, tick=None, ahead=None):
        def step(m, _):
            if ahead is not None:
                ahead(m)
            if tick is not None:
                tick_gen(tick + m)
            if first is not None:
                first(m)
            behind(prev, cur, m)
            if second is not None:
                second(m)
            if tick is not None:
                tick_rest(tick + m)
            return 0

        lax.fori_loop(0, M, step, 0)

    def arrived(copies):
        for cp in copies:
            cp.wait()

    end_o0 = functools.partial(finish_norm, 0, 1, N2)
    end_f0 = functools.partial(finish_norm, 1, 0, N1)
    end_o1 = functools.partial(finish_norm, 1, 1, N2, within=True)
    end_n1 = functools.partial(finish_dn2, 1)
    end_c1 = functools.partial(finish_dn1, 1)
    end_n0 = functools.partial(finish_dn2, 0)
    end_c0 = functools.partial(finish_dn1, 0)

    arrived(load_conv(0) + [load_stream(m) for m in range(M)])
    send_first_halos()
    for cp in [load_og, load_down(1)] + load_ffn(0):
        cp.start()

    conv_fwd_a(0, jnp.int32(0))

    def o0(m, _):
        conv_fwd_b(0, m)
        pl.when(m < M - 1)(lambda: conv_fwd_a(0, m + 1))
        pl.when(m >= 2)(lambda: end_o0(m - 2))
        gather_dyn(0, m, 0)

        @pl.when(m == 0)
        def _():
            arrived([load_og, load_down(1)])

        mid(m)
        down_back(m)
        gather_dyn(0, m, 1)
        return 0

    lax.fori_loop(0, M, o0, 0)
    for cp in [load_down(0)] + load_conv(1):
        cp.start()
    arrived(load_ffn(0))

    def f0(m, _):
        agcopy(0, N2, m).wait()
        ffn_fwd(0, m)
        pl.when(m == 0)(lambda: load_down(0).wait())
        ffn_down(0, m)
        gather_dyn(2 * M, m, 0)

        @pl.when(m == M - 1)
        def _():
            arrived(load_conv(1) + [tap_copy])
            conv_fwd_a(1, 0)

        pl.when(m < 2)(lambda: end_o0(m + M - 2))
        pl.when(m >= 2)(lambda: end_f0(m - 2))
        mid(m)
        gather_dyn(2 * M, m, 1)
        return 0

    lax.fori_loop(0, M, f0, 0)
    for cp in load_ffn(1):
        cp.start()

    def ffn_both(m):
        agcopy(1, N2, m).wait()
        ffn_fwd(1, m)

    def o1(m, _):
        conv_fwd_b(1, m)
        pl.when(m < M - 1)(lambda: conv_fwd_a(1, m + 1))
        end_o1(m)
        pl.when(m == 1)(lambda: arrived(load_ffn(1)))
        pl.when(m >= 1)(lambda: ffn_both(m - 1))
        pl.when(m < 2)(lambda: end_f0(m + 2))
        return 0

    lax.fori_loop(0, M, o1, 0)
    agcopy(1, N2, M - 1).wait()
    ffn_fwd(1, M - 1, 0, 1)
    tick_gen(0)
    ffn_fwd(1, M - 1, 1)

    def start_c1(m):
        agcopy(1, DO, m).wait()
        conv_bwd_a(1, m)

    def last_only(fn):
        return lambda m: pl.when(m == M - 1)(lambda: fn(0))

    def next_one(fn):
        return lambda m: pl.when(m < M - 1)(lambda: fn(m + 1))

    phase(None, end_n1, lambda m: ffn_bwd(1, m), tick=1, ahead=last_only(start_c1))
    for cp in load_ffn(0):
        cp.start()
    phase(end_n1, end_c1, None, lambda m: conv_bwd_b(1, m), tick=1 + M, ahead=next_one(start_c1))
    for cp in load_conv(0):
        cp.start()
    arrived(load_ffn(0))

    def n0(m):
        ffn_bwd(0, m)

    def n0_tick(m, _):
        pl.when(m == 0)(lambda: agcopy(0, DF, 0).wait())
        pl.when(m == 1)(lambda: agcopy(0, DF, 1).wait())

        @pl.when(m == 2)
        def _():
            agcopy(0, DF, 2).wait()
            agcopy(0, DF, 3).wait()

        tick_gen(1 + 2 * M + m)
        n0(m)
        behind(end_c1, end_n0, m)
        tick_rest(1 + 2 * M + m)
        return 0

    lax.fori_loop(0, M, n0_tick, 0)
    load_down(1).start()
    load_down(1).wait()
    arrived(load_conv(0))

    def f1(m):
        agcopy(0, DO, m).wait()
        ffn_down(1, m)

    def start_c0(m):
        conv_bwd_a(0, m)

    phase(end_n0, finish_stream, f1, tick=1 + 3 * M, ahead=last_only(start_c0))

    def c0(m):
        for cp in stream_copies(m):
            cp.wait()
        conv_bwd_b(0, m)

    phase(finish_stream, end_c0, None, c0, tick=1 + 4 * M, ahead=next_one(start_c0))
    t = 1 + 5 * M
    tick_gen(t)
    mid(M - 1)
    end_c0(M - 2)
    tick_rest(t)
    tick_gen(t + 1)
    end_c0(M - 1)

    for i in range(4):
        SM[i : i + 1] = jnp.sum(GACC[i], axis=0, keepdims=True)
    SM[4:8] = jnp.zeros((4, D), f32)
    for l in range(2):
        for k in range(3):
            SM[4 + l : 5 + l, k * C : (k + 1) * C] = jnp.sum(CACC[l, k], axis=0, keepdims=True)

    def small(i):
        return remote(SM, SMR.at[i], sms.at[i], smr.at[i], [sib, *parts][i])

    small(0).start()
    tick_rest(t + 1)
    t += 2
    for i in range(4):
        tick_gen(t)
        small(i).wait()
        if i == 0:
            SM[0:4] += SMR[0, 0:4]
        else:
            SM[...] += SMR[i]
        if i < 3:
            small(i + 1).start()
        tick_rest(t)
        t += 1
    own = pl.ds(pl.multiple_of(tp * C, 128), C)
    NORM_OUT[...] = SM[0:2, own]
    FFN_OUT[...] = SM[2:4, own]
    for l in range(2):
        for k in range(3):
            CONV_OUT[k, l : l + 1, :] = SM[4 + l : 5 + l, k * C : (k + 1) * C]
    small_out = [
        pltpu.make_async_copy(src, dst, load_sem.at[16 + i])
        for i, (src, dst) in enumerate(((NORM_OUT, out_norm), (FFN_OUT, out_ffn), (CONV_OUT, out_conv)))
    ]
    for cp in small_out:
        cp.start()
    while t < UNITS + 3:
        tick_gen(t)
        tick_rest(t)
        t += 1
    unit_wait(UNITS - 1)
    for cp in small_out:
        cp.wait()
    for m in range(M):
        for cp in grad_copies(m):
            cp.wait()


def fused_call(stream_in, norm_gain, win, taps, wout, ffn_gain, wgate, wup, wdown, out_grad):
    M, TOK, D = stream_in.shape
    C, F = wout.shape[1], wgate.shape[2]
    U = 384
    rb = U // 4
    ra = U - rb
    half = TOK // 2
    vm = pltpu.VMEM
    dma = pltpu.SemaphoreType.DMA
    S = SLOTS
    anys = pl.BlockSpec(memory_space=pl.ANY)
    return pl.pallas_call(
        functools.partial(fused, (M, TOK, D, C, F, U)),
        out_shape=[
            jax.ShapeDtypeStruct((M, TOK, D), bf16),
            jax.ShapeDtypeStruct((M, TOK, D), bf16),
            jax.ShapeDtypeStruct((LAYERS, C), f32),
            jax.ShapeDtypeStruct((LAYERS, 3, 128, C), bf16),
            jax.ShapeDtypeStruct((3, LAYERS, C), f32),
            jax.ShapeDtypeStruct((LAYERS, C, 128), bf16),
            jax.ShapeDtypeStruct((LAYERS, C), f32),
            jax.ShapeDtypeStruct((LAYERS, 128, F), bf16),
            jax.ShapeDtypeStruct((LAYERS, 128, F), bf16),
            jax.ShapeDtypeStruct((LAYERS, F, 128), bf16),
        ],
        in_specs=[anys] * 10,
        out_specs=[anys] * 10,
        scratch_shapes=[
            vm((LAYERS, 4, M, TOK, D), bf16),
            vm((LAYERS, M, TOK, 3 * F + 4 * C), bf16),
            vm((D, 3 * C), bf16),
            vm((C, D), bf16),
            vm((D, 2 * F), bf16),
            vm((F, D), bf16),
            vm((M, half, D), f32),
            vm((M, half, D), f32),
            vm((M, half, 2 * LAYERS), f32),
            vm((M, TOK, D), bf16),
            vm((M, half, D), bf16),
            vm((M, half, D), bf16),
            vm((S, 8, ra, 128), bf16),
            vm((S, 8, rb, 128), bf16),
            vm((S, 4, ra, 128), bf16),
            vm((S, 2, ra, 128), bf16),
            vm((S, 1, ra, 128), bf16),
            vm((S, 4, rb, 128), bf16),
            vm((S, 2, rb, 128), bf16),
            vm((S, 1, rb, 128), bf16),
            vm((U, M * TOK), bf16),
            vm((U, 128), bf16),
            vm((128, U), bf16),
            vm((8, D), f32),
            vm((TOK + 8, C), f32),
            vm((2, TOK + 8, C), f32),
            vm((TOK, C), f32),
            vm((LAYERS, M * 8, C), f32),
            vm((M, 8, C), f32),
            vm((LAYERS, M, 8, C), f32),
            vm((4, LAYERS, D), f32),
            vm((3, LAYERS, C), f32),
            vm((3, LAYERS, C), f32),
            vm((4, 8, D), f32),
            vm((LAYERS, 3, 8, C), f32),
            vm((4, 8, D), f32),
            vm((LAYERS, D), bf16),
            vm((LAYERS, D), bf16),
            vm((3, LAYERS, C), bf16),
            vm((LAYERS, C), f32),
            vm((LAYERS, C), f32),
            vm((3, LAYERS, C), f32),
            dma((19,)),
            dma((M,)), dma((M,)), dma((M,)), dma((M,)), dma((M,)), dma((M,)),
            dma, dma((2,)), dma((2, LAYERS, M)), dma((2,)), dma((M + 1,)), dma((4, 5)), dma((4, 5)),
            dma((2, 3, S)), dma((2, 3, S)),
            dma((2,)), dma((M,)), dma((M,)), dma((M,)), dma((4,)), dma((4,)),
        ],
        name="fused",
        compiler_params=pltpu.CompilerParams(
            collective_id=0, has_side_effects=True, vmem_limit_bytes=VMEM_BYTES
        ),
    )(stream_in, norm_gain, win, taps, wout, ffn_gain, wgate, wup, wdown, out_grad)


def handed_on(kinds, *refs):
    count = len(kinds)
    srcs, dsts, bufs, wides = (refs[k * count : (k + 1) * count] for k in range(4))
    sin, sout = refs[-2:]
    chunks = [(i, k) for i in range(count) for k in range(srcs[i].shape[0])]
    ins = [pltpu.make_async_copy(srcs[i].at[k], bufs[i].at[k], sin.at[i, k]) for i, k in chunks]
    outs = [
        pltpu.make_async_copy((wides if kinds[i] else bufs)[i].at[k], dsts[i].at[k], sout.at[i, k]) for i, k in chunks
    ]
    for cp in ins:
        cp.start()
    for (i, k), first, second in zip(chunks, ins, outs):
        first.wait()
        if kinds[i]:
            ref, wide = bufs[i].at[k], wides[i].at[k]
            rows = 64
            lead = ref.shape[:-2]

            def step(r, _):
                cut = pl.ds(pl.multiple_of(lax.rem(r, ref.shape[-2] // rows) * rows, rows), rows)
                at = (lax.div(r, ref.shape[-2] // rows), cut) if lead else (cut,)
                wide[at] = ref[at].astype(f32)
                return 0

            lax.fori_loop(0, (lead[0] if lead else 1) * ref.shape[-2] // rows, step, 0)
        second.start()
    for cp in outs:
        cp.wait()


def hand_on(arrays, types):
    anys = pl.BlockSpec(memory_space=pl.ANY)
    most = max(a.shape[0] for a in arrays)
    kinds = tuple(a.dtype != t for a, t in zip(arrays, types))
    return pl.pallas_call(
        functools.partial(handed_on, kinds),
        out_shape=[jax.ShapeDtypeStruct(a.shape, t) for a, t in zip(arrays, types)],
        in_specs=[anys] * len(arrays),
        out_specs=[anys] * len(arrays),
        scratch_shapes=[pltpu.VMEM(a.shape, a.dtype) for a in arrays]
        + [pltpu.VMEM(a.shape if k else (8, 128), f32) for a, k in zip(arrays, kinds)]
        + [pltpu.SemaphoreType.DMA((len(arrays), most))] * 2,
        name="hand_on",
        compiler_params=pltpu.CompilerParams(vmem_limit_bytes=VMEM_BYTES),
    )(*arrays)


def body_fused(
    stream_in, norm_gain, in_proj, conv_taps, out_proj, ffn_gain, gate_proj, up_proj, down_proj, out_grad
):
    results = fused_call(
        stream_in, norm_gain, jnp.transpose(in_proj, (0, 2, 1, 3)), jnp.transpose(conv_taps, (1, 0, 2)),
        out_proj, ffn_gain, gate_proj, up_proj, down_proj, out_grad,
    )
    (out_stream, out_sgrad, norm_g, in_g, conv_g, out_g, ffn_g, gate_g, up_g, down_g) = hand_on(
        results, [bf16] + [f32] * 9
    )
    in_g = jnp.transpose(in_g, (0, 2, 1, 3))
    conv_g = jnp.transpose(conv_g, (1, 0, 2))
    return (out_stream, out_sgrad, norm_g, in_g, conv_g, out_g, ffn_g, gate_g, up_g, down_g)


def solution(mesh):
    in_specs = (
        P(None, "seq", None),
        P(),
        P(None, None, None, "tp"),
        P(None, None, "tp"),
        P(None, "tp", None),
        P(),
        P(None, None, "tp"),
        P(None, None, "tp"),
        P(None, "tp", None),
        P(None, "seq", None),
    )
    out_specs = (
        P(None, "seq", None),
        P(None, "seq", None),
        P(None, "tp"),
        P(None, "seq", None, "tp"),
        P(None, None, "tp"),
        P(None, "tp", "seq"),
        P(None, "tp"),
        P(None, "seq", "tp"),
        P(None, "seq", "tp"),
        P(None, "tp", "seq"),
    )
    chosen = body_fused if (mesh.shape["seq"], mesh.shape["tp"]) == (8, 4) else body
    return jax.shard_map(chosen, mesh=mesh, in_specs=in_specs, out_specs=out_specs, check_vma=False)
```

```python
import functools

import jax
import jax.numpy as jnp
from jax import lax
from jax.experimental import pallas as pl
from jax.experimental.pallas import tpu as pltpu
from jax.sharding import PartitionSpec as P

LAYERS = 2


EPS = 1e-05


def passed_along(block, axis, distance):
    devices = range(lax.axis_size(axis))
    route = [(i - distance, i) for i in devices if i - distance in devices]
    return lax.ppermute(block, axis, route)


def norm_rate(hidden):
    return lax.rsqrt(jnp.mean(hidden * hidden, axis=-1, keepdims=True) + EPS)


def norm_back(grad_in, gain, normed_val, rate):
    scaled = grad_in * gain
    return rate * (scaled - normed_val * jnp.mean(scaled * normed_val, axis=-1, keepdims=True))


def reduce_weights(grads):
    return (
        lax.psum_scatter(
            grads[0].astype(jnp.bfloat16), "seq", scatter_dimension=1, tiled=True
        ).astype(jnp.float32),
        lax.psum_scatter(
            grads[1].astype(jnp.bfloat16), "seq", scatter_dimension=2, tiled=True
        ).astype(jnp.float32),
        lax.psum_scatter(
            grads[2].astype(jnp.bfloat16), "seq", scatter_dimension=1, tiled=True
        ).astype(jnp.float32),
        lax.psum_scatter(
            grads[3].astype(jnp.bfloat16), "seq", scatter_dimension=1, tiled=True
        ).astype(jnp.float32),
        lax.psum_scatter(
            grads[4].astype(jnp.bfloat16), "seq", scatter_dimension=2, tiled=True
        ).astype(jnp.float32),
    )


def reduce_small(grads):
    return lax.psum((grads[0], grads[1], grads[2]), "seq")


def body(
    stream_in,
    norm_gain,
    in_proj,
    conv_taps,
    out_proj,
    ffn_gain,
    gate_proj,
    up_proj,
    down_proj,
    out_grad,
):
    f32 = jnp.float32
    bf16 = jnp.bfloat16
    width = in_proj.shape[-1]
    offset = lax.axis_index("tp") * width
    hidden = stream_in.astype(f32)
    kept = []
    for layer in range(LAYERS):
        gain_one = norm_gain[layer].astype(f32)
        gain_two = ffn_gain[layer].astype(f32)
        taps = conv_taps[layer].astype(f32)
        rate_one = norm_rate(hidden)
        normed_one = hidden * rate_one
        first = (normed_one * gain_one).astype(bf16)
        proj = jnp.einsum("msd,dkc->mskc", first, in_proj[layer], preferred_element_type=f32)
        bgate = proj[:, :, 0]
        cgate = proj[:, :, 1]
        xinput = proj[:, :, 2]
        mixed = (bgate * xinput).astype(bf16)
        prior = passed_along(mixed[:, -2:], "seq", 1)
        extended = jnp.concatenate([prior, mixed], axis=1).astype(f32)
        conved = (
            taps[0] * extended[:, :-2] + taps[1] * extended[:, 1:-1] + taps[2] * extended[:, 2:]
        )
        gated = (cgate * conved).astype(bf16)
        partial_out = jnp.einsum("msc,cd->msd", gated, out_proj[layer], preferred_element_type=f32)
        middle = hidden + lax.psum(partial_out, "tp")
        rate_two = norm_rate(middle)
        normed_two = middle * rate_two
        second = (normed_two * gain_two).astype(bf16)
        gate_val = jnp.einsum("msd,df->msf", second, gate_proj[layer], preferred_element_type=f32)
        up_val = jnp.einsum("msd,df->msf", second, up_proj[layer], preferred_element_type=f32)
        sigma = jax.nn.sigmoid(gate_val)
        silu_val = gate_val * sigma
        act = (silu_val * up_val).astype(bf16)
        partial_ffn = jnp.einsum("msf,fd->msd", act, down_proj[layer], preferred_element_type=f32)
        kept.append(
            (
                rate_one,
                normed_one,
                first,
                bgate,
                cgate,
                xinput,
                extended,
                conved,
                gated,
                rate_two,
                normed_two,
                second,
                gate_val,
                up_val,
                sigma,
                silu_val,
                act,
            )
        )
        hidden = middle + lax.psum(partial_ffn, "tp")
    grad_h = out_grad.astype(f32)
    collected = [None] * LAYERS
    for layer in reversed(range(LAYERS)):
        (
            rate_one,
            normed_one,
            first,
            bgate,
            cgate,
            xinput,
            extended,
            conved,
            gated,
            rate_two,
            normed_two,
            second,
            gate_val,
            up_val,
            sigma,
            silu_val,
            act,
        ) = kept[layer]
        gain_one = norm_gain[layer].astype(f32)
        gain_two = ffn_gain[layer].astype(f32)
        taps = conv_taps[layer].astype(f32)
        grad_f = grad_h.astype(bf16)
        grad_act = jnp.einsum("msd,fd->msf", grad_f, down_proj[layer], preferred_element_type=f32)
        down_g = jnp.einsum("msf,msd->fd", act, grad_f, preferred_element_type=f32)
        grad_gate = (grad_act * up_val * sigma * (1.0 + gate_val * (1.0 - sigma))).astype(bf16)
        grad_up = (grad_act * silu_val).astype(bf16)
        part_two = jnp.einsum(
            "msf,df->msd", grad_gate, gate_proj[layer], preferred_element_type=f32
        )
        part_two = part_two + jnp.einsum(
            "msf,df->msd", grad_up, up_proj[layer], preferred_element_type=f32
        )
        gate_g = jnp.einsum("msd,msf->df", second, grad_gate, preferred_element_type=f32)
        up_g = jnp.einsum("msd,msf->df", second, grad_up, preferred_element_type=f32)
        grad_two = lax.psum(part_two.astype(jnp.bfloat16), "tp").astype(jnp.float32)
        ffn_gain_g = jnp.sum(grad_two * normed_two, axis=(0, 1))
        grad_mid = grad_h + norm_back(grad_two, gain_two, normed_two, rate_two)
        grad_o = grad_mid.astype(bf16)
        grad_gated = jnp.einsum("msd,cd->msc", grad_o, out_proj[layer], preferred_element_type=f32)
        out_g = jnp.einsum("msc,msd->cd", gated, grad_o, preferred_element_type=f32)
        grad_conv = grad_gated * cgate
        grad_cgate = grad_gated * conved
        after = passed_along(grad_conv[:, :2], "seq", -1)
        grad_ext = jnp.concatenate([grad_conv, after], axis=1)
        grad_mixed = (
            taps[2] * grad_ext[:, :-2] + taps[1] * grad_ext[:, 1:-1] + taps[0] * grad_ext[:, 2:]
        )
        count = grad_conv.shape[1]
        conv_g = jnp.stack(
            [jnp.sum(grad_conv * extended[:, k : k + count], axis=(0, 1)) for k in range(3)], axis=0
        )
        grad_proj = jnp.stack([grad_mixed * xinput, grad_cgate, grad_mixed * bgate], axis=2).astype(
            bf16
        )
        part_one = jnp.einsum(
            "mskc,dkc->msd", grad_proj, in_proj[layer], preferred_element_type=f32
        )
        in_g = jnp.einsum("msd,mskc->dkc", first, grad_proj, preferred_element_type=f32)
        grad_one = lax.psum(part_one.astype(jnp.bfloat16), "tp").astype(jnp.float32)
        norm_gain_g = jnp.sum(grad_one * normed_one, axis=(0, 1))
        grad_h = grad_mid + norm_back(grad_one, gain_one, normed_one, rate_one)
        norm_piece = lax.dynamic_slice_in_dim(norm_gain_g, offset, width)
        ffn_piece = lax.dynamic_slice_in_dim(ffn_gain_g, offset, width)
        small = (norm_piece, conv_g, ffn_piece)
        large = (in_g, out_g, gate_g, up_g, down_g)
        collected[layer] = (small, large)
    norm_stack = jnp.stack([c[0][0] for c in collected], axis=0)
    conv_stack = jnp.stack([c[0][1] for c in collected], axis=0)
    ffn_stack = jnp.stack([c[0][2] for c in collected], axis=0)
    large_stack = tuple((jnp.stack([c[1][i] for c in collected], axis=0) for i in range(5)))
    large_stack = reduce_weights(large_stack)
    norm_stack, conv_stack, ffn_stack = reduce_small((norm_stack, conv_stack, ffn_stack))
    stream_out = hidden.astype(bf16)
    in_grad, out_grad_w, gate_grad, up_grad, down_grad = large_stack
    return (
        stream_out,
        grad_h,
        norm_stack,
        in_grad,
        conv_stack,
        out_grad_w,
        ffn_stack,
        gate_grad,
        up_grad,
        down_grad,
    )


VMEM_BYTES = 64 * 2**20
MESH = pl.DeviceIdType.MESH
f32 = jnp.float32
bf16 = jnp.bfloat16
NN = (((1,), (0,)), ((), ()))
NT = (((1,), (1,)), ((), ()))
ORDERS = ((0, 1, 2), (1, 0, 2))
SLOTS = 4
WIDE = 1024
N1, N2, DF, DO = range(4)


def rem(a, b):
    return a % b if isinstance(a, int) else lax.rem(a, b)


def div(a, b):
    return a // b if isinstance(a, int) else lax.div(a, b)


def cases(value, branches):
    for low, high, fn in branches:
        if isinstance(value, int):
            if low <= value < high:
                fn()
        else:
            pl.when((value >= low) & (value < high))(fn)


def mm(lhs, rhs, dims=NN):
    return lax.dot_general(lhs, rhs, dims, preferred_element_type=f32)


def fused(
    dims,
    stream_in, norm_gain, win, taps, wout, ffn_gain, wgate, wup, wdown, out_grad,
    out_stream, out_sgrad, out_norm, out_in, out_conv, out_out, out_ffn, out_gate, out_up, out_down,
    L, R, WIN, WOUT, WGU, WD, H, DH, RATE, PB, PR, XR,
    GA, GB, RA0, RA1, RA2, RB0, RB1, RB2, RT, FO, FT, RZ, zs, zr, SM,
    EXT, DYE, CF, HALO, HALO2, DHALO, GAIN, TAPS, TAPS2, GACC, CACC, SMR,
    GAIN_IN, FGAIN_IN, TAPS_IN, NORM_OUT, FFN_OUT, CONV_OUT,
    load_sem, ps, pr, xs, xr, ags, agr, hs, dhs, hr, hs2, hr2, gs, gr, rss, rsr, fos, oss, sts, str_, sms, smr,
):
    M, TOK, D, C, F, U = dims
    half = TOK // 2
    CS, CA, CP, CZ = 0, F, 3 * F, 3 * F + 3 * C
    PER = (CZ + C) // U
    first_units = [(1, 0, 128), (1, 128, U - 128)]
    TURN = PER + 2
    table = first_units + [(1, k * U, U) for k in range(1, PER)] + [(1, PER * U, CZ + C - PER * U)]
    table += [(0, k * U, U) for k in range(PER)]
    table += [(0, k, 128) for k in range(PER * U, CZ + C, 128)]
    UNITS = len(table)
    LAST = UNITS - 1
    whole = (128, 128, 0)
    splits = {w: (w, w - w // 4, w // 4) for w in (128, 256, U)}
    seq = lax.axis_index("seq")
    tp = lax.axis_index("tp")
    n = lax.axis_size("seq")
    core = lax.rem(tp, 2)
    xi = lax.div(tp, 2)
    sib = {"seq": seq, "tp": tp + 1 - 2 * core}
    xpart = {"seq": seq, "tp": tp + 2 - 4 * xi}
    bits = [lax.rem(lax.div(seq, 1 << k), 2) for k in range(3)]
    parts = [{"seq": seq + (1 << k) - 2 * (1 << k) * bits[k], "tp": tp} for k in range(3)]
    nxt = {"seq": lax.rem(seq + 1, n), "tp": tp}
    prv = {"seq": lax.rem(seq + n - 1, n), "tp": tp}
    mine = pl.ds(pl.multiple_of(core * half, half), half)
    theirs = pl.ds(pl.multiple_of((1 - core) * half, half), half)

    def remote(src, dst, ssem, rsem, dev):
        return pltpu.make_async_remote_copy(
            src_ref=src, dst_ref=dst, send_sem=ssem, recv_sem=rsem, device_id=dev, device_id_type=MESH
        )

    def load_stream(m):
        return pltpu.make_async_copy(stream_in.at[m], L.at[0, N1, m], load_sem.at[m])

    def load_conv(l):
        return [
            pltpu.make_async_copy(win.at[l, k], WIN.at[:, pl.ds(k * C, C)], load_sem.at[4 + k])
            for k in range(3)
        ] + [pltpu.make_async_copy(wout.at[l], WOUT, load_sem.at[7])]

    def load_ffn(l):
        return [
            pltpu.make_async_copy(
                src.at[l, :, pl.ds(t * U, U)], WGU.at[:, pl.ds((2 * t + i) * U, U)], load_sem.at[10 + 2 * t + i]
            )
            for t in range(F // U)
            for i, src in enumerate((wgate, wup))
        ]

    def load_down(l):
        return pltpu.make_async_copy(wdown.at[l], WD, load_sem.at[9])

    load_og = pltpu.make_async_copy(out_grad, L.at[1, DF], load_sem.at[8])
    for cp in load_conv(0) + [load_stream(m) for m in range(M)]:
        cp.start()

    barrier = pltpu.get_barrier_semaphore()
    zcross = {"seq": n - 1 - seq + 2 * lax.rem(seq, 2) - 1, "tp": tp}
    others = [sib, xpart, nxt, prv, zcross] + parts
    for dev in others:
        pl.semaphore_signal(barrier, inc=1, device_id=dev, device_id_type=MESH)

    small_in = [
        pltpu.make_async_copy(src, dst, load_sem.at[16 + i])
        for i, (src, dst) in enumerate(((norm_gain, GAIN_IN), (ffn_gain, FGAIN_IN), (taps, TAPS_IN)))
    ]
    for cp in small_in:
        cp.start()
    for cp in small_in:
        cp.wait()
    GAIN[0] = GAIN_IN[...].astype(f32)
    GAIN[1] = FGAIN_IN[...].astype(f32)
    GAIN[2] = 1.0 / GAIN_IN[...].astype(f32)
    GAIN[3] = 1.0 / FGAIN_IN[...].astype(f32)
    TAPS[...] = TAPS_IN[...].astype(f32)
    GACC[...] = jnp.zeros_like(GACC)
    CACC[...] = jnp.zeros_like(CACC)

    pl.semaphore_wait(barrier, len(others))

    zpos, ypos = lax.div(seq, 2), lax.rem(seq, 2)
    zfar, znear = lax.rem(zpos + 2, 4), zpos + 1 - 2 * lax.rem(zpos, 2)
    strip = D // 8

    def piece(s, z):
        rows = pl.ds(pl.multiple_of(ypos * strip, strip), strip)
        if s < 3:
            return L.at[0, DO, 1 + s, rows, pl.ds(pl.multiple_of(z * TOK, TOK), TOK)]
        return L.at[0, DO, 0, pl.ds(pl.multiple_of(ypos * strip + z * (C // 8), 16), C // 8)]

    def gathers(s, step):
        def send(i, src, dst, dev):
            return remote(src, dst, gs.at[s, i], gr.at[s, i], dev)

        if step == 0:
            if s < 3:
                src = win.at[1, s, pl.ds(pl.multiple_of(zpos * TOK + ypos * strip, strip), strip)]
            else:
                src = wout.at[1, pl.ds(pl.multiple_of(ypos * strip + zpos * (C // 8), 16), C // 8)]
            return [send(0, src, piece(s, zpos), xpart)]
        if step == 1:
            return [send(1, piece(s, zpos), piece(s, zpos), parts[2])]
        if step == 2:
            return [send(2 + i, piece(s, z), piece(s, z), parts[1]) for i, z in enumerate((zpos, zfar))]
        half_ref = L.at[0, DO, (1 + s) % 4, pl.ds(pl.multiple_of(ypos * strip, strip), strip)]
        return [send(4, half_ref, half_ref, parts[0])]

    def gather_at(j):
        for s in range(4):
            for step, when in enumerate((s, s + 2, s + 4, 7 + 2 * s)):
                if j == when:
                    for cp in gathers(s, step):
                        cp.wait()
                    if step < 3:
                        for cp in gathers(s, step + 1):
                            cp.start()

    def gather_dyn(base, m, late):
        for i in range(M):
            pl.when(m == i)(functools.partial(gather_at, base + 2 * i + late))

    for s in range(4):
        for cp in gathers(s, 0):
            cp.start()
    tap_copy = remote(TAPS, TAPS2, hs2.at[1], hr2.at[M], xpart)
    tap_copy.start()

    def pcopy(m):
        return remote(PB.at[m, theirs], PR.at[m], ps.at[m], pr.at[m], sib)

    def xcopy(m):
        return remote(PB.at[m, mine], XR.at[m], xs.at[m], xr.at[m], xpart)

    def mid(m):
        pcopy(m).wait()

        def chunk(i, _):
            off = pl.multiple_of(i * 32, 32)
            rows = pl.ds(pl.multiple_of(core * half + off, 32), 32)
            got = PR[m, pl.ds(off, 32)].astype(f32) + PB[m, rows].astype(f32)
            PB[m, rows] = got.astype(bf16)
            return 0

        lax.fori_loop(0, half // 32, chunk, 0, unroll=True)
        xcopy(m).start()

    def agcopy(l, kind, m):
        ref = L.at[l, kind, m, mine]
        return remote(ref, ref, ags.at[m], agr.at[m], sib)

    def rows_loop(m, body, received=XR):
        def chunk(i, _):
            off = pl.multiple_of(i * 32, 32)
            rows = pl.ds(pl.multiple_of(core * half + off, 32), 32)
            total = PB[m, rows].astype(f32) + received[m, pl.ds(off, 32)].astype(f32)
            body(pl.ds(off, 32), rows, total)
            return 0

        lax.fori_loop(0, half // 32, chunk, 0, unroll=True)

    def rate_of(val):
        return lax.rsqrt(jnp.mean(val * val, axis=-1, keepdims=True) + EPS)

    def finish_norm(l, which, kind, m, within=False):
        if within:
            pcopy(m).wait()
        else:
            xcopy(m).wait()
        gain = GAIN[which, l : l + 1, :]

        def body(loc, rows, total):
            hid = H[m, loc] + total
            H[m, loc] = hid
            rate = rate_of(hid)
            RATE[m, loc, 2 * l + which : 2 * l + which + 1] = rate
            L[l, kind, m, rows] = (hid * rate * gain).astype(bf16)

        rows_loop(m, body, PR if within else XR)
        agcopy(l, kind, m).start()

    def stream_copies(m):
        ref = PB.at[m, mine]
        return (
            pltpu.make_async_copy(ref, out_stream.at[m, mine], oss.at[m]),
            remote(ref, out_stream.at[m, mine], sts.at[m], str_.at[m], sib),
        )

    def finish_stream(m):
        xcopy(m).wait()

        def body(loc, rows, total):
            PB[m, rows] = (H[m, loc] + total).astype(bf16)

        rows_loop(m, body)
        for cp in stream_copies(m):
            cp.start()

    def norm_back(l, which, kind, m, emit):
        xcopy(m).wait()
        gain = GAIN[which, l : l + 1, :]
        inv = GAIN[2 + which, l : l + 1, :]

        def body(loc, rows, total):
            nrm = L[l, kind, m, rows].astype(f32) * inv
            prod = total * nrm
            GACC[2 * which + l] += prod[0:8] + prod[8:16] + prod[16:24] + prod[24:32]
            mean = jnp.mean(prod * gain, axis=-1, keepdims=True)
            emit(loc, rows, RATE[m, loc, 2 * l + which : 2 * l + which + 1] * (total * gain - nrm * mean))

        rows_loop(m, body)

    def finish_dn2(l, m):
        def emit(loc, rows, delta):
            prev = L[1, DF, m, rows].astype(f32) if l == 1 else DH[m, loc]
            new = prev + delta
            DH[m, loc] = new
            L[l, DO, m, rows] = new.astype(bf16)

        norm_back(l, 1, N2, m, emit)
        agcopy(l, DO, m).start()

    def finish_dn1(l, m):
        def emit(loc, rows, delta):
            new = DH[m, loc] + delta
            if l == 1:
                DH[m, loc] = new
                L[0, DF, m, rows] = new.astype(bf16)
            else:
                PB[m, rows] = new.astype(bf16)

        norm_back(l, 0, N1, m, emit)
        if l == 1:
            agcopy(0, DF, m).start()
        else:
            for cp in grad_copies(m):
                cp.start()

    def grad_copies(m):
        return (
            pltpu.make_async_copy(PB.at[m, mine], out_sgrad.at[m, mine], oss.at[m]),
            remote(PB.at[m, mine], out_sgrad.at[m, mine], ags.at[m], agr.at[m], sib),
        )

    def put_partial(m, tile):
        def step(j, _):
            cols = pl.ds(pl.multiple_of(j * WIDE, WIDE), WIDE)
            PB[m, :, cols] = tile(cols).astype(bf16)
            return 0

        lax.fori_loop(0, D // WIDE, step, 0)
        pcopy(m).start()

    def halo_rows(m):
        return pl.ds(m * 8 if isinstance(m, int) else pl.multiple_of(m * 8, 8), 8)

    def hcopy(l, m):
        return remote(EXT.at[pl.ds(TOK, 8)], HALO.at[l, halo_rows(m)], hs, hr.at[0, l, m], nxt)

    def dhcopy(l, m):
        return remote(DYE.at[rem(m, 2), pl.ds(0, 8)], DHALO.at[l, m], dhs.at[rem(m, 2)], hr.at[1, l, m], prv)

    def hcopy2(m):
        return remote(DYE.at[1, pl.ds(TOK, 8)], HALO2.at[m], hs2.at[0], hr2.at[m], nxt)

    def tap(l, k):
        return TAPS[k, l : l + 1, :]

    def conv_of(ext, halo, taps_ref, l):
        ext[0:8] = jnp.where(seq == 0, 0.0, halo)
        t = [taps_ref[k, l : l + 1, :] for k in range(3)]
        return t[0] * ext[6 : 6 + TOK] + t[1] * ext[7 : 7 + TOK] + t[2] * ext[8 : 8 + TOK]

    def conv_now(l, m):
        return conv_of(EXT, HALO[l, halo_rows(m)], TAPS, l)

    def other_in(k):
        blocks = [L[0, DO, 1 + k, :, r * TOK : (r + 1) * TOK] for r in range(D // TOK)]
        return jnp.concatenate(blocks, axis=0)

    first_halos = remote(DYE.at[1, pl.ds(0, 8 * M)], HALO.at[0], hs, hr.at[0, 0, 0], nxt)

    def send_first_halos():
        val = jnp.concatenate([L[0, N1, m, TOK - 16 : TOK] for m in range(M)], axis=0).astype(f32)
        p = mm((val * rate_of(val) * GAIN[0, 0:1, :]).astype(bf16), WIN[...])
        bx = (p[:, 0:C] * p[:, 2 * C : 3 * C]).astype(bf16).astype(f32)
        for m in range(M):
            DYE[1, 8 * m : 8 * m + 8] = bx[16 * m + 8 : 16 * m + 16]
        first_halos.start()

    def conv_fwd_a(l, m):
        if l == 0:
            gain = GAIN[0, 0:1, :]
            hid = L[0, N1, m, mine].astype(f32)
            H[m] = hid
            RATE[m, :, 0:1] = rate_of(hid)

            def chunk(i, _):
                rows = pl.ds(pl.multiple_of(i * 32, 32), 32)
                val = L[0, N1, m, rows].astype(f32)
                L[0, N1, m, rows] = (val * rate_of(val) * gain).astype(bf16)
                return 0

            lax.fori_loop(0, TOK // 32, chunk, 0)
        else:
            agcopy(1, N1, m).wait()
        first = L[l, N1, m]
        p = mm(first, WIN[...])
        bgate, cgate, xin = p[:, 0:C], p[:, C : 2 * C], p[:, 2 * C : 3 * C]
        R[l, m, :, CP : CP + 3 * C] = p.astype(bf16)
        EXT[8 : 8 + TOK] = (bgate * xin).astype(bf16).astype(f32)
        DYE[0, 0:TOK] = cgate
        if l == 1:
            hcopy(l, m).start()
            p = mm(first, jnp.concatenate([other_in(k) for k in range(3)], axis=1))
            DYE[1, 8 : 8 + TOK] = (p[:, 0:C] * p[:, 2 * C : 3 * C]).astype(bf16).astype(f32)
            hcopy2(m).start()
            CF[...] = p[:, C : 2 * C]

    def conv_fwd_b(l, m):
        if l == 0:
            pl.when(m == 0)(lambda: first_halos.wait())
        else:
            hcopy(l, m).wait()
        gated = (DYE[0, 0:TOK] * conv_now(l, m)).astype(bf16)
        R[l, m, :, CZ : CZ + C] = gated
        if l == 0:
            put_partial(m, lambda cols: mm(R[l, m, :, CZ : CZ + C], WOUT[:, cols]))
        else:
            hcopy2(m).wait()
            L[0, DF, m, :, 0:C] = (CF[...] * conv_of(DYE.at[1], HALO2[m], TAPS2, l)).astype(bf16)
            put_partial(
                m,
                lambda cols: mm(R[l, m, :, CZ : CZ + C], WOUT[:, cols])
                + mm(L[0, DF, m, :, 0:C], L[0, DO, 0, :, cols]),
            )

    def down_back(m):
        ds = mm(L[1, DF, m], WD[...], NT).astype(bf16)
        for t in range(F // U):
            R[1, m, :, CA + (2 * t + 1) * U : CA + (2 * t + 2) * U] = ds[:, t * U : (t + 1) * U]

    def ffn_fwd(l, m, low=0, high=F // U):
        def step(t):
            off, off2 = t * U, 2 * t * U
            ab = mm(L[l, N2, m], WGU[:, pl.ds(off2, 2 * U)])
            a, b = ab[:, 0:U], ab[:, U : 2 * U]
            sig = jax.nn.sigmoid(a)
            silu = a * sig
            R[l, m, :, pl.ds(CS + off, U)] = (silu * b).astype(bf16)
            if l == 0:
                R[l, m, :, pl.ds(CA + off2, 2 * U)] = ab.astype(bf16)
            else:
                ds = R[l, m, :, pl.ds(CA + U + off2, U)].astype(f32)
                R[l, m, :, pl.ds(CA + off2, U)] = (ds * b * sig * (1.0 + a * (1.0 - sig))).astype(bf16)
                R[l, m, :, pl.ds(CA + U + off2, U)] = (ds * silu).astype(bf16)

        for t in range(low, high):
            step(t)

    def ffn_down(l, m):
        put_partial(m, lambda cols: mm(R[l, m, :, CS : CS + F], WD[:, cols]))

    def ffn_bwd(l, m):
        if l == 0:
            def step(t):
                off, off2 = t * U, 2 * t * U
                a = R[l, m, :, pl.ds(CA + off2, U)].astype(f32)
                b = R[l, m, :, pl.ds(CA + U + off2, U)].astype(f32)
                sig = jax.nn.sigmoid(a)
                ds = mm(L[l, DF, m], WD[pl.ds(off, U), :], NT)
                R[l, m, :, pl.ds(CA + off2, U)] = (ds * b * sig * (1.0 + a * (1.0 - sig))).astype(bf16)
                R[l, m, :, pl.ds(CA + U + off2, U)] = (ds * a * sig).astype(bf16)

            for t in range(F // U):
                step(t)
        put_partial(m, lambda cols: mm(R[l, m, :, CA : CA + 2 * F], WGU[cols, :], NT))

    def conv_bwd_a(l, m):
        dz = mm(L[l, DO, m], WOUT[...], NT)
        bgate = R[l, m, :, CP : CP + C].astype(f32)
        xin = R[l, m, :, CP + 2 * C : CP + 3 * C].astype(f32)
        EXT[8 : 8 + TOK] = (bgate * xin).astype(bf16).astype(f32)
        dy = dz * R[l, m, :, CP + C : CP + 2 * C].astype(f32)
        DYE[rem(m, 2), 0:TOK] = dy
        dhcopy(l, m).start()
        R[l, m, :, CP + C : CP + 2 * C] = (dz * conv_now(l, m)).astype(bf16)
        for k in range(3):
            prod = dy * EXT[6 + k : 6 + k + TOK]
            CACC[l, k] += jnp.sum(prod.reshape(TOK // 8, 8, C), axis=0)

    def conv_bwd_b(l, m):
        dhcopy(l, m).wait()
        s = rem(m, 2)
        DYE[s, TOK : TOK + 8] = jnp.where(seq == n - 1, 0.0, DHALO[l, m])
        dbx = (
            tap(l, 2) * DYE[s, 0:TOK] + tap(l, 1) * DYE[s, 1 : 1 + TOK] + tap(l, 0) * DYE[s, 2 : 2 + TOK]
        )
        bgate = R[l, m, :, CP : CP + C].astype(f32)
        xin = R[l, m, :, CP + 2 * C : CP + 3 * C].astype(f32)
        R[l, m, :, CP : CP + C] = (dbx * xin).astype(bf16)
        R[l, m, :, CP + 2 * C : CP + 3 * C] = (dbx * bgate).astype(bf16)
        put_partial(m, lambda cols: mm(R[l, m, :, CP : CP + 3 * C], WIN[cols, :], NT))

    lanes = ((GA, (RA0, RA1, RA2)), (GB, (RB0, RB1, RB2)))

    def keep(lane, step):
        b = [bits[o] for o in ORDERS[lane]]
        return [b[0] * 4, b[0] * 4 + b[1] * 2, b[0] * 4 + b[1] * 2 + b[2]][step]

    def unit_at(t):
        if isinstance(t, int):
            return table[t][:2]
        k = jnp.where(t < TURN, t - 1, t - TURN)
        return jnp.where(t < TURN, 1, 0), jnp.where(t < 2, t * 128, k * U)

    def sized(t, fn):
        if isinstance(t, int):
            fn(splits[table[t][2]])
            return
        pl.when(t == 0)(lambda: fn(splits[128]))
        pl.when((t == 1) | (t == TURN - 1))(lambda: fn(splits[256]))
        pl.when((t > 1) & (t != TURN - 1))(lambda: fn(splits[U]))

    def rs_copy(lane, step, t, rows):
        G, recv = lanes[lane]
        slot = rem(t, SLOTS)
        size = 4 >> step
        o = ORDERS[lane][step]
        off = keep(lane, step) + size - 2 * size * bits[o]
        cut = pl.ds(0, rows[1 + lane])
        return remote(
            G.at[slot, pl.ds(off, size), cut], recv[step].at[slot, :, cut],
            rss.at[lane, step, slot], rsr.at[lane, step, slot], parts[o],
        )

    def rs_gen(t):
        l, start = unit_at(t)
        kind = jnp.where(start < CA, DF, jnp.where(start < CP, N2, jnp.where(start < CZ, N1, DO)))
        slot = rem(t, SLOTS)

        def make(rows):
            wide, cut, _ = rows
            cols = pl.ds(start if isinstance(start, int) else pl.multiple_of(start, 128), wide)
            for m in range(M):
                RT[0:wide, m * TOK : (m + 1) * TOK] = R[l, m, :, cols].T

            def step(j, _):
                src = L[l, kind, :, :, pl.ds(pl.multiple_of(j * 512, 512), 512)].reshape(M * TOK, 512)
                res = mm(RT[0:wide], src).astype(bf16)
                for q in range(4):
                    lo, y = q // 2, q % 2
                    block = res[:, q * 128 : (q + 1) * 128]
                    GA[slot, y * 4 + lo * 2 + j, 0:cut] = block[:cut]
                    if cut < wide:
                        GB[slot, lo * 4 + y * 2 + j, 0 : wide - cut] = block[cut:]
                return 0

            lax.fori_loop(0, D // 512, step, 0)
            for lane in range(2):
                if rows[1 + lane]:
                    rs_copy(lane, 0, t, rows).start()

        if isinstance(t, int) and t == LAST:
            make(whole)
        else:
            sized(t, make)

    def last_copies():
        base = bits[0] * 4
        for i, (flip, dev) in enumerate(((1, parts[2]), (2, parts[1]), (3, zcross))):
            to = (bits[1] if flip < 2 else 1 - bits[1]) * 2 + (bits[2] if flip == 2 else 1 - bits[2])
            yield remote(GA.at[LAST % SLOTS, base + to, pl.ds(0, 128)], RZ.at[i], zs.at[i], zr.at[i], dev)

    def last_add():
        slot = LAST % SLOTS
        rs_copy(0, 0, LAST, whole).wait()
        base = keep(0, 0)
        for i in range(4):
            GA[slot, base + i, 0:128] = (
                GA[slot, base + i, 0:128].astype(f32) + RA0[slot, i, 0:128].astype(f32)
            ).astype(bf16)
        for cp in last_copies():
            cp.start()

    def last_sum():
        unit_wait(LAST - 1)
        for cp in last_copies():
            cp.wait()
        total = GA[LAST % SLOTS, keep(0, 2), 0:128].astype(f32) + RZ[0].astype(f32)
        FO[0:128] = (total + (RZ[1].astype(f32) + RZ[2].astype(f32))).astype(bf16)
        for cp in unit_copies(LAST, 5, 128):
            cp.start()

    def rs_add(step, t):
        slot = rem(t, SLOTS)

        def go(rows):
            for lane in range(2):
                G, recv = lanes[lane]
                rs_copy(lane, step, t, rows).wait()
                base = keep(lane, step)
                cut = rows[1 + lane]

                def add(i, _):
                    G[slot, base + i, 0:cut] = (
                        G[slot, base + i, 0:cut].astype(f32) + recv[step][slot, i, 0:cut].astype(f32)
                    ).astype(bf16)
                    return 0

                lax.fori_loop(0, 4 >> step, add, 0)
                rs_copy(lane, step + 1, t, rows).start()

        sized(t, go)

    def unit_copies(t, which, wide):
        l, start = unit_at(t)

        def at(off):
            return pl.ds(off if isinstance(off, int) else pl.multiple_of(off, 128), wide)

        tile = at(div(start - CA, 2 * U) * U)
        if which == 0:
            pairs = [(FO.at[pl.ds(0, wide)], out_down.at[l, at(start)])]
        elif which == 1:
            pairs = [(FT, out_gate.at[l, :, tile])]
        elif which == 2:
            pairs = [(FT, out_up.at[l, :, tile])]
        elif which == 3:
            pairs = [(FT.at[:, pl.ds(0, C)], out_in.at[l, 0]),
                     (FT.at[:, pl.ds(C, U - C)], out_in.at[l, 1, :, pl.ds(0, U - C)])]
        elif which == 4:
            pairs = [(FT.at[:, pl.ds(0, 2 * C - U)], out_in.at[l, 1, :, pl.ds(U - C, 2 * C - U)]),
                     (FT.at[:, pl.ds(2 * C - U, C)], out_in.at[l, 2])]
        else:
            pairs = [(FO.at[pl.ds(0, wide)], out_out.at[l, at(start - CZ)])]
        return [pltpu.make_async_copy(a, b, fos.at[i]) for i, (a, b) in enumerate(pairs)]

    def by_target(t, fn):
        if isinstance(t, int):
            _, start, wide = table[t]
            if start < CA:
                which = 0
            elif start < CP:
                which = 1 + (start - CA) // U % 2
            else:
                which = 5 if start >= CZ else 3 + (start - CP) // U
            fn(which, wide)
            return
        _, start = unit_at(t)
        pl.when(t == 0)(lambda: fn(0, 128))
        pl.when(t == 1)(lambda: fn(0, 256))
        pl.when((t > 1) & (start < CA))(lambda: fn(0, U))
        for i in range(2):
            odd = lax.rem(lax.div(start, U) + CA // U, 2) == i
            pl.when((start >= CA) & (start < CP) & odd)(functools.partial(fn, 1 + i, U))
            pl.when(start == CP + i * U)(functools.partial(fn, 3 + i, U))
        pl.when(start == CZ)(lambda: fn(5, 256))

    def unit_wait(t):
        def go(which, wide):
            for cp in unit_copies(t, which, wide):
                cp.wait()

        by_target(t, go)

    def rs_last(t):
        slot = rem(t, SLOTS)
        if isinstance(t, int):
            if t >= 1:
                unit_wait(t - 1)
        else:
            pl.when(t >= 1)(lambda: unit_wait(t - 1))

        def go(rows):
            wide, cut, _ = rows
            for lane in range(2):
                rs_copy(lane, 2, t, rows).wait()
            FO[0:cut] = (GA[slot, keep(0, 2), 0:cut].astype(f32) + RA2[slot, 0, 0:cut].astype(f32)).astype(bf16)
            FO[cut:wide] = (
                GB[slot, keep(1, 2), 0 : wide - cut].astype(f32) + RB2[slot, 0, 0 : wide - cut].astype(f32)
            ).astype(bf16)

        sized(t, go)

        def send(which, wide):
            if which in (1, 2, 3, 4):
                FT[...] = FO[...].T
            for cp in unit_copies(t, which, wide):
                cp.start()

        by_target(t, send)

    def tick_gen(t):
        if not isinstance(t, int) or t < UNITS:
            rs_gen(t)

    def tick_rest(t):
        steps = (functools.partial(rs_add, 0), functools.partial(rs_add, 1), rs_last)
        for lag, fn in enumerate(steps, 1):
            if isinstance(t, int):
                if 0 <= t - lag < LAST:
                    fn(t - lag)
                elif t - lag == LAST and lag == 1:
                    last_add()
            else:
                pl.when(t >= lag)(functools.partial(fn, t - lag))

    def behind(prev, cur, m):
        if prev is None:
            pl.when(m > 0)(lambda: mid(m - 1))
        else:
            mid(lax.rem(m + M - 1, M))
            pl.when(m < 2)(lambda: prev(m + M - 2))
        pl.when(m >= 2)(lambda: cur(m - 2))

    def phase(prev, cur, first, second=None, tick=None, ahead=None):
        def step(m, _):
            if ahead is not None:
                ahead(m)
            if tick is not None:
                tick_gen(tick + m)
            if first is not None:
                first(m)
            behind(prev, cur, m)
            if second is not None:
                second(m)
            if tick is not None:
                tick_rest(tick + m)
            return 0

        lax.fori_loop(0, M, step, 0)

    def arrived(copies):
        for cp in copies:
            cp.wait()

    end_o0 = functools.partial(finish_norm, 0, 1, N2)
    end_f0 = functools.partial(finish_norm, 1, 0, N1)
    end_o1 = functools.partial(finish_norm, 1, 1, N2, within=True)
    end_n1 = functools.partial(finish_dn2, 1)
    end_c1 = functools.partial(finish_dn1, 1)
    end_n0 = functools.partial(finish_dn2, 0)
    end_c0 = functools.partial(finish_dn1, 0)

    arrived(load_conv(0) + [load_stream(m) for m in range(M)])
    send_first_halos()
    for cp in [load_og, load_down(1)] + load_ffn(0):
        cp.start()

    conv_fwd_a(0, jnp.int32(0))

    def o0(m, _):
        conv_fwd_b(0, m)
        pl.when(m < M - 1)(lambda: conv_fwd_a(0, m + 1))
        pl.when(m >= 2)(lambda: end_o0(m - 2))
        gather_dyn(0, m, 0)

        @pl.when(m == 0)
        def _():
            arrived([load_og, load_down(1)])

        mid(m)
        down_back(m)
        gather_dyn(0, m, 1)
        return 0

    lax.fori_loop(0, M, o0, 0)
    for cp in [load_down(0)] + load_conv(1):
        cp.start()
    arrived(load_ffn(0))

    def f0(m, _):
        agcopy(0, N2, m).wait()
        ffn_fwd(0, m)
        pl.when(m == 0)(lambda: load_down(0).wait())
        ffn_down(0, m)
        gather_dyn(2 * M, m, 0)

        @pl.when(m == M - 1)
        def _():
            arrived(load_conv(1) + [tap_copy])
            conv_fwd_a(1, 0)

        pl.when(m < 2)(lambda: end_o0(m + M - 2))
        pl.when(m >= 2)(lambda: end_f0(m - 2))
        mid(m)
        gather_dyn(2 * M, m, 1)
        return 0

    lax.fori_loop(0, M, f0, 0)
    for cp in load_ffn(1):
        cp.start()

    def ffn_both(m):
        agcopy(1, N2, m).wait()
        ffn_fwd(1, m)

    def o1(m, _):
        conv_fwd_b(1, m)
        pl.when(m < M - 1)(lambda: conv_fwd_a(1, m + 1))
        end_o1(m)
        pl.when(m == 1)(lambda: arrived(load_ffn(1)))
        pl.when(m >= 1)(lambda: ffn_both(m - 1))
        pl.when(m < 2)(lambda: end_f0(m + 2))
        return 0

    lax.fori_loop(0, M, o1, 0)
    agcopy(1, N2, M - 1).wait()
    ffn_fwd(1, M - 1, 0, 1)
    tick_gen(0)
    ffn_fwd(1, M - 1, 1)

    def start_c1(m):
        agcopy(1, DO, m).wait()
        conv_bwd_a(1, m)

    def last_only(fn):
        return lambda m: pl.when(m == M - 1)(lambda: fn(0))

    def next_one(fn):
        return lambda m: pl.when(m < M - 1)(lambda: fn(m + 1))

    phase(None, end_n1, lambda m: ffn_bwd(1, m), tick=1, ahead=last_only(start_c1))
    for cp in load_ffn(0):
        cp.start()
    phase(end_n1, end_c1, None, lambda m: conv_bwd_b(1, m), tick=1 + M, ahead=next_one(start_c1))
    for cp in load_conv(0):
        cp.start()
    arrived(load_ffn(0))

    def n0(m):
        ffn_bwd(0, m)

    def n0_tick(m, _):
        pl.when(m == 0)(lambda: agcopy(0, DF, 0).wait())
        pl.when(m == 1)(lambda: agcopy(0, DF, 1).wait())

        @pl.when(m == 2)
        def _():
            agcopy(0, DF, 2).wait()
            agcopy(0, DF, 3).wait()

        tick_gen(1 + 2 * M + m)
        n0(m)
        behind(end_c1, end_n0, m)
        tick_rest(1 + 2 * M + m)
        return 0

    lax.fori_loop(0, M, n0_tick, 0)
    load_down(1).start()
    load_down(1).wait()
    arrived(load_conv(0))

    def f1(m):
        agcopy(0, DO, m).wait()
        ffn_down(1, m)

    def start_c0(m):
        conv_bwd_a(0, m)

    phase(end_n0, finish_stream, f1, tick=1 + 3 * M, ahead=last_only(start_c0))

    def c0(m):
        for cp in stream_copies(m):
            cp.wait()
        conv_bwd_b(0, m)

    phase(finish_stream, end_c0, None, c0, tick=1 + 4 * M, ahead=next_one(start_c0))
    t = 1 + 5 * M
    tick_gen(t)
    mid(M - 1)
    end_c0(M - 2)
    tick_rest(t)
    tick_gen(t + 1)
    end_c0(M - 1)

    for i in range(4):
        SM[i : i + 1] = jnp.sum(GACC[i], axis=0, keepdims=True)
    SM[4:8] = jnp.zeros((4, D), f32)
    for l in range(2):
        for k in range(3):
            SM[4 + l : 5 + l, k * C : (k + 1) * C] = jnp.sum(CACC[l, k], axis=0, keepdims=True)

    def small(i):
        return remote(SM, SMR.at[i], sms.at[i], smr.at[i], [sib, *parts][i])

    small(0).start()
    tick_rest(t + 1)
    t += 2
    for i in range(4):
        tick_gen(t)
        small(i).wait()
        if i == 0:
            SM[0:4] += SMR[0, 0:4]
        else:
            SM[...] += SMR[i]
        if i < 3:
            small(i + 1).start()
        tick_rest(t)
        t += 1
    own = pl.ds(pl.multiple_of(tp * C, 128), C)
    NORM_OUT[...] = SM[0:2, own]
    FFN_OUT[...] = SM[2:4, own]
    for l in range(2):
        for k in range(3):
            CONV_OUT[k, l : l + 1, :] = SM[4 + l : 5 + l, k * C : (k + 1) * C]
    small_out = [
        pltpu.make_async_copy(src, dst, load_sem.at[16 + i])
        for i, (src, dst) in enumerate(((NORM_OUT, out_norm), (FFN_OUT, out_ffn), (CONV_OUT, out_conv)))
    ]
    for cp in small_out:
        cp.start()
    while t < UNITS + 2:
        tick_gen(t)
        tick_rest(t)
        t += 1
    last_sum()
    unit_wait(LAST)
    for cp in small_out:
        cp.wait()
    for m in range(M):
        for cp in grad_copies(m):
            cp.wait()


def fused_call(stream_in, norm_gain, win, taps, wout, ffn_gain, wgate, wup, wdown, out_grad):
    M, TOK, D = stream_in.shape
    C, F = wout.shape[1], wgate.shape[2]
    U = 384
    rb = U // 4
    ra = U - rb
    half = TOK // 2
    vm = pltpu.VMEM
    dma = pltpu.SemaphoreType.DMA
    S = SLOTS
    anys = pl.BlockSpec(memory_space=pl.ANY)
    return pl.pallas_call(
        functools.partial(fused, (M, TOK, D, C, F, U)),
        out_shape=[
            jax.ShapeDtypeStruct((M, TOK, D), bf16),
            jax.ShapeDtypeStruct((M, TOK, D), bf16),
            jax.ShapeDtypeStruct((LAYERS, C), f32),
            jax.ShapeDtypeStruct((LAYERS, 3, 128, C), bf16),
            jax.ShapeDtypeStruct((3, LAYERS, C), f32),
            jax.ShapeDtypeStruct((LAYERS, C, 128), bf16),
            jax.ShapeDtypeStruct((LAYERS, C), f32),
            jax.ShapeDtypeStruct((LAYERS, 128, F), bf16),
            jax.ShapeDtypeStruct((LAYERS, 128, F), bf16),
            jax.ShapeDtypeStruct((LAYERS, F, 128), bf16),
        ],
        in_specs=[anys] * 10,
        out_specs=[anys] * 10,
        scratch_shapes=[
            vm((LAYERS, 4, M, TOK, D), bf16),
            vm((LAYERS, M, TOK, 3 * F + 4 * C), bf16),
            vm((D, 3 * C), bf16),
            vm((C, D), bf16),
            vm((D, 2 * F), bf16),
            vm((F, D), bf16),
            vm((M, half, D), f32),
            vm((M, half, D), f32),
            vm((M, half, 2 * LAYERS), f32),
            vm((M, TOK, D), bf16),
            vm((M, half, D), bf16),
            vm((M, half, D), bf16),
            vm((S, 8, ra, 128), bf16),
            vm((S, 8, rb, 128), bf16),
            vm((S, 4, ra, 128), bf16),
            vm((S, 2, ra, 128), bf16),
            vm((S, 1, ra, 128), bf16),
            vm((S, 4, rb, 128), bf16),
            vm((S, 2, rb, 128), bf16),
            vm((S, 1, rb, 128), bf16),
            vm((U, M * TOK), bf16),
            vm((U, 128), bf16),
            vm((128, U), bf16),
            vm((3, 128, 128), bf16),
            dma((3,)),
            dma((3,)),
            vm((8, D), f32),
            vm((TOK + 8, C), f32),
            vm((2, TOK + 8, C), f32),
            vm((TOK, C), f32),
            vm((LAYERS, M * 8, C), f32),
            vm((M, 8, C), f32),
            vm((LAYERS, M, 8, C), f32),
            vm((4, LAYERS, D), f32),
            vm((3, LAYERS, C), f32),
            vm((3, LAYERS, C), f32),
            vm((4, 8, D), f32),
            vm((LAYERS, 3, 8, C), f32),
            vm((4, 8, D), f32),
            vm((LAYERS, D), bf16),
            vm((LAYERS, D), bf16),
            vm((3, LAYERS, C), bf16),
            vm((LAYERS, C), f32),
            vm((LAYERS, C), f32),
            vm((3, LAYERS, C), f32),
            dma((19,)),
            dma((M,)), dma((M,)), dma((M,)), dma((M,)), dma((M,)), dma((M,)),
            dma, dma((2,)), dma((2, LAYERS, M)), dma((2,)), dma((M + 1,)), dma((4, 5)), dma((4, 5)),
            dma((2, 3, S)), dma((2, 3, S)),
            dma((2,)), dma((M,)), dma((M,)), dma((M,)), dma((4,)), dma((4,)),
        ],
        name="fused",
        compiler_params=pltpu.CompilerParams(
            collective_id=0, has_side_effects=True, vmem_limit_bytes=VMEM_BYTES
        ),
    )(stream_in, norm_gain, win, taps, wout, ffn_gain, wgate, wup, wdown, out_grad)


def handed_on(kinds, *refs):
    count = len(kinds)
    srcs, dsts, bufs, wides = (refs[k * count : (k + 1) * count] for k in range(4))
    sin, sout = refs[-2:]
    chunks = [(i, k) for i in range(count) for k in range(srcs[i].shape[0])]
    ins = [pltpu.make_async_copy(srcs[i].at[k], bufs[i].at[k], sin.at[i, k]) for i, k in chunks]
    outs = [
        pltpu.make_async_copy((wides if kinds[i] else bufs)[i].at[k], dsts[i].at[k], sout.at[i, k]) for i, k in chunks
    ]
    for cp in ins:
        cp.start()
    for (i, k), first, second in zip(chunks, ins, outs):
        first.wait()
        if kinds[i]:
            ref, wide = bufs[i].at[k], wides[i].at[k]
            rows = 128
            lead = ref.shape[:-2]

            def step(r, _):
                cut = pl.ds(pl.multiple_of(lax.rem(r, ref.shape[-2] // rows) * rows, rows), rows)
                at = (lax.div(r, ref.shape[-2] // rows), cut) if lead else (cut,)
                wide[at] = ref[at].astype(f32)
                return 0

            lax.fori_loop(0, (lead[0] if lead else 1) * ref.shape[-2] // rows, step, 0, unroll=True)
        second.start()
    for cp in outs:
        cp.wait()


def hand_on(arrays, types):
    anys = pl.BlockSpec(memory_space=pl.ANY)
    most = max(a.shape[0] for a in arrays)
    kinds = tuple(a.dtype != t for a, t in zip(arrays, types))
    return pl.pallas_call(
        functools.partial(handed_on, kinds),
        out_shape=[jax.ShapeDtypeStruct(a.shape, t) for a, t in zip(arrays, types)],
        in_specs=[anys] * len(arrays),
        out_specs=[anys] * len(arrays),
        scratch_shapes=[pltpu.VMEM(a.shape, a.dtype) for a in arrays]
        + [pltpu.VMEM(a.shape if k else (8, 128), f32) for a, k in zip(arrays, kinds)]
        + [pltpu.SemaphoreType.DMA((len(arrays), most))] * 2,
        name="hand_on",
        compiler_params=pltpu.CompilerParams(vmem_limit_bytes=VMEM_BYTES),
    )(*arrays)


def body_fused(
    stream_in, norm_gain, in_proj, conv_taps, out_proj, ffn_gain, gate_proj, up_proj, down_proj, out_grad
):
    results = fused_call(
        stream_in, norm_gain, jnp.transpose(in_proj, (0, 2, 1, 3)), jnp.transpose(conv_taps, (1, 0, 2)),
        out_proj, ffn_gain, gate_proj, up_proj, down_proj, out_grad,
    )
    (out_stream, out_sgrad, norm_g, in_g, conv_g, out_g, ffn_g, gate_g, up_g, down_g) = hand_on(
        results, [bf16] + [f32] * 9
    )
    in_g = jnp.transpose(in_g, (0, 2, 1, 3))
    conv_g = jnp.transpose(conv_g, (1, 0, 2))
    return (out_stream, out_sgrad, norm_g, in_g, conv_g, out_g, ffn_g, gate_g, up_g, down_g)


def solution(mesh):
    in_specs = (
        P(None, "seq", None),
        P(),
        P(None, None, None, "tp"),
        P(None, None, "tp"),
        P(None, "tp", None),
        P(),
        P(None, None, "tp"),
        P(None, None, "tp"),
        P(None, "tp", None),
        P(None, "seq", None),
    )
    out_specs = (
        P(None, "seq", None),
        P(None, "seq", None),
        P(None, "tp"),
        P(None, "seq", None, "tp"),
        P(None, None, "tp"),
        P(None, "tp", "seq"),
        P(None, "tp"),
        P(None, "seq", "tp"),
        P(None, "seq", "tp"),
        P(None, "tp", "seq"),
    )
    chosen = body_fused if (mesh.shape["seq"], mesh.shape["tp"]) == (8, 4) else body
    return jax.shard_map(chosen, mesh=mesh, in_specs=in_specs, out_specs=out_specs, check_vma=False)
```

```python
import functools

import jax
import jax.numpy as jnp
from jax import lax
from jax.experimental import pallas as pl
from jax.experimental.pallas import tpu as pltpu
from jax.sharding import PartitionSpec as P

LAYERS = 2


EPS = 1e-05


def passed_along(block, axis, distance):
    devices = range(lax.axis_size(axis))
    route = [(i - distance, i) for i in devices if i - distance in devices]
    return lax.ppermute(block, axis, route)


def norm_rate(hidden):
    return lax.rsqrt(jnp.mean(hidden * hidden, axis=-1, keepdims=True) + EPS)


def norm_back(grad_in, gain, normed_val, rate):
    scaled = grad_in * gain
    return rate * (scaled - normed_val * jnp.mean(scaled * normed_val, axis=-1, keepdims=True))


def reduce_weights(grads):
    return (
        lax.psum_scatter(
            grads[0].astype(jnp.bfloat16), "seq", scatter_dimension=1, tiled=True
        ).astype(jnp.float32),
        lax.psum_scatter(
            grads[1].astype(jnp.bfloat16), "seq", scatter_dimension=2, tiled=True
        ).astype(jnp.float32),
        lax.psum_scatter(
            grads[2].astype(jnp.bfloat16), "seq", scatter_dimension=1, tiled=True
        ).astype(jnp.float32),
        lax.psum_scatter(
            grads[3].astype(jnp.bfloat16), "seq", scatter_dimension=1, tiled=True
        ).astype(jnp.float32),
        lax.psum_scatter(
            grads[4].astype(jnp.bfloat16), "seq", scatter_dimension=2, tiled=True
        ).astype(jnp.float32),
    )


def reduce_small(grads):
    return lax.psum((grads[0], grads[1], grads[2]), "seq")


def body(
    stream_in,
    norm_gain,
    in_proj,
    conv_taps,
    out_proj,
    ffn_gain,
    gate_proj,
    up_proj,
    down_proj,
    out_grad,
):
    f32 = jnp.float32
    bf16 = jnp.bfloat16
    width = in_proj.shape[-1]
    offset = lax.axis_index("tp") * width
    hidden = stream_in.astype(f32)
    kept = []
    for layer in range(LAYERS):
        gain_one = norm_gain[layer].astype(f32)
        gain_two = ffn_gain[layer].astype(f32)
        taps = conv_taps[layer].astype(f32)
        rate_one = norm_rate(hidden)
        normed_one = hidden * rate_one
        first = (normed_one * gain_one).astype(bf16)
        proj = jnp.einsum("msd,dkc->mskc", first, in_proj[layer], preferred_element_type=f32)
        bgate = proj[:, :, 0]
        cgate = proj[:, :, 1]
        xinput = proj[:, :, 2]
        mixed = (bgate * xinput).astype(bf16)
        prior = passed_along(mixed[:, -2:], "seq", 1)
        extended = jnp.concatenate([prior, mixed], axis=1).astype(f32)
        conved = (
            taps[0] * extended[:, :-2] + taps[1] * extended[:, 1:-1] + taps[2] * extended[:, 2:]
        )
        gated = (cgate * conved).astype(bf16)
        partial_out = jnp.einsum("msc,cd->msd", gated, out_proj[layer], preferred_element_type=f32)
        middle = hidden + lax.psum(partial_out, "tp")
        rate_two = norm_rate(middle)
        normed_two = middle * rate_two
        second = (normed_two * gain_two).astype(bf16)
        gate_val = jnp.einsum("msd,df->msf", second, gate_proj[layer], preferred_element_type=f32)
        up_val = jnp.einsum("msd,df->msf", second, up_proj[layer], preferred_element_type=f32)
        sigma = jax.nn.sigmoid(gate_val)
        silu_val = gate_val * sigma
        act = (silu_val * up_val).astype(bf16)
        partial_ffn = jnp.einsum("msf,fd->msd", act, down_proj[layer], preferred_element_type=f32)
        kept.append(
            (
                rate_one,
                normed_one,
                first,
                bgate,
                cgate,
                xinput,
                extended,
                conved,
                gated,
                rate_two,
                normed_two,
                second,
                gate_val,
                up_val,
                sigma,
                silu_val,
                act,
            )
        )
        hidden = middle + lax.psum(partial_ffn, "tp")
    grad_h = out_grad.astype(f32)
    collected = [None] * LAYERS
    for layer in reversed(range(LAYERS)):
        (
            rate_one,
            normed_one,
            first,
            bgate,
            cgate,
            xinput,
            extended,
            conved,
            gated,
            rate_two,
            normed_two,
            second,
            gate_val,
            up_val,
            sigma,
            silu_val,
            act,
        ) = kept[layer]
        gain_one = norm_gain[layer].astype(f32)
        gain_two = ffn_gain[layer].astype(f32)
        taps = conv_taps[layer].astype(f32)
        grad_f = grad_h.astype(bf16)
        grad_act = jnp.einsum("msd,fd->msf", grad_f, down_proj[layer], preferred_element_type=f32)
        down_g = jnp.einsum("msf,msd->fd", act, grad_f, preferred_element_type=f32)
        grad_gate = (grad_act * up_val * sigma * (1.0 + gate_val * (1.0 - sigma))).astype(bf16)
        grad_up = (grad_act * silu_val).astype(bf16)
        part_two = jnp.einsum(
            "msf,df->msd", grad_gate, gate_proj[layer], preferred_element_type=f32
        )
        part_two = part_two + jnp.einsum(
            "msf,df->msd", grad_up, up_proj[layer], preferred_element_type=f32
        )
        gate_g = jnp.einsum("msd,msf->df", second, grad_gate, preferred_element_type=f32)
        up_g = jnp.einsum("msd,msf->df", second, grad_up, preferred_element_type=f32)
        grad_two = lax.psum(part_two.astype(jnp.bfloat16), "tp").astype(jnp.float32)
        ffn_gain_g = jnp.sum(grad_two * normed_two, axis=(0, 1))
        grad_mid = grad_h + norm_back(grad_two, gain_two, normed_two, rate_two)
        grad_o = grad_mid.astype(bf16)
        grad_gated = jnp.einsum("msd,cd->msc", grad_o, out_proj[layer], preferred_element_type=f32)
        out_g = jnp.einsum("msc,msd->cd", gated, grad_o, preferred_element_type=f32)
        grad_conv = grad_gated * cgate
        grad_cgate = grad_gated * conved
        after = passed_along(grad_conv[:, :2], "seq", -1)
        grad_ext = jnp.concatenate([grad_conv, after], axis=1)
        grad_mixed = (
            taps[2] * grad_ext[:, :-2] + taps[1] * grad_ext[:, 1:-1] + taps[0] * grad_ext[:, 2:]
        )
        count = grad_conv.shape[1]
        conv_g = jnp.stack(
            [jnp.sum(grad_conv * extended[:, k : k + count], axis=(0, 1)) for k in range(3)], axis=0
        )
        grad_proj = jnp.stack([grad_mixed * xinput, grad_cgate, grad_mixed * bgate], axis=2).astype(
            bf16
        )
        part_one = jnp.einsum(
            "mskc,dkc->msd", grad_proj, in_proj[layer], preferred_element_type=f32
        )
        in_g = jnp.einsum("msd,mskc->dkc", first, grad_proj, preferred_element_type=f32)
        grad_one = lax.psum(part_one.astype(jnp.bfloat16), "tp").astype(jnp.float32)
        norm_gain_g = jnp.sum(grad_one * normed_one, axis=(0, 1))
        grad_h = grad_mid + norm_back(grad_one, gain_one, normed_one, rate_one)
        norm_piece = lax.dynamic_slice_in_dim(norm_gain_g, offset, width)
        ffn_piece = lax.dynamic_slice_in_dim(ffn_gain_g, offset, width)
        small = (norm_piece, conv_g, ffn_piece)
        large = (in_g, out_g, gate_g, up_g, down_g)
        collected[layer] = (small, large)
    norm_stack = jnp.stack([c[0][0] for c in collected], axis=0)
    conv_stack = jnp.stack([c[0][1] for c in collected], axis=0)
    ffn_stack = jnp.stack([c[0][2] for c in collected], axis=0)
    large_stack = tuple((jnp.stack([c[1][i] for c in collected], axis=0) for i in range(5)))
    large_stack = reduce_weights(large_stack)
    norm_stack, conv_stack, ffn_stack = reduce_small((norm_stack, conv_stack, ffn_stack))
    stream_out = hidden.astype(bf16)
    in_grad, out_grad_w, gate_grad, up_grad, down_grad = large_stack
    return (
        stream_out,
        grad_h,
        norm_stack,
        in_grad,
        conv_stack,
        out_grad_w,
        ffn_stack,
        gate_grad,
        up_grad,
        down_grad,
    )


VMEM_BYTES = 64 * 2**20
MESH = pl.DeviceIdType.MESH
f32 = jnp.float32
bf16 = jnp.bfloat16
NN = (((1,), (0,)), ((), ()))
NT = (((1,), (1,)), ((), ()))
ORDERS = ((0, 1, 2), (1, 0, 2))
SLOTS = 4
WIDE = 1024
N1, N2, DF, DO = range(4)


def rem(a, b):
    return a % b if isinstance(a, int) else lax.rem(a, b)


def div(a, b):
    return a // b if isinstance(a, int) else lax.div(a, b)


def cases(value, branches):
    for low, high, fn in branches:
        if isinstance(value, int):
            if low <= value < high:
                fn()
        else:
            pl.when((value >= low) & (value < high))(fn)


def mm(lhs, rhs, dims=NN):
    return lax.dot_general(lhs, rhs, dims, preferred_element_type=f32)


def fused(
    dims,
    stream_in, norm_gain, win, taps, wout, ffn_gain, wgate, wup, wdown, out_grad,
    out_stream, out_sgrad, out_norm, out_in, out_conv, out_out, out_ffn, out_gate, out_up, out_down,
    L, R, WIN, WOUT, WGU, WD, H, DH, RATE, PB, PR, XR,
    GA, GB, RA0, RA1, RA2, RB0, RB1, RB2, RT, FO, FT, RZ, zs, zr, SM,
    EXT, DYE, CF, HALO, HALO2, DHALO, GAIN, TAPS, TAPS2, GACC, CACC, SMR,
    NORM_OUT, FFN_OUT, CONV_OUT,
    load_sem, ps, pr, xs, xr, ags, agr, hs, dhs, hr, hs2, hr2, gs, gr, rss, rsr, fos, oss, sts, str_, sms, smr,
):
    M, TOK, D, C, F, U = dims
    half = TOK // 2
    CS, CA, CP, CZ = 0, F, 3 * F, 3 * F + 3 * C
    PER = (CZ + C) // U
    first_units = [(1, 0, 128), (1, 128, U - 128)]
    TURN = PER + 2
    table = first_units + [(1, k * U, U) for k in range(1, PER)] + [(1, PER * U, CZ + C - PER * U)]
    table += [(0, k * U, U) for k in range(PER)]
    table += [(0, k, 128) for k in range(PER * U, CZ + C, 128)]
    UNITS = len(table)
    LAST = UNITS - 1
    whole = (128, 128, 0)
    splits = {w: (w, w - w // 4, w // 4) for w in (128, 256, U)}
    seq = lax.axis_index("seq")
    tp = lax.axis_index("tp")
    n = lax.axis_size("seq")
    core = lax.rem(tp, 2)
    xi = lax.div(tp, 2)
    sib = {"seq": seq, "tp": tp + 1 - 2 * core}
    xpart = {"seq": seq, "tp": tp + 2 - 4 * xi}
    bits = [lax.rem(lax.div(seq, 1 << k), 2) for k in range(3)]
    parts = [{"seq": seq + (1 << k) - 2 * (1 << k) * bits[k], "tp": tp} for k in range(3)]
    nxt = {"seq": lax.rem(seq + 1, n), "tp": tp}
    prv = {"seq": lax.rem(seq + n - 1, n), "tp": tp}
    mine = pl.ds(pl.multiple_of(core * half, half), half)
    theirs = pl.ds(pl.multiple_of((1 - core) * half, half), half)

    def remote(src, dst, ssem, rsem, dev):
        return pltpu.make_async_remote_copy(
            src_ref=src, dst_ref=dst, send_sem=ssem, recv_sem=rsem, device_id=dev, device_id_type=MESH
        )

    def load_stream(m):
        return pltpu.make_async_copy(stream_in.at[m], L.at[0, N1, m], load_sem.at[m])

    def load_conv(l):
        return [
            pltpu.make_async_copy(win.at[l, k], WIN.at[:, pl.ds(k * C, C)], load_sem.at[4 + k])
            for k in range(3)
        ] + [pltpu.make_async_copy(wout.at[l], WOUT, load_sem.at[7])]

    def load_ffn(l):
        return [
            pltpu.make_async_copy(
                src.at[l, :, pl.ds(t * U, U)], WGU.at[:, pl.ds((2 * t + i) * U, U)], load_sem.at[10 + 2 * t + i]
            )
            for t in range(F // U)
            for i, src in enumerate((wgate, wup))
        ]

    def load_down(l):
        return pltpu.make_async_copy(wdown.at[l], WD, load_sem.at[9])

    load_og = pltpu.make_async_copy(out_grad, L.at[1, DF], load_sem.at[8])
    for cp in load_conv(0) + [load_stream(m) for m in range(M)]:
        cp.start()

    barrier = pltpu.get_barrier_semaphore()
    zcross = {"seq": n - 1 - seq + 2 * lax.rem(seq, 2) - 1, "tp": tp}
    others = [sib, xpart, nxt, prv, zcross] + parts
    for dev in others:
        pl.semaphore_signal(barrier, inc=1, device_id=dev, device_id_type=MESH)

    GAIN[0] = norm_gain[...].astype(f32)
    GAIN[1] = ffn_gain[...].astype(f32)
    GAIN[2] = 1.0 / norm_gain[...].astype(f32)
    GAIN[3] = 1.0 / ffn_gain[...].astype(f32)
    TAPS[...] = taps[...].astype(f32)
    GACC[...] = jnp.zeros_like(GACC)
    CACC[...] = jnp.zeros_like(CACC)

    pl.semaphore_wait(barrier, len(others))

    zpos, ypos = lax.div(seq, 2), lax.rem(seq, 2)
    zfar, znear = lax.rem(zpos + 2, 4), zpos + 1 - 2 * lax.rem(zpos, 2)
    strip = D // 8

    def piece(s, z):
        rows = pl.ds(pl.multiple_of(ypos * strip, strip), strip)
        if s < 3:
            return L.at[0, DO, 1 + s, rows, pl.ds(pl.multiple_of(z * TOK, TOK), TOK)]
        return L.at[0, DO, 0, pl.ds(pl.multiple_of(ypos * strip + z * (C // 8), 16), C // 8)]

    def gathers(s, step):
        def send(i, src, dst, dev):
            return remote(src, dst, gs.at[s, i], gr.at[s, i], dev)

        if step == 0:
            if s < 3:
                src = win.at[1, s, pl.ds(pl.multiple_of(zpos * TOK + ypos * strip, strip), strip)]
            else:
                src = wout.at[1, pl.ds(pl.multiple_of(ypos * strip + zpos * (C // 8), 16), C // 8)]
            return [send(0, src, piece(s, zpos), xpart)]
        if step == 1:
            return [send(1, piece(s, zpos), piece(s, zpos), parts[2])]
        if step == 2:
            return [send(2 + i, piece(s, z), piece(s, z), parts[1]) for i, z in enumerate((zpos, zfar))]
        half_ref = L.at[0, DO, (1 + s) % 4, pl.ds(pl.multiple_of(ypos * strip, strip), strip)]
        return [send(4, half_ref, half_ref, parts[0])]

    def gather_at(j):
        for s in range(4):
            for step, when in enumerate((s, s + 2, s + 4, 7 + 2 * s)):
                if j == when:
                    for cp in gathers(s, step):
                        cp.wait()
                    if step < 3:
                        for cp in gathers(s, step + 1):
                            cp.start()

    def gather_dyn(base, m, late):
        for i in range(M):
            pl.when(m == i)(functools.partial(gather_at, base + 2 * i + late))

    for s in range(4):
        for cp in gathers(s, 0):
            cp.start()
    tap_copy = remote(TAPS, TAPS2, hs2.at[1], hr2.at[M], xpart)
    tap_copy.start()

    def pcopy(m):
        return remote(PB.at[m, theirs], PR.at[m], ps.at[m], pr.at[m], sib)

    def xcopy(m):
        return remote(PB.at[m, mine], XR.at[m], xs.at[m], xr.at[m], xpart)

    def mid(m):
        pcopy(m).wait()

        def chunk(i, _):
            off = pl.multiple_of(i * 32, 32)
            rows = pl.ds(pl.multiple_of(core * half + off, 32), 32)
            got = PR[m, pl.ds(off, 32)].astype(f32) + PB[m, rows].astype(f32)
            PB[m, rows] = got.astype(bf16)
            return 0

        lax.fori_loop(0, half // 32, chunk, 0, unroll=True)
        xcopy(m).start()

    def agcopy(l, kind, m):
        ref = L.at[l, kind, m, mine]
        return remote(ref, ref, ags.at[m], agr.at[m], sib)

    def rows_loop(m, body, received=XR):
        def chunk(i, _):
            off = pl.multiple_of(i * 32, 32)
            rows = pl.ds(pl.multiple_of(core * half + off, 32), 32)
            total = PB[m, rows].astype(f32) + received[m, pl.ds(off, 32)].astype(f32)
            body(pl.ds(off, 32), rows, total)
            return 0

        lax.fori_loop(0, half // 32, chunk, 0, unroll=True)

    def rate_of(val):
        return lax.rsqrt(jnp.mean(val * val, axis=-1, keepdims=True) + EPS)

    def finish_norm(l, which, kind, m, within=False):
        if within:
            pcopy(m).wait()
        else:
            xcopy(m).wait()
        gain = GAIN[which, l : l + 1, :]

        def body(loc, rows, total):
            hid = H[m, loc] + total
            H[m, loc] = hid
            rate = rate_of(hid)
            RATE[m, loc, 2 * l + which : 2 * l + which + 1] = rate
            L[l, kind, m, rows] = (hid * rate * gain).astype(bf16)

        rows_loop(m, body, PR if within else XR)
        agcopy(l, kind, m).start()

    def stream_copies(m):
        ref = PB.at[m, mine]
        return (
            pltpu.make_async_copy(ref, out_stream.at[m, mine], oss.at[m]),
            remote(ref, out_stream.at[m, mine], sts.at[m], str_.at[m], sib),
        )

    def finish_stream(m):
        xcopy(m).wait()

        def body(loc, rows, total):
            PB[m, rows] = (H[m, loc] + total).astype(bf16)

        rows_loop(m, body)
        for cp in stream_copies(m):
            cp.start()

    def norm_back(l, which, kind, m, emit):
        xcopy(m).wait()
        gain = GAIN[which, l : l + 1, :]
        inv = GAIN[2 + which, l : l + 1, :]

        def body(loc, rows, total):
            nrm = L[l, kind, m, rows].astype(f32) * inv
            prod = total * nrm
            GACC[2 * which + l] += prod[0:8] + prod[8:16] + prod[16:24] + prod[24:32]
            mean = jnp.mean(prod * gain, axis=-1, keepdims=True)
            emit(loc, rows, RATE[m, loc, 2 * l + which : 2 * l + which + 1] * (total * gain - nrm * mean))

        rows_loop(m, body)

    def finish_dn2(l, m):
        def emit(loc, rows, delta):
            prev = L[1, DF, m, rows].astype(f32) if l == 1 else DH[m, loc]
            new = prev + delta
            DH[m, loc] = new
            L[l, DO, m, rows] = new.astype(bf16)

        norm_back(l, 1, N2, m, emit)
        agcopy(l, DO, m).start()

    def finish_dn1(l, m):
        def emit(loc, rows, delta):
            new = DH[m, loc] + delta
            if l == 1:
                DH[m, loc] = new
                L[0, DF, m, rows] = new.astype(bf16)
            else:
                PB[m, rows] = new.astype(bf16)

        norm_back(l, 0, N1, m, emit)
        if l == 1:
            agcopy(0, DF, m).start()
        else:
            for cp in grad_copies(m):
                cp.start()

    def grad_copies(m):
        return (
            pltpu.make_async_copy(PB.at[m, mine], out_sgrad.at[m, mine], oss.at[m]),
            remote(PB.at[m, mine], out_sgrad.at[m, mine], ags.at[m], agr.at[m], sib),
        )

    def put_partial(m, tile):
        def step(j, _):
            cols = pl.ds(pl.multiple_of(j * WIDE, WIDE), WIDE)
            PB[m, :, cols] = tile(cols).astype(bf16)
            return 0

        lax.fori_loop(0, D // WIDE, step, 0)
        pcopy(m).start()

    def halo_rows(m):
        return pl.ds(m * 8 if isinstance(m, int) else pl.multiple_of(m * 8, 8), 8)

    def hcopy(l, m):
        return remote(EXT.at[pl.ds(TOK, 8)], HALO.at[l, halo_rows(m)], hs, hr.at[0, l, m], nxt)

    def dhcopy(l, m):
        return remote(DYE.at[rem(m, 2), pl.ds(0, 8)], DHALO.at[l, m], dhs.at[rem(m, 2)], hr.at[1, l, m], prv)

    def hcopy2(m):
        return remote(DYE.at[1, pl.ds(TOK, 8)], HALO2.at[m], hs2.at[0], hr2.at[m], nxt)

    def tap(l, k):
        return TAPS[k, l : l + 1, :]

    def conv_of(ext, halo, taps_ref, l):
        ext[0:8] = jnp.where(seq == 0, 0.0, halo)
        t = [taps_ref[k, l : l + 1, :] for k in range(3)]
        return t[0] * ext[6 : 6 + TOK] + t[1] * ext[7 : 7 + TOK] + t[2] * ext[8 : 8 + TOK]

    def conv_now(l, m):
        return conv_of(EXT, HALO[l, halo_rows(m)], TAPS, l)

    def other_in(k):
        blocks = [L[0, DO, 1 + k, :, r * TOK : (r + 1) * TOK] for r in range(D // TOK)]
        return jnp.concatenate(blocks, axis=0)

    first_halos = remote(DYE.at[1, pl.ds(0, 8 * M)], HALO.at[0], hs, hr.at[0, 0, 0], nxt)

    def send_first_halos():
        val = jnp.concatenate([L[0, N1, m, TOK - 16 : TOK] for m in range(M)], axis=0).astype(f32)
        p = mm((val * rate_of(val) * GAIN[0, 0:1, :]).astype(bf16), WIN[...])
        bx = (p[:, 0:C] * p[:, 2 * C : 3 * C]).astype(bf16).astype(f32)
        for m in range(M):
            DYE[1, 8 * m : 8 * m + 8] = bx[16 * m + 8 : 16 * m + 16]
        first_halos.start()

    def conv_fwd_a(l, m):
        if l == 0:
            gain = GAIN[0, 0:1, :]
            hid = L[0, N1, m, mine].astype(f32)
            H[m] = hid
            RATE[m, :, 0:1] = rate_of(hid)

            def chunk(i, _):
                rows = pl.ds(pl.multiple_of(i * 32, 32), 32)
                val = L[0, N1, m, rows].astype(f32)
                L[0, N1, m, rows] = (val * rate_of(val) * gain).astype(bf16)
                return 0

            lax.fori_loop(0, TOK // 32, chunk, 0)
        else:
            agcopy(1, N1, m).wait()
        first = L[l, N1, m]
        p = mm(first, WIN[...])
        bgate, cgate, xin = p[:, 0:C], p[:, C : 2 * C], p[:, 2 * C : 3 * C]
        R[l, m, :, CP : CP + 3 * C] = p.astype(bf16)
        EXT[8 : 8 + TOK] = (bgate * xin).astype(bf16).astype(f32)
        DYE[0, 0:TOK] = cgate
        if l == 1:
            hcopy(l, m).start()
            p = mm(first, jnp.concatenate([other_in(k) for k in range(3)], axis=1))
            DYE[1, 8 : 8 + TOK] = (p[:, 0:C] * p[:, 2 * C : 3 * C]).astype(bf16).astype(f32)
            hcopy2(m).start()
            CF[...] = p[:, C : 2 * C]

    def conv_fwd_b(l, m):
        if l == 0:
            pl.when(m == 0)(lambda: first_halos.wait())
        else:
            hcopy(l, m).wait()
        gated = (DYE[0, 0:TOK] * conv_now(l, m)).astype(bf16)
        R[l, m, :, CZ : CZ + C] = gated
        if l == 0:
            put_partial(m, lambda cols: mm(R[l, m, :, CZ : CZ + C], WOUT[:, cols]))
        else:
            hcopy2(m).wait()
            L[0, DF, m, :, 0:C] = (CF[...] * conv_of(DYE.at[1], HALO2[m], TAPS2, l)).astype(bf16)
            put_partial(
                m,
                lambda cols: mm(R[l, m, :, CZ : CZ + C], WOUT[:, cols])
                + mm(L[0, DF, m, :, 0:C], L[0, DO, 0, :, cols]),
            )

    def down_back(m):
        ds = mm(L[1, DF, m], WD[...], NT).astype(bf16)
        for t in range(F // U):
            R[1, m, :, CA + (2 * t + 1) * U : CA + (2 * t + 2) * U] = ds[:, t * U : (t + 1) * U]

    def ffn_fwd(l, m, low=0, high=F // U):
        def step(t):
            off, off2 = t * U, 2 * t * U
            ab = mm(L[l, N2, m], WGU[:, pl.ds(off2, 2 * U)])
            a, b = ab[:, 0:U], ab[:, U : 2 * U]
            sig = jax.nn.sigmoid(a)
            silu = a * sig
            R[l, m, :, pl.ds(CS + off, U)] = (silu * b).astype(bf16)
            if l == 0:
                R[l, m, :, pl.ds(CA + off2, 2 * U)] = ab.astype(bf16)
            else:
                ds = R[l, m, :, pl.ds(CA + U + off2, U)].astype(f32)
                R[l, m, :, pl.ds(CA + off2, U)] = (ds * b * sig * (1.0 + a * (1.0 - sig))).astype(bf16)
                R[l, m, :, pl.ds(CA + U + off2, U)] = (ds * silu).astype(bf16)

        for t in range(low, high):
            step(t)

    def ffn_down(l, m):
        put_partial(m, lambda cols: mm(R[l, m, :, CS : CS + F], WD[:, cols]))

    def ffn_bwd(l, m):
        if l == 0:
            def step(t):
                off, off2 = t * U, 2 * t * U
                a = R[l, m, :, pl.ds(CA + off2, U)].astype(f32)
                b = R[l, m, :, pl.ds(CA + U + off2, U)].astype(f32)
                sig = jax.nn.sigmoid(a)
                ds = mm(L[l, DF, m], WD[pl.ds(off, U), :], NT)
                R[l, m, :, pl.ds(CA + off2, U)] = (ds * b * sig * (1.0 + a * (1.0 - sig))).astype(bf16)
                R[l, m, :, pl.ds(CA + U + off2, U)] = (ds * a * sig).astype(bf16)

            for t in range(F // U):
                step(t)
        put_partial(m, lambda cols: mm(R[l, m, :, CA : CA + 2 * F], WGU[cols, :], NT))

    def conv_bwd_a(l, m):
        dz = mm(L[l, DO, m], WOUT[...], NT)
        bgate = R[l, m, :, CP : CP + C].astype(f32)
        xin = R[l, m, :, CP + 2 * C : CP + 3 * C].astype(f32)
        EXT[8 : 8 + TOK] = (bgate * xin).astype(bf16).astype(f32)
        dy = dz * R[l, m, :, CP + C : CP + 2 * C].astype(f32)
        DYE[rem(m, 2), 0:TOK] = dy
        dhcopy(l, m).start()
        R[l, m, :, CP + C : CP + 2 * C] = (dz * conv_now(l, m)).astype(bf16)
        for k in range(3):
            prod = dy * EXT[6 + k : 6 + k + TOK]
            CACC[l, k] += jnp.sum(prod.reshape(TOK // 8, 8, C), axis=0)

    def conv_bwd_b(l, m):
        dhcopy(l, m).wait()
        s = rem(m, 2)
        DYE[s, TOK : TOK + 8] = jnp.where(seq == n - 1, 0.0, DHALO[l, m])
        dbx = (
            tap(l, 2) * DYE[s, 0:TOK] + tap(l, 1) * DYE[s, 1 : 1 + TOK] + tap(l, 0) * DYE[s, 2 : 2 + TOK]
        )
        bgate = R[l, m, :, CP : CP + C].astype(f32)
        xin = R[l, m, :, CP + 2 * C : CP + 3 * C].astype(f32)
        R[l, m, :, CP : CP + C] = (dbx * xin).astype(bf16)
        R[l, m, :, CP + 2 * C : CP + 3 * C] = (dbx * bgate).astype(bf16)
        put_partial(m, lambda cols: mm(R[l, m, :, CP : CP + 3 * C], WIN[cols, :], NT))

    lanes = ((GA, (RA0, RA1, RA2)), (GB, (RB0, RB1, RB2)))

    def keep(lane, step):
        b = [bits[o] for o in ORDERS[lane]]
        return [b[0] * 4, b[0] * 4 + b[1] * 2, b[0] * 4 + b[1] * 2 + b[2]][step]

    def unit_at(t):
        if isinstance(t, int):
            return table[t][:2]
        k = jnp.where(t < TURN, t - 1, t - TURN)
        return jnp.where(t < TURN, 1, 0), jnp.where(t < 2, t * 128, k * U)

    def sized(t, fn):
        if isinstance(t, int):
            fn(splits[table[t][2]])
            return
        pl.when(t == 0)(lambda: fn(splits[128]))
        pl.when((t == 1) | (t == TURN - 1))(lambda: fn(splits[256]))
        pl.when((t > 1) & (t != TURN - 1))(lambda: fn(splits[U]))

    def rs_copy(lane, step, t, rows):
        G, recv = lanes[lane]
        slot = rem(t, SLOTS)
        size = 4 >> step
        o = ORDERS[lane][step]
        off = keep(lane, step) + size - 2 * size * bits[o]
        cut = pl.ds(0, rows[1 + lane])
        return remote(
            G.at[slot, pl.ds(off, size), cut], recv[step].at[slot, :, cut],
            rss.at[lane, step, slot], rsr.at[lane, step, slot], parts[o],
        )

    def rs_gen(t):
        l, start = unit_at(t)
        kind = jnp.where(start < CA, DF, jnp.where(start < CP, N2, jnp.where(start < CZ, N1, DO)))
        slot = rem(t, SLOTS)

        def make(rows):
            wide, cut, _ = rows
            cols = pl.ds(start if isinstance(start, int) else pl.multiple_of(start, 128), wide)
            for m in range(M):
                RT[0:wide, m * TOK : (m + 1) * TOK] = R[l, m, :, cols].T

            def step(j, _):
                src = L[l, kind, :, :, pl.ds(pl.multiple_of(j * 512, 512), 512)].reshape(M * TOK, 512)
                res = mm(RT[0:wide], src).astype(bf16)
                for q in range(4):
                    lo, y = q // 2, q % 2
                    block = res[:, q * 128 : (q + 1) * 128]
                    GA[slot, y * 4 + lo * 2 + j, 0:cut] = block[:cut]
                    if cut < wide:
                        GB[slot, lo * 4 + y * 2 + j, 0 : wide - cut] = block[cut:]
                return 0

            lax.fori_loop(0, D // 512, step, 0)
            for lane in range(2):
                if rows[1 + lane]:
                    rs_copy(lane, 0, t, rows).start()

        if isinstance(t, int) and t == LAST:
            make(whole)
        else:
            sized(t, make)

    def last_copies():
        base = bits[0] * 4
        for i, (flip, dev) in enumerate(((1, parts[2]), (2, parts[1]), (3, zcross))):
            to = (bits[1] if flip < 2 else 1 - bits[1]) * 2 + (bits[2] if flip == 2 else 1 - bits[2])
            yield remote(GA.at[LAST % SLOTS, base + to, pl.ds(0, 128)], RZ.at[i], zs.at[i], zr.at[i], dev)

    def last_add():
        slot = LAST % SLOTS
        rs_copy(0, 0, LAST, whole).wait()
        base = keep(0, 0)
        for i in range(4):
            GA[slot, base + i, 0:128] = (
                GA[slot, base + i, 0:128].astype(f32) + RA0[slot, i, 0:128].astype(f32)
            ).astype(bf16)
        for cp in last_copies():
            cp.start()

    def last_sum():
        unit_wait(LAST - 1)
        for cp in last_copies():
            cp.wait()
        total = GA[LAST % SLOTS, keep(0, 2), 0:128].astype(f32) + RZ[0].astype(f32)
        FO[0:128] = (total + (RZ[1].astype(f32) + RZ[2].astype(f32))).astype(bf16)
        for cp in unit_copies(LAST, 5, 128):
            cp.start()

    def rs_add(step, t):
        slot = rem(t, SLOTS)

        def go(rows):
            for lane in range(2):
                G, recv = lanes[lane]
                rs_copy(lane, step, t, rows).wait()
                base = keep(lane, step)
                cut = rows[1 + lane]

                def add(i, _):
                    G[slot, base + i, 0:cut] = (
                        G[slot, base + i, 0:cut].astype(f32) + recv[step][slot, i, 0:cut].astype(f32)
                    ).astype(bf16)
                    return 0

                lax.fori_loop(0, 4 >> step, add, 0)
                rs_copy(lane, step + 1, t, rows).start()

        sized(t, go)

    def unit_copies(t, which, wide):
        l, start = unit_at(t)

        def at(off):
            return pl.ds(off if isinstance(off, int) else pl.multiple_of(off, 128), wide)

        tile = at(div(start - CA, 2 * U) * U)
        if which == 0:
            pairs = [(FO.at[pl.ds(0, wide)], out_down.at[l, at(start)])]
        elif which == 1:
            pairs = [(FT, out_gate.at[l, :, tile])]
        elif which == 2:
            pairs = [(FT, out_up.at[l, :, tile])]
        elif which == 3:
            pairs = [(FT.at[:, pl.ds(0, C)], out_in.at[l, 0]),
                     (FT.at[:, pl.ds(C, U - C)], out_in.at[l, 1, :, pl.ds(0, U - C)])]
        elif which == 4:
            pairs = [(FT.at[:, pl.ds(0, 2 * C - U)], out_in.at[l, 1, :, pl.ds(U - C, 2 * C - U)]),
                     (FT.at[:, pl.ds(2 * C - U, C)], out_in.at[l, 2])]
        else:
            pairs = [(FO.at[pl.ds(0, wide)], out_out.at[l, at(start - CZ)])]
        return [pltpu.make_async_copy(a, b, fos.at[i]) for i, (a, b) in enumerate(pairs)]

    def by_target(t, fn):
        if isinstance(t, int):
            _, start, wide = table[t]
            if start < CA:
                which = 0
            elif start < CP:
                which = 1 + (start - CA) // U % 2
            else:
                which = 5 if start >= CZ else 3 + (start - CP) // U
            fn(which, wide)
            return
        _, start = unit_at(t)
        pl.when(t == 0)(lambda: fn(0, 128))
        pl.when(t == 1)(lambda: fn(0, 256))
        pl.when((t > 1) & (start < CA))(lambda: fn(0, U))
        for i in range(2):
            odd = lax.rem(lax.div(start, U) + CA // U, 2) == i
            pl.when((start >= CA) & (start < CP) & odd)(functools.partial(fn, 1 + i, U))
            pl.when(start == CP + i * U)(functools.partial(fn, 3 + i, U))
        pl.when(start == CZ)(lambda: fn(5, 256))

    def unit_wait(t):
        def go(which, wide):
            for cp in unit_copies(t, which, wide):
                cp.wait()

        by_target(t, go)

    def rs_last(t):
        slot = rem(t, SLOTS)
        if isinstance(t, int):
            if t >= 1:
                unit_wait(t - 1)
        else:
            pl.when(t >= 1)(lambda: unit_wait(t - 1))

        def go(rows):
            wide, cut, _ = rows
            for lane in range(2):
                rs_copy(lane, 2, t, rows).wait()
            FO[0:cut] = (GA[slot, keep(0, 2), 0:cut].astype(f32) + RA2[slot, 0, 0:cut].astype(f32)).astype(bf16)
            FO[cut:wide] = (
                GB[slot, keep(1, 2), 0 : wide - cut].astype(f32) + RB2[slot, 0, 0 : wide - cut].astype(f32)
            ).astype(bf16)

        sized(t, go)

        def send(which, wide):
            if which in (1, 2, 3, 4):
                FT[...] = FO[...].T
            for cp in unit_copies(t, which, wide):
                cp.start()

        by_target(t, send)

    def tick_gen(t):
        if not isinstance(t, int) or t < UNITS:
            rs_gen(t)

    def tick_rest(t):
        steps = (functools.partial(rs_add, 0), functools.partial(rs_add, 1), rs_last)
        for lag, fn in enumerate(steps, 1):
            if isinstance(t, int):
                if 0 <= t - lag < LAST:
                    fn(t - lag)
                elif t - lag == LAST and lag == 1:
                    last_add()
            else:
                pl.when(t >= lag)(functools.partial(fn, t - lag))

    def behind(prev, cur, m):
        if prev is None:
            pl.when(m > 0)(lambda: mid(m - 1))
        else:
            mid(lax.rem(m + M - 1, M))
            pl.when(m < 2)(lambda: prev(m + M - 2))
        pl.when(m >= 2)(lambda: cur(m - 2))

    def phase(prev, cur, first, second=None, tick=None, ahead=None):
        def step(m, _):
            if ahead is not None:
                ahead(m)
            if tick is not None:
                tick_gen(tick + m)
            if first is not None:
                first(m)
            behind(prev, cur, m)
            if second is not None:
                second(m)
            if tick is not None:
                tick_rest(tick + m)
            return 0

        lax.fori_loop(0, M, step, 0)

    def arrived(copies):
        for cp in copies:
            cp.wait()

    end_o0 = functools.partial(finish_norm, 0, 1, N2)
    end_f0 = functools.partial(finish_norm, 1, 0, N1)
    end_o1 = functools.partial(finish_norm, 1, 1, N2, within=True)
    end_n1 = functools.partial(finish_dn2, 1)
    end_c1 = functools.partial(finish_dn1, 1)
    end_n0 = functools.partial(finish_dn2, 0)
    end_c0 = functools.partial(finish_dn1, 0)

    arrived(load_conv(0) + [load_stream(m) for m in range(M)])
    send_first_halos()
    for cp in [load_og, load_down(1)] + load_ffn(0):
        cp.start()

    conv_fwd_a(0, jnp.int32(0))
    gather_at(0)

    def o0(m, _):
        conv_fwd_b(0, m)
        pl.when(m < M - 1)(lambda: conv_fwd_a(0, m + 1))
        pl.when(m >= 2)(lambda: end_o0(m - 2))
        gather_dyn(1, m, 0)

        @pl.when(m == 0)
        def _():
            arrived([load_og, load_down(1)])

        mid(m)
        down_back(m)
        gather_dyn(1, m, 1)
        return 0

    lax.fori_loop(0, M, o0, 0)
    for cp in [load_down(0)] + load_conv(1):
        cp.start()
    arrived(load_ffn(0))

    def f0(m, _):
        agcopy(0, N2, m).wait()
        ffn_fwd(0, m)
        pl.when(m == 0)(lambda: load_down(0).wait())
        ffn_down(0, m)
        gather_dyn(2 * M + 1, m, 0)

        @pl.when(m == M - 1)
        def _():
            arrived(load_conv(1) + [tap_copy])
            conv_fwd_a(1, 0)

        pl.when(m < 2)(lambda: end_o0(m + M - 2))
        pl.when(m >= 2)(lambda: end_f0(m - 2))
        mid(m)
        gather_dyn(2 * M + 1, m, 1)
        return 0

    lax.fori_loop(0, M, f0, 0)
    for cp in load_ffn(1):
        cp.start()

    def ffn_both(m):
        agcopy(1, N2, m).wait()
        ffn_fwd(1, m)

    def o1(m, _):
        conv_fwd_b(1, m)
        pl.when(m < M - 1)(lambda: conv_fwd_a(1, m + 1))
        end_o1(m)
        pl.when(m == 1)(lambda: arrived(load_ffn(1)))
        pl.when(m >= 1)(lambda: ffn_both(m - 1))
        pl.when(m < 2)(lambda: end_f0(m + 2))
        return 0

    lax.fori_loop(0, M, o1, 0)
    agcopy(1, N2, M - 1).wait()
    ffn_fwd(1, M - 1, 0, 1)
    tick_gen(0)
    ffn_fwd(1, M - 1, 1)

    def start_c1(m):
        agcopy(1, DO, m).wait()
        conv_bwd_a(1, m)

    def last_only(fn):
        return lambda m: pl.when(m == M - 1)(lambda: fn(0))

    def next_one(fn):
        return lambda m: pl.when(m < M - 1)(lambda: fn(m + 1))

    phase(None, end_n1, lambda m: ffn_bwd(1, m), tick=1, ahead=last_only(start_c1))
    for cp in load_ffn(0):
        cp.start()
    phase(end_n1, end_c1, None, lambda m: conv_bwd_b(1, m), tick=1 + M, ahead=next_one(start_c1))
    for cp in load_conv(0):
        cp.start()
    arrived(load_ffn(0))

    def n0(m):
        ffn_bwd(0, m)

    def n0_tick(m, _):
        pl.when(m == 0)(lambda: agcopy(0, DF, 0).wait())
        pl.when(m == 1)(lambda: agcopy(0, DF, 1).wait())

        @pl.when(m == 2)
        def _():
            agcopy(0, DF, 2).wait()
            agcopy(0, DF, 3).wait()

        tick_gen(1 + 2 * M + m)
        n0(m)
        behind(end_c1, end_n0, m)
        tick_rest(1 + 2 * M + m)
        return 0

    lax.fori_loop(0, M, n0_tick, 0)
    load_down(1).start()
    load_down(1).wait()
    arrived(load_conv(0))

    def f1(m):
        agcopy(0, DO, m).wait()
        ffn_down(1, m)

    def start_c0(m):
        conv_bwd_a(0, m)

    phase(end_n0, finish_stream, f1, tick=1 + 3 * M, ahead=last_only(start_c0))

    def c0(m):
        for cp in stream_copies(m):
            cp.wait()
        conv_bwd_b(0, m)

    phase(finish_stream, end_c0, None, c0, tick=1 + 4 * M, ahead=next_one(start_c0))
    t = 1 + 5 * M
    tick_gen(t)
    mid(M - 1)
    end_c0(M - 2)
    tick_rest(t)
    tick_gen(t + 1)
    end_c0(M - 1)

    for i in range(4):
        SM[i : i + 1] = jnp.sum(GACC[i], axis=0, keepdims=True)
    SM[4:8] = jnp.zeros((4, D), f32)
    for l in range(2):
        for k in range(3):
            SM[4 + l : 5 + l, k * C : (k + 1) * C] = jnp.sum(CACC[l, k], axis=0, keepdims=True)

    def small(i):
        return remote(SM, SMR.at[i], sms.at[i], smr.at[i], [sib, *parts][i])

    small(0).start()
    tick_rest(t + 1)
    t += 2
    for i in range(4):
        tick_gen(t)
        small(i).wait()
        if i == 0:
            SM[0:4] += SMR[0, 0:4]
        else:
            SM[...] += SMR[i]
        if i < 3:
            small(i + 1).start()
        tick_rest(t)
        t += 1
    own = pl.ds(pl.multiple_of(tp * C, 128), C)
    NORM_OUT[...] = SM[0:2, own]
    FFN_OUT[...] = SM[2:4, own]
    for l in range(2):
        for k in range(3):
            CONV_OUT[k, l : l + 1, :] = SM[4 + l : 5 + l, k * C : (k + 1) * C]
    small_out = [
        pltpu.make_async_copy(src, dst, load_sem.at[16 + i])
        for i, (src, dst) in enumerate(((NORM_OUT, out_norm), (FFN_OUT, out_ffn), (CONV_OUT, out_conv)))
    ]
    for cp in small_out:
        cp.start()
    while t < UNITS + 2:
        tick_gen(t)
        tick_rest(t)
        t += 1
    last_sum()
    unit_wait(LAST)
    for cp in small_out:
        cp.wait()
    for m in range(M):
        for cp in grad_copies(m):
            cp.wait()


def fused_call(stream_in, norm_gain, win, taps, wout, ffn_gain, wgate, wup, wdown, out_grad):
    M, TOK, D = stream_in.shape
    C, F = wout.shape[1], wgate.shape[2]
    U = 384
    rb = U // 4
    ra = U - rb
    half = TOK // 2
    vm = pltpu.VMEM
    dma = pltpu.SemaphoreType.DMA
    S = SLOTS
    anys = pl.BlockSpec(memory_space=pl.ANY)
    vmem = pl.BlockSpec(memory_space=pltpu.VMEM)
    return pl.pallas_call(
        functools.partial(fused, (M, TOK, D, C, F, U)),
        out_shape=[
            jax.ShapeDtypeStruct((M, TOK, D), bf16),
            jax.ShapeDtypeStruct((M, TOK, D), bf16),
            jax.ShapeDtypeStruct((LAYERS, C), f32),
            jax.ShapeDtypeStruct((LAYERS, 3, 128, C), bf16),
            jax.ShapeDtypeStruct((3, LAYERS, C), f32),
            jax.ShapeDtypeStruct((LAYERS, C, 128), bf16),
            jax.ShapeDtypeStruct((LAYERS, C), f32),
            jax.ShapeDtypeStruct((LAYERS, 128, F), bf16),
            jax.ShapeDtypeStruct((LAYERS, 128, F), bf16),
            jax.ShapeDtypeStruct((LAYERS, F, 128), bf16),
        ],
        in_specs=[anys, vmem, anys, vmem, anys, vmem, anys, anys, anys, anys],
        out_specs=[anys] * 10,
        scratch_shapes=[
            vm((LAYERS, 4, M, TOK, D), bf16),
            vm((LAYERS, M, TOK, 3 * F + 4 * C), bf16),
            vm((D, 3 * C), bf16),
            vm((C, D), bf16),
            vm((D, 2 * F), bf16),
            vm((F, D), bf16),
            vm((M, half, D), f32),
            vm((M, half, D), f32),
            vm((M, half, 2 * LAYERS), f32),
            vm((M, TOK, D), bf16),
            vm((M, half, D), bf16),
            vm((M, half, D), bf16),
            vm((S, 8, ra, 128), bf16),
            vm((S, 8, rb, 128), bf16),
            vm((S, 4, ra, 128), bf16),
            vm((S, 2, ra, 128), bf16),
            vm((S, 1, ra, 128), bf16),
            vm((S, 4, rb, 128), bf16),
            vm((S, 2, rb, 128), bf16),
            vm((S, 1, rb, 128), bf16),
            vm((U, M * TOK), bf16),
            vm((U, 128), bf16),
            vm((128, U), bf16),
            vm((3, 128, 128), bf16),
            dma((3,)),
            dma((3,)),
            vm((8, D), f32),
            vm((TOK + 8, C), f32),
            vm((2, TOK + 8, C), f32),
            vm((TOK, C), f32),
            vm((LAYERS, M * 8, C), f32),
            vm((M, 8, C), f32),
            vm((LAYERS, M, 8, C), f32),
            vm((4, LAYERS, D), f32),
            vm((3, LAYERS, C), f32),
            vm((3, LAYERS, C), f32),
            vm((4, 8, D), f32),
            vm((LAYERS, 3, 8, C), f32),
            vm((4, 8, D), f32),
            vm((LAYERS, C), f32),
            vm((LAYERS, C), f32),
            vm((3, LAYERS, C), f32),
            dma((19,)),
            dma((M,)), dma((M,)), dma((M,)), dma((M,)), dma((M,)), dma((M,)),
            dma, dma((2,)), dma((2, LAYERS, M)), dma((2,)), dma((M + 1,)), dma((4, 5)), dma((4, 5)),
            dma((2, 3, S)), dma((2, 3, S)),
            dma((2,)), dma((M,)), dma((M,)), dma((M,)), dma((4,)), dma((4,)),
        ],
        name="fused",
        compiler_params=pltpu.CompilerParams(
            collective_id=0, has_side_effects=True, vmem_limit_bytes=VMEM_BYTES
        ),
    )(stream_in, norm_gain, win, taps, wout, ffn_gain, wgate, wup, wdown, out_grad)


def handed_on(kinds, split, *refs):
    count = len(kinds)
    srcs, dsts, bufs, wides = (refs[k * count : (k + 1) * count] for k in range(4))
    sin, sout = refs[-2:]
    chunks = [(i, k) for i in range(count) for k in (range(srcs[i].shape[0]) if i in split else (0,))]

    def part(ref, i, k):
        return ref.at[k] if i in split else ref

    ins = [pltpu.make_async_copy(part(srcs[i], i, k), part(bufs[i], i, k), sin.at[i, k]) for i, k in chunks]
    outs = [
        pltpu.make_async_copy(part((wides if kinds[i] else bufs)[i], i, k), part(dsts[i], i, k), sout.at[i, k])
        for i, k in chunks
    ]
    for cp in ins:
        cp.start()
    for (i, k), first, second in zip(chunks, ins, outs):
        first.wait()
        if kinds[i]:
            ref, wide = bufs[i].at[k], wides[i].at[k]
            rows = 128
            lead = ref.shape[:-2]

            def step(r, _):
                cut = pl.ds(pl.multiple_of(lax.rem(r, ref.shape[-2] // rows) * rows, rows), rows)
                at = (lax.div(r, ref.shape[-2] // rows), cut) if lead else (cut,)
                wide[at] = ref[at].astype(f32)
                return 0

            lax.fori_loop(0, (lead[0] if lead else 1) * ref.shape[-2] // rows, step, 0, unroll=True)
        second.start()
    for cp in outs:
        cp.wait()


def hand_on(arrays, types):
    anys = pl.BlockSpec(memory_space=pl.ANY)
    most = max(a.shape[0] for a in arrays)
    kinds = tuple(a.dtype != t for a, t in zip(arrays, types))
    split = tuple(i for i, a in enumerate(arrays) if a.size > 16384)
    return pl.pallas_call(
        functools.partial(handed_on, kinds, split),
        out_shape=[jax.ShapeDtypeStruct(a.shape, t) for a, t in zip(arrays, types)],
        in_specs=[anys] * len(arrays),
        out_specs=[anys] * len(arrays),
        scratch_shapes=[pltpu.VMEM(a.shape, a.dtype) for a in arrays]
        + [pltpu.VMEM(a.shape if k else (8, 128), f32) for a, k in zip(arrays, kinds)]
        + [pltpu.SemaphoreType.DMA((len(arrays), most))] * 2,
        name="hand_on",
        compiler_params=pltpu.CompilerParams(vmem_limit_bytes=VMEM_BYTES),
    )(*arrays)


def body_fused(
    stream_in, norm_gain, in_proj, conv_taps, out_proj, ffn_gain, gate_proj, up_proj, down_proj, out_grad
):
    results = fused_call(
        stream_in, norm_gain, jnp.transpose(in_proj, (0, 2, 1, 3)), jnp.transpose(conv_taps, (1, 0, 2)),
        out_proj, ffn_gain, gate_proj, up_proj, down_proj, out_grad,
    )
    (out_stream, out_sgrad, norm_g, in_g, conv_g, out_g, ffn_g, gate_g, up_g, down_g) = hand_on(
        results, [bf16] + [f32] * 9
    )
    in_g = jnp.transpose(in_g, (0, 2, 1, 3))
    conv_g = jnp.transpose(conv_g, (1, 0, 2))
    return (out_stream, out_sgrad, norm_g, in_g, conv_g, out_g, ffn_g, gate_g, up_g, down_g)


def solution(mesh):
    in_specs = (
        P(None, "seq", None),
        P(),
        P(None, None, None, "tp"),
        P(None, None, "tp"),
        P(None, "tp", None),
        P(),
        P(None, None, "tp"),
        P(None, None, "tp"),
        P(None, "tp", None),
        P(None, "seq", None),
    )
    out_specs = (
        P(None, "seq", None),
        P(None, "seq", None),
        P(None, "tp"),
        P(None, "seq", None, "tp"),
        P(None, None, "tp"),
        P(None, "tp", "seq"),
        P(None, "tp"),
        P(None, "seq", "tp"),
        P(None, "seq", "tp"),
        P(None, "tp", "seq"),
    )
    chosen = body_fused if (mesh.shape["seq"], mesh.shape["tp"]) == (8, 4) else body
    return jax.shard_map(chosen, mesh=mesh, in_specs=in_specs, out_specs=out_specs, check_vma=False)
```

```python
import functools

import jax
import jax.numpy as jnp
from jax import lax
from jax.experimental import pallas as pl
from jax.experimental.pallas import tpu as pltpu
from jax.sharding import PartitionSpec as P

LAYERS = 2


EPS = 1e-05


def passed_along(block, axis, distance):
    devices = range(lax.axis_size(axis))
    route = [(i - distance, i) for i in devices if i - distance in devices]
    return lax.ppermute(block, axis, route)


def norm_rate(hidden):
    return lax.rsqrt(jnp.mean(hidden * hidden, axis=-1, keepdims=True) + EPS)


def norm_back(grad_in, gain, normed_val, rate):
    scaled = grad_in * gain
    return rate * (scaled - normed_val * jnp.mean(scaled * normed_val, axis=-1, keepdims=True))


def reduce_weights(grads):
    return (
        lax.psum_scatter(
            grads[0].astype(jnp.bfloat16), "seq", scatter_dimension=1, tiled=True
        ).astype(jnp.float32),
        lax.psum_scatter(
            grads[1].astype(jnp.bfloat16), "seq", scatter_dimension=2, tiled=True
        ).astype(jnp.float32),
        lax.psum_scatter(
            grads[2].astype(jnp.bfloat16), "seq", scatter_dimension=1, tiled=True
        ).astype(jnp.float32),
        lax.psum_scatter(
            grads[3].astype(jnp.bfloat16), "seq", scatter_dimension=1, tiled=True
        ).astype(jnp.float32),
        lax.psum_scatter(
            grads[4].astype(jnp.bfloat16), "seq", scatter_dimension=2, tiled=True
        ).astype(jnp.float32),
    )


def reduce_small(grads):
    return lax.psum((grads[0], grads[1], grads[2]), "seq")


def body(
    stream_in,
    norm_gain,
    in_proj,
    conv_taps,
    out_proj,
    ffn_gain,
    gate_proj,
    up_proj,
    down_proj,
    out_grad,
):
    f32 = jnp.float32
    bf16 = jnp.bfloat16
    width = in_proj.shape[-1]
    offset = lax.axis_index("tp") * width
    hidden = stream_in.astype(f32)
    kept = []
    for layer in range(LAYERS):
        gain_one = norm_gain[layer].astype(f32)
        gain_two = ffn_gain[layer].astype(f32)
        taps = conv_taps[layer].astype(f32)
        rate_one = norm_rate(hidden)
        normed_one = hidden * rate_one
        first = (normed_one * gain_one).astype(bf16)
        proj = jnp.einsum("msd,dkc->mskc", first, in_proj[layer], preferred_element_type=f32)
        bgate = proj[:, :, 0]
        cgate = proj[:, :, 1]
        xinput = proj[:, :, 2]
        mixed = (bgate * xinput).astype(bf16)
        prior = passed_along(mixed[:, -2:], "seq", 1)
        extended = jnp.concatenate([prior, mixed], axis=1).astype(f32)
        conved = (
            taps[0] * extended[:, :-2] + taps[1] * extended[:, 1:-1] + taps[2] * extended[:, 2:]
        )
        gated = (cgate * conved).astype(bf16)
        partial_out = jnp.einsum("msc,cd->msd", gated, out_proj[layer], preferred_element_type=f32)
        middle = hidden + lax.psum(partial_out, "tp")
        rate_two = norm_rate(middle)
        normed_two = middle * rate_two
        second = (normed_two * gain_two).astype(bf16)
        gate_val = jnp.einsum("msd,df->msf", second, gate_proj[layer], preferred_element_type=f32)
        up_val = jnp.einsum("msd,df->msf", second, up_proj[layer], preferred_element_type=f32)
        sigma = jax.nn.sigmoid(gate_val)
        silu_val = gate_val * sigma
        act = (silu_val * up_val).astype(bf16)
        partial_ffn = jnp.einsum("msf,fd->msd", act, down_proj[layer], preferred_element_type=f32)
        kept.append(
            (
                rate_one,
                normed_one,
                first,
                bgate,
                cgate,
                xinput,
                extended,
                conved,
                gated,
                rate_two,
                normed_two,
                second,
                gate_val,
                up_val,
                sigma,
                silu_val,
                act,
            )
        )
        hidden = middle + lax.psum(partial_ffn, "tp")
    grad_h = out_grad.astype(f32)
    collected = [None] * LAYERS
    for layer in reversed(range(LAYERS)):
        (
            rate_one,
            normed_one,
            first,
            bgate,
            cgate,
            xinput,
            extended,
            conved,
            gated,
            rate_two,
            normed_two,
            second,
            gate_val,
            up_val,
            sigma,
            silu_val,
            act,
        ) = kept[layer]
        gain_one = norm_gain[layer].astype(f32)
        gain_two = ffn_gain[layer].astype(f32)
        taps = conv_taps[layer].astype(f32)
        grad_f = grad_h.astype(bf16)
        grad_act = jnp.einsum("msd,fd->msf", grad_f, down_proj[layer], preferred_element_type=f32)
        down_g = jnp.einsum("msf,msd->fd", act, grad_f, preferred_element_type=f32)
        grad_gate = (grad_act * up_val * sigma * (1.0 + gate_val * (1.0 - sigma))).astype(bf16)
        grad_up = (grad_act * silu_val).astype(bf16)
        part_two = jnp.einsum(
            "msf,df->msd", grad_gate, gate_proj[layer], preferred_element_type=f32
        )
        part_two = part_two + jnp.einsum(
            "msf,df->msd", grad_up, up_proj[layer], preferred_element_type=f32
        )
        gate_g = jnp.einsum("msd,msf->df", second, grad_gate, preferred_element_type=f32)
        up_g = jnp.einsum("msd,msf->df", second, grad_up, preferred_element_type=f32)
        grad_two = lax.psum(part_two.astype(jnp.bfloat16), "tp").astype(jnp.float32)
        ffn_gain_g = jnp.sum(grad_two * normed_two, axis=(0, 1))
        grad_mid = grad_h + norm_back(grad_two, gain_two, normed_two, rate_two)
        grad_o = grad_mid.astype(bf16)
        grad_gated = jnp.einsum("msd,cd->msc", grad_o, out_proj[layer], preferred_element_type=f32)
        out_g = jnp.einsum("msc,msd->cd", gated, grad_o, preferred_element_type=f32)
        grad_conv = grad_gated * cgate
        grad_cgate = grad_gated * conved
        after = passed_along(grad_conv[:, :2], "seq", -1)
        grad_ext = jnp.concatenate([grad_conv, after], axis=1)
        grad_mixed = (
            taps[2] * grad_ext[:, :-2] + taps[1] * grad_ext[:, 1:-1] + taps[0] * grad_ext[:, 2:]
        )
        count = grad_conv.shape[1]
        conv_g = jnp.stack(
            [jnp.sum(grad_conv * extended[:, k : k + count], axis=(0, 1)) for k in range(3)], axis=0
        )
        grad_proj = jnp.stack([grad_mixed * xinput, grad_cgate, grad_mixed * bgate], axis=2).astype(
            bf16
        )
        part_one = jnp.einsum(
            "mskc,dkc->msd", grad_proj, in_proj[layer], preferred_element_type=f32
        )
        in_g = jnp.einsum("msd,mskc->dkc", first, grad_proj, preferred_element_type=f32)
        grad_one = lax.psum(part_one.astype(jnp.bfloat16), "tp").astype(jnp.float32)
        norm_gain_g = jnp.sum(grad_one * normed_one, axis=(0, 1))
        grad_h = grad_mid + norm_back(grad_one, gain_one, normed_one, rate_one)
        norm_piece = lax.dynamic_slice_in_dim(norm_gain_g, offset, width)
        ffn_piece = lax.dynamic_slice_in_dim(ffn_gain_g, offset, width)
        small = (norm_piece, conv_g, ffn_piece)
        large = (in_g, out_g, gate_g, up_g, down_g)
        collected[layer] = (small, large)
    norm_stack = jnp.stack([c[0][0] for c in collected], axis=0)
    conv_stack = jnp.stack([c[0][1] for c in collected], axis=0)
    ffn_stack = jnp.stack([c[0][2] for c in collected], axis=0)
    large_stack = tuple((jnp.stack([c[1][i] for c in collected], axis=0) for i in range(5)))
    large_stack = reduce_weights(large_stack)
    norm_stack, conv_stack, ffn_stack = reduce_small((norm_stack, conv_stack, ffn_stack))
    stream_out = hidden.astype(bf16)
    in_grad, out_grad_w, gate_grad, up_grad, down_grad = large_stack
    return (
        stream_out,
        grad_h,
        norm_stack,
        in_grad,
        conv_stack,
        out_grad_w,
        ffn_stack,
        gate_grad,
        up_grad,
        down_grad,
    )


VMEM_BYTES = 64 * 2**20
MESH = pl.DeviceIdType.MESH
f32 = jnp.float32
bf16 = jnp.bfloat16
NN = (((1,), (0,)), ((), ()))
NT = (((1,), (1,)), ((), ()))
ORDERS = ((0, 1, 2), (1, 0, 2))
SLOTS = 4
WIDE = 1024
N1, N2, DF, DO = range(4)


def rem(a, b):
    return a % b if isinstance(a, int) else lax.rem(a, b)


def div(a, b):
    return a // b if isinstance(a, int) else lax.div(a, b)


def cases(value, branches):
    for low, high, fn in branches:
        if isinstance(value, int):
            if low <= value < high:
                fn()
        else:
            pl.when((value >= low) & (value < high))(fn)


def mm(lhs, rhs, dims=NN):
    return lax.dot_general(lhs, rhs, dims, preferred_element_type=f32)


def fused(
    dims,
    stream_in, norm_gain, win, taps, wout, ffn_gain, wgate, wup, wdown, out_grad,
    out_stream, out_sgrad, out_norm, out_in, out_conv, out_out, out_ffn, out_gate, out_up, out_down,
    L, R, WIN, WOUT, WGU, WD, H, DH, RATE, PB, PR, XR,
    GA, GB, RA0, RA1, RA2, RB0, RB1, RB2, RT, FO, FT, RZ, zs, zr, SM,
    EXT, DYE, CF, HALO, HALO2, DHALO, GAIN, TAPS, TAPS2, GACC, CACC, SMR,
    NORM_OUT, FFN_OUT, CONV_OUT,
    load_sem, ps, pr, xs, xr, ags, agr, hs, dhs, hr, hs2, hr2, gs, gr, rss, rsr, fos, oss, sts, str_, sms, smr,
):
    M, TOK, D, C, F, U = dims
    half = TOK // 2
    CS, CA, CP, CZ = 0, F, 3 * F, 3 * F + 3 * C
    PER = (CZ + C) // U
    first_units = [(1, 0, 128), (1, 128, U - 128)]
    TURN = PER + 2
    table = first_units + [(1, k * U, U) for k in range(1, PER)] + [(1, PER * U, CZ + C - PER * U)]
    table += [(0, k * U, U) for k in range(PER)]
    table += [(0, k, 128) for k in range(PER * U, CZ + C, 128)]
    UNITS = len(table)
    LAST = UNITS - 1
    whole = (128, 128, 0)
    splits = {w: (w, w - w // 4, w // 4) for w in (128, 256, U)}
    seq = lax.axis_index("seq")
    tp = lax.axis_index("tp")
    n = lax.axis_size("seq")
    core = lax.rem(tp, 2)
    xi = lax.div(tp, 2)
    sib = {"seq": seq, "tp": tp + 1 - 2 * core}
    xpart = {"seq": seq, "tp": tp + 2 - 4 * xi}
    bits = [lax.rem(lax.div(seq, 1 << k), 2) for k in range(3)]
    parts = [{"seq": seq + (1 << k) - 2 * (1 << k) * bits[k], "tp": tp} for k in range(3)]
    nxt = {"seq": lax.rem(seq + 1, n), "tp": tp}
    prv = {"seq": lax.rem(seq + n - 1, n), "tp": tp}
    mine = pl.ds(pl.multiple_of(core * half, half), half)
    theirs = pl.ds(pl.multiple_of((1 - core) * half, half), half)

    def remote(src, dst, ssem, rsem, dev):
        return pltpu.make_async_remote_copy(
            src_ref=src, dst_ref=dst, send_sem=ssem, recv_sem=rsem, device_id=dev, device_id_type=MESH
        )

    def load_stream(m):
        return pltpu.make_async_copy(stream_in.at[m], L.at[0, N1, m], load_sem.at[m])

    def load_conv(l):
        return [
            pltpu.make_async_copy(win.at[l, k], WIN.at[:, pl.ds(k * C, C)], load_sem.at[4 + k])
            for k in range(3)
        ] + [pltpu.make_async_copy(wout.at[l], WOUT, load_sem.at[7])]

    def load_ffn(l):
        return [
            pltpu.make_async_copy(
                src.at[l, :, pl.ds(t * U, U)], WGU.at[:, pl.ds((2 * t + i) * U, U)], load_sem.at[10 + 2 * t + i]
            )
            for t in range(F // U)
            for i, src in enumerate((wgate, wup))
        ]

    def load_down(l):
        return pltpu.make_async_copy(wdown.at[l], WD, load_sem.at[9])

    load_og = pltpu.make_async_copy(out_grad, L.at[1, DF], load_sem.at[8])
    for cp in load_conv(0) + [load_stream(m) for m in range(M)]:
        cp.start()

    barrier = pltpu.get_barrier_semaphore()
    zcross = {"seq": n - 1 - seq + 2 * lax.rem(seq, 2) - 1, "tp": tp}
    others = [sib, xpart, nxt, prv, zcross] + parts
    for dev in others:
        pl.semaphore_signal(barrier, inc=1, device_id=dev, device_id_type=MESH)

    GAIN[0] = norm_gain[...].astype(f32)
    GAIN[1] = ffn_gain[...].astype(f32)
    GAIN[2] = 1.0 / norm_gain[...].astype(f32)
    GAIN[3] = 1.0 / ffn_gain[...].astype(f32)
    TAPS[...] = taps[...].astype(f32)
    GACC[...] = jnp.zeros_like(GACC)
    CACC[...] = jnp.zeros_like(CACC)

    pl.semaphore_wait(barrier, len(others))

    zpos, ypos = lax.div(seq, 2), lax.rem(seq, 2)
    zfar, znear = lax.rem(zpos + 2, 4), zpos + 1 - 2 * lax.rem(zpos, 2)
    strip = D // 8

    def piece(s, z):
        rows = pl.ds(pl.multiple_of(ypos * strip, strip), strip)
        if s < 3:
            return L.at[0, DO, 1 + s, rows, pl.ds(pl.multiple_of(z * TOK, TOK), TOK)]
        return L.at[0, DO, 0, pl.ds(pl.multiple_of(ypos * strip + z * (C // 8), 16), C // 8)]

    def gathers(s, step):
        def send(i, src, dst, dev):
            return remote(src, dst, gs.at[s, i], gr.at[s, i], dev)

        if step == 0:
            if s < 3:
                src = win.at[1, s, pl.ds(pl.multiple_of(zpos * TOK + ypos * strip, strip), strip)]
            else:
                src = wout.at[1, pl.ds(pl.multiple_of(ypos * strip + zpos * (C // 8), 16), C // 8)]
            return [send(0, src, piece(s, zpos), xpart)]
        if step == 1:
            return [send(1, piece(s, zpos), piece(s, zpos), parts[2])]
        if step == 2:
            return [send(2 + i, piece(s, z), piece(s, z), parts[1]) for i, z in enumerate((zpos, zfar))]
        half_ref = L.at[0, DO, (1 + s) % 4, pl.ds(pl.multiple_of(ypos * strip, strip), strip)]
        return [send(4, half_ref, half_ref, parts[0])]

    def gather_at(j):
        for s in range(4):
            for step, when in enumerate((s, s + 2, s + 4, 7 + 2 * s)):
                if j == when:
                    for cp in gathers(s, step):
                        cp.wait()
                    if step < 3:
                        for cp in gathers(s, step + 1):
                            cp.start()

    def gather_dyn(base, m, late):
        for i in range(M):
            pl.when(m == i)(functools.partial(gather_at, base + 2 * i + late))

    for s in range(4):
        for cp in gathers(s, 0):
            cp.start()
    tap_copy = remote(TAPS, TAPS2, hs2.at[1], hr2.at[M], xpart)
    tap_copy.start()

    def pcopy(m):
        return remote(PB.at[m, theirs], PR.at[m], ps.at[m], pr.at[m], sib)

    def xcopy(m):
        return remote(PB.at[m, mine], XR.at[m], xs.at[m], xr.at[m], xpart)

    def mid(m):
        pcopy(m).wait()

        def chunk(i, _):
            off = pl.multiple_of(i * 32, 32)
            rows = pl.ds(pl.multiple_of(core * half + off, 32), 32)
            got = PR[m, pl.ds(off, 32)].astype(f32) + PB[m, rows].astype(f32)
            PB[m, rows] = got.astype(bf16)
            return 0

        lax.fori_loop(0, half // 32, chunk, 0, unroll=True)
        xcopy(m).start()

    def agcopy(l, kind, m):
        ref = L.at[l, kind, m, mine]
        return remote(ref, ref, ags.at[m], agr.at[m], sib)

    def rows_loop(m, body, received=XR):
        def chunk(i, _):
            off = pl.multiple_of(i * 32, 32)
            rows = pl.ds(pl.multiple_of(core * half + off, 32), 32)
            total = PB[m, rows].astype(f32) + received[m, pl.ds(off, 32)].astype(f32)
            body(pl.ds(off, 32), rows, total)
            return 0

        lax.fori_loop(0, half // 32, chunk, 0, unroll=True)

    def rate_of(val):
        return lax.rsqrt(jnp.mean(val * val, axis=-1, keepdims=True) + EPS)

    def finish_norm(l, which, kind, m, within=False):
        if within:
            pcopy(m).wait()
        else:
            xcopy(m).wait()
        gain = GAIN[which, l : l + 1, :]

        def body(loc, rows, total):
            hid = H[m, loc] + total
            H[m, loc] = hid
            rate = rate_of(hid)
            RATE[m, loc, 2 * l + which : 2 * l + which + 1] = rate
            L[l, kind, m, rows] = (hid * rate * gain).astype(bf16)

        rows_loop(m, body, PR if within else XR)
        agcopy(l, kind, m).start()

    def stream_copies(m):
        ref = PB.at[m, mine]
        return (
            pltpu.make_async_copy(ref, out_stream.at[m, mine], oss.at[m]),
            remote(ref, out_stream.at[m, mine], sts.at[m], str_.at[m], sib),
        )

    def finish_stream(m):
        xcopy(m).wait()

        def body(loc, rows, total):
            PB[m, rows] = (H[m, loc] + total).astype(bf16)

        rows_loop(m, body)
        for cp in stream_copies(m):
            cp.start()

    def norm_back(l, which, kind, m, emit):
        xcopy(m).wait()
        gain = GAIN[which, l : l + 1, :]
        inv = GAIN[2 + which, l : l + 1, :]

        def body(loc, rows, total):
            nrm = L[l, kind, m, rows].astype(f32) * inv
            prod = total * nrm
            GACC[2 * which + l] += prod[0:8] + prod[8:16] + prod[16:24] + prod[24:32]
            mean = jnp.mean(prod * gain, axis=-1, keepdims=True)
            emit(loc, rows, RATE[m, loc, 2 * l + which : 2 * l + which + 1] * (total * gain - nrm * mean))

        rows_loop(m, body)

    def finish_dn2(l, m):
        def emit(loc, rows, delta):
            prev = L[1, DF, m, rows].astype(f32) if l == 1 else DH[m, loc]
            new = prev + delta
            DH[m, loc] = new
            L[l, DO, m, rows] = new.astype(bf16)

        norm_back(l, 1, N2, m, emit)
        agcopy(l, DO, m).start()

    def finish_dn1(l, m):
        def emit(loc, rows, delta):
            new = DH[m, loc] + delta
            if l == 1:
                DH[m, loc] = new
                L[0, DF, m, rows] = new.astype(bf16)
            else:
                PB[m, rows] = new.astype(bf16)

        norm_back(l, 0, N1, m, emit)
        if l == 1:
            agcopy(0, DF, m).start()
        else:
            for cp in grad_copies(m):
                cp.start()

    def grad_copies(m):
        return (
            pltpu.make_async_copy(PB.at[m, mine], out_sgrad.at[m, mine], oss.at[m]),
            remote(PB.at[m, mine], out_sgrad.at[m, mine], ags.at[m], agr.at[m], sib),
        )

    def put_partial(m, tile):
        def step(j, _):
            cols = pl.ds(pl.multiple_of(j * WIDE, WIDE), WIDE)
            PB[m, :, cols] = tile(cols).astype(bf16)
            return 0

        lax.fori_loop(0, D // WIDE, step, 0)
        pcopy(m).start()

    def halo_rows(m):
        return pl.ds(m * 8 if isinstance(m, int) else pl.multiple_of(m * 8, 8), 8)

    def hcopy(l, m):
        return remote(EXT.at[pl.ds(TOK, 8)], HALO.at[l, halo_rows(m)], hs, hr.at[0, l, m], nxt)

    def dhcopy(l, m):
        return remote(DYE.at[rem(m, 2), pl.ds(0, 8)], DHALO.at[l, m], dhs.at[rem(m, 2)], hr.at[1, l, m], prv)

    def hcopy2(m):
        return remote(DYE.at[1, pl.ds(TOK, 8)], HALO2.at[m], hs2.at[0], hr2.at[m], nxt)

    def tap(l, k):
        return TAPS[k, l : l + 1, :]

    def conv_of(ext, halo, taps_ref, l):
        ext[0:8] = jnp.where(seq == 0, 0.0, halo)
        t = [taps_ref[k, l : l + 1, :] for k in range(3)]
        return t[0] * ext[6 : 6 + TOK] + t[1] * ext[7 : 7 + TOK] + t[2] * ext[8 : 8 + TOK]

    def conv_now(l, m):
        return conv_of(EXT, HALO[l, halo_rows(m)], TAPS, l)

    def other_in(k):
        blocks = [L[0, DO, 1 + k, :, r * TOK : (r + 1) * TOK] for r in range(D // TOK)]
        return jnp.concatenate(blocks, axis=0)

    first_halos = remote(DYE.at[1, pl.ds(0, 8 * M)], HALO.at[0], hs, hr.at[0, 0, 0], nxt)

    def send_first_halos():
        val = jnp.concatenate([L[0, N1, m, TOK - 16 : TOK] for m in range(M)], axis=0).astype(f32)
        p = mm((val * rate_of(val) * GAIN[0, 0:1, :]).astype(bf16), WIN[...])
        bx = (p[:, 0:C] * p[:, 2 * C : 3 * C]).astype(bf16).astype(f32)
        for m in range(M):
            DYE[1, 8 * m : 8 * m + 8] = bx[16 * m + 8 : 16 * m + 16]
        first_halos.start()

    def conv_fwd_a(l, m):
        if l == 0:
            gain = GAIN[0, 0:1, :]
            hid = L[0, N1, m, mine].astype(f32)
            H[m] = hid
            RATE[m, :, 0:1] = rate_of(hid)

            def chunk(i, _):
                rows = pl.ds(pl.multiple_of(i * 32, 32), 32)
                val = L[0, N1, m, rows].astype(f32)
                L[0, N1, m, rows] = (val * rate_of(val) * gain).astype(bf16)
                return 0

            lax.fori_loop(0, TOK // 32, chunk, 0)
        else:
            agcopy(1, N1, m).wait()
        first = L[l, N1, m]
        p = mm(first, WIN[...])
        bgate, cgate, xin = p[:, 0:C], p[:, C : 2 * C], p[:, 2 * C : 3 * C]
        R[l, m, :, CP : CP + 3 * C] = p.astype(bf16)
        EXT[8 : 8 + TOK] = (bgate * xin).astype(bf16).astype(f32)
        DYE[0, 0:TOK] = cgate
        if l == 1:
            hcopy(l, m).start()
            p = mm(first, jnp.concatenate([other_in(k) for k in range(3)], axis=1))
            DYE[1, 8 : 8 + TOK] = (p[:, 0:C] * p[:, 2 * C : 3 * C]).astype(bf16).astype(f32)
            hcopy2(m).start()
            CF[...] = p[:, C : 2 * C]

    def conv_fwd_b(l, m):
        if l == 0:
            pl.when(m == 0)(lambda: first_halos.wait())
        else:
            hcopy(l, m).wait()
        gated = (DYE[0, 0:TOK] * conv_now(l, m)).astype(bf16)
        R[l, m, :, CZ : CZ + C] = gated
        if l == 0:
            put_partial(m, lambda cols: mm(R[l, m, :, CZ : CZ + C], WOUT[:, cols]))
        else:
            hcopy2(m).wait()
            L[0, DF, m, :, 0:C] = (CF[...] * conv_of(DYE.at[1], HALO2[m], TAPS2, l)).astype(bf16)
            put_partial(
                m,
                lambda cols: mm(R[l, m, :, CZ : CZ + C], WOUT[:, cols])
                + mm(L[0, DF, m, :, 0:C], L[0, DO, 0, :, cols]),
            )

    def down_back(m):
        ds = mm(L[1, DF, m], WD[...], NT).astype(bf16)
        for t in range(F // U):
            R[1, m, :, CA + (2 * t + 1) * U : CA + (2 * t + 2) * U] = ds[:, t * U : (t + 1) * U]

    def ffn_fwd(l, m, low=0, high=F // U):
        def step(t):
            off, off2 = t * U, 2 * t * U
            ab = mm(L[l, N2, m], WGU[:, pl.ds(off2, 2 * U)])
            a, b = ab[:, 0:U], ab[:, U : 2 * U]
            sig = jax.nn.sigmoid(a)
            silu = a * sig
            R[l, m, :, pl.ds(CS + off, U)] = (silu * b).astype(bf16)
            if l == 0:
                R[l, m, :, pl.ds(CA + off2, 2 * U)] = ab.astype(bf16)
            else:
                ds = R[l, m, :, pl.ds(CA + U + off2, U)].astype(f32)
                R[l, m, :, pl.ds(CA + off2, U)] = (ds * b * sig * (1.0 + a * (1.0 - sig))).astype(bf16)
                R[l, m, :, pl.ds(CA + U + off2, U)] = (ds * silu).astype(bf16)

        for t in range(low, high):
            step(t)

    def ffn_down(l, m):
        put_partial(m, lambda cols: mm(R[l, m, :, CS : CS + F], WD[:, cols]))

    def ffn_bwd(l, m):
        if l == 0:
            def step(t):
                off, off2 = t * U, 2 * t * U
                a = R[l, m, :, pl.ds(CA + off2, U)].astype(f32)
                b = R[l, m, :, pl.ds(CA + U + off2, U)].astype(f32)
                sig = jax.nn.sigmoid(a)
                ds = mm(L[l, DF, m], WD[pl.ds(off, U), :], NT)
                R[l, m, :, pl.ds(CA + off2, U)] = (ds * b * sig * (1.0 + a * (1.0 - sig))).astype(bf16)
                R[l, m, :, pl.ds(CA + U + off2, U)] = (ds * a * sig).astype(bf16)

            for t in range(F // U):
                step(t)
        put_partial(m, lambda cols: mm(R[l, m, :, CA : CA + 2 * F], WGU[cols, :], NT))

    def conv_bwd_a(l, m):
        dz = mm(L[l, DO, m], WOUT[...], NT)
        bgate = R[l, m, :, CP : CP + C].astype(f32)
        xin = R[l, m, :, CP + 2 * C : CP + 3 * C].astype(f32)
        EXT[8 : 8 + TOK] = (bgate * xin).astype(bf16).astype(f32)
        dy = dz * R[l, m, :, CP + C : CP + 2 * C].astype(f32)
        DYE[rem(m, 2), 0:TOK] = dy
        dhcopy(l, m).start()
        R[l, m, :, CP + C : CP + 2 * C] = (dz * conv_now(l, m)).astype(bf16)
        for k in range(3):
            prod = dy * EXT[6 + k : 6 + k + TOK]
            CACC[l, k] += jnp.sum(prod.reshape(TOK // 8, 8, C), axis=0)

    def conv_bwd_b(l, m):
        dhcopy(l, m).wait()
        s = rem(m, 2)
        DYE[s, TOK : TOK + 8] = jnp.where(seq == n - 1, 0.0, DHALO[l, m])
        dbx = (
            tap(l, 2) * DYE[s, 0:TOK] + tap(l, 1) * DYE[s, 1 : 1 + TOK] + tap(l, 0) * DYE[s, 2 : 2 + TOK]
        )
        bgate = R[l, m, :, CP : CP + C].astype(f32)
        xin = R[l, m, :, CP + 2 * C : CP + 3 * C].astype(f32)
        R[l, m, :, CP : CP + C] = (dbx * xin).astype(bf16)
        R[l, m, :, CP + 2 * C : CP + 3 * C] = (dbx * bgate).astype(bf16)
        put_partial(m, lambda cols: mm(R[l, m, :, CP : CP + 3 * C], WIN[cols, :], NT))

    lanes = ((GA, (RA0, RA1, RA2)), (GB, (RB0, RB1, RB2)))

    def keep(lane, step):
        b = [bits[o] for o in ORDERS[lane]]
        return [b[0] * 4, b[0] * 4 + b[1] * 2, b[0] * 4 + b[1] * 2 + b[2]][step]

    def unit_at(t):
        if isinstance(t, int):
            return table[t][:2]
        k = jnp.where(t < TURN, t - 1, t - TURN)
        return jnp.where(t < TURN, 1, 0), jnp.where(t < 2, t * 128, k * U)

    def sized(t, fn):
        if isinstance(t, int):
            fn(splits[table[t][2]])
            return
        pl.when(t == 0)(lambda: fn(splits[128]))
        pl.when((t == 1) | (t == TURN - 1))(lambda: fn(splits[256]))
        pl.when((t > 1) & (t != TURN - 1))(lambda: fn(splits[U]))

    def rs_copy(lane, step, t, rows):
        G, recv = lanes[lane]
        slot = rem(t, SLOTS)
        size = 4 >> step
        o = ORDERS[lane][step]
        off = keep(lane, step) + size - 2 * size * bits[o]
        cut = pl.ds(0, rows[1 + lane])
        return remote(
            G.at[slot, pl.ds(off, size), cut], recv[step].at[slot, :, cut],
            rss.at[lane, step, slot], rsr.at[lane, step, slot], parts[o],
        )

    def rs_gen(t):
        l, start = unit_at(t)
        kind = jnp.where(start < CA, DF, jnp.where(start < CP, N2, jnp.where(start < CZ, N1, DO)))
        slot = rem(t, SLOTS)

        def make(rows):
            wide, cut, _ = rows
            cols = pl.ds(start if isinstance(start, int) else pl.multiple_of(start, 128), wide)
            for m in range(M):
                RT[0:wide, m * TOK : (m + 1) * TOK] = R[l, m, :, cols].T

            def step(j, _):
                src = L[l, kind, :, :, pl.ds(pl.multiple_of(j * 512, 512), 512)].reshape(M * TOK, 512)
                res = mm(RT[0:wide], src).astype(bf16)
                for q in range(4):
                    lo, y = q // 2, q % 2
                    block = res[:, q * 128 : (q + 1) * 128]
                    GA[slot, y * 4 + lo * 2 + j, 0:cut] = block[:cut]
                    if cut < wide:
                        GB[slot, lo * 4 + y * 2 + j, 0 : wide - cut] = block[cut:]
                return 0

            lax.fori_loop(0, D // 512, step, 0)
            for lane in range(2):
                if rows[1 + lane]:
                    rs_copy(lane, 0, t, rows).start()

        if isinstance(t, int) and t == LAST:
            make(whole)
        else:
            sized(t, make)

    def last_copies():
        base = bits[0] * 4
        for i, (flip, dev) in enumerate(((1, parts[2]), (2, parts[1]), (3, zcross))):
            to = (bits[1] if flip < 2 else 1 - bits[1]) * 2 + (bits[2] if flip == 2 else 1 - bits[2])
            yield remote(GA.at[LAST % SLOTS, base + to, pl.ds(0, 128)], RZ.at[i], zs.at[i], zr.at[i], dev)

    def last_add():
        slot = LAST % SLOTS
        rs_copy(0, 0, LAST, whole).wait()
        base = keep(0, 0)
        for i in range(4):
            GA[slot, base + i, 0:128] = (
                GA[slot, base + i, 0:128].astype(f32) + RA0[slot, i, 0:128].astype(f32)
            ).astype(bf16)
        for cp in last_copies():
            cp.start()

    def last_sum():
        unit_wait(LAST - 1)
        for cp in last_copies():
            cp.wait()
        total = GA[LAST % SLOTS, keep(0, 2), 0:128].astype(f32) + RZ[0].astype(f32)
        FO[0:128] = (total + (RZ[1].astype(f32) + RZ[2].astype(f32))).astype(bf16)
        for cp in unit_copies(LAST, 5, 128):
            cp.start()

    def rs_add(step, t):
        slot = rem(t, SLOTS)

        def go(rows):
            for lane in range(2):
                G, recv = lanes[lane]
                rs_copy(lane, step, t, rows).wait()
                base = keep(lane, step)
                cut = rows[1 + lane]

                def add(i, _):
                    G[slot, base + i, 0:cut] = (
                        G[slot, base + i, 0:cut].astype(f32) + recv[step][slot, i, 0:cut].astype(f32)
                    ).astype(bf16)
                    return 0

                lax.fori_loop(0, 4 >> step, add, 0)
                rs_copy(lane, step + 1, t, rows).start()

        sized(t, go)

    def unit_copies(t, which, wide):
        l, start = unit_at(t)

        def at(off):
            return pl.ds(off if isinstance(off, int) else pl.multiple_of(off, 128), wide)

        tile = at(div(start - CA, 2 * U) * U)
        if which == 0:
            pairs = [(FO.at[pl.ds(0, wide)], out_down.at[l, at(start)])]
        elif which == 1:
            pairs = [(FT, out_gate.at[l, :, tile])]
        elif which == 2:
            pairs = [(FT, out_up.at[l, :, tile])]
        elif which == 3:
            pairs = [(FT.at[:, pl.ds(0, C)], out_in.at[l, 0]),
                     (FT.at[:, pl.ds(C, U - C)], out_in.at[l, 1, :, pl.ds(0, U - C)])]
        elif which == 4:
            pairs = [(FT.at[:, pl.ds(0, 2 * C - U)], out_in.at[l, 1, :, pl.ds(U - C, 2 * C - U)]),
                     (FT.at[:, pl.ds(2 * C - U, C)], out_in.at[l, 2])]
        else:
            pairs = [(FO.at[pl.ds(0, wide)], out_out.at[l, at(start - CZ)])]
        return [pltpu.make_async_copy(a, b, fos.at[i]) for i, (a, b) in enumerate(pairs)]

    def by_target(t, fn):
        if isinstance(t, int):
            _, start, wide = table[t]
            if start < CA:
                which = 0
            elif start < CP:
                which = 1 + (start - CA) // U % 2
            else:
                which = 5 if start >= CZ else 3 + (start - CP) // U
            fn(which, wide)
            return
        _, start = unit_at(t)
        pl.when(t == 0)(lambda: fn(0, 128))
        pl.when(t == 1)(lambda: fn(0, 256))
        pl.when((t > 1) & (start < CA))(lambda: fn(0, U))
        for i in range(2):
            odd = lax.rem(lax.div(start, U) + CA // U, 2) == i
            pl.when((start >= CA) & (start < CP) & odd)(functools.partial(fn, 1 + i, U))
            pl.when(start == CP + i * U)(functools.partial(fn, 3 + i, U))
        pl.when(start == CZ)(lambda: fn(5, 256))

    def unit_wait(t):
        def go(which, wide):
            for cp in unit_copies(t, which, wide):
                cp.wait()

        by_target(t, go)

    def rs_last(t):
        slot = rem(t, SLOTS)
        if isinstance(t, int):
            if t >= 1:
                unit_wait(t - 1)
        else:
            pl.when(t >= 1)(lambda: unit_wait(t - 1))

        def go(rows):
            wide, cut, _ = rows
            for lane in range(2):
                rs_copy(lane, 2, t, rows).wait()
            FO[0:cut] = (GA[slot, keep(0, 2), 0:cut].astype(f32) + RA2[slot, 0, 0:cut].astype(f32)).astype(bf16)
            FO[cut:wide] = (
                GB[slot, keep(1, 2), 0 : wide - cut].astype(f32) + RB2[slot, 0, 0 : wide - cut].astype(f32)
            ).astype(bf16)

        sized(t, go)

        def send(which, wide):
            if which in (1, 2, 3, 4):
                FT[...] = FO[...].T
            for cp in unit_copies(t, which, wide):
                cp.start()

        by_target(t, send)

    def tick_gen(t):
        if not isinstance(t, int) or t < UNITS:
            rs_gen(t)

    def tick_rest(t):
        steps = (functools.partial(rs_add, 0), functools.partial(rs_add, 1), rs_last)
        for lag, fn in enumerate(steps, 1):
            if isinstance(t, int):
                if 0 <= t - lag < LAST:
                    fn(t - lag)
                elif t - lag == LAST and lag == 1:
                    last_add()
            else:
                pl.when(t >= lag)(functools.partial(fn, t - lag))

    def behind(prev, cur, m):
        if prev is None:
            pl.when(m > 0)(lambda: mid(m - 1))
        else:
            mid(lax.rem(m + M - 1, M))
            pl.when(m < 2)(lambda: prev(m + M - 2))
        pl.when(m >= 2)(lambda: cur(m - 2))

    def phase(prev, cur, first, second=None, tick=None, ahead=None):
        def step(m, _):
            if ahead is not None:
                ahead(m)
            if tick is not None:
                tick_gen(tick + m)
            if first is not None:
                first(m)
            behind(prev, cur, m)
            if second is not None:
                second(m)
            if tick is not None:
                tick_rest(tick + m)
            return 0

        lax.fori_loop(0, M, step, 0)

    def arrived(copies):
        for cp in copies:
            cp.wait()

    end_o0 = functools.partial(finish_norm, 0, 1, N2)
    end_f0 = functools.partial(finish_norm, 1, 0, N1)
    end_o1 = functools.partial(finish_norm, 1, 1, N2, within=True)
    end_n1 = functools.partial(finish_dn2, 1)
    end_c1 = functools.partial(finish_dn1, 1)
    end_n0 = functools.partial(finish_dn2, 0)
    end_c0 = functools.partial(finish_dn1, 0)

    arrived(load_conv(0) + [load_stream(m) for m in range(M)])
    send_first_halos()
    for cp in [load_og, load_down(1)] + load_ffn(0):
        cp.start()

    conv_fwd_a(0, jnp.int32(0))
    gather_at(0)

    def o0(m, _):
        conv_fwd_b(0, m)
        pl.when(m < M - 1)(lambda: conv_fwd_a(0, m + 1))
        pl.when(m >= 2)(lambda: end_o0(m - 2))
        gather_dyn(1, m, 0)

        @pl.when(m == 0)
        def _():
            arrived([load_og, load_down(1)])

        mid(m)
        down_back(m)
        gather_dyn(1, m, 1)
        return 0

    lax.fori_loop(0, M, o0, 0)
    for cp in [load_down(0)] + load_conv(1):
        cp.start()
    arrived(load_ffn(0))

    def f0(m, _):
        agcopy(0, N2, m).wait()
        ffn_fwd(0, m)
        pl.when(m == 0)(lambda: load_down(0).wait())
        ffn_down(0, m)
        gather_dyn(2 * M + 1, m, 0)

        @pl.when(m == M - 1)
        def _():
            arrived(load_conv(1) + [tap_copy])
            conv_fwd_a(1, 0)

        pl.when(m < 2)(lambda: end_o0(m + M - 2))
        pl.when(m >= 2)(lambda: end_f0(m - 2))
        mid(m)
        gather_dyn(2 * M + 1, m, 1)
        return 0

    lax.fori_loop(0, M, f0, 0)
    for cp in load_ffn(1):
        cp.start()

    def ffn_both(m):
        agcopy(1, N2, m).wait()
        ffn_fwd(1, m)

    def o1(m, _):
        conv_fwd_b(1, m)
        pl.when(m < M - 1)(lambda: conv_fwd_a(1, m + 1))
        end_o1(m)
        pl.when(m == 1)(lambda: arrived(load_ffn(1)))
        pl.when(m >= 1)(lambda: ffn_both(m - 1))
        pl.when(m < 2)(lambda: end_f0(m + 2))
        return 0

    lax.fori_loop(0, M, o1, 0)
    agcopy(1, N2, M - 1).wait()
    ffn_fwd(1, M - 1, 0, 1)
    tick_gen(0)
    ffn_fwd(1, M - 1, 1)

    def start_c1(m):
        agcopy(1, DO, m).wait()
        conv_bwd_a(1, m)

    def last_only(fn):
        return lambda m: pl.when(m == M - 1)(lambda: fn(0))

    def next_one(fn):
        return lambda m: pl.when(m < M - 1)(lambda: fn(m + 1))

    phase(None, end_n1, lambda m: ffn_bwd(1, m), tick=1, ahead=last_only(start_c1))
    for cp in load_ffn(0):
        cp.start()
    phase(end_n1, end_c1, None, lambda m: conv_bwd_b(1, m), tick=1 + M, ahead=next_one(start_c1))
    for cp in load_conv(0):
        cp.start()
    arrived(load_ffn(0))

    def n0(m):
        ffn_bwd(0, m)

    def n0_tick(m, _):
        pl.when(m == 0)(lambda: agcopy(0, DF, 0).wait())
        pl.when(m == 1)(lambda: agcopy(0, DF, 1).wait())

        @pl.when(m == 2)
        def _():
            agcopy(0, DF, 2).wait()
            agcopy(0, DF, 3).wait()

        tick_gen(1 + 2 * M + m)
        n0(m)
        behind(end_c1, end_n0, m)
        tick_rest(1 + 2 * M + m)
        return 0

    lax.fori_loop(0, M, n0_tick, 0)
    load_down(1).start()
    load_down(1).wait()
    arrived(load_conv(0))

    def f1(m):
        agcopy(0, DO, m).wait()
        ffn_down(1, m)

    def start_c0(m):
        conv_bwd_a(0, m)

    phase(end_n0, finish_stream, f1, tick=1 + 3 * M, ahead=last_only(start_c0))

    def c0(m):
        for cp in stream_copies(m):
            cp.wait()
        conv_bwd_b(0, m)

    phase(finish_stream, end_c0, None, c0, tick=1 + 4 * M, ahead=next_one(start_c0))
    t = 1 + 5 * M
    tick_gen(t)
    mid(M - 1)
    end_c0(M - 2)
    tick_rest(t)
    tick_gen(t + 1)
    end_c0(M - 1)

    for i in range(4):
        SM[i : i + 1] = jnp.sum(GACC[i], axis=0, keepdims=True)
    SM[4:8] = jnp.zeros((4, D), f32)
    for l in range(2):
        for k in range(3):
            SM[4 + l : 5 + l, k * C : (k + 1) * C] = jnp.sum(CACC[l, k], axis=0, keepdims=True)

    def small(i):
        return remote(SM, SMR.at[i], sms.at[i], smr.at[i], [sib, *parts][i])

    small(0).start()
    tick_rest(t + 1)
    t += 2
    for i in range(4):
        tick_gen(t)
        tick_rest(t)
        t += 1
        while i == 3 and t < UNITS + 2:
            tick_rest(t)
            t += 1
        small(i).wait()
        if i == 0:
            SM[0:4] += SMR[0, 0:4]
        else:
            SM[...] += SMR[i]
        if i < 3:
            small(i + 1).start()
    own = pl.ds(pl.multiple_of(tp * C, 128), C)
    NORM_OUT[...] = SM[0:2, own]
    FFN_OUT[...] = SM[2:4, own]
    for l in range(2):
        for k in range(3):
            CONV_OUT[k, l : l + 1, :] = SM[4 + l : 5 + l, k * C : (k + 1) * C]
    small_out = [
        pltpu.make_async_copy(src, dst, load_sem.at[16 + i])
        for i, (src, dst) in enumerate(((NORM_OUT, out_norm), (FFN_OUT, out_ffn), (CONV_OUT, out_conv)))
    ]
    for cp in small_out:
        cp.start()
    last_sum()
    unit_wait(LAST)
    for cp in small_out:
        cp.wait()
    for m in range(M):
        for cp in grad_copies(m):
            cp.wait()


def fused_call(stream_in, norm_gain, win, taps, wout, ffn_gain, wgate, wup, wdown, out_grad):
    M, TOK, D = stream_in.shape
    C, F = wout.shape[1], wgate.shape[2]
    U = 384
    rb = U // 4
    ra = U - rb
    half = TOK // 2
    vm = pltpu.VMEM
    dma = pltpu.SemaphoreType.DMA
    S = SLOTS
    anys = pl.BlockSpec(memory_space=pl.ANY)
    vmem = pl.BlockSpec(memory_space=pltpu.VMEM)
    return pl.pallas_call(
        functools.partial(fused, (M, TOK, D, C, F, U)),
        out_shape=[
            jax.ShapeDtypeStruct((M, TOK, D), bf16),
            jax.ShapeDtypeStruct((M, TOK, D), bf16),
            jax.ShapeDtypeStruct((LAYERS, C), f32),
            jax.ShapeDtypeStruct((LAYERS, 3, 128, C), bf16),
            jax.ShapeDtypeStruct((3, LAYERS, C), f32),
            jax.ShapeDtypeStruct((LAYERS, C, 128), bf16),
            jax.ShapeDtypeStruct((LAYERS, C), f32),
            jax.ShapeDtypeStruct((LAYERS, 128, F), bf16),
            jax.ShapeDtypeStruct((LAYERS, 128, F), bf16),
            jax.ShapeDtypeStruct((LAYERS, F, 128), bf16),
        ],
        in_specs=[anys, vmem, anys, vmem, anys, vmem, anys, anys, anys, anys],
        out_specs=[anys] * 10,
        scratch_shapes=[
            vm((LAYERS, 4, M, TOK, D), bf16),
            vm((LAYERS, M, TOK, 3 * F + 4 * C), bf16),
            vm((D, 3 * C), bf16),
            vm((C, D), bf16),
            vm((D, 2 * F), bf16),
            vm((F, D), bf16),
            vm((M, half, D), f32),
            vm((M, half, D), f32),
            vm((M, half, 2 * LAYERS), f32),
            vm((M, TOK, D), bf16),
            vm((M, half, D), bf16),
            vm((M, half, D), bf16),
            vm((S, 8, ra, 128), bf16),
            vm((S, 8, rb, 128), bf16),
            vm((S, 4, ra, 128), bf16),
            vm((S, 2, ra, 128), bf16),
            vm((S, 1, ra, 128), bf16),
            vm((S, 4, rb, 128), bf16),
            vm((S, 2, rb, 128), bf16),
            vm((S, 1, rb, 128), bf16),
            vm((U, M * TOK), bf16),
            vm((U, 128), bf16),
            vm((128, U), bf16),
            vm((3, 128, 128), bf16),
            dma((3,)),
            dma((3,)),
            vm((8, D), f32),
            vm((TOK + 8, C), f32),
            vm((2, TOK + 8, C), f32),
            vm((TOK, C), f32),
            vm((LAYERS, M * 8, C), f32),
            vm((M, 8, C), f32),
            vm((LAYERS, M, 8, C), f32),
            vm((4, LAYERS, D), f32),
            vm((3, LAYERS, C), f32),
            vm((3, LAYERS, C), f32),
            vm((4, 8, D), f32),
            vm((LAYERS, 3, 8, C), f32),
            vm((4, 8, D), f32),
            vm((LAYERS, C), f32),
            vm((LAYERS, C), f32),
            vm((3, LAYERS, C), f32),
            dma((19,)),
            dma((M,)), dma((M,)), dma((M,)), dma((M,)), dma((M,)), dma((M,)),
            dma, dma((2,)), dma((2, LAYERS, M)), dma((2,)), dma((M + 1,)), dma((4, 5)), dma((4, 5)),
            dma((2, 3, S)), dma((2, 3, S)),
            dma((2,)), dma((M,)), dma((M,)), dma((M,)), dma((4,)), dma((4,)),
        ],
        name="fused",
        compiler_params=pltpu.CompilerParams(
            collective_id=0, has_side_effects=True, vmem_limit_bytes=VMEM_BYTES
        ),
    )(stream_in, norm_gain, win, taps, wout, ffn_gain, wgate, wup, wdown, out_grad)


def handed_on(kinds, split, *refs):
    count = len(kinds)
    srcs, dsts, bufs, wides = (refs[k * count : (k + 1) * count] for k in range(4))
    sin, sout = refs[-2:]
    chunks = [(i, k) for i in range(count) for k in (range(srcs[i].shape[0]) if i in split else (0,))]
    chunks.sort(key=lambda c: -dsts[c[0]].size * (2 if kinds[c[0]] else 1))

    def part(ref, i, k):
        return ref.at[k] if i in split else ref

    ins = [pltpu.make_async_copy(part(srcs[i], i, k), part(bufs[i], i, k), sin.at[i, k]) for i, k in chunks]
    outs = [
        pltpu.make_async_copy(part((wides if kinds[i] else bufs)[i], i, k), part(dsts[i], i, k), sout.at[i, k])
        for i, k in chunks
    ]
    for cp in ins:
        cp.start()
    for (i, k), first, second in zip(chunks, ins, outs):
        first.wait()
        if kinds[i]:
            ref, wide = bufs[i].at[k], wides[i].at[k]
            rows = 128
            lead = ref.shape[:-2]

            def step(r, _):
                cut = pl.ds(pl.multiple_of(lax.rem(r, ref.shape[-2] // rows) * rows, rows), rows)
                at = (lax.div(r, ref.shape[-2] // rows), cut) if lead else (cut,)
                wide[at] = ref[at].astype(f32)
                return 0

            lax.fori_loop(0, (lead[0] if lead else 1) * ref.shape[-2] // rows, step, 0, unroll=True)
        second.start()
    for cp in outs:
        cp.wait()


def hand_on(arrays, types):
    anys = pl.BlockSpec(memory_space=pl.ANY)
    most = max(a.shape[0] for a in arrays)
    kinds = tuple(a.dtype != t for a, t in zip(arrays, types))
    split = tuple(i for i, a in enumerate(arrays) if a.size > 16384)
    return pl.pallas_call(
        functools.partial(handed_on, kinds, split),
        out_shape=[jax.ShapeDtypeStruct(a.shape, t) for a, t in zip(arrays, types)],
        in_specs=[anys] * len(arrays),
        out_specs=[anys] * len(arrays),
        scratch_shapes=[pltpu.VMEM(a.shape, a.dtype) for a in arrays]
        + [pltpu.VMEM(a.shape if k else (8, 128), f32) for a, k in zip(arrays, kinds)]
        + [pltpu.SemaphoreType.DMA((len(arrays), most))] * 2,
        name="hand_on",
        compiler_params=pltpu.CompilerParams(vmem_limit_bytes=VMEM_BYTES),
    )(*arrays)


def body_fused(
    stream_in, norm_gain, in_proj, conv_taps, out_proj, ffn_gain, gate_proj, up_proj, down_proj, out_grad
):
    results = fused_call(
        stream_in, norm_gain, jnp.transpose(in_proj, (0, 2, 1, 3)), jnp.transpose(conv_taps, (1, 0, 2)),
        out_proj, ffn_gain, gate_proj, up_proj, down_proj, out_grad,
    )
    (out_stream, out_sgrad, norm_g, in_g, conv_g, out_g, ffn_g, gate_g, up_g, down_g) = hand_on(
        results, [bf16] + [f32] * 9
    )
    in_g = jnp.transpose(in_g, (0, 2, 1, 3))
    conv_g = jnp.transpose(conv_g, (1, 0, 2))
    return (out_stream, out_sgrad, norm_g, in_g, conv_g, out_g, ffn_g, gate_g, up_g, down_g)


def solution(mesh):
    in_specs = (
        P(None, "seq", None),
        P(),
        P(None, None, None, "tp"),
        P(None, None, "tp"),
        P(None, "tp", None),
        P(),
        P(None, None, "tp"),
        P(None, None, "tp"),
        P(None, "tp", None),
        P(None, "seq", None),
    )
    out_specs = (
        P(None, "seq", None),
        P(None, "seq", None),
        P(None, "tp"),
        P(None, "seq", None, "tp"),
        P(None, None, "tp"),
        P(None, "tp", "seq"),
        P(None, "tp"),
        P(None, "seq", "tp"),
        P(None, "seq", "tp"),
        P(None, "tp", "seq"),
    )
    chosen = body_fused if (mesh.shape["seq"], mesh.shape["tp"]) == (8, 4) else body
    return jax.shard_map(chosen, mesh=mesh, in_specs=in_specs, out_specs=out_specs, check_vma=False)
```

```python
import functools

import jax
import jax.numpy as jnp
from jax import lax
from jax.experimental import pallas as pl
from jax.experimental.pallas import tpu as pltpu
from jax.sharding import PartitionSpec as P

LAYERS = 2


EPS = 1e-05


def passed_along(block, axis, distance):
    devices = range(lax.axis_size(axis))
    route = [(i - distance, i) for i in devices if i - distance in devices]
    return lax.ppermute(block, axis, route)


def norm_rate(hidden):
    return lax.rsqrt(jnp.mean(hidden * hidden, axis=-1, keepdims=True) + EPS)


def norm_back(grad_in, gain, normed_val, rate):
    scaled = grad_in * gain
    return rate * (scaled - normed_val * jnp.mean(scaled * normed_val, axis=-1, keepdims=True))


def reduce_weights(grads):
    return (
        lax.psum_scatter(
            grads[0].astype(jnp.bfloat16), "seq", scatter_dimension=1, tiled=True
        ).astype(jnp.float32),
        lax.psum_scatter(
            grads[1].astype(jnp.bfloat16), "seq", scatter_dimension=2, tiled=True
        ).astype(jnp.float32),
        lax.psum_scatter(
            grads[2].astype(jnp.bfloat16), "seq", scatter_dimension=1, tiled=True
        ).astype(jnp.float32),
        lax.psum_scatter(
            grads[3].astype(jnp.bfloat16), "seq", scatter_dimension=1, tiled=True
        ).astype(jnp.float32),
        lax.psum_scatter(
            grads[4].astype(jnp.bfloat16), "seq", scatter_dimension=2, tiled=True
        ).astype(jnp.float32),
    )


def reduce_small(grads):
    return lax.psum((grads[0], grads[1], grads[2]), "seq")


def body(
    stream_in,
    norm_gain,
    in_proj,
    conv_taps,
    out_proj,
    ffn_gain,
    gate_proj,
    up_proj,
    down_proj,
    out_grad,
):
    f32 = jnp.float32
    bf16 = jnp.bfloat16
    width = in_proj.shape[-1]
    offset = lax.axis_index("tp") * width
    hidden = stream_in.astype(f32)
    kept = []
    for layer in range(LAYERS):
        gain_one = norm_gain[layer].astype(f32)
        gain_two = ffn_gain[layer].astype(f32)
        taps = conv_taps[layer].astype(f32)
        rate_one = norm_rate(hidden)
        normed_one = hidden * rate_one
        first = (normed_one * gain_one).astype(bf16)
        proj = jnp.einsum("msd,dkc->mskc", first, in_proj[layer], preferred_element_type=f32)
        bgate = proj[:, :, 0]
        cgate = proj[:, :, 1]
        xinput = proj[:, :, 2]
        mixed = (bgate * xinput).astype(bf16)
        prior = passed_along(mixed[:, -2:], "seq", 1)
        extended = jnp.concatenate([prior, mixed], axis=1).astype(f32)
        conved = (
            taps[0] * extended[:, :-2] + taps[1] * extended[:, 1:-1] + taps[2] * extended[:, 2:]
        )
        gated = (cgate * conved).astype(bf16)
        partial_out = jnp.einsum("msc,cd->msd", gated, out_proj[layer], preferred_element_type=f32)
        middle = hidden + lax.psum(partial_out, "tp")
        rate_two = norm_rate(middle)
        normed_two = middle * rate_two
        second = (normed_two * gain_two).astype(bf16)
        gate_val = jnp.einsum("msd,df->msf", second, gate_proj[layer], preferred_element_type=f32)
        up_val = jnp.einsum("msd,df->msf", second, up_proj[layer], preferred_element_type=f32)
        sigma = jax.nn.sigmoid(gate_val)
        silu_val = gate_val * sigma
        act = (silu_val * up_val).astype(bf16)
        partial_ffn = jnp.einsum("msf,fd->msd", act, down_proj[layer], preferred_element_type=f32)
        kept.append(
            (
                rate_one,
                normed_one,
                first,
                bgate,
                cgate,
                xinput,
                extended,
                conved,
                gated,
                rate_two,
                normed_two,
                second,
                gate_val,
                up_val,
                sigma,
                silu_val,
                act,
            )
        )
        hidden = middle + lax.psum(partial_ffn, "tp")
    grad_h = out_grad.astype(f32)
    collected = [None] * LAYERS
    for layer in reversed(range(LAYERS)):
        (
            rate_one,
            normed_one,
            first,
            bgate,
            cgate,
            xinput,
            extended,
            conved,
            gated,
            rate_two,
            normed_two,
            second,
            gate_val,
            up_val,
            sigma,
            silu_val,
            act,
        ) = kept[layer]
        gain_one = norm_gain[layer].astype(f32)
        gain_two = ffn_gain[layer].astype(f32)
        taps = conv_taps[layer].astype(f32)
        grad_f = grad_h.astype(bf16)
        grad_act = jnp.einsum("msd,fd->msf", grad_f, down_proj[layer], preferred_element_type=f32)
        down_g = jnp.einsum("msf,msd->fd", act, grad_f, preferred_element_type=f32)
        grad_gate = (grad_act * up_val * sigma * (1.0 + gate_val * (1.0 - sigma))).astype(bf16)
        grad_up = (grad_act * silu_val).astype(bf16)
        part_two = jnp.einsum(
            "msf,df->msd", grad_gate, gate_proj[layer], preferred_element_type=f32
        )
        part_two = part_two + jnp.einsum(
            "msf,df->msd", grad_up, up_proj[layer], preferred_element_type=f32
        )
        gate_g = jnp.einsum("msd,msf->df", second, grad_gate, preferred_element_type=f32)
        up_g = jnp.einsum("msd,msf->df", second, grad_up, preferred_element_type=f32)
        grad_two = lax.psum(part_two.astype(jnp.bfloat16), "tp").astype(jnp.float32)
        ffn_gain_g = jnp.sum(grad_two * normed_two, axis=(0, 1))
        grad_mid = grad_h + norm_back(grad_two, gain_two, normed_two, rate_two)
        grad_o = grad_mid.astype(bf16)
        grad_gated = jnp.einsum("msd,cd->msc", grad_o, out_proj[layer], preferred_element_type=f32)
        out_g = jnp.einsum("msc,msd->cd", gated, grad_o, preferred_element_type=f32)
        grad_conv = grad_gated * cgate
        grad_cgate = grad_gated * conved
        after = passed_along(grad_conv[:, :2], "seq", -1)
        grad_ext = jnp.concatenate([grad_conv, after], axis=1)
        grad_mixed = (
            taps[2] * grad_ext[:, :-2] + taps[1] * grad_ext[:, 1:-1] + taps[0] * grad_ext[:, 2:]
        )
        count = grad_conv.shape[1]
        conv_g = jnp.stack(
            [jnp.sum(grad_conv * extended[:, k : k + count], axis=(0, 1)) for k in range(3)], axis=0
        )
        grad_proj = jnp.stack([grad_mixed * xinput, grad_cgate, grad_mixed * bgate], axis=2).astype(
            bf16
        )
        part_one = jnp.einsum(
            "mskc,dkc->msd", grad_proj, in_proj[layer], preferred_element_type=f32
        )
        in_g = jnp.einsum("msd,mskc->dkc", first, grad_proj, preferred_element_type=f32)
        grad_one = lax.psum(part_one.astype(jnp.bfloat16), "tp").astype(jnp.float32)
        norm_gain_g = jnp.sum(grad_one * normed_one, axis=(0, 1))
        grad_h = grad_mid + norm_back(grad_one, gain_one, normed_one, rate_one)
        norm_piece = lax.dynamic_slice_in_dim(norm_gain_g, offset, width)
        ffn_piece = lax.dynamic_slice_in_dim(ffn_gain_g, offset, width)
        small = (norm_piece, conv_g, ffn_piece)
        large = (in_g, out_g, gate_g, up_g, down_g)
        collected[layer] = (small, large)
    norm_stack = jnp.stack([c[0][0] for c in collected], axis=0)
    conv_stack = jnp.stack([c[0][1] for c in collected], axis=0)
    ffn_stack = jnp.stack([c[0][2] for c in collected], axis=0)
    large_stack = tuple((jnp.stack([c[1][i] for c in collected], axis=0) for i in range(5)))
    large_stack = reduce_weights(large_stack)
    norm_stack, conv_stack, ffn_stack = reduce_small((norm_stack, conv_stack, ffn_stack))
    stream_out = hidden.astype(bf16)
    in_grad, out_grad_w, gate_grad, up_grad, down_grad = large_stack
    return (
        stream_out,
        grad_h,
        norm_stack,
        in_grad,
        conv_stack,
        out_grad_w,
        ffn_stack,
        gate_grad,
        up_grad,
        down_grad,
    )


VMEM_BYTES = 64 * 2**20
MESH = pl.DeviceIdType.MESH
f32 = jnp.float32
bf16 = jnp.bfloat16
NN = (((1,), (0,)), ((), ()))
NT = (((1,), (1,)), ((), ()))
ORDERS = ((0, 1, 2), (1, 0, 2))
SLOTS = 4
WIDE = 1024
N1, N2, DF, DO = range(4)


def rem(a, b):
    return a % b if isinstance(a, int) else lax.rem(a, b)


def div(a, b):
    return a // b if isinstance(a, int) else lax.div(a, b)


def cases(value, branches):
    for low, high, fn in branches:
        if isinstance(value, int):
            if low <= value < high:
                fn()
        else:
            pl.when((value >= low) & (value < high))(fn)


def mm(lhs, rhs, dims=NN):
    return lax.dot_general(lhs, rhs, dims, preferred_element_type=f32)


def fused(
    dims,
    stream_in, norm_gain, win, taps, wout, ffn_gain, wgate, wup, wdown, out_grad,
    out_stream, out_sgrad, out_norm, out_in, out_conv, out_out, out_ffn, out_gate, out_up, out_down,
    L, R, WIN, WOUT, WGU, WD, H, DH, RATE, PB, PR, XR,
    GA, GB, RA0, RA1, RA2, RB0, RB1, RB2, RT, FO, FT, RZ, zs, zr, SM,
    EXT, DYE, CF, HALO, HALO2, DHALO, GAIN, TAPS, TAPS2, GACC, CACC, SMR,
    NORM_OUT, FFN_OUT, CONV_OUT,
    load_sem, ps, pr, xs, xr, ags, agr, hs, dhs, hr, hs2, hr2, gs, gr, rss, rsr, fos, oss, sts, str_, sms, smr,
):
    M, TOK, D, C, F, U = dims
    half = TOK // 2
    CS, CA, CP, CZ = 0, F, 3 * F, 3 * F + 3 * C
    PER = (CZ + C) // U
    first_units = [(1, 0, 128), (1, 128, U - 128)]
    TURN = PER + 2
    table = first_units + [(1, k * U, U) for k in range(1, PER)] + [(1, PER * U, CZ + C - PER * U)]
    table += [(0, k * U, U) for k in range(PER)]
    table += [(0, k, 128) for k in range(PER * U, CZ + C, 128)]
    UNITS = len(table)
    LAST = UNITS - 1
    whole = (128, 128, 0)
    splits = {w: (w, w - w // 4, w // 4) for w in (128, 256, U)}
    seq = lax.axis_index("seq")
    tp = lax.axis_index("tp")
    n = lax.axis_size("seq")
    core = lax.rem(tp, 2)
    xi = lax.div(tp, 2)
    sib = {"seq": seq, "tp": tp + 1 - 2 * core}
    xpart = {"seq": seq, "tp": tp + 2 - 4 * xi}
    bits = [lax.rem(lax.div(seq, 1 << k), 2) for k in range(3)]
    parts = [{"seq": seq + (1 << k) - 2 * (1 << k) * bits[k], "tp": tp} for k in range(3)]
    nxt = {"seq": lax.rem(seq + 1, n), "tp": tp}
    prv = {"seq": lax.rem(seq + n - 1, n), "tp": tp}
    mine = pl.ds(pl.multiple_of(core * half, half), half)
    theirs = pl.ds(pl.multiple_of((1 - core) * half, half), half)

    def remote(src, dst, ssem, rsem, dev):
        return pltpu.make_async_remote_copy(
            src_ref=src, dst_ref=dst, send_sem=ssem, recv_sem=rsem, device_id=dev, device_id_type=MESH
        )

    def load_stream(m):
        return pltpu.make_async_copy(stream_in.at[m], L.at[0, N1, m], load_sem.at[m])

    def load_conv(l):
        return [
            pltpu.make_async_copy(win.at[l, k], WIN.at[:, pl.ds(k * C, C)], load_sem.at[4 + k])
            for k in range(3)
        ] + [pltpu.make_async_copy(wout.at[l], WOUT, load_sem.at[7])]

    def load_ffn(l):
        return [
            pltpu.make_async_copy(
                src.at[l, :, pl.ds(t * U, U)], WGU.at[:, pl.ds((2 * t + i) * U, U)], load_sem.at[10 + 2 * t + i]
            )
            for t in range(F // U)
            for i, src in enumerate((wgate, wup))
        ]

    def load_down(l):
        return pltpu.make_async_copy(wdown.at[l], WD, load_sem.at[9])

    load_og = pltpu.make_async_copy(out_grad, L.at[1, DF], load_sem.at[8])
    for cp in load_conv(0) + [load_stream(m) for m in range(M)]:
        cp.start()

    barrier = pltpu.get_barrier_semaphore()
    zcross = {"seq": n - 1 - seq + 2 * lax.rem(seq, 2) - 1, "tp": tp}
    others = [sib, xpart, nxt, prv, zcross] + parts
    for dev in others:
        pl.semaphore_signal(barrier, inc=1, device_id=dev, device_id_type=MESH)

    GAIN[0] = norm_gain[...].astype(f32)
    GAIN[1] = ffn_gain[...].astype(f32)
    GAIN[2] = 1.0 / norm_gain[...].astype(f32)
    GAIN[3] = 1.0 / ffn_gain[...].astype(f32)
    TAPS[...] = taps[...].astype(f32)
    GACC[...] = jnp.zeros_like(GACC)
    CACC[...] = jnp.zeros_like(CACC)

    pl.semaphore_wait(barrier, len(others))

    zpos, ypos = lax.div(seq, 2), lax.rem(seq, 2)
    zfar, znear = lax.rem(zpos + 2, 4), zpos + 1 - 2 * lax.rem(zpos, 2)
    strip = D // 8

    def piece(s, z):
        rows = pl.ds(pl.multiple_of(ypos * strip, strip), strip)
        if s < 3:
            return L.at[0, DO, 1 + s, rows, pl.ds(pl.multiple_of(z * TOK, TOK), TOK)]
        return L.at[0, DO, 0, pl.ds(pl.multiple_of(ypos * strip + z * (C // 8), 16), C // 8)]

    def gathers(s, step):
        def send(i, src, dst, dev):
            return remote(src, dst, gs.at[s, i], gr.at[s, i], dev)

        if step == 0:
            if s < 3:
                src = win.at[1, s, pl.ds(pl.multiple_of(zpos * TOK + ypos * strip, strip), strip)]
            else:
                src = wout.at[1, pl.ds(pl.multiple_of(ypos * strip + zpos * (C // 8), 16), C // 8)]
            return [send(0, src, piece(s, zpos), xpart)]
        if step == 1:
            return [send(1, piece(s, zpos), piece(s, zpos), parts[2])]
        if step == 2:
            return [send(2 + i, piece(s, z), piece(s, z), parts[1]) for i, z in enumerate((zpos, zfar))]
        half_ref = L.at[0, DO, (1 + s) % 4, pl.ds(pl.multiple_of(ypos * strip, strip), strip)]
        return [send(4, half_ref, half_ref, parts[0])]

    def gather_at(j):
        for s in range(4):
            for step, when in enumerate((s, s + 2, s + 4, 7 + 2 * s)):
                if j == when:
                    for cp in gathers(s, step):
                        cp.wait()
                    if step < 3:
                        for cp in gathers(s, step + 1):
                            cp.start()

    def gather_dyn(base, m, late):
        for i in range(M):
            pl.when(m == i)(functools.partial(gather_at, base + 2 * i + late))

    for s in range(4):
        for cp in gathers(s, 0):
            cp.start()
    tap_copy = remote(TAPS, TAPS2, hs2.at[1], hr2.at[M], xpart)
    tap_copy.start()

    def pcopy(m):
        return remote(PB.at[m, theirs], PR.at[m], ps.at[m], pr.at[m], sib)

    def xcopy(m):
        return remote(PB.at[m, mine], XR.at[m], xs.at[m], xr.at[m], xpart)

    def mid(m):
        pcopy(m).wait()

        def chunk(i, _):
            off = pl.multiple_of(i * 32, 32)
            rows = pl.ds(pl.multiple_of(core * half + off, 32), 32)
            got = PR[m, pl.ds(off, 32)].astype(f32) + PB[m, rows].astype(f32)
            PB[m, rows] = got.astype(bf16)
            return 0

        lax.fori_loop(0, half // 32, chunk, 0, unroll=True)
        xcopy(m).start()

    def agcopy(l, kind, m):
        ref = L.at[l, kind, m, mine]
        return remote(ref, ref, ags.at[m], agr.at[m], sib)

    def rows_loop(m, body, received=XR):
        def chunk(i, _):
            off = pl.multiple_of(i * 32, 32)
            rows = pl.ds(pl.multiple_of(core * half + off, 32), 32)
            total = PB[m, rows].astype(f32) + received[m, pl.ds(off, 32)].astype(f32)
            body(pl.ds(off, 32), rows, total)
            return 0

        lax.fori_loop(0, half // 32, chunk, 0, unroll=True)

    def rate_of(val):
        return lax.rsqrt(jnp.mean(val * val, axis=-1, keepdims=True) + EPS)

    def finish_norm(l, which, kind, m, within=False):
        if within:
            pcopy(m).wait()
        else:
            xcopy(m).wait()
        gain = GAIN[which, l : l + 1, :]

        def body(loc, rows, total):
            hid = H[m, loc] + total
            H[m, loc] = hid
            rate = rate_of(hid)
            RATE[m, loc, 2 * l + which : 2 * l + which + 1] = rate
            L[l, kind, m, rows] = (hid * rate * gain).astype(bf16)

        rows_loop(m, body, PR if within else XR)
        agcopy(l, kind, m).start()

    def stream_copies(m):
        ref = PB.at[m, mine]
        return (
            pltpu.make_async_copy(ref, out_stream.at[m, mine], oss.at[m]),
            remote(ref, out_stream.at[m, mine], sts.at[m], str_.at[m], sib),
        )

    def finish_stream(m):
        xcopy(m).wait()

        def body(loc, rows, total):
            PB[m, rows] = (H[m, loc] + total).astype(bf16)

        rows_loop(m, body)
        for cp in stream_copies(m):
            cp.start()

    def norm_back(l, which, kind, m, emit):
        xcopy(m).wait()
        gain = GAIN[which, l : l + 1, :]
        inv = GAIN[2 + which, l : l + 1, :]

        def body(loc, rows, total):
            nrm = L[l, kind, m, rows].astype(f32) * inv
            prod = total * nrm
            GACC[2 * which + l] += prod[0:8] + prod[8:16] + prod[16:24] + prod[24:32]
            mean = jnp.mean(prod * gain, axis=-1, keepdims=True)
            emit(loc, rows, RATE[m, loc, 2 * l + which : 2 * l + which + 1] * (total * gain - nrm * mean))

        rows_loop(m, body)

    def finish_dn2(l, m):
        def emit(loc, rows, delta):
            prev = L[1, DF, m, rows].astype(f32) if l == 1 else DH[m, loc]
            new = prev + delta
            DH[m, loc] = new
            L[l, DO, m, rows] = new.astype(bf16)

        norm_back(l, 1, N2, m, emit)
        agcopy(l, DO, m).start()

    def finish_dn1(l, m):
        def emit(loc, rows, delta):
            new = DH[m, loc] + delta
            if l == 1:
                DH[m, loc] = new
                L[0, DF, m, rows] = new.astype(bf16)
            else:
                PB[m, rows] = new.astype(bf16)

        norm_back(l, 0, N1, m, emit)
        if l == 1:
            agcopy(0, DF, m).start()
        else:
            for cp in grad_copies(m):
                cp.start()

    def grad_copies(m):
        return (
            pltpu.make_async_copy(PB.at[m, mine], out_sgrad.at[m, mine], oss.at[m]),
            remote(PB.at[m, mine], out_sgrad.at[m, mine], ags.at[m], agr.at[m], sib),
        )

    def put_partial(m, tile):
        def step(j, _):
            cols = pl.ds(pl.multiple_of(j * WIDE, WIDE), WIDE)
            PB[m, :, cols] = tile(cols).astype(bf16)
            return 0

        lax.fori_loop(0, D // WIDE, step, 0)
        pcopy(m).start()

    def halo_rows(m):
        return pl.ds(m * 8 if isinstance(m, int) else pl.multiple_of(m * 8, 8), 8)

    def hcopy(l, m):
        return remote(EXT.at[pl.ds(TOK, 8)], HALO.at[l, halo_rows(m)], hs, hr.at[0, l, m], nxt)

    def dhcopy(l, m):
        return remote(DYE.at[rem(m, 2), pl.ds(0, 8)], DHALO.at[l, m], dhs.at[rem(m, 2)], hr.at[1, l, m], prv)

    def hcopy2(m):
        return remote(DYE.at[1, pl.ds(TOK, 8)], HALO2.at[m], hs2.at[0], hr2.at[m], nxt)

    def tap(l, k):
        return TAPS[k, l : l + 1, :]

    def conv_of(ext, halo, taps_ref, l):
        ext[0:8] = jnp.where(seq == 0, 0.0, halo)
        t = [taps_ref[k, l : l + 1, :] for k in range(3)]
        return t[0] * ext[6 : 6 + TOK] + t[1] * ext[7 : 7 + TOK] + t[2] * ext[8 : 8 + TOK]

    def conv_now(l, m):
        return conv_of(EXT, HALO[l, halo_rows(m)], TAPS, l)

    def other_in(k):
        blocks = [L[0, DO, 1 + k, :, r * TOK : (r + 1) * TOK] for r in range(D // TOK)]
        return jnp.concatenate(blocks, axis=0)

    first_halos = remote(DYE.at[1, pl.ds(0, 8 * M)], HALO.at[0], hs, hr.at[0, 0, 0], nxt)

    def send_first_halos():
        val = jnp.concatenate([L[0, N1, m, TOK - 16 : TOK] for m in range(M)], axis=0).astype(f32)
        p = mm((val * rate_of(val) * GAIN[0, 0:1, :]).astype(bf16), WIN[...])
        bx = (p[:, 0:C] * p[:, 2 * C : 3 * C]).astype(bf16).astype(f32)
        for m in range(M):
            DYE[1, 8 * m : 8 * m + 8] = bx[16 * m + 8 : 16 * m + 16]
        first_halos.start()

    def conv_fwd_a(l, m):
        if l == 0:
            gain = GAIN[0, 0:1, :]
            hid = L[0, N1, m, mine].astype(f32)
            H[m] = hid
            RATE[m, :, 0:1] = rate_of(hid)

            def chunk(i, _):
                rows = pl.ds(pl.multiple_of(i * 32, 32), 32)
                val = L[0, N1, m, rows].astype(f32)
                L[0, N1, m, rows] = (val * rate_of(val) * gain).astype(bf16)
                return 0

            lax.fori_loop(0, TOK // 32, chunk, 0)
        else:
            agcopy(1, N1, m).wait()
        first = L[l, N1, m]
        p = mm(first, WIN[...])
        bgate, cgate, xin = p[:, 0:C], p[:, C : 2 * C], p[:, 2 * C : 3 * C]
        R[l, m, :, CP : CP + 3 * C] = p.astype(bf16)
        EXT[8 : 8 + TOK] = (bgate * xin).astype(bf16).astype(f32)
        DYE[0, 0:TOK] = cgate
        if l == 1:
            hcopy(l, m).start()
            p = mm(first, jnp.concatenate([other_in(k) for k in range(3)], axis=1))
            DYE[1, 8 : 8 + TOK] = (p[:, 0:C] * p[:, 2 * C : 3 * C]).astype(bf16).astype(f32)
            hcopy2(m).start()
            CF[...] = p[:, C : 2 * C]

    def conv_fwd_b(l, m):
        if l == 0:
            pl.when(m == 0)(lambda: first_halos.wait())
        else:
            hcopy(l, m).wait()
        gated = (DYE[0, 0:TOK] * conv_now(l, m)).astype(bf16)
        R[l, m, :, CZ : CZ + C] = gated
        if l == 0:
            put_partial(m, lambda cols: mm(R[l, m, :, CZ : CZ + C], WOUT[:, cols]))
        else:
            hcopy2(m).wait()
            L[0, DF, m, :, 0:C] = (CF[...] * conv_of(DYE.at[1], HALO2[m], TAPS2, l)).astype(bf16)
            put_partial(
                m,
                lambda cols: mm(R[l, m, :, CZ : CZ + C], WOUT[:, cols])
                + mm(L[0, DF, m, :, 0:C], L[0, DO, 0, :, cols]),
            )

    def down_back(m):
        ds = mm(L[1, DF, m], WD[...], NT).astype(bf16)
        for t in range(F // U):
            R[1, m, :, CA + (2 * t + 1) * U : CA + (2 * t + 2) * U] = ds[:, t * U : (t + 1) * U]

    def ffn_fwd(l, m, low=0, high=F // U):
        def step(t):
            off, off2 = t * U, 2 * t * U
            ab = mm(L[l, N2, m], WGU[:, pl.ds(off2, 2 * U)])
            a, b = ab[:, 0:U], ab[:, U : 2 * U]
            sig = jax.nn.sigmoid(a)
            silu = a * sig
            R[l, m, :, pl.ds(CS + off, U)] = (silu * b).astype(bf16)
            if l == 0:
                R[l, m, :, pl.ds(CA + off2, 2 * U)] = ab.astype(bf16)
            else:
                ds = R[l, m, :, pl.ds(CA + U + off2, U)].astype(f32)
                R[l, m, :, pl.ds(CA + off2, U)] = (ds * b * sig * (1.0 + a * (1.0 - sig))).astype(bf16)
                R[l, m, :, pl.ds(CA + U + off2, U)] = (ds * silu).astype(bf16)

        for t in range(low, high):
            step(t)

    def ffn_down(l, m):
        put_partial(m, lambda cols: mm(R[l, m, :, CS : CS + F], WD[:, cols]))

    def ffn_bwd(l, m):
        if l == 0:
            def step(t):
                off, off2 = t * U, 2 * t * U
                a = R[l, m, :, pl.ds(CA + off2, U)].astype(f32)
                b = R[l, m, :, pl.ds(CA + U + off2, U)].astype(f32)
                sig = jax.nn.sigmoid(a)
                ds = mm(L[l, DF, m], WD[pl.ds(off, U), :], NT)
                R[l, m, :, pl.ds(CA + off2, U)] = (ds * b * sig * (1.0 + a * (1.0 - sig))).astype(bf16)
                R[l, m, :, pl.ds(CA + U + off2, U)] = (ds * a * sig).astype(bf16)

            for t in range(F // U):
                step(t)
        put_partial(m, lambda cols: mm(R[l, m, :, CA : CA + 2 * F], WGU[cols, :], NT))

    def conv_bwd_a(l, m):
        dz = mm(L[l, DO, m], WOUT[...], NT)
        bgate = R[l, m, :, CP : CP + C].astype(f32)
        xin = R[l, m, :, CP + 2 * C : CP + 3 * C].astype(f32)
        EXT[8 : 8 + TOK] = (bgate * xin).astype(bf16).astype(f32)
        dy = dz * R[l, m, :, CP + C : CP + 2 * C].astype(f32)
        DYE[rem(m, 2), 0:TOK] = dy
        dhcopy(l, m).start()
        R[l, m, :, CP + C : CP + 2 * C] = (dz * conv_now(l, m)).astype(bf16)
        for k in range(3):
            prod = dy * EXT[6 + k : 6 + k + TOK]
            CACC[l, k] += jnp.sum(prod.reshape(TOK // 8, 8, C), axis=0)

    def conv_bwd_b(l, m):
        dhcopy(l, m).wait()
        s = rem(m, 2)
        DYE[s, TOK : TOK + 8] = jnp.where(seq == n - 1, 0.0, DHALO[l, m])
        dbx = (
            tap(l, 2) * DYE[s, 0:TOK] + tap(l, 1) * DYE[s, 1 : 1 + TOK] + tap(l, 0) * DYE[s, 2 : 2 + TOK]
        )
        bgate = R[l, m, :, CP : CP + C].astype(f32)
        xin = R[l, m, :, CP + 2 * C : CP + 3 * C].astype(f32)
        R[l, m, :, CP : CP + C] = (dbx * xin).astype(bf16)
        R[l, m, :, CP + 2 * C : CP + 3 * C] = (dbx * bgate).astype(bf16)
        put_partial(m, lambda cols: mm(R[l, m, :, CP : CP + 3 * C], WIN[cols, :], NT))

    lanes = ((GA, (RA0, RA1, RA2)), (GB, (RB0, RB1, RB2)))

    def keep(lane, step):
        b = [bits[o] for o in ORDERS[lane]]
        return [b[0] * 4, b[0] * 4 + b[1] * 2, b[0] * 4 + b[1] * 2 + b[2]][step]

    def unit_at(t):
        if isinstance(t, int):
            return table[t][:2]
        k = jnp.where(t < TURN, t - 1, t - TURN)
        return jnp.where(t < TURN, 1, 0), jnp.where(t < 2, t * 128, k * U)

    def sized(t, fn):
        if isinstance(t, int):
            fn(splits[table[t][2]])
            return
        pl.when(t == 0)(lambda: fn(splits[128]))
        pl.when((t == 1) | (t == TURN - 1))(lambda: fn(splits[256]))
        pl.when((t > 1) & (t != TURN - 1))(lambda: fn(splits[U]))

    def rs_copy(lane, step, t, rows):
        G, recv = lanes[lane]
        slot = rem(t, SLOTS)
        size = 4 >> step
        o = ORDERS[lane][step]
        off = keep(lane, step) + size - 2 * size * bits[o]
        cut = pl.ds(0, rows[1 + lane])
        return remote(
            G.at[slot, pl.ds(off, size), cut], recv[step].at[slot, :, cut],
            rss.at[lane, step, slot], rsr.at[lane, step, slot], parts[o],
        )

    def rs_gen(t):
        l, start = unit_at(t)
        kind = jnp.where(start < CA, DF, jnp.where(start < CP, N2, jnp.where(start < CZ, N1, DO)))
        slot = rem(t, SLOTS)

        def make(rows):
            wide, cut, _ = rows
            cols = pl.ds(start if isinstance(start, int) else pl.multiple_of(start, 128), wide)
            for m in range(M):
                RT[0:wide, m * TOK : (m + 1) * TOK] = R[l, m, :, cols].T

            def step(j, _):
                src = L[l, kind, :, :, pl.ds(pl.multiple_of(j * 512, 512), 512)].reshape(M * TOK, 512)
                res = mm(RT[0:wide], src).astype(bf16)
                for q in range(4):
                    lo, y = q // 2, q % 2
                    block = res[:, q * 128 : (q + 1) * 128]
                    GA[slot, y * 4 + lo * 2 + j, 0:cut] = block[:cut]
                    if cut < wide:
                        GB[slot, lo * 4 + y * 2 + j, 0 : wide - cut] = block[cut:]
                return 0

            lax.fori_loop(0, D // 512, step, 0)
            for lane in range(2):
                if rows[1 + lane]:
                    rs_copy(lane, 0, t, rows).start()

        if isinstance(t, int) and t == LAST:
            make(whole)
        else:
            sized(t, make)

    def last_copies():
        base = bits[0] * 4
        for i, (flip, dev) in enumerate(((1, parts[2]), (2, parts[1]), (3, zcross))):
            to = (bits[1] if flip < 2 else 1 - bits[1]) * 2 + (bits[2] if flip == 2 else 1 - bits[2])
            yield remote(GA.at[LAST % SLOTS, base + to, pl.ds(0, 128)], RZ.at[i], zs.at[i], zr.at[i], dev)

    def last_add():
        slot = LAST % SLOTS
        rs_copy(0, 0, LAST, whole).wait()
        base = keep(0, 0)
        for i in range(4):
            GA[slot, base + i, 0:128] = (
                GA[slot, base + i, 0:128].astype(f32) + RA0[slot, i, 0:128].astype(f32)
            ).astype(bf16)
        for cp in last_copies():
            cp.start()

    def last_sum():
        unit_wait(LAST - 1)
        for cp in last_copies():
            cp.wait()
        total = GA[LAST % SLOTS, keep(0, 2), 0:128].astype(f32) + RZ[0].astype(f32)
        FO[0:128] = (total + (RZ[1].astype(f32) + RZ[2].astype(f32))).astype(bf16)
        for cp in unit_copies(LAST, 5, 128):
            cp.start()

    def rs_add(step, t):
        slot = rem(t, SLOTS)

        def go(rows):
            for lane in range(2):
                G, recv = lanes[lane]
                rs_copy(lane, step, t, rows).wait()
                base = keep(lane, step)
                cut = rows[1 + lane]

                def add(i, _):
                    G[slot, base + i, 0:cut] = (
                        G[slot, base + i, 0:cut].astype(f32) + recv[step][slot, i, 0:cut].astype(f32)
                    ).astype(bf16)
                    return 0

                lax.fori_loop(0, 4 >> step, add, 0)
                rs_copy(lane, step + 1, t, rows).start()

        sized(t, go)

    def unit_copies(t, which, wide):
        l, start = unit_at(t)

        def at(off):
            return pl.ds(off if isinstance(off, int) else pl.multiple_of(off, 128), wide)

        tile = at(div(start - CA, 2 * U) * U)
        if which == 0:
            pairs = [(FO.at[pl.ds(0, wide)], out_down.at[l, at(start)])]
        elif which == 1:
            pairs = [(FT, out_gate.at[l, :, tile])]
        elif which == 2:
            pairs = [(FT, out_up.at[l, :, tile])]
        elif which == 3:
            pairs = [(FT.at[:, pl.ds(0, C)], out_in.at[l, 0]),
                     (FT.at[:, pl.ds(C, U - C)], out_in.at[l, 1, :, pl.ds(0, U - C)])]
        elif which == 4:
            pairs = [(FT.at[:, pl.ds(0, 2 * C - U)], out_in.at[l, 1, :, pl.ds(U - C, 2 * C - U)]),
                     (FT.at[:, pl.ds(2 * C - U, C)], out_in.at[l, 2])]
        else:
            pairs = [(FO.at[pl.ds(0, wide)], out_out.at[l, at(start - CZ)])]
        return [pltpu.make_async_copy(a, b, fos.at[i]) for i, (a, b) in enumerate(pairs)]

    def by_target(t, fn):
        if isinstance(t, int):
            _, start, wide = table[t]
            if start < CA:
                which = 0
            elif start < CP:
                which = 1 + (start - CA) // U % 2
            else:
                which = 5 if start >= CZ else 3 + (start - CP) // U
            fn(which, wide)
            return
        _, start = unit_at(t)
        pl.when(t == 0)(lambda: fn(0, 128))
        pl.when(t == 1)(lambda: fn(0, 256))
        pl.when((t > 1) & (start < CA))(lambda: fn(0, U))
        for i in range(2):
            odd = lax.rem(lax.div(start, U) + CA // U, 2) == i
            pl.when((start >= CA) & (start < CP) & odd)(functools.partial(fn, 1 + i, U))
            pl.when(start == CP + i * U)(functools.partial(fn, 3 + i, U))
        pl.when(start == CZ)(lambda: fn(5, 256))

    def unit_wait(t):
        def go(which, wide):
            for cp in unit_copies(t, which, wide):
                cp.wait()

        by_target(t, go)

    def rs_last(t):
        slot = rem(t, SLOTS)
        if isinstance(t, int):
            if t >= 1:
                unit_wait(t - 1)
        else:
            pl.when(t >= 1)(lambda: unit_wait(t - 1))

        def go(rows):
            wide, cut, _ = rows
            for lane in range(2):
                rs_copy(lane, 2, t, rows).wait()
            FO[0:cut] = (GA[slot, keep(0, 2), 0:cut].astype(f32) + RA2[slot, 0, 0:cut].astype(f32)).astype(bf16)
            FO[cut:wide] = (
                GB[slot, keep(1, 2), 0 : wide - cut].astype(f32) + RB2[slot, 0, 0 : wide - cut].astype(f32)
            ).astype(bf16)

        sized(t, go)

        def send(which, wide):
            if which in (1, 2, 3, 4):
                FT[...] = FO[...].T
            for cp in unit_copies(t, which, wide):
                cp.start()

        by_target(t, send)

    def tick_gen(t):
        if not isinstance(t, int) or t < UNITS:
            rs_gen(t)

    def tick_rest(t):
        steps = (functools.partial(rs_add, 0), functools.partial(rs_add, 1), rs_last)
        for lag, fn in enumerate(steps, 1):
            if isinstance(t, int):
                if 0 <= t - lag < LAST:
                    fn(t - lag)
                elif t - lag == LAST and lag == 1:
                    last_add()
            else:
                pl.when(t >= lag)(functools.partial(fn, t - lag))

    def behind(prev, cur, m):
        if prev is None:
            pl.when(m > 0)(lambda: mid(m - 1))
        else:
            mid(lax.rem(m + M - 1, M))
            pl.when(m < 2)(lambda: prev(m + M - 2))
        pl.when(m >= 2)(lambda: cur(m - 2))

    def phase(prev, cur, first, second=None, tick=None, ahead=None):
        def step(m, _):
            if ahead is not None:
                ahead(m)
            if tick == 1:
                pl.when(m > 0)(lambda: tick_gen(tick + m))
            elif tick is not None:
                tick_gen(tick + m)
            if first is not None:
                first(m)
            behind(prev, cur, m)
            if second is not None:
                second(m)
            if tick is not None:
                tick_rest(tick + m)
            return 0

        lax.fori_loop(0, M, step, 0)

    def arrived(copies):
        for cp in copies:
            cp.wait()

    end_o0 = functools.partial(finish_norm, 0, 1, N2)
    end_f0 = functools.partial(finish_norm, 1, 0, N1)
    end_o1 = functools.partial(finish_norm, 1, 1, N2, within=True)
    end_n1 = functools.partial(finish_dn2, 1)
    end_c1 = functools.partial(finish_dn1, 1)
    end_n0 = functools.partial(finish_dn2, 0)
    end_c0 = functools.partial(finish_dn1, 0)

    arrived(load_conv(0) + [load_stream(m) for m in range(M)])
    send_first_halos()
    for cp in [load_og, load_down(1)] + load_ffn(0):
        cp.start()

    conv_fwd_a(0, jnp.int32(0))
    gather_at(0)

    def o0(m, _):
        conv_fwd_b(0, m)
        pl.when(m < M - 1)(lambda: conv_fwd_a(0, m + 1))
        pl.when(m >= 2)(lambda: end_o0(m - 2))
        gather_dyn(1, m, 0)

        @pl.when(m == 0)
        def _():
            arrived([load_og, load_down(1)])

        mid(m)
        down_back(m)
        gather_dyn(1, m, 1)
        return 0

    lax.fori_loop(0, M, o0, 0)
    for cp in [load_down(0)] + load_conv(1):
        cp.start()
    arrived(load_ffn(0))

    def f0(m, _):
        agcopy(0, N2, m).wait()
        ffn_fwd(0, m)
        pl.when(m == 0)(lambda: load_down(0).wait())
        ffn_down(0, m)
        gather_dyn(2 * M + 1, m, 0)

        @pl.when(m == M - 1)
        def _():
            arrived(load_conv(1) + [tap_copy])
            conv_fwd_a(1, 0)

        pl.when(m < 2)(lambda: end_o0(m + M - 2))
        pl.when(m >= 2)(lambda: end_f0(m - 2))
        mid(m)
        gather_dyn(2 * M + 1, m, 1)
        return 0

    lax.fori_loop(0, M, f0, 0)
    for cp in load_ffn(1):
        cp.start()

    def ffn_both(m):
        agcopy(1, N2, m).wait()
        ffn_fwd(1, m)

    def o1(m, _):
        conv_fwd_b(1, m)
        pl.when(m < M - 1)(lambda: conv_fwd_a(1, m + 1))
        end_o1(m)
        pl.when(m == 1)(lambda: arrived(load_ffn(1)))
        pl.when(m >= 1)(lambda: ffn_both(m - 1))
        pl.when(m < 2)(lambda: end_f0(m + 2))
        return 0

    lax.fori_loop(0, M, o1, 0)
    agcopy(1, N2, M - 1).wait()
    ffn_fwd(1, M - 1, 0, 1)
    tick_gen(0)
    tick_gen(1)
    ffn_fwd(1, M - 1, 1)

    def start_c1(m):
        agcopy(1, DO, m).wait()
        conv_bwd_a(1, m)

    def last_only(fn):
        return lambda m: pl.when(m == M - 1)(lambda: fn(0))

    def next_one(fn):
        return lambda m: pl.when(m < M - 1)(lambda: fn(m + 1))

    phase(None, end_n1, lambda m: ffn_bwd(1, m), tick=1, ahead=last_only(start_c1))
    for cp in load_ffn(0):
        cp.start()
    phase(end_n1, end_c1, None, lambda m: conv_bwd_b(1, m), tick=1 + M, ahead=next_one(start_c1))
    for cp in load_conv(0):
        cp.start()
    arrived(load_ffn(0))

    def n0(m):
        ffn_bwd(0, m)

    def n0_tick(m, _):
        pl.when(m == 0)(lambda: agcopy(0, DF, 0).wait())
        pl.when(m == 1)(lambda: agcopy(0, DF, 1).wait())

        @pl.when(m == 2)
        def _():
            agcopy(0, DF, 2).wait()
            agcopy(0, DF, 3).wait()

        tick_gen(1 + 2 * M + m)
        n0(m)
        behind(end_c1, end_n0, m)
        tick_rest(1 + 2 * M + m)
        return 0

    lax.fori_loop(0, M, n0_tick, 0)
    load_down(1).start()
    load_down(1).wait()
    arrived(load_conv(0))

    def f1(m):
        agcopy(0, DO, m).wait()
        ffn_down(1, m)

    def start_c0(m):
        conv_bwd_a(0, m)

    phase(end_n0, finish_stream, f1, tick=1 + 3 * M, ahead=last_only(start_c0))

    def c0(m):
        for cp in stream_copies(m):
            cp.wait()
        conv_bwd_b(0, m)

    phase(finish_stream, end_c0, None, c0, tick=1 + 4 * M, ahead=next_one(start_c0))
    t = 1 + 5 * M
    tick_gen(t)
    mid(M - 1)
    end_c0(M - 2)
    tick_rest(t)
    tick_gen(t + 1)
    end_c0(M - 1)

    for i in range(4):
        SM[i : i + 1] = jnp.sum(GACC[i], axis=0, keepdims=True)
    SM[4:8] = jnp.zeros((4, D), f32)
    for l in range(2):
        for k in range(3):
            SM[4 + l : 5 + l, k * C : (k + 1) * C] = jnp.sum(CACC[l, k], axis=0, keepdims=True)

    def small(i):
        return remote(SM, SMR.at[i], sms.at[i], smr.at[i], [sib, *parts][i])

    small(0).start()
    tick_rest(t + 1)
    t += 2
    for i in range(4):
        tick_gen(t)
        tick_rest(t)
        t += 1
        while i == 3 and t < UNITS + 2:
            tick_rest(t)
            t += 1
        small(i).wait()
        if i == 0:
            SM[0:4] += SMR[0, 0:4]
        else:
            SM[...] += SMR[i]
        if i < 3:
            small(i + 1).start()
    own = pl.ds(pl.multiple_of(tp * C, 128), C)
    NORM_OUT[...] = SM[0:2, own]
    FFN_OUT[...] = SM[2:4, own]
    for l in range(2):
        for k in range(3):
            CONV_OUT[k, l : l + 1, :] = SM[4 + l : 5 + l, k * C : (k + 1) * C]
    small_out = [
        pltpu.make_async_copy(src, dst, load_sem.at[16 + i])
        for i, (src, dst) in enumerate(((NORM_OUT, out_norm), (FFN_OUT, out_ffn), (CONV_OUT, out_conv)))
    ]
    for cp in small_out:
        cp.start()
    last_sum()
    unit_wait(LAST)
    for cp in small_out:
        cp.wait()
    for m in range(M):
        for cp in grad_copies(m):
            cp.wait()


def fused_call(stream_in, norm_gain, win, taps, wout, ffn_gain, wgate, wup, wdown, out_grad):
    M, TOK, D = stream_in.shape
    C, F = wout.shape[1], wgate.shape[2]
    U = 384
    rb = U // 4
    ra = U - rb
    half = TOK // 2
    vm = pltpu.VMEM
    dma = pltpu.SemaphoreType.DMA
    S = SLOTS
    anys = pl.BlockSpec(memory_space=pl.ANY)
    vmem = pl.BlockSpec(memory_space=pltpu.VMEM)
    return pl.pallas_call(
        functools.partial(fused, (M, TOK, D, C, F, U)),
        out_shape=[
            jax.ShapeDtypeStruct((M, TOK, D), bf16),
            jax.ShapeDtypeStruct((M, TOK, D), bf16),
            jax.ShapeDtypeStruct((LAYERS, C), f32),
            jax.ShapeDtypeStruct((LAYERS, 3, 128, C), bf16),
            jax.ShapeDtypeStruct((3, LAYERS, C), f32),
            jax.ShapeDtypeStruct((LAYERS, C, 128), bf16),
            jax.ShapeDtypeStruct((LAYERS, C), f32),
            jax.ShapeDtypeStruct((LAYERS, 128, F), bf16),
            jax.ShapeDtypeStruct((LAYERS, 128, F), bf16),
            jax.ShapeDtypeStruct((LAYERS, F, 128), bf16),
        ],
        in_specs=[anys, vmem, anys, vmem, anys, vmem, anys, anys, anys, anys],
        out_specs=[anys] * 10,
        scratch_shapes=[
            vm((LAYERS, 4, M, TOK, D), bf16),
            vm((LAYERS, M, TOK, 3 * F + 4 * C), bf16),
            vm((D, 3 * C), bf16),
            vm((C, D), bf16),
            vm((D, 2 * F), bf16),
            vm((F, D), bf16),
            vm((M, half, D), f32),
            vm((M, half, D), f32),
            vm((M, half, 2 * LAYERS), f32),
            vm((M, TOK, D), bf16),
            vm((M, half, D), bf16),
            vm((M, half, D), bf16),
            vm((S, 8, ra, 128), bf16),
            vm((S, 8, rb, 128), bf16),
            vm((S, 4, ra, 128), bf16),
            vm((S, 2, ra, 128), bf16),
            vm((S, 1, ra, 128), bf16),
            vm((S, 4, rb, 128), bf16),
            vm((S, 2, rb, 128), bf16),
            vm((S, 1, rb, 128), bf16),
            vm((U, M * TOK), bf16),
            vm((U, 128), bf16),
            vm((128, U), bf16),
            vm((3, 128, 128), bf16),
            dma((3,)),
            dma((3,)),
            vm((8, D), f32),
            vm((TOK + 8, C), f32),
            vm((2, TOK + 8, C), f32),
            vm((TOK, C), f32),
            vm((LAYERS, M * 8, C), f32),
            vm((M, 8, C), f32),
            vm((LAYERS, M, 8, C), f32),
            vm((4, LAYERS, D), f32),
            vm((3, LAYERS, C), f32),
            vm((3, LAYERS, C), f32),
            vm((4, 8, D), f32),
            vm((LAYERS, 3, 8, C), f32),
            vm((4, 8, D), f32),
            vm((LAYERS, C), f32),
            vm((LAYERS, C), f32),
            vm((3, LAYERS, C), f32),
            dma((19,)),
            dma((M,)), dma((M,)), dma((M,)), dma((M,)), dma((M,)), dma((M,)),
            dma, dma((2,)), dma((2, LAYERS, M)), dma((2,)), dma((M + 1,)), dma((4, 5)), dma((4, 5)),
            dma((2, 3, S)), dma((2, 3, S)),
            dma((2,)), dma((M,)), dma((M,)), dma((M,)), dma((4,)), dma((4,)),
        ],
        name="fused",
        compiler_params=pltpu.CompilerParams(
            collective_id=0, has_side_effects=True, vmem_limit_bytes=VMEM_BYTES
        ),
    )(stream_in, norm_gain, win, taps, wout, ffn_gain, wgate, wup, wdown, out_grad)


def handed_on(kinds, split, *refs):
    count = len(kinds)
    srcs, dsts, bufs, wides = (refs[k * count : (k + 1) * count] for k in range(4))
    sin, sout = refs[-2:]
    chunks = [(i, k) for i in range(count) for k in (range(srcs[i].shape[0]) if i in split else (0,))]
    chunks.sort(key=lambda c: -dsts[c[0]].size * (2 if kinds[c[0]] else 1))

    def part(ref, i, k):
        return ref.at[k] if i in split else ref

    ins = [pltpu.make_async_copy(part(srcs[i], i, k), part(bufs[i], i, k), sin.at[i, k]) for i, k in chunks]
    outs = [
        pltpu.make_async_copy(part((wides if kinds[i] else bufs)[i], i, k), part(dsts[i], i, k), sout.at[i, k])
        for i, k in chunks
    ]
    for cp in ins:
        cp.start()
    for (i, k), first, second in zip(chunks, ins, outs):
        first.wait()
        if kinds[i]:
            ref, wide = bufs[i].at[k], wides[i].at[k]
            rows = 128
            lead = ref.shape[:-2]

            def step(r, _):
                cut = pl.ds(pl.multiple_of(lax.rem(r, ref.shape[-2] // rows) * rows, rows), rows)
                at = (lax.div(r, ref.shape[-2] // rows), cut) if lead else (cut,)
                wide[at] = ref[at].astype(f32)
                return 0

            lax.fori_loop(0, (lead[0] if lead else 1) * ref.shape[-2] // rows, step, 0, unroll=True)
        second.start()
    for cp in outs:
        cp.wait()


def hand_on(arrays, types):
    anys = pl.BlockSpec(memory_space=pl.ANY)
    most = max(a.shape[0] for a in arrays)
    kinds = tuple(a.dtype != t for a, t in zip(arrays, types))
    split = tuple(i for i, a in enumerate(arrays) if a.size > 16384)
    return pl.pallas_call(
        functools.partial(handed_on, kinds, split),
        out_shape=[jax.ShapeDtypeStruct(a.shape, t) for a, t in zip(arrays, types)],
        in_specs=[anys] * len(arrays),
        out_specs=[anys] * len(arrays),
        scratch_shapes=[pltpu.VMEM(a.shape, a.dtype) for a in arrays]
        + [pltpu.VMEM(a.shape if k else (8, 128), f32) for a, k in zip(arrays, kinds)]
        + [pltpu.SemaphoreType.DMA((len(arrays), most))] * 2,
        name="hand_on",
        compiler_params=pltpu.CompilerParams(vmem_limit_bytes=VMEM_BYTES),
    )(*arrays)


def body_fused(
    stream_in, norm_gain, in_proj, conv_taps, out_proj, ffn_gain, gate_proj, up_proj, down_proj, out_grad
):
    results = fused_call(
        stream_in, norm_gain, jnp.transpose(in_proj, (0, 2, 1, 3)), jnp.transpose(conv_taps, (1, 0, 2)),
        out_proj, ffn_gain, gate_proj, up_proj, down_proj, out_grad,
    )
    (out_stream, out_sgrad, norm_g, in_g, conv_g, out_g, ffn_g, gate_g, up_g, down_g) = hand_on(
        results, [bf16] + [f32] * 9
    )
    in_g = jnp.transpose(in_g, (0, 2, 1, 3))
    conv_g = jnp.transpose(conv_g, (1, 0, 2))
    return (out_stream, out_sgrad, norm_g, in_g, conv_g, out_g, ffn_g, gate_g, up_g, down_g)


def solution(mesh):
    in_specs = (
        P(None, "seq", None),
        P(),
        P(None, None, None, "tp"),
        P(None, None, "tp"),
        P(None, "tp", None),
        P(),
        P(None, None, "tp"),
        P(None, None, "tp"),
        P(None, "tp", None),
        P(None, "seq", None),
    )
    out_specs = (
        P(None, "seq", None),
        P(None, "seq", None),
        P(None, "tp"),
        P(None, "seq", None, "tp"),
        P(None, None, "tp"),
        P(None, "tp", "seq"),
        P(None, "tp"),
        P(None, "seq", "tp"),
        P(None, "seq", "tp"),
        P(None, "tp", "seq"),
    )
    chosen = body_fused if (mesh.shape["seq"], mesh.shape["tp"]) == (8, 4) else body
    return jax.shard_map(chosen, mesh=mesh, in_specs=in_specs, out_specs=out_specs, check_vma=False)
```
